32 devices in a mesh: ctx: 8 (over z, y), head: 4 (over x, core).
Axes of the slice: x: 2, y: 2, z: 4, core: 2. Of those that a mesh axis runs over, the one named last changes fastest.
Arguments:
- inputs: bfloat16 [2048, 2048], P('ctx', 'head'), may hold values from -6 to 6
- cotangent: bfloat16 [2048, 2048], P('ctx', 'head'), may hold values from -6 to 6
- w_query: float32 [2048, 2048], P('ctx', 'head'), may hold values from -0.125 to 0.125
- w_key: float32 [2048, 2048], P('ctx', 'head'), may hold values from -0.125 to 0.125
- w_value: float32 [2048, 2048], P('ctx', 'head'), may hold values from -0.125 to 0.125
- w_out: float32 [2048, 2048], P('head', 'ctx'), may hold values from -0.125 to 0.125
- w_gate: float32 [2048, 8192], P('ctx', 'head'), may hold values from -0.125 to 0.125
- w_up: float32 [2048, 8192], P('ctx', 'head'), may hold values from -0.125 to 0.125
- w_down: float32 [8192, 2048], P('head', 'ctx'), may hold values from -0.0625 to 0.0625
- query_gain: float32 [2048], P('head'), may hold values from 0.8 to 2
- key_gain: float32 [2048], P('head'), may hold values from 0.8 to 2
- attn_gain: float32 [2048], P('head'), may hold values from 0.5 to 1.5
- ffn_gain: float32 [2048], P('head'), may hold values from 0.5 to 1.5
- lengths: int32 [4], replicated, may hold values from 1 to 1824, 2048 in all
- block_order: int32 [64], replicated, may hold values from 0 to 63, as said below
Outputs:
- outputs: bfloat16 [2048, 2048], P('ctx', 'head')
- input_grad: bfloat16 [2048, 2048], P('ctx', 'head')
- grad_query: float32 [2048, 2048], P('ctx', 'head')
- grad_key: float32 [2048, 2048], P('ctx', 'head')
- grad_value: float32 [2048, 2048], P('ctx', 'head')
- grad_out: float32 [2048, 2048], P('head', 'ctx')
- grad_gate: float32 [2048, 8192], P('ctx', 'head')
- grad_up: float32 [2048, 8192], P('ctx', 'head')
- grad_down: float32 [8192, 2048], P('head', 'ctx')
- query_gain_grad: float32 [2048], P('head')
- key_gain_grad: float32 [2048], P('head')
- attn_gain_grad: float32 [2048], P('head')
- ffn_gain_grad: float32 [2048], P('head')
The draws below stay inside these ranges and needn't reach their ends.
Inputs may be any that keep to these rules, and one draw needn't show every extreme that they name: `block_order`: every value appears once. Entries j * 8 to (j + 1) * 8 - 1 (the blocks stored on index j of ctx) take every remainder modulo 2048 / 256 exactly once. `lengths`: they sum to 2048; the longest has exactly 1824 tokens.
All inputs are finite; a program needn't handle non-finite values.
Results may differ from the reference program's by a relative error of at most 0.025.
Values may be sent and summed in bfloat16 or wider, within the bound.
A program may use at most 192 MiB of HBM per device.

```python
import math
import jax
import jax.numpy as jnp
import numpy as np
from jax import lax

D = 2048
H = 16
HD = 128
FF = 8192
TOK_DEV = 256
NSEQ = 4
TOKENS = 2048
BLOCK = 32
LONGEST = 1824


def draw_block_order(key, part):
    key = jax.random.fold_in(key, 11)
    shard_count = TOKENS // TOK_DEV
    source_keys = jax.random.split(jax.random.fold_in(key, 1), shard_count)
    target_keys = jax.random.split(jax.random.fold_in(key, 2), shard_count)

    def shuffled(single):
        return jax.random.permutation(single, shard_count)
    spreads = jax.vmap(shuffled)(source_keys)
    ranking = jax.vmap(shuffled)(target_keys)
    sources = jnp.broadcast_to(jnp.arange(shard_count, dtype=jnp.int32)[:, None], (shard_count, shard_count))
    places = ranking[spreads, sources]
    return (places * shard_count + spreads).reshape(-1).astype(jnp.int32)


def levels(stream_key, shape, cuts, least, high):
    loudness = 1.0
    for axis_at, blocks in cuts:
        steps = jax.random.uniform(jax.random.fold_in(jax.random.fold_in(stream_key, 6), axis_at), (blocks,), jnp.float32, least / len(cuts), high / len(cuts))
        loudness = loudness * jnp.repeat(jnp.exp(steps), shape[axis_at] // blocks).reshape((-1,) + (1,) * (len(shape) - 1 - axis_at))
    return loudness


def profile(amount, total, reach, slope):
    weights = [(1 << 20) // math.isqrt(standing ** slope) + 1 for standing in range(2, amount + 1)]
    rest, given = total - reach - (amount - 1), [1] * (amount - 1)
    while rest > 0:
        candidates = [i for i in range(amount - 1) if given[i] < reach]
        whole, remaining = sum([weights[i] for i in candidates]), rest
        for i in candidates:
            more = min(reach - given[i], max(1, remaining * weights[i] // whole), rest)
            given[i] = given[i] + more
            rest = rest - more
    return np.array([reach] + given)


def ragged_sizes(own_key, count, total, limit, lean):
    if count == 2:
        one = jax.random.randint(own_key, (), max(1, total - limit), min(limit, total - 1) + 1)
        return jnp.stack([one, total - one])
    sizes = jnp.asarray(profile(count, total, limit, lean), jnp.int32)
    pairs = (count - 1) // 2
    donor, taker = sizes[1:1 + 2 * pairs:2], sizes[2:2 + 2 * pairs:2]
    slack = jnp.minimum(donor - 1, limit - taker)
    shifted = jax.random.randint(jax.random.fold_in(own_key, 1), (pairs,), 0, 1 << 20) % (slack + 1)
    sizes = sizes.at[1:1 + 2 * pairs:2].set(donor - shifted).at[2:2 + 2 * pairs:2].set(taker + shifted)
    return sizes[jax.random.permutation(jax.random.fold_in(own_key, 2), count)]


def bell_draw(own_key, extent, width, bound, cuts=(), held_as=jnp.bfloat16):
    values = jax.random.normal(own_key, extent, jnp.float32) * width
    if len(cuts) > 0:
        values = levels(own_key, extent, cuts, -0.22, 0.18) * values
    return jnp.clip(values, min=-bound, max=bound).astype(held_as)


def setup_inputs(seed: int = 0) -> dict:
    arg_keys = jax.random.split(jax.random.key(seed), 16)
    return {
        "inputs": bell_draw(arg_keys[0], (TOKENS, D), 1.0, 6.0, ((0, 8), (1, 4))),
        "cotangent": bell_draw(arg_keys[1], (TOKENS, D), 1.0, 6.0, ((0, 8), (1, 4))),
        "w_query": bell_draw(arg_keys[2], (D, D), D ** -0.5, 0.125, ((0, 8), (1, 4)), jnp.float32),
        "w_key": bell_draw(arg_keys[3], (D, D), D ** -0.5, 0.125, ((0, 8), (1, 4)), jnp.float32),
        "w_value": bell_draw(arg_keys[4], (D, D), D ** -0.5, 0.125, ((0, 8), (1, 4)), jnp.float32),
        "w_out": bell_draw(arg_keys[5], (D, D), D ** -0.5, 0.125, ((0, 4), (1, 8)), jnp.float32),
        "w_gate": bell_draw(arg_keys[6], (D, FF), D ** -0.5, 0.125, ((0, 8), (1, 4)), jnp.float32),
        "w_up": bell_draw(arg_keys[7], (D, FF), D ** -0.5, 0.125, ((0, 8), (1, 4)), jnp.float32),
        "w_down": bell_draw(arg_keys[8], (FF, D), FF ** -0.5, 0.0625, ((0, 4), (1, 8)), jnp.float32),
        "query_gain": jnp.clip(0.8 + 1.2 * jax.random.uniform(arg_keys[9], (D,), jnp.float32) ** levels(arg_keys[9], (D,), ((0, 4),), -0.2, 0.2), 0.8, 2.0),
        "key_gain": jnp.clip(0.8 + 1.2 * jax.random.uniform(arg_keys[10], (D,), jnp.float32) ** levels(arg_keys[10], (D,), ((0, 4),), -0.2, 0.2), 0.8, 2.0),
        "attn_gain": jnp.clip(0.5 + 1.0 * jax.random.uniform(arg_keys[11], (D,), jnp.float32) ** levels(arg_keys[11], (D,), ((0, 4),), -0.2, 0.2), 0.5, 1.5),
        "ffn_gain": jnp.clip(0.5 + 1.0 * jax.random.uniform(arg_keys[12], (D,), jnp.float32) ** levels(arg_keys[12], (D,), ((0, 4),), -0.2, 0.2), 0.5, 1.5),
        "lengths": ragged_sizes(arg_keys[13], NSEQ, TOKENS, LONGEST, 2).astype(jnp.int32),
        "block_order": draw_block_order(jax.random.fold_in(arg_keys[15], 71), 0),
    }


@jax.custom_vjp
def low(v):
    return lax.optimization_barrier(v.astype(jnp.bfloat16)).astype(jnp.float32)

@jax.custom_vjp
def low_back(v):
    return v

def low_keep(v):
    return (low(v), None)

def low_pass(kept, grad):
    return (grad,)

def back_keep(v):
    return (v, None)

def back_low(kept, grad):
    return (low(grad),)
low.defvjp(low_keep, low_pass)
low_back.defvjp(back_keep, back_low)
EPSILON = 1e-06
ROPE_THETA = 500000.0
MASKED = -1e+30
HIGHEST = lax.Precision.HIGHEST

def matmul(left, right):
    return jnp.dot(left, right, precision=HIGHEST, preferred_element_type=jnp.float32)

def sequence_tables(logical, lengths):
    seq_ends = jnp.cumsum(lengths).astype(jnp.int32)
    seq_starts = seq_ends - lengths
    number = lax.optimization_barrier(jnp.sum((logical[:, None] >= seq_ends[None, :]).astype(jnp.int32), axis=1))
    member = number[:, None] == jnp.arange(lengths.shape[0], dtype=jnp.int32)[None, :]
    offset = logical - lax.optimization_barrier(jnp.sum(jnp.where(member, seq_starts[None, :], 0), axis=1))
    return (number, offset)

def rotate(values, offset):
    half_dim = HD // 2
    inverse = jnp.power(ROPE_THETA, -jnp.arange(half_dim, dtype=jnp.float32) * 2.0 / HD)
    angles = offset.astype(jnp.float32)[:, None] * inverse[None, :]
    cosine = jnp.cos(angles)[:, None, :]
    sine_part = jnp.sin(angles)[:, None, :]
    first_half = values[..., :half_dim]
    second_half = values[..., half_dim:]
    return jnp.concatenate([first_half * cosine - second_half * sine_part, second_half * cosine + first_half * sine_part], axis=-1)

def rms_scale(values):
    return lax.rsqrt(lax.optimization_barrier(jnp.mean(values * values, axis=-1, keepdims=True)) + EPSILON)

def attend(query_rot, key_rot, value_low, number, logical):
    span_rows = math.gcd(TOKENS, 512)
    scaling = 1.0 / math.sqrt(HD)

    def one_block(pieces):
        query_piece, number_piece, logical_piece = pieces
        raw_scores = low_back(jnp.einsum('qhd,khd->hqk', query_piece, key_rot, precision=HIGHEST) * scaling)
        allowed = (number_piece[:, None] == number[None, :]) & (logical[None, :] <= logical_piece[:, None])
        probabilities = jax.nn.softmax(jnp.where(allowed[None], raw_scores, MASKED), axis=-1)
        return jnp.einsum('hqk,khd->qhd', low(probabilities), value_low, precision=HIGHEST)
    blocked = (query_rot.reshape(TOKENS // span_rows, span_rows, H, HD), number.reshape(TOKENS // span_rows, span_rows), logical.reshape(TOKENS // span_rows, span_rows))
    result = lax.map(jax.checkpoint(one_block), blocked)
    return result.reshape(TOKENS, D)

def reference(inputs, cotangent, w_query, w_key, w_value, w_out, w_gate, w_up, w_down, query_gain, key_gain, attn_gain, ffn_gain, lengths, block_order):
    logical = (block_order[:, None] * BLOCK + jnp.arange(BLOCK, dtype=jnp.int32)[None, :]).reshape(-1).astype(jnp.int32)
    number, offset = sequence_tables(logical, lengths)

    def block_forward(source, wq_arg, wk_arg, wv_arg, wo_arg, wg_arg, wu_arg, wd_arg, qg_arg, kg_arg, ag_arg, fg_arg):
        query_proj = low_back(matmul(source, low(wq_arg)))
        key_proj = low_back(matmul(source, low(wk_arg)))
        value_proj = low_back(matmul(source, low(wv_arg)))
        query_normed = query_proj * rms_scale(query_proj) * qg_arg
        key_normed = key_proj * rms_scale(key_proj) * kg_arg
        query_rot = low(rotate(query_normed.reshape(TOKENS, H, HD), offset))
        key_rot = low(rotate(key_normed.reshape(TOKENS, H, HD), offset))
        value_low = low(value_proj).reshape(TOKENS, H, HD)
        attended = low(low_back(attend(query_rot, key_rot, value_low, number, logical)))
        branch_attn = low_back(matmul(attended, low(wo_arg)))
        residual = source + branch_attn * rms_scale(branch_attn) * ag_arg
        residual_low = low(residual)
        gate_proj = low_back(matmul(residual_low, low(wg_arg)))
        up_proj = low_back(matmul(residual_low, low(wu_arg)))
        mixed_hidden = low(jax.nn.silu(gate_proj) * up_proj)
        branch_ffn = low_back(matmul(mixed_hidden, low(wd_arg)))
        return residual + branch_ffn * rms_scale(branch_ffn) * fg_arg
    result, pullback = jax.vjp(block_forward, inputs.astype(jnp.float32), w_query, w_key, w_value, w_out, w_gate, w_up, w_down, query_gain, key_gain, attn_gain, ffn_gain)
    gradients = pullback(cotangent.astype(jnp.float32))
    return (result.astype(jnp.bfloat16), gradients[0].astype(jnp.bfloat16), gradients[1], gradients[2], gradients[3], gradients[4], gradients[5], gradients[6], gradients[7], gradients[8], gradients[9], gradients[10], gradients[11])
```

```python
import math

import jax
import jax.numpy as jnp
from jax import lax
from jax.experimental import pallas as pl
from jax.experimental.pallas import tpu as pltpu
from jax.sharding import Mesh
from jax.sharding import PartitionSpec as P

D = 2048
HD = 128


EPSILON = 1e-06
ROPE_THETA = 500000.0
MASKED = -1e30


BF = jnp.bfloat16
F32 = jnp.float32
MESH = pl.DeviceIdType.MESH
AXES = ("z", "y", "x", "core")
CTX = ("z", "y")
STRIP = 16
ANY = pl.BlockSpec(memory_space=pl.ANY)
VMEM = pl.BlockSpec(memory_space=pltpu.VMEM)
DMA = pltpu.SemaphoreType.DMA
BIG_VMEM = 56 * 1024 * 1024


def place():
    return tuple(lax.axis_index(name) for name in AXES)


def greet(targets):
    barrier = pltpu.get_barrier_semaphore()
    for target in targets:
        pl.semaphore_signal(barrier, inc=1, device_id=target, device_id_type=MESH)
    pl.semaphore_wait(barrier, len(targets))


def near_first(step, z):
    high = z // 2
    low = z + high * (3 - 2 * z)
    value = (low, 1 - low, 2, 3)[step]
    return value + high * (3 - 2 * value)


def plane_axes(me):
    z, y, x, k = me
    a = x * (1 - k) + y * k
    b = y * (1 - k) + x * k

    def slot(zp, ap, bp):
        yp = bp * (1 - k) + ap * k
        xp = ap * (1 - k) + bp * k
        return zp * 4 + yp * 2 + xp

    dev_a = (z, y * (1 - k) + (1 - y) * k, (1 - x) * (1 - k) + x * k, k)
    dev_b = (z, (1 - y) * (1 - k) + y * k, x * (1 - k) + (1 - x) * k, k)
    return a, b, slot, dev_a, dev_b


def plane_neighbours(me):
    z, y, x, k = me
    up = z + 1 - 2 * (z // 3)
    down = z - 1 + 2 * ((3 - z) // 3)
    return [(z, 1 - y, x, k), (z, y, 1 - x, k)], up, down


def greet_plane(me, others=()):
    z, y, x, k = me
    barrier = pltpu.get_barrier_semaphore()
    targets = [(z, 1 - y, x, k), (z, y, 1 - x, k), *others]
    for target in targets:
        pl.semaphore_signal(barrier, inc=1, device_id=target, device_id_type=MESH)

    @pl.when(z < 3)
    def _():
        pl.semaphore_signal(barrier, inc=1, device_id=(z + 1, y, x, k), device_id_type=MESH)

    @pl.when(z > 0)
    def _():
        pl.semaphore_signal(barrier, inc=1, device_id=(z - 1, y, x, k), device_id_type=MESH)

    inner = (z + 2) // 3 - z // 3
    pl.semaphore_wait(barrier, len(targets) + 1 + inner)


GATHER_SEMS = [DMA((16,)), DMA((4,)), DMA((4,)), DMA((4,)), DMA((8,))]


def gather_plane(me, own_ref, view, sems):
    z, y, x, k = me
    recv, up_send, down_send, a_send, b_send = sems
    a, b, slot, dev_a, dev_b = plane_axes(me)
    own = slot(z, a, b)

    def copy(src, index, send_sem, device):
        return pltpu.make_async_remote_copy(
            src_ref=src,
            dst_ref=view(index),
            send_sem=send_sem,
            recv_sem=recv.at[index],
            device_id=device,
            device_id_type=MESH,
        )

    def landed(index):
        copy(view(index), index, a_send.at[0], dev_a).wait_recv()

    for step in range(5):
        if step < 4:
            zp = near_first(step, z)
            index = slot(zp, a, b)
            if step == 0:
                src = own_ref
            else:
                landed(index)
                src = view(index)

            @pl.when((zp <= z) & (z < 3))
            def _():
                copy(src, index, up_send.at[zp], (z + 1, y, x, k)).start()

            @pl.when((zp >= z) & (z > 0))
            def _():
                copy(src, index, down_send.at[zp], (z - 1, y, x, k)).start()

            copy(src, index, a_send.at[step], dev_a).start()
            copy(src, index, b_send.at[step], dev_b).start()
        if step > 0:
            index = slot(near_first(step - 1, z), 1 - a, b)
            landed(index)
            copy(view(index), index, b_send.at[3 + step], dev_b).start()
    for step in range(4):
        zp = near_first(step, z)
        landed(slot(zp, a, 1 - b))
        landed(slot(zp, 1 - a, 1 - b))
    for step in range(4):
        zp = near_first(step, z)
        for ap, number in ((a, step), (1 - a, 4 + step)):
            index = slot(zp, ap, b)
            copy(view(index), index, b_send.at[number], dev_b).wait_send()
        index = slot(zp, a, b)
        copy(view(index), index, a_send.at[step], dev_a).wait_send()

        @pl.when((zp <= z) & (z < 3))
        def _():
            copy(view(index), index, up_send.at[zp], (z + 1, y, x, k)).wait_send()

        @pl.when((zp >= z) & (z > 0))
        def _():
            copy(view(index), index, down_send.at[zp], (z - 1, y, x, k)).wait_send()


def reduce_scratch(rows, width):
    return [
        pltpu.VMEM((4, 2, rows, width), BF),
        pltpu.VMEM((4, 2, rows, width), BF),
        pltpu.VMEM((4, rows, width), BF),
        pltpu.VMEM((4, rows, width), BF),
        pltpu.VMEM((4, rows, width), BF),
        pltpu.VMEM((4, rows, width), BF),
        pltpu.VMEM((4, rows, width), BF),
        DMA((8,)),
        DMA((8,)),
        DMA((8,)),
        DMA((4,)),
        DMA((4,)),
        DMA((4,)),
        DMA((4,)),
        DMA((4,)),
    ]


def reduce_plane(me, view, rows, scratch, finish):
    z, y, x, k = me
    (mine, from_b, to_a, from_a, to_z, from_low, from_high) = scratch[:7]
    (load_sem, b_send, b_recv, a_send, a_recv, z_send, low_recv, high_recv) = scratch[7:]
    a, b, slot, dev_a, dev_b = plane_axes(me)
    order = [near_first(step, z) for step in (3, 2, 1, 0)]

    def copy_b(zp, ap):
        return pltpu.make_async_remote_copy(
            src_ref=view(slot(zp, ap, 1 - b)),
            dst_ref=from_b.at[zp, ap],
            send_sem=b_send.at[zp * 2 + ap],
            recv_sem=b_recv.at[zp * 2 + ap],
            device_id=dev_b,
            device_id_type=MESH,
        )

    def copy_a(zp):
        return pltpu.make_async_remote_copy(
            src_ref=to_a.at[zp],
            dst_ref=from_a.at[zp],
            send_sem=a_send.at[zp],
            recv_sem=a_recv.at[zp],
            device_id=dev_a,
            device_id_type=MESH,
        )

    def copy_up(zp):
        return pltpu.make_async_remote_copy(
            src_ref=to_z.at[zp],
            dst_ref=from_low.at[zp],
            send_sem=z_send.at[zp],
            recv_sem=low_recv.at[zp],
            device_id=(z + 1, y, x, k),
            device_id_type=MESH,
        )

    def copy_down(zp):
        return pltpu.make_async_remote_copy(
            src_ref=to_z.at[zp],
            dst_ref=from_high.at[zp],
            send_sem=z_send.at[zp],
            recv_sem=high_recv.at[zp],
            device_id=(z - 1, y, x, k),
            device_id_type=MESH,
        )

    def load(zp, ap):
        return pltpu.make_async_copy(
            view(slot(zp, ap, b)), mine.at[zp, ap], load_sem.at[zp * 2 + ap]
        )

    for zp in order:
        for ap in (1 - a, a):
            copy_b(zp, ap).start()
    for zp in order:
        for ap in (1 - a, a):
            load(zp, ap).start()

    def strips(work):
        def body(i, carry):
            work(pl.ds(pl.multiple_of(i * STRIP, STRIP), STRIP))
            return carry

        lax.fori_loop(0, rows // STRIP, body, 0)

    for step in range(5):
        if step < 4:
            zp = order[step]
            load(zp, 1 - a).wait()
            copy_b(zp, 1 - a).wait_recv()

            def first(strip, zp=zp):
                to_a[zp, strip] = (
                    mine[zp, 1 - a, strip].astype(F32) + from_b[zp, 1 - a, strip].astype(F32)
                ).astype(BF)

            strips(first)
            copy_a(zp).start()
        if step > 0:
            zp = order[step - 1]
            load(zp, a).wait()
            copy_b(zp, a).wait_recv()
            copy_a(zp).wait_recv()

            def own_sum(strip, zp=zp):
                return (
                    mine[zp, a, strip].astype(F32)
                    + from_b[zp, a, strip].astype(F32)
                    + from_a[zp, strip].astype(F32)
                )

            if step < 4:
                upward = zp > z

                @pl.when(upward & (z > 0))
                def _(zp=zp, own_sum=own_sum):
                    pltpu.make_async_remote_copy(
                        src_ref=to_z.at[zp],
                        dst_ref=from_low.at[zp],
                        send_sem=z_send.at[zp],
                        recv_sem=low_recv.at[zp],
                        device_id=(z, y, x, k),
                        device_id_type=MESH,
                    ).wait_recv()

                    def work(strip):
                        to_z[zp, strip] = (own_sum(strip) + from_low[zp, strip].astype(F32)).astype(BF)

                    strips(work)

                @pl.when(jnp.logical_not(upward) & (z < 3))
                def _(zp=zp, own_sum=own_sum):
                    pltpu.make_async_remote_copy(
                        src_ref=to_z.at[zp],
                        dst_ref=from_high.at[zp],
                        send_sem=z_send.at[zp],
                        recv_sem=high_recv.at[zp],
                        device_id=(z, y, x, k),
                        device_id_type=MESH,
                    ).wait_recv()

                    def work(strip):
                        to_z[zp, strip] = (own_sum(strip) + from_high[zp, strip].astype(F32)).astype(BF)

                    strips(work)

                @pl.when((z == 0) | (z == 3))
                def _(zp=zp, own_sum=own_sum):
                    def work(strip):
                        to_z[zp, strip] = own_sum(strip).astype(BF)

                    strips(work)

                @pl.when(upward)
                def _(zp=zp):
                    copy_up(zp).start()

                @pl.when(jnp.logical_not(upward))
                def _(zp=zp):
                    copy_down(zp).start()

            else:

                @pl.when(z == 0)
                def _():
                    copy_down(z).wait_recv()
                    strips(lambda s: finish(s, own_sum(s) + from_high[z, s].astype(F32)))

                @pl.when(z == 3)
                def _():
                    copy_up(z).wait_recv()
                    strips(lambda s: finish(s, own_sum(s) + from_low[z, s].astype(F32)))

                @pl.when((z > 0) & (z < 3))
                def _():
                    copy_up(z).wait_recv()
                    copy_down(z).wait_recv()
                    strips(
                        lambda s: finish(
                            s,
                            own_sum(s) + from_low[z, s].astype(F32) + from_high[z, s].astype(F32),
                        )
                    )

    def settle():
        for zp in order:
            copy_b(zp, 0).wait_send()
            copy_b(zp, 1).wait_send()
            copy_a(zp).wait_send()
        for zp in order[:3]:
            copy_up(zp).wait_send()

    return settle


def own_tile(me):
    z, y, x, k = me
    return z * 2 + y


def gather_view(out_ref, rows):
    def view(slot):
        return out_ref.at[pl.ds(pl.multiple_of(slot * rows, rows), rows), :]

    return view


def hand_out_copies(me, own_ref, out_ref, send, recv):
    z, y, x, k = me
    rows, width = own_ref.shape
    part = width // 4
    target_rows = pl.ds(pl.multiple_of(k * 2 * rows + x * rows, rows), rows)

    def copy(xt, kt, number):
        return pltpu.make_async_remote_copy(
            src_ref=own_ref.at[:, pl.ds(pl.multiple_of((2 * xt + kt) * part, part), part)],
            dst_ref=out_ref.at[target_rows, :],
            send_sem=send.at[number],
            recv_sem=recv.at[number],
            device_id=(z, y, xt, kt),
            device_id_type=MESH,
        )

    local = pltpu.make_async_copy(
        own_ref.at[:, pl.ds(pl.multiple_of((2 * x + k) * part, part), part)],
        out_ref.at[target_rows, :],
        recv.at[3],
    )
    return [copy(x, 1 - k, 0), copy(1 - x, k, 1), copy(1 - x, 1 - k, 2)], local


def pair_devices(me):
    z, y, x, k = me
    return [(z, y, x, 1 - k), (z, y, 1 - x, 1 - k)]


def row_scale(values):
    return lax.rsqrt(jnp.sum(values * values, axis=1, keepdims=True) / values.shape[1] + EPSILON)


def norm_back_strip(grad, values, gain):
    scale = row_scale(values)
    term = grad * values * scale
    weighted = grad * gain
    dot = jnp.sum(weighted * values, axis=1, keepdims=True)
    back = scale * weighted - values * (scale * scale * scale * dot / values.shape[1])
    return back, term[:8] + term[8:]


def comm_call(body, name, number, out_shape, in_specs, out_specs, scratch, cost=None):
    return pl.pallas_call(
        body,
        name=name,
        out_shape=out_shape,
        in_specs=in_specs,
        out_specs=out_specs,
        scratch_shapes=scratch,
        cost_estimate=cost,
        compiler_params=pltpu.CompilerParams(
            collective_id=number, has_side_effects=True, vmem_limit_bytes=BIG_VMEM
        ),
    )


def same_x_greet(me):
    z, y, x, k = me
    barrier = pltpu.get_barrier_semaphore()
    number = z * 4 + y * 2 + k

    def body(i, carry):
        other = lax.rem(number + i, 16)
        pl.semaphore_signal(
            barrier,
            inc=1,
            device_id=(other // 4, (other // 2) % 2, x, other % 2),
            device_id_type=MESH,
        )
        return carry

    lax.fori_loop(1, 16, body, 0)
    for kt in (k, 1 - k):
        pl.semaphore_signal(barrier, inc=1, device_id=(z, y, 1 - x, kt), device_id_type=MESH)
    pl.semaphore_wait(barrier, 17)


def open_layer(inputs, cotangent, blob, gains):
    rows, part = inputs.shape
    half = rows // 2
    quarter = half // 2

    def body(in_ref, cot_ref, blob_ref, gain_ref, full_ref, own_cot_ref, wall_ref, gains_ref, *scratch):
        shard, cot_half, pair_send, pair_recv, local_sem = scratch[:5]
        deal_send, deal_recv, share_send, share_recv, gain_send, gain_recv, cot_sems = scratch[5:12]
        gather_sems = scratch[12:]
        me = z, y, x, k = place()
        ctx = own_tile(me)
        sibling = (z, y, x, 1 - k)
        same_x_greet(me)

        def pair_copy(src, dst, number):
            columns = pl.ds(pl.multiple_of(k * part, part), part)
            remote = pltpu.make_async_remote_copy(
                src_ref=src.at[pl.ds(pl.multiple_of((1 - k) * half, half), half), :],
                dst_ref=dst.at[:, columns],
                send_sem=pair_send.at[number],
                recv_sem=pair_recv.at[number],
                device_id=sibling,
                device_id_type=MESH,
            )
            local = pltpu.make_async_copy(
                src.at[pl.ds(pl.multiple_of(k * half, half), half), :],
                dst.at[:, columns],
                local_sem.at[number],
            )
            remote.start()
            local.start()
            return remote, local

        first = pair_copy(in_ref, shard, 0)
        second = pair_copy(cot_ref, cot_half, 1)

        def deal(e):
            return pltpu.make_async_remote_copy(
                src_ref=blob_ref.at[e],
                dst_ref=wall_ref.at[:, ctx, e % 2],
                send_sem=deal_send.at[e],
                recv_sem=deal_recv.at[ctx],
                device_id=(2 * k + e // 4, (e // 2) % 2, x, e % 2),
                device_id_type=MESH,
            )

        def deal_own(e):
            return pltpu.make_async_copy(
                blob_ref.at[e], wall_ref.at[:, ctx, k], deal_recv.at[ctx]
            )

        stays = k == z // 2
        own_e = (z % 2) * 4 + y * 2 + k
        for e in range(8):

            @pl.when(jnp.logical_not(stays & (own_e == e)))
            def _(e=e):
                deal(e).start()

            @pl.when(stays & (own_e == e))
            def _(e=e):
                deal_own(e).start()

        def gain_copy(xt, kt, number):
            return pltpu.make_async_remote_copy(
                src_ref=gain_ref,
                dst_ref=gains_ref.at[:, pl.ds(pl.multiple_of((2 * x + k) * part, part), part)],
                send_sem=gain_send.at[number],
                recv_sem=gain_recv.at[number],
                device_id=(z, y, xt, kt),
                device_id_type=MESH,
            )

        gain_copies = [gain_copy(x, 1 - k, 0), gain_copy(1 - x, k, 1), gain_copy(1 - x, 1 - k, 2)]
        for copy in gain_copies:
            copy.start()
        gain_local = pltpu.make_async_copy(
            gain_ref,
            gains_ref.at[:, pl.ds(pl.multiple_of((2 * x + k) * part, part), part)],
            local_sem.at[2],
        )
        gain_local.start()

        first[0].wait_recv()
        first[1].wait()

        def view(slot):
            return full_ref.at[
                pl.ds(pl.multiple_of((slot // 2) * half, half), half),
                pl.ds(pl.multiple_of((slot % 2) * 2 * part, 2 * part), 2 * part),
            ]

        own_slot = ctx * 2 + x
        own_local = pltpu.make_async_copy(shard, view(own_slot), local_sem.at[3])
        own_local.start()
        second[0].wait_recv()
        second[1].wait()
        wide = pl.ds(pl.multiple_of(x * 2 * part, 2 * part), 2 * part)
        cot_remote = pltpu.make_async_remote_copy(
            src_ref=cot_half.at[pl.ds(pl.multiple_of((1 - x) * quarter, quarter), quarter), :],
            dst_ref=own_cot_ref.at[:, wide],
            send_sem=cot_sems.at[0],
            recv_sem=cot_sems.at[1],
            device_id=(z, y, 1 - x, k),
            device_id_type=MESH,
        )
        cot_remote.start()
        cot_local = pltpu.make_async_copy(
            cot_half.at[pl.ds(pl.multiple_of(x * quarter, quarter), quarter), :],
            own_cot_ref.at[:, wide],
            cot_sems.at[2],
        )
        cot_local.start()
        gather_plane(me, shard, view, gather_sems)
        for c in range(8):

            def wait_deal(c=c):
                pltpu.make_async_copy(
                    blob_ref.at[0], wall_ref.at[:, c, k], deal_recv.at[c]
                ).wait()

            wait_deal()
        share = pltpu.make_async_remote_copy(
            src_ref=wall_ref.at[:, :, k],
            dst_ref=wall_ref.at[:, :, k],
            send_sem=share_send,
            recv_sem=share_recv,
            device_id=sibling,
            device_id_type=MESH,
        )
        share.start()
        for e in range(8):

            @pl.when(jnp.logical_not(stays & (own_e == e)))
            def _(e=e):
                deal(e).wait_send()

        own_local.wait()
        first[0].wait_send()
        second[0].wait_send()
        for copy in gain_copies:
            copy.wait()
        gain_local.wait()
        cot_remote.wait()
        cot_local.wait()
        share.wait_send()
        pltpu.make_async_remote_copy(
            src_ref=wall_ref.at[:, :, 1 - k],
            dst_ref=wall_ref.at[:, :, 1 - k],
            send_sem=share_send,
            recv_sem=share_recv,
            device_id=sibling,
            device_id_type=MESH,
        ).wait_recv()

    shape = jax.ShapeDtypeStruct
    return comm_call(
        body,
        "open_layer",
        0,
        (
            shape((8 * half, 4 * part), BF),
            shape((quarter, 4 * part), BF),
            shape((4, 8, 2, HD, HD), BF),
            shape((4, 4 * part), F32),
        ),
        [ANY, ANY, ANY, ANY],
        (ANY, ANY, ANY, ANY),
        [
            pltpu.VMEM((half, 2 * part), BF),
            pltpu.VMEM((half, 2 * part), BF),
            DMA((2,)),
            DMA((2,)),
            DMA((4,)),
            DMA((8,)),
            DMA((8,)),
            DMA,
            DMA,
            DMA((3,)),
            DMA((3,)),
            DMA((3,)),
            *GATHER_SEMS,
        ],
    )(inputs, cotangent, blob, gains)


def plane_totals(terms, number, share=None):
    count = terms.shape[0]

    def body(*refs):
        if share is None:
            term_ref, total_ref, buffer, send, recv, local = refs
        else:
            term_ref, a_ref, b_ref, total_ref, other_ref, a_out, b_out, buffer, send, recv, local, pair_send, pair_recv = refs
        me = z, y, x, k = place()
        own = z * 4 + y * 2 + x
        barrier = pltpu.get_barrier_semaphore()

        def device(i):
            other = lax.rem(own + i, 16)
            return (other // 4, (other // 2) % 2, other % 2, k)

        def call(i, carry):
            pl.semaphore_signal(barrier, inc=1, device_id=device(i), device_id_type=MESH)
            return carry

        lax.fori_loop(1, 16, call, 0)
        sibling = (z, y, x, 1 - k)
        if share is not None:
            pl.semaphore_signal(barrier, inc=1, device_id=sibling, device_id_type=MESH)
        pl.semaphore_wait(barrier, 15 if share is None else 16)

        def copy(i):
            return pltpu.make_async_remote_copy(
                src_ref=term_ref,
                dst_ref=buffer.at[own],
                send_sem=send.at[i],
                recv_sem=recv.at[own],
                device_id=device(i),
                device_id_type=MESH,
            )

        def begin(i, carry):
            copy(i).start()
            return carry

        lax.fori_loop(1, 16, begin, 0)

        def pair(src, dst, n):
            return pltpu.make_async_remote_copy(
                src_ref=src,
                dst_ref=dst,
                send_sem=pair_send.at[n],
                recv_sem=pair_recv.at[n],
                device_id=sibling,
                device_id_type=MESH,
            )

        if share is not None:
            pairs = [pair(a_ref, a_out, 0), pair(b_ref, b_out, 1)]
            for c in pairs:
                c.start()

        total_ref[...] = term_ref[...]

        def add(i, carry):
            other = lax.rem(own + i, 16)
            pltpu.make_async_remote_copy(
                src_ref=term_ref,
                dst_ref=buffer.at[other],
                send_sem=send.at[0],
                recv_sem=recv.at[other],
                device_id=device(i),
                device_id_type=MESH,
            ).wait_recv()
            total_ref[...] += buffer[other]
            return carry

        lax.fori_loop(1, 16, add, 0)
        if share is not None:
            last = pair(total_ref.at[pl.ds(count // 2, count // 2), :], other_ref, 2)
            last.start()
            for c in (*pairs, last):
                c.wait()

        def finish(i, carry):
            copy(i).wait_send()
            return carry

        lax.fori_loop(1, 16, finish, 0)

    shape = jax.ShapeDtypeStruct
    scratch = [pltpu.VMEM((16, count, 128), F32), DMA((16,)), DMA((16,)), DMA]
    if share is None:
        return comm_call(
            body, "plane_totals", number, shape(terms.shape, F32), [VMEM], VMEM, scratch
        )(terms)
    return comm_call(
        body,
        "plane_totals_keys",
        number,
        (
            shape(terms.shape, F32),
            shape((count // 2, 128), F32),
            shape(share[0].shape, share[0].dtype),
            shape(share[1].shape, share[1].dtype),
        ),
        [VMEM, ANY, ANY],
        (VMEM, VMEM, ANY, ANY),
        [*scratch, DMA((3,)), DMA((3,))],
    )(terms, *share)


def after_attention(terms, source, gain):
    tokens, width = terms.shape
    rows = tokens // 16

    def body(term_ref, source_ref, gain_ref, full_ref, own_ref, branch_ref, shard, local, *scratch):
        me = place()
        greet_plane(me)

        def finish(strip, total):
            branch_ref[strip] = total
            h = source_ref[strip].astype(F32) + total * row_scale(total) * gain_ref[...]
            own_ref[strip] = h
            shard[strip] = h.astype(BF)

        settle = reduce_plane(me, gather_view(term_ref, rows), rows, scratch[:15], finish)
        view = gather_view(full_ref, rows)
        keep = pltpu.make_async_copy(shard, view(me[0] * 4 + me[1] * 2 + me[2]), local)
        keep.start()
        gather_plane(me, shard, view, scratch[15:])
        keep.wait()
        settle()

    shape = jax.ShapeDtypeStruct
    return comm_call(
        body,
        "after_attention",
        2,
        (shape((tokens, width), BF), shape((rows, width), F32), shape((rows, width), F32)),
        [ANY, VMEM, VMEM],
        (ANY, VMEM, VMEM),
        [pltpu.VMEM((rows, width), BF), DMA, *reduce_scratch(rows, width), *GATHER_SEMS],
    )(terms, source, gain)


def after_ffn(terms, residual, cotangent, gain):
    tokens, width = terms.shape
    rows = tokens // 16

    def body(term_ref, res_ref, cot_ref, gain_ref, full_ref, out_ref, gg_ref, shard, result, local, out_send, out_recv, *scratch):
        me = place()
        greet_plane(me, pair_devices(me))
        gg_ref[...] = jnp.zeros_like(gg_ref)

        def finish(strip, total):
            gain_row = gain_ref[...]
            out = res_ref[strip] + total * row_scale(total) * gain_row
            result[strip] = out.astype(BF)
            back, term = norm_back_strip(cot_ref[strip].astype(F32), total, gain_row)
            gg_ref[...] += term
            shard[strip] = back.astype(BF)

        settle = reduce_plane(me, gather_view(term_ref, rows), rows, scratch[:15], finish)
        view = gather_view(full_ref, rows)
        keep = pltpu.make_async_copy(shard, view(me[0] * 4 + me[1] * 2 + me[2]), local)
        keep.start()
        copies, own = hand_out_copies(me, result, out_ref, out_send, out_recv)
        for copy in copies:
            copy.start()
        own.start()
        gather_plane(me, shard, view, scratch[15:])
        keep.wait()
        settle()
        own.wait()
        for copy in copies:
            copy.wait()

    shape = jax.ShapeDtypeStruct
    return comm_call(
        body,
        "after_ffn",
        3,
        (shape((tokens, width), BF), shape((rows * 4, width // 4), BF), shape((8, width), F32)),
        [ANY, VMEM, VMEM, VMEM],
        (ANY, ANY, VMEM),
        [
            pltpu.VMEM((rows, width), BF),
            pltpu.VMEM((rows, width), BF),
            DMA,
            DMA((3,)),
            DMA((4,)),
            *reduce_scratch(rows, width),
            *GATHER_SEMS,
        ],
    )(terms, residual, cotangent, gain)


def after_ffn_back(terms, cotangent, branch, gain):
    tokens, width = terms.shape
    rows = tokens // 16

    def body(term_ref, cot_ref, branch_ref, gain_ref, full_ref, own_ref, gg_ref, shard, local, *scratch):
        me = place()
        greet_plane(me)
        gg_ref[...] = jnp.zeros_like(gg_ref)

        def finish(strip, total):
            grad = cot_ref[strip].astype(F32) + total
            own_ref[strip] = grad
            back, term = norm_back_strip(grad, branch_ref[strip], gain_ref[...])
            gg_ref[...] += term
            shard[strip] = back.astype(BF)

        settle = reduce_plane(me, gather_view(term_ref, rows), rows, scratch[:15], finish)
        view = gather_view(full_ref, rows)
        keep = pltpu.make_async_copy(shard, view(me[0] * 4 + me[1] * 2 + me[2]), local)
        keep.start()
        gather_plane(me, shard, view, scratch[15:])
        keep.wait()
        settle()

    shape = jax.ShapeDtypeStruct
    return comm_call(
        body,
        "after_ffn_back",
        4,
        (shape((tokens, width), BF), shape((rows, width), F32), shape((8, width), F32)),
        [ANY, VMEM, VMEM, VMEM],
        (ANY, VMEM, VMEM),
        [pltpu.VMEM((rows, width), BF), DMA, *reduce_scratch(rows, width), *GATHER_SEMS],
    )(terms, cotangent, branch, gain)


def close_layer(terms, grad, blob):
    tokens, width = terms.shape
    rows = tokens // 16

    def body(term_ref, grad_ref, blob_ref, out_ref, back_ref, result, out_send, out_recv, deal_send, deal_recv, *scratch):
        me = z, y, x, k = place()
        same_x_greet(me)
        head = z // 2
        number = ((z % 2) * 2 + y) * 2 + k

        def deal(c):
            return pltpu.make_async_remote_copy(
                src_ref=blob_ref.at[c],
                dst_ref=back_ref.at[number],
                send_sem=deal_send.at[c],
                recv_sem=deal_recv.at[number],
                device_id=(c // 2, c % 2, x, head),
                device_id_type=MESH,
            )

        stays = k == z // 2
        ctx = own_tile(me)
        for c in range(8):

            @pl.when(jnp.logical_not(stays & (ctx == c)))
            def _(c=c):
                deal(c).start()

            @pl.when(stays & (ctx == c))
            def _(c=c):
                pltpu.make_async_copy(
                    blob_ref.at[c], back_ref.at[number], deal_recv.at[number]
                ).start()

        def finish(strip, total):
            result[strip] = (grad_ref[strip] + total).astype(BF)

        settle = reduce_plane(me, gather_view(term_ref, rows), rows, scratch, finish)
        copies, own = hand_out_copies(me, result, out_ref, out_send, out_recv)
        for copy in copies:
            copy.start()
        own.start()
        settle()
        own.wait()
        for copy in copies:
            copy.wait()
        for c in range(8):

            @pl.when(jnp.logical_not(stays & (ctx == c)))
            def _(c=c):
                deal(c).wait_send()

            pltpu.make_async_copy(blob_ref.at[c], back_ref.at[c], deal_recv.at[c]).wait()

    shape = jax.ShapeDtypeStruct
    return comm_call(
        body,
        "close_layer",
        5,
        (shape((rows * 4, width // 4), BF), shape(blob.shape, BF)),
        [ANY, VMEM, ANY],
        (ANY, ANY),
        [
            pltpu.VMEM((rows, width), BF),
            DMA((3,)),
            DMA((4,)),
            DMA((8,)),
            DMA((8,)),
            *reduce_scratch(rows, width),
        ],
    )(terms, grad, blob)


QUERY_ROWS = 256


def masked_scores(q, keys, low, high, logical):
    raw = lax.dot_general(q, keys, (((1,), (1,)), ((), ())), preferred_element_type=F32)
    allowed = (logical >= low) & (logical <= high)
    return raw * (1.0 / math.sqrt(HD)), allowed


def attend(query, keys, values, low, high, logical):
    tokens, total = query.shape[0], keys.shape[0]

    def body(q_ref, k_ref, v_ref, low_ref, high_ref, log_ref, out_ref, lse_ref):
        raw, allowed = masked_scores(q_ref[...], k_ref[...], low_ref[...], high_ref[...], log_ref[...])
        raw = jnp.where(allowed, raw, MASKED)
        top = jnp.max(raw, axis=1, keepdims=True)
        weights = jnp.where(allowed, jnp.exp(raw - top), 0.0)
        total_weight = jnp.sum(weights, axis=1, keepdims=True)
        weights = (weights / total_weight).astype(BF)
        out_ref[...] = jnp.dot(weights, v_ref[...], preferred_element_type=F32)
        lse_ref[...] = top + jnp.log(total_weight)

    row = pl.BlockSpec((QUERY_ROWS, HD), lambda i: (i, 0))
    single = pl.BlockSpec((QUERY_ROWS, 1), lambda i: (i, 0))
    whole = pl.BlockSpec((total, HD), lambda i: (0, 0))
    line = pl.BlockSpec((1, total), lambda i: (0, 0))
    return pl.pallas_call(
        body,
        name="attend",
        grid=(tokens // QUERY_ROWS,),
        out_shape=(
            jax.ShapeDtypeStruct((tokens, HD), F32),
            jax.ShapeDtypeStruct((tokens, 1), F32),
        ),
        in_specs=[row, whole, whole, single, single, line],
        out_specs=(row, single),
        compiler_params=pltpu.CompilerParams(vmem_limit_bytes=BIG_VMEM),
    )(query, keys, values, low, high, logical)


def attend_back(query, keys, values, low, high, logical, lse, grad, delta):
    tokens, total = query.shape[0], keys.shape[0]

    def body(q_ref, k_ref, v_ref, low_ref, high_ref, log_ref, lse_ref, g_ref, d_ref, dq_ref, dk_ref, dv_ref):
        @pl.when(pl.program_id(0) == 0)
        def _():
            dk_ref[...] = jnp.zeros_like(dk_ref)
            dv_ref[...] = jnp.zeros_like(dv_ref)

        q, keys_all, g = q_ref[...], k_ref[...], g_ref[...]
        raw, allowed = masked_scores(q, keys_all, low_ref[...], high_ref[...], log_ref[...])
        weights = jnp.where(allowed, jnp.exp(raw - lse_ref[...]), 0.0)
        dp = lax.dot_general(g, v_ref[...], (((1,), (1,)), ((), ())), preferred_element_type=F32)
        ds = (weights * (dp - d_ref[...])).astype(BF)
        scaling = 1.0 / math.sqrt(HD)
        dq_ref[...] = jnp.dot(ds, keys_all, preferred_element_type=F32) * scaling
        across = (((0,), (0,)), ((), ()))
        dk_ref[...] += lax.dot_general(ds, q, across, preferred_element_type=F32) * scaling
        dv_ref[...] += lax.dot_general(weights.astype(BF), g, across, preferred_element_type=F32)

    row = pl.BlockSpec((QUERY_ROWS, HD), lambda i: (i, 0))
    single = pl.BlockSpec((QUERY_ROWS, 1), lambda i: (i, 0))
    whole = pl.BlockSpec((total, HD), lambda i: (0, 0))
    line = pl.BlockSpec((1, total), lambda i: (0, 0))
    return pl.pallas_call(
        body,
        name="attend_back",
        grid=(tokens // QUERY_ROWS,),
        out_shape=(
            jax.ShapeDtypeStruct((tokens, HD), F32),
            jax.ShapeDtypeStruct((total, HD), F32),
            jax.ShapeDtypeStruct((total, HD), F32),
        ),
        in_specs=[row, whole, whole, single, single, line, single, row, single],
        out_specs=(row, whole, whole),
        compiler_params=pltpu.CompilerParams(vmem_limit_bytes=BIG_VMEM),
    )(query, keys, values, low, high, logical, lse, grad, delta)


def rotary_tables(offset):
    half_dim = HD // 2
    inverse = jnp.power(ROPE_THETA, -jnp.arange(half_dim, dtype=F32) * 2.0 / HD)
    angles = offset.astype(F32)[:, None] * inverse[None, :]
    return jnp.cos(angles), jnp.sin(angles)


def turn(values, tables, sign):
    cosine, sine_part = tables
    first, second = values[:, : HD // 2], sign * values[:, HD // 2 :]
    return jnp.concatenate(
        [first * cosine - second * sine_part, (second * cosine + first * sine_part) * sign], axis=1
    )


def swap_cores(values):
    return lax.ppermute(values, "core", [(0, 1), (1, 0)])


def dotf(left, right, dims):
    return lax.dot_general(left, right, (dims, ((), ())), preferred_element_type=F32)


def plane_layer(
    inputs,
    cotangent,
    w_query,
    w_key,
    w_value,
    w_out,
    w_gate,
    w_up,
    w_down,
    query_gain,
    key_gain,
    attn_gain,
    ffn_gain,
    lengths,
    block_order,
):
    z, y, x, k = place()
    ctx = z * 2 + y
    tok_rows, width_part = inputs.shape
    plane_rows = tok_rows // 2
    tokens = 8 * plane_rows
    hidden = w_gate.shape[1] // 8

    order = block_order.reshape(8, 2, -1)
    block_rows = plane_rows // order.shape[2]

    def logical_of(core):
        blocks = lax.dynamic_index_in_dim(order, core, 1, keepdims=False).reshape(-1)
        return (
            blocks[:, None] * block_rows + jnp.arange(block_rows, dtype=jnp.int32)[None, :]
        ).reshape(-1)

    logical_own, logical_other = logical_of(k), logical_of(1 - k)
    offset_own = sequence_tables(logical_own, lengths)[1]
    offset_other = sequence_tables(logical_other, lengths)[1]
    tables_own, tables_other = rotary_tables(offset_own), rotary_tables(offset_other)
    low = (logical_own - offset_own)[:, None]
    high = logical_own[:, None]
    logical_keys = jnp.concatenate([logical_own, logical_other])[None, :]

    def columns(weight):
        return jnp.transpose(weight.astype(BF).reshape(2, HD, 4, HD), (2, 0, 1, 3))

    out_part = jnp.transpose(w_out.astype(BF).reshape(4, HD, 2, HD), (0, 2, 1, 3))
    blob = jnp.stack([columns(w_query), columns(w_key), columns(w_value), out_part], axis=2)
    gains = jnp.stack([query_gain, key_gain, attn_gain, ffn_gain])
    full_in, own_cot, wall, gains_full = open_layer(
        inputs, cotangent, blob.reshape(8, 4, HD, HD), gains
    )
    head = x * 8 + ctx
    attn_gain_row, ffn_gain_row = gains_full[2:3], gains_full[3:4]
    query_gain_row = lax.dynamic_slice_in_dim(gains_full[0], head * HD, HD)[None, :]
    key_gain_row = lax.dynamic_slice_in_dim(gains_full[1], head * HD, HD)[None, :]

    def ffn_columns(weight):
        return jnp.transpose(weight.astype(BF).reshape(-1, 8, hidden), (1, 0, 2))

    ffn_blob = jnp.stack(
        [
            ffn_columns(w_gate),
            ffn_columns(w_up),
            w_down.astype(BF).reshape(8, hidden, -1),
        ],
        axis=1,
    )
    ffn_mine = lax.all_to_all(ffn_blob, CTX, split_axis=0, concat_axis=0, tiled=True)
    ffn_other = swap_cores(ffn_mine)

    def up_like(i):
        return jnp.concatenate(
            [ffn_mine[:, i].reshape(D, hidden), ffn_other[:, i].reshape(D, hidden)], axis=1
        )

    gate_w, up_w = up_like(0), up_like(1)
    down_w = jnp.concatenate(
        [
            jnp.transpose(ffn_mine[:, 2], (1, 0, 2)).reshape(hidden, D),
            jnp.transpose(ffn_other[:, 2], (1, 0, 2)).reshape(hidden, D),
        ],
        axis=0,
    )

    qkv_w = wall[:3].reshape(3, D, HD)
    out_w = jnp.transpose(wall[3].reshape(16, HD, HD), (1, 0, 2)).reshape(HD, D)
    rows_dims = ((1,), (0,))
    query_proj = dotf(full_in, qkv_w[0], rows_dims)
    key_proj = dotf(full_in, qkv_w[1], rows_dims)
    value_low = dotf(full_in, qkv_w[2], rows_dims).astype(BF)
    squares = jnp.concatenate(
        [jnp.sum(query_proj * query_proj, axis=1), jnp.sum(key_proj * key_proj, axis=1)]
    ).reshape(-1, 128)
    totals, key_total_other, key_other, value_other = plane_totals(
        squares, 1, (key_proj, value_low)
    )
    totals = totals.reshape(2, tokens)
    query_scale = lax.rsqrt(totals[0] / D + EPSILON)[:, None]
    key_scale = lax.rsqrt(totals[1] / D + EPSILON)[:, None]
    key_scale_other = lax.rsqrt(key_total_other.reshape(tokens) / D + EPSILON)[:, None]
    query_rot = turn(query_proj * query_scale * query_gain_row, tables_own, 1.0).astype(BF)
    key_rot = turn(key_proj * key_scale * key_gain_row, tables_own, 1.0).astype(BF)
    key_rot_other = turn(key_other * key_scale_other * key_gain_row, tables_other, 1.0).astype(BF)
    keys_all = jnp.concatenate([key_rot, key_rot_other], axis=0)
    values_all = jnp.concatenate([value_low, value_other], axis=0)
    attended, lse = attend(query_rot, keys_all, values_all, low, high, logical_keys)
    attended_low = attended.astype(BF)
    source_own = lax.dynamic_slice_in_dim(full_in, (ctx * 2 + x) * (tokens // 16), tokens // 16)
    residual_full, residual_own, branch_own = after_attention(
        dotf(attended_low, out_w, rows_dims).astype(BF), source_own, attn_gain_row
    )

    gate_proj = dotf(residual_full, gate_w, rows_dims)
    up_proj = dotf(residual_full, up_w, rows_dims)
    gate_sigmoid = jax.nn.sigmoid(gate_proj)
    mixed = (gate_proj * gate_sigmoid * up_proj).astype(BF)
    grad_ffn, outputs, ffn_gain_term = after_ffn(
        dotf(mixed, down_w, rows_dims).astype(BF), residual_own, own_cot, ffn_gain_row
    )

    sum_rows = ((0,), (0,))
    turned = ((1,), (1,))
    grad_mixed = dotf(grad_ffn, down_w, turned)
    grad_gate = (
        grad_mixed * up_proj * gate_sigmoid * (1.0 + gate_proj * (1.0 - gate_sigmoid))
    ).astype(BF)
    grad_up = (grad_mixed * gate_proj * gate_sigmoid).astype(BF)
    resid_term = dotf(grad_gate, gate_w, turned) + dotf(grad_up, up_w, turned)
    grad_attn, grad_own, attn_gain_term = after_ffn_back(
        resid_term.astype(BF), own_cot, branch_own, attn_gain_row
    )
    gate_grad = dotf(residual_full, grad_gate, sum_rows)
    up_grad = dotf(residual_full, grad_up, sum_rows)
    down_grad = dotf(mixed, grad_ffn, sum_rows)
    mine_grads = (gate_grad[:, :hidden], up_grad[:, :hidden], down_grad[:hidden])
    other_grads = (gate_grad[:, hidden:], up_grad[:, hidden:], down_grad[hidden:])

    def ffn_stack(grads):
        return jnp.stack(
            [
                grads[0].reshape(8, -1, hidden),
                grads[1].reshape(8, -1, hidden),
                jnp.transpose(grads[2].reshape(hidden, 8, -1), (1, 0, 2)),
            ],
            axis=1,
        )

    from_other = swap_cores(ffn_stack(other_grads).astype(BF))
    ffn_sum = (ffn_stack(mine_grads) + from_other.astype(F32)).astype(BF)
    ffn_back = lax.all_to_all(ffn_sum, CTX, split_axis=0, concat_axis=0, tiled=True).astype(F32)
    grad_w_gate = jnp.transpose(ffn_back[:, 0], (1, 0, 2)).reshape(w_gate.shape)
    grad_w_up = jnp.transpose(ffn_back[:, 1], (1, 0, 2)).reshape(w_up.shape)
    grad_w_down = ffn_back[:, 2].reshape(w_down.shape)

    grad_heads = dotf(grad_attn, out_w, turned).astype(BF)
    delta = jnp.sum(grad_heads.astype(F32) * attended, axis=1, keepdims=True)
    grad_query_rot, grad_keys, grad_values = attend_back(
        query_rot, keys_all, values_all, low, high, logical_keys, lse, grad_heads, delta
    )
    both = jnp.concatenate([grad_keys[tokens:], grad_values[tokens:]], axis=1).astype(BF)
    received = swap_cores(both).astype(F32)
    grad_key_rot = grad_keys[:tokens] + received[:, :HD]
    grad_value_low = (grad_values[:tokens] + received[:, HD:]).astype(BF)
    grad_query_normed = turn(grad_query_rot, tables_own, -1.0)
    grad_key_normed = turn(grad_key_rot, tables_own, -1.0)
    query_gain_term = jnp.sum(grad_query_normed * query_proj * query_scale, axis=0)
    key_gain_term = jnp.sum(grad_key_normed * key_proj * key_scale, axis=0)
    weighted_query = grad_query_normed * query_gain_row
    weighted_key = grad_key_normed * key_gain_row
    dots = jnp.concatenate(
        [jnp.sum(weighted_query * query_proj, axis=1), jnp.sum(weighted_key * key_proj, axis=1)]
    ).reshape(-1, 128)
    dots = plane_totals(dots, 6).reshape(2, tokens, 1)
    grad_query_low = (
        query_scale * weighted_query - query_proj * (query_scale * query_scale * query_scale * dots[0] / D)
    ).astype(BF)
    grad_key_low = (
        key_scale * weighted_key - key_proj * (key_scale * key_scale * key_scale * dots[1] / D)
    ).astype(BF)
    grad_qkv = jnp.concatenate([grad_query_low, grad_key_low, grad_value_low], axis=1)
    input_term = dotf(grad_qkv, jnp.transpose(qkv_w, (1, 0, 2)).reshape(D, 3 * HD), turned)
    qkv_grad = dotf(full_in, grad_qkv, sum_rows)
    out_grad = dotf(attended_low, grad_attn, sum_rows)
    wall_grad = jnp.concatenate(
        [
            jnp.transpose(qkv_grad.reshape(8, 2, HD, 3, HD), (1, 0, 3, 2, 4)),
            jnp.transpose(out_grad.reshape(HD, 8, 2, HD), (2, 1, 0, 3))[:, :, None],
        ],
        axis=2,
    )
    to_other = lax.dynamic_index_in_dim(wall_grad, 1 - k, 0, keepdims=False).astype(BF)
    to_owner = (
        lax.dynamic_index_in_dim(wall_grad, k, 0, keepdims=False)
        + swap_cores(to_other).astype(F32)
    ).astype(BF)
    input_grad, wall_back = close_layer(input_term.astype(BF), grad_own, to_owner)
    wall_back = wall_back.astype(F32).reshape(4, 2, 4, HD, HD)

    def columns_back(i):
        return jnp.transpose(wall_back[:, :, i], (1, 2, 0, 3)).reshape(w_query.shape)

    grad_w_out = jnp.transpose(wall_back[:, :, 3], (0, 2, 1, 3)).reshape(w_out.shape)

    def all_features(term):
        return lax.dynamic_update_slice_in_dim(jnp.zeros((D,), F32), term, head * HD, 0)

    gain_totals = lax.psum(
        jnp.stack(
            [
                all_features(query_gain_term),
                all_features(key_gain_term),
                jnp.sum(attn_gain_term, axis=0),
                jnp.sum(ffn_gain_term, axis=0),
            ]
        ),
        AXES,
    )
    gain_grads = lax.dynamic_slice_in_dim(gain_totals, (2 * x + k) * width_part, width_part, 1)
    return (
        outputs,
        input_grad,
        columns_back(0),
        columns_back(1),
        columns_back(2),
        grad_w_out,
        grad_w_gate,
        grad_w_up,
        grad_w_down,
        gain_grads[0],
        gain_grads[1],
        gain_grads[2],
        gain_grads[3],
    )


def full_rows(piece):
    return lax.all_gather(piece, "head", axis=1, tiled=True)


def head_sums(term):
    return lax.psum_scatter(
        term.astype(jnp.bfloat16), "head", scatter_dimension=1, tiled=True
    ).astype(jnp.float32)


def row_single(term):
    return lax.psum(term, "head")


def row_pair(first, second):
    return lax.psum((first, second), "head")


def gather_weights(w_query, w_key, w_value, w_out, w_gate, w_up, w_down):
    row_parts = (
        lax.all_gather(w_query.astype(jnp.bfloat16), "ctx", axis=0, tiled=True),
        lax.all_gather(w_key.astype(jnp.bfloat16), "ctx", axis=0, tiled=True),
        lax.all_gather(w_value.astype(jnp.bfloat16), "ctx", axis=0, tiled=True),
        lax.all_gather(w_gate.astype(jnp.bfloat16), "ctx", axis=0, tiled=True),
        lax.all_gather(w_up.astype(jnp.bfloat16), "ctx", axis=0, tiled=True),
    )
    col_parts = (
        lax.all_gather(w_out.astype(jnp.bfloat16), "ctx", axis=1, tiled=True),
        lax.all_gather(w_down.astype(jnp.bfloat16), "ctx", axis=1, tiled=True),
    )
    return tuple(row_parts) + tuple(col_parts)


def sequence_tables(logical, lengths):
    seq_ends = jnp.cumsum(lengths)
    seq_starts = seq_ends - lengths
    number = jnp.sum((logical[:, None] >= seq_ends[None, :]).astype(jnp.int32), axis=1)
    member = number[:, None] == jnp.arange(lengths.shape[0], dtype=jnp.int32)[None, :]
    offset = logical - jnp.sum(jnp.where(member, seq_starts[None, :], 0), axis=1)
    return (number, offset)


def rotate(values, offset):
    half_dim = HD // 2
    inverse = jnp.power(ROPE_THETA, -jnp.arange(half_dim, dtype=jnp.float32) * 2.0 / HD)
    angles = offset.astype(jnp.float32)[:, None] * inverse[None, :]
    cosine = jnp.cos(angles)[:, None, :]
    sine_part = jnp.sin(angles)[:, None, :]
    first_half = values[..., :half_dim]
    second_half = values[..., half_dim:]
    return jnp.concatenate(
        [
            first_half * cosine - second_half * sine_part,
            second_half * cosine + first_half * sine_part,
        ],
        axis=-1,
    )


def norm_backward(grad_in, values, factor, gain):
    gain_term = jnp.sum(grad_in * values * factor[:, None], axis=0)
    weighted = grad_in * gain
    row_dot = row_single(jnp.sum(weighted * values, axis=1))
    grad_values = (
        factor[:, None] * weighted - values * (factor * factor * factor * row_dot / D)[:, None]
    )
    return (grad_values, gain_term)


def on_device(
    inputs,
    cotangent,
    w_query,
    w_key,
    w_value,
    w_out,
    w_gate,
    w_up,
    w_down,
    query_gain,
    key_gain,
    attn_gain,
    ffn_gain,
    lengths,
    block_order,
):
    shards = lax.axis_size("ctx")
    position = lax.axis_index("ctx")
    tok_rows, width_part = inputs.shape
    block_rows = tok_rows // shards
    total_tokens = tok_rows * shards
    local_heads = width_part // HD
    scaling = 1.0 / math.sqrt(HD)
    shard_range = jnp.arange(shards, dtype=jnp.int32)
    order_table = block_order.reshape(shards, shards)
    target = order_table % shards
    choose = target[:, :, None] == shard_range[None, None, :]
    stream = jnp.sum(jnp.where(choose, order_table[:, :, None], 0), axis=1)
    stream_blocks = jnp.transpose(stream).reshape(-1)
    logical = (
        stream_blocks[:, None] * block_rows + jnp.arange(block_rows, dtype=jnp.int32)[None, :]
    ).reshape(-1)
    own_target = lax.dynamic_index_in_dim(target, position, 0, keepdims=False)
    send_order = jnp.sum(
        jnp.where(own_target[:, None] == shard_range[None, :], shard_range[:, None], 0), axis=0
    )

    def deal_out(values):
        return values.reshape(shards, block_rows, width_part)[send_order].reshape(
            tok_rows, width_part
        )

    def undeal(values):
        return values.reshape(shards, block_rows, width_part)[own_target].reshape(
            tok_rows, width_part
        )

    local_in, local_cot = (
        lax.all_to_all(deal_out(inputs), "ctx", split_axis=0, concat_axis=0, tiled=True),
        lax.all_to_all(deal_out(cotangent), "ctx", split_axis=0, concat_axis=0, tiled=True),
    )
    number_all, offset_all = sequence_tables(logical, lengths)
    number_own = lax.dynamic_slice_in_dim(number_all, position * tok_rows, tok_rows)
    offset_own = lax.dynamic_slice_in_dim(offset_all, position * tok_rows, tok_rows)
    logical_own = lax.dynamic_slice_in_dim(logical, position * tok_rows, tok_rows)
    query_full, key_full, value_full, gate_full, up_full, out_full, down_full = gather_weights(
        w_query, w_key, w_value, w_out, w_gate, w_up, w_down
    )
    full_in = full_rows(local_in)
    query_proj = jnp.dot(full_in, query_full, preferred_element_type=jnp.float32)
    key_proj = jnp.dot(full_in, key_full, preferred_element_type=jnp.float32)
    value_proj = jnp.dot(full_in, value_full, preferred_element_type=jnp.float32)
    query_sq, key_sq = row_pair(
        jnp.sum(query_proj * query_proj, axis=1), jnp.sum(key_proj * key_proj, axis=1)
    )
    query_scale = lax.rsqrt(query_sq / D + EPSILON)
    key_scale = lax.rsqrt(key_sq / D + EPSILON)
    query_rot = rotate(
        (query_proj * query_scale[:, None] * query_gain).reshape(tok_rows, local_heads, HD),
        offset_own,
    ).astype(jnp.bfloat16)
    key_rot = rotate(
        (key_proj * key_scale[:, None] * key_gain).reshape(tok_rows, local_heads, HD), offset_own
    ).astype(jnp.bfloat16)
    value_low = value_proj.astype(jnp.bfloat16).reshape(tok_rows, local_heads, HD)
    keys_all, values_all = (
        lax.all_gather(key_rot, "ctx", axis=0, tiled=True),
        lax.all_gather(value_low, "ctx", axis=0, tiled=True),
    )
    key_span = math.gcd(total_tokens, 1024)
    key_turns = total_tokens // key_span
    pieces = (
        keys_all.reshape(key_turns, key_span, local_heads, HD),
        values_all.reshape(key_turns, key_span, local_heads, HD),
        number_all.reshape(key_turns, key_span),
        logical.reshape(key_turns, key_span),
    )

    def scores_of(key_piece, number_piece, logical_piece):
        raw_scores = (
            jnp.einsum("qhd,khd->hqk", query_rot, key_piece, preferred_element_type=jnp.float32)
            * scaling
        )
        allowed = (number_own[:, None] == number_piece[None, :]) & (
            logical_piece[None, :] <= logical_own[:, None]
        )
        return (raw_scores, allowed)

    def stat_turn(running, piece_set):
        running_max, running_sum = running
        raw_scores, allowed = scores_of(piece_set[0], piece_set[2], piece_set[3])
        masked_scores = jnp.where(allowed[None], raw_scores, MASKED)
        new_max = jnp.maximum(running_max, jnp.max(masked_scores, axis=2))
        fresh = jnp.sum(
            jnp.where(allowed[None], jnp.exp(masked_scores - new_max[..., None]), 0.0), axis=2
        )
        return ((new_max, running_sum * jnp.exp(running_max - new_max) + fresh), None)

    start_max = jnp.full((local_heads, tok_rows), MASKED, jnp.float32)
    start_sum = jnp.zeros((local_heads, tok_rows), jnp.float32)
    final_max, final_sum = lax.scan(stat_turn, (start_max, start_sum), pieces)[0]
    log_total = final_max + jnp.log(final_sum)

    def out_turn(accum, piece_set):
        raw_scores, allowed = scores_of(piece_set[0], piece_set[2], piece_set[3])
        weights_low = jnp.where(
            allowed[None], jnp.exp(raw_scores - log_total[..., None]), 0.0
        ).astype(jnp.bfloat16)
        return (
            accum
            + jnp.einsum(
                "hqk,khd->qhd", weights_low, piece_set[1], preferred_element_type=jnp.float32
            ),
            None,
        )

    attended = lax.scan(out_turn, jnp.zeros((tok_rows, local_heads, HD), jnp.float32), pieces)[0]
    attended_low = attended.reshape(tok_rows, width_part).astype(jnp.bfloat16)
    attn_part = head_sums(jnp.dot(attended_low, out_full, preferred_element_type=jnp.float32))
    attn_scale = lax.rsqrt(row_single(jnp.sum(attn_part * attn_part, axis=1)) / D + EPSILON)
    residual = local_in.astype(jnp.float32) + attn_part * attn_scale[:, None] * attn_gain
    residual_full = full_rows(residual.astype(jnp.bfloat16))
    gate_proj = jnp.dot(residual_full, gate_full, preferred_element_type=jnp.float32)
    up_proj = jnp.dot(residual_full, up_full, preferred_element_type=jnp.float32)
    gate_sigmoid = jax.nn.sigmoid(gate_proj)
    mixed_hidden = (gate_proj * gate_sigmoid * up_proj).astype(jnp.bfloat16)
    ffn_part = head_sums(jnp.dot(mixed_hidden, down_full, preferred_element_type=jnp.float32))
    ffn_scale = lax.rsqrt(row_single(jnp.sum(ffn_part * ffn_part, axis=1)) / D + EPSILON)
    result = residual + ffn_part * ffn_scale[:, None] * ffn_gain
    query_full, key_full, value_full, gate_full, up_full, out_full, down_full = gather_weights(
        w_query, w_key, w_value, w_out, w_gate, w_up, w_down
    )
    grad_result = local_cot.astype(jnp.float32)
    grad_ffn, ffn_gain_term = norm_backward(grad_result, ffn_part, ffn_scale, ffn_gain)
    grad_ffn_low = full_rows(grad_ffn.astype(jnp.bfloat16))
    down_grad = jnp.einsum(
        "tf,td->fd", mixed_hidden, grad_ffn_low, preferred_element_type=jnp.float32
    )
    grad_mixed = jnp.einsum(
        "td,fd->tf", grad_ffn_low, down_full, preferred_element_type=jnp.float32
    )
    grad_gate_low = (
        grad_mixed * up_proj * gate_sigmoid * (1.0 + gate_proj * (1.0 - gate_sigmoid))
    ).astype(jnp.bfloat16)
    grad_up_low = (grad_mixed * gate_proj * gate_sigmoid).astype(jnp.bfloat16)
    gate_grad = jnp.einsum(
        "td,tf->df", residual_full, grad_gate_low, preferred_element_type=jnp.float32
    )
    up_grad = jnp.einsum(
        "td,tf->df", residual_full, grad_up_low, preferred_element_type=jnp.float32
    )
    resid_term = jnp.einsum(
        "tf,df->td", grad_gate_low, gate_full, preferred_element_type=jnp.float32
    ) + jnp.einsum("tf,df->td", grad_up_low, up_full, preferred_element_type=jnp.float32)
    grad_residual = grad_result + head_sums(resid_term)
    grad_attn, attn_gain_term = norm_backward(grad_residual, attn_part, attn_scale, attn_gain)
    grad_attn_low = full_rows(grad_attn.astype(jnp.bfloat16))
    out_grad = jnp.einsum(
        "te,td->ed", attended_low, grad_attn_low, preferred_element_type=jnp.float32
    )
    grad_heads = (
        jnp.einsum("td,ed->te", grad_attn_low, out_full, preferred_element_type=jnp.float32)
        .astype(jnp.bfloat16)
        .reshape(tok_rows, local_heads, HD)
    )
    row_delta = jnp.transpose(jnp.sum(grad_heads.astype(jnp.float32) * attended, axis=2))

    def score_grads(key_piece, value_piece, number_piece, logical_piece):
        raw_scores, allowed = scores_of(key_piece, number_piece, logical_piece)
        probabilities = jnp.where(allowed[None], jnp.exp(raw_scores - log_total[..., None]), 0.0)
        grad_probs = jnp.einsum(
            "qhd,khd->hqk", grad_heads, value_piece, preferred_element_type=jnp.float32
        )
        grad_scores = (probabilities * (grad_probs - row_delta[..., None])).astype(jnp.bfloat16)
        return (probabilities, grad_scores)

    zero_heads = jnp.zeros((tok_rows, local_heads, HD), jnp.float32)

    def back_turn(grad_acc, piece_set):
        key_piece, value_piece, number_piece, logical_piece = piece_set
        probabilities, grad_scores = score_grads(
            key_piece, value_piece, number_piece, logical_piece
        )
        grad_acc = (
            grad_acc
            + jnp.einsum("hqk,khd->qhd", grad_scores, key_piece, preferred_element_type=jnp.float32)
            * scaling
        )
        key_term = (
            jnp.einsum("hqk,qhd->khd", grad_scores, query_rot, preferred_element_type=jnp.float32)
            * scaling
        )
        value_term = jnp.einsum(
            "hqk,qhd->khd",
            probabilities.astype(jnp.bfloat16),
            grad_heads,
            preferred_element_type=jnp.float32,
        )
        return (grad_acc, (key_term, value_term))

    grad_query_rot, key_value_terms = lax.scan(back_turn, zero_heads, pieces)
    key_terms = key_value_terms[0].reshape(total_tokens, local_heads, HD)
    value_terms = key_value_terms[1].reshape(total_tokens, local_heads, HD)
    grad_key_rot, grad_value_own = (
        lax.psum_scatter(
            key_terms.astype(jnp.bfloat16), "ctx", scatter_dimension=0, tiled=True
        ).astype(jnp.float32),
        lax.psum_scatter(
            value_terms.astype(jnp.bfloat16), "ctx", scatter_dimension=0, tiled=True
        ).astype(jnp.float32),
    )
    grad_query_normed = rotate(grad_query_rot, -offset_own).reshape(tok_rows, width_part)
    grad_key_normed = rotate(grad_key_rot, -offset_own).reshape(tok_rows, width_part)
    query_gain_term = jnp.sum(grad_query_normed * query_proj * query_scale[:, None], axis=0)
    key_gain_term = jnp.sum(grad_key_normed * key_proj * key_scale[:, None], axis=0)
    weighted_query = grad_query_normed * query_gain
    weighted_key = grad_key_normed * key_gain
    query_dot, key_dot = row_pair(
        jnp.sum(weighted_query * query_proj, axis=1), jnp.sum(weighted_key * key_proj, axis=1)
    )
    grad_query_low = (
        query_scale[:, None] * weighted_query
        - query_proj * (query_scale * query_scale * query_scale * query_dot / D)[:, None]
    ).astype(jnp.bfloat16)
    grad_key_low = (
        key_scale[:, None] * weighted_key
        - key_proj * (key_scale * key_scale * key_scale * key_dot / D)[:, None]
    ).astype(jnp.bfloat16)
    grad_value_low = grad_value_own.reshape(tok_rows, width_part).astype(jnp.bfloat16)
    query_grad = jnp.einsum(
        "td,te->de", full_in, grad_query_low, preferred_element_type=jnp.float32
    )
    key_grad = jnp.einsum("td,te->de", full_in, grad_key_low, preferred_element_type=jnp.float32)
    value_grad = jnp.einsum(
        "td,te->de", full_in, grad_value_low, preferred_element_type=jnp.float32
    )
    input_term = jnp.einsum(
        "te,de->td", grad_query_low, query_full, preferred_element_type=jnp.float32
    )
    input_term = input_term + jnp.einsum(
        "te,de->td", grad_key_low, key_full, preferred_element_type=jnp.float32
    )
    input_term = input_term + jnp.einsum(
        "te,de->td", grad_value_low, value_full, preferred_element_type=jnp.float32
    )
    grad_input = grad_residual + head_sums(input_term)
    row_grads = (
        lax.psum_scatter(
            query_grad.astype(jnp.bfloat16), "ctx", scatter_dimension=0, tiled=True
        ).astype(jnp.float32),
        lax.psum_scatter(
            key_grad.astype(jnp.bfloat16), "ctx", scatter_dimension=0, tiled=True
        ).astype(jnp.float32),
        lax.psum_scatter(
            value_grad.astype(jnp.bfloat16), "ctx", scatter_dimension=0, tiled=True
        ).astype(jnp.float32),
        lax.psum_scatter(
            gate_grad.astype(jnp.bfloat16), "ctx", scatter_dimension=0, tiled=True
        ).astype(jnp.float32),
        lax.psum_scatter(
            up_grad.astype(jnp.bfloat16), "ctx", scatter_dimension=0, tiled=True
        ).astype(jnp.float32),
    )
    col_grads = (
        lax.psum_scatter(
            out_grad.astype(jnp.bfloat16), "ctx", scatter_dimension=1, tiled=True
        ).astype(jnp.float32),
        lax.psum_scatter(
            down_grad.astype(jnp.bfloat16), "ctx", scatter_dimension=1, tiled=True
        ).astype(jnp.float32),
    )
    gain_totals = lax.psum((query_gain_term, key_gain_term, attn_gain_term, ffn_gain_term), "ctx")
    back_result, back_grad = (
        lax.all_to_all(result.astype(jnp.bfloat16), "ctx", split_axis=0, concat_axis=0, tiled=True),
        lax.all_to_all(
            grad_input.astype(jnp.bfloat16), "ctx", split_axis=0, concat_axis=0, tiled=True
        ),
    )
    return (
        undeal(back_result),
        undeal(back_grad),
        row_grads[0],
        row_grads[1],
        row_grads[2],
        col_grads[0],
        row_grads[3],
        row_grads[4],
        col_grads[1],
        gain_totals[0],
        gain_totals[1],
        gain_totals[2],
        gain_totals[3],
    )


def sharded(layer, mesh, ctx, head):
    wide, tall, line = P(ctx, head), P(head, ctx), P(head)
    return jax.shard_map(
        layer,
        mesh=mesh,
        in_specs=(
            *(wide,) * 5,
            tall,
            wide,
            wide,
            tall,
            *(line,) * 4,
            P(),
            P(),
        ),
        out_specs=(*(wide,) * 5, tall, wide, wide, tall, *(line,) * 4),
        check_vma=False,
    )


def solution(mesh):
    if dict(mesh.shape) == {"ctx": 8, "head": 4}:
        split = Mesh(mesh.devices.reshape(4, 2, 2, 2), AXES)
        return sharded(plane_layer, split, CTX, ("x", "core"))
    return sharded(on_device, mesh, "ctx", "head")
```

```python
import math

import jax
import jax.numpy as jnp
from jax import lax
from jax.experimental import pallas as pl
from jax.experimental.pallas import tpu as pltpu
from jax.sharding import Mesh
from jax.sharding import PartitionSpec as P

D = 2048
HD = 128


EPSILON = 1e-06
ROPE_THETA = 500000.0
MASKED = -1e30


BF = jnp.bfloat16
F32 = jnp.float32
MESH = pl.DeviceIdType.MESH
AXES = ("z", "y", "x", "core")
CTX = ("z", "y")
STRIP = 16
ANY = pl.BlockSpec(memory_space=pl.ANY)
VMEM = pl.BlockSpec(memory_space=pltpu.VMEM)
DMA = pltpu.SemaphoreType.DMA
BIG_VMEM = 56 * 1024 * 1024


def place():
    return tuple(lax.axis_index(name) for name in AXES)


def greet(targets):
    barrier = pltpu.get_barrier_semaphore()
    for target in targets:
        pl.semaphore_signal(barrier, inc=1, device_id=target, device_id_type=MESH)
    pl.semaphore_wait(barrier, len(targets))


def near_first(step, z):
    high = z // 2
    low = z + high * (3 - 2 * z)
    value = (low, 1 - low, 2, 3)[step]
    return value + high * (3 - 2 * value)


def plane_axes(me):
    z, y, x, k = me
    a = x * (1 - k) + y * k
    b = y * (1 - k) + x * k

    def slot(zp, ap, bp):
        yp = bp * (1 - k) + ap * k
        xp = ap * (1 - k) + bp * k
        return zp * 4 + yp * 2 + xp

    dev_a = (z, y * (1 - k) + (1 - y) * k, (1 - x) * (1 - k) + x * k, k)
    dev_b = (z, (1 - y) * (1 - k) + y * k, x * (1 - k) + (1 - x) * k, k)
    return a, b, slot, dev_a, dev_b


def plane_neighbours(me):
    z, y, x, k = me
    up = z + 1 - 2 * (z // 3)
    down = z - 1 + 2 * ((3 - z) // 3)
    return [(z, 1 - y, x, k), (z, y, 1 - x, k)], up, down


def greet_plane(me, others=()):
    z, y, x, k = me
    barrier = pltpu.get_barrier_semaphore()
    targets = [(z, 1 - y, x, k), (z, y, 1 - x, k), *others]
    for target in targets:
        pl.semaphore_signal(barrier, inc=1, device_id=target, device_id_type=MESH)

    @pl.when(z < 3)
    def _():
        pl.semaphore_signal(barrier, inc=1, device_id=(z + 1, y, x, k), device_id_type=MESH)

    @pl.when(z > 0)
    def _():
        pl.semaphore_signal(barrier, inc=1, device_id=(z - 1, y, x, k), device_id_type=MESH)

    inner = (z + 2) // 3 - z // 3
    pl.semaphore_wait(barrier, len(targets) + 1 + inner)


GATHER_SEMS = [DMA((16,)), DMA((4,)), DMA((4,)), DMA((4,)), DMA((8,))]


def gather_plane(me, own_ref, view, sems, between=lambda step: None):
    z, y, x, k = me
    recv, up_send, down_send, a_send, b_send = sems
    a, b, slot, dev_a, dev_b = plane_axes(me)
    own = slot(z, a, b)

    def copy(src, index, send_sem, device):
        return pltpu.make_async_remote_copy(
            src_ref=src,
            dst_ref=view(index),
            send_sem=send_sem,
            recv_sem=recv.at[index],
            device_id=device,
            device_id_type=MESH,
        )

    def landed(index):
        copy(view(index), index, a_send.at[0], dev_a).wait_recv()

    for step in range(5):
        if step < 4:
            zp = near_first(step, z)
            index = slot(zp, a, b)
            if step == 0:
                src = own_ref
            else:
                landed(index)
                src = view(index)

            @pl.when((zp <= z) & (z < 3))
            def _():
                copy(src, index, up_send.at[zp], (z + 1, y, x, k)).start()

            @pl.when((zp >= z) & (z > 0))
            def _():
                copy(src, index, down_send.at[zp], (z - 1, y, x, k)).start()

            copy(src, index, a_send.at[step], dev_a).start()
            copy(src, index, b_send.at[step], dev_b).start()
        if step > 0:
            index = slot(near_first(step - 1, z), 1 - a, b)
            landed(index)
            copy(view(index), index, b_send.at[3 + step], dev_b).start()
        between(step)
    for step in range(4):
        zp = near_first(step, z)
        landed(slot(zp, a, 1 - b))
        landed(slot(zp, 1 - a, 1 - b))
    for step in range(4):
        zp = near_first(step, z)
        for ap, number in ((a, step), (1 - a, 4 + step)):
            index = slot(zp, ap, b)
            copy(view(index), index, b_send.at[number], dev_b).wait_send()
        index = slot(zp, a, b)
        copy(view(index), index, a_send.at[step], dev_a).wait_send()

        @pl.when((zp <= z) & (z < 3))
        def _():
            copy(view(index), index, up_send.at[zp], (z + 1, y, x, k)).wait_send()

        @pl.when((zp >= z) & (z > 0))
        def _():
            copy(view(index), index, down_send.at[zp], (z - 1, y, x, k)).wait_send()


def reduce_scratch(rows, width):
    return [
        pltpu.VMEM((4, 2, rows, width), BF),
        pltpu.VMEM((4, rows, width), BF),
        pltpu.VMEM((4, rows, width), BF),
        pltpu.VMEM((4, rows, width), BF),
        pltpu.VMEM((4, rows, width), BF),
        pltpu.VMEM((4, rows, width), BF),
        DMA((8,)),
        DMA((8,)),
        DMA((4,)),
        DMA((4,)),
        DMA((4,)),
        DMA((4,)),
        DMA((4,)),
    ]


N_REDUCE = 13


def strips(rows, work, strip=STRIP):
    def body(i, carry):
        work(pl.ds(pl.multiple_of(i * strip, strip), strip))
        return carry

    lax.fori_loop(0, rows // strip, body, 0)


def reduce_plane(me, terms, rows, scratch, produce, finish, after_terms=lambda: None):
    z, y, x, k = me
    (from_b, to_a, from_a, to_z, from_low, from_high) = scratch[:6]
    (b_send, b_recv, a_send, a_recv, z_send, low_recv, high_recv) = scratch[6:]
    a, b, slot, dev_a, dev_b = plane_axes(me)
    order = [near_first(step, z) for step in (3, 2, 1, 0)]

    def start_of(zp, ap, bp):
        return pl.multiple_of(slot(zp, ap, bp) * rows, rows)

    def copy_b(zp, ap):
        return pltpu.make_async_remote_copy(
            src_ref=terms.at[pl.ds(start_of(zp, ap, 1 - b), rows), :],
            dst_ref=from_b.at[zp, ap],
            send_sem=b_send.at[zp * 2 + ap],
            recv_sem=b_recv.at[zp * 2 + ap],
            device_id=dev_b,
            device_id_type=MESH,
        )

    def copy_a(zp):
        return pltpu.make_async_remote_copy(
            src_ref=to_a.at[zp],
            dst_ref=from_a.at[zp],
            send_sem=a_send.at[zp],
            recv_sem=a_recv.at[zp],
            device_id=dev_a,
            device_id_type=MESH,
        )

    def copy_z(zp, target, recv, to):
        return pltpu.make_async_remote_copy(
            src_ref=to_z.at[zp],
            dst_ref=target.at[zp],
            send_sem=z_send.at[zp],
            recv_sem=recv.at[zp],
            device_id=(to, y, x, k),
            device_id_type=MESH,
        )

    def copy_up(zp):
        return copy_z(zp, from_low, low_recv, z + 1)

    def copy_down(zp):
        return copy_z(zp, from_high, high_recv, z - 1)

    def mine(zp, ap, strip):
        at = pl.ds(pl.multiple_of(start_of(zp, ap, b) + strip.start, STRIP), STRIP)
        return terms[at, :].astype(F32)

    for zp in order:
        produce(zp)
        for ap in (1 - a, a):
            copy_b(zp, ap).start()
    after_terms()

    for step in range(5):
        if step < 4:
            zp = order[step]
            copy_b(zp, 1 - a).wait_recv()

            def first(strip, zp=zp):
                to_a[zp, strip] = (
                    mine(zp, 1 - a, strip) + from_b[zp, 1 - a, strip].astype(F32)
                ).astype(BF)

            strips(rows, first)
            copy_a(zp).start()
        if step > 0:
            zp = order[step - 1]
            copy_b(zp, a).wait_recv()
            copy_a(zp).wait_recv()

            def own_sum(strip, zp=zp):
                return (
                    mine(zp, a, strip)
                    + from_b[zp, a, strip].astype(F32)
                    + from_a[zp, strip].astype(F32)
                )

            if step < 4:
                upward = zp > z

                @pl.when(upward & (z > 0))
                def _(zp=zp, own_sum=own_sum):
                    copy_up(zp).wait_recv()

                    def work(strip):
                        to_z[zp, strip] = (own_sum(strip) + from_low[zp, strip].astype(F32)).astype(BF)

                    strips(rows, work)

                @pl.when(jnp.logical_not(upward) & (z < 3))
                def _(zp=zp, own_sum=own_sum):
                    copy_down(zp).wait_recv()

                    def work(strip):
                        to_z[zp, strip] = (own_sum(strip) + from_high[zp, strip].astype(F32)).astype(BF)

                    strips(rows, work)

                @pl.when((z == 0) | (z == 3))
                def _(zp=zp, own_sum=own_sum):
                    def work(strip):
                        to_z[zp, strip] = own_sum(strip).astype(BF)

                    strips(rows, work)

                @pl.when(upward)
                def _(zp=zp):
                    copy_up(zp).start()

                @pl.when(jnp.logical_not(upward))
                def _(zp=zp):
                    copy_down(zp).start()

            else:

                @pl.when(z == 0)
                def _():
                    copy_down(z).wait_recv()
                    strips(rows, lambda s: finish(s, own_sum(s) + from_high[z, s].astype(F32)))

                @pl.when(z == 3)
                def _():
                    copy_up(z).wait_recv()
                    strips(rows, lambda s: finish(s, own_sum(s) + from_low[z, s].astype(F32)))

                @pl.when((z > 0) & (z < 3))
                def _():
                    copy_up(z).wait_recv()
                    copy_down(z).wait_recv()
                    strips(
                        rows,
                        lambda s: finish(
                            s,
                            own_sum(s) + from_low[z, s].astype(F32) + from_high[z, s].astype(F32),
                        ),
                    )

    def settle():
        for zp in order:
            copy_b(zp, 0).wait_send()
            copy_b(zp, 1).wait_send()
            copy_a(zp).wait_send()
        for zp in order[:3]:
            copy_up(zp).wait_send()

    return settle


def own_tile(me):
    z, y, x, k = me
    return z * 2 + y


def gather_view(out_ref, rows):
    def view(slot):
        return out_ref.at[pl.ds(pl.multiple_of(slot * rows, rows), rows), :]

    return view


def hand_out_copies(me, own_ref, out_ref, send, recv):
    z, y, x, k = me
    rows, width = own_ref.shape
    part = width // 4
    target_rows = pl.ds(pl.multiple_of(k * 2 * rows + x * rows, rows), rows)

    def copy(xt, kt, number):
        return pltpu.make_async_remote_copy(
            src_ref=own_ref.at[:, pl.ds(pl.multiple_of((2 * xt + kt) * part, part), part)],
            dst_ref=out_ref.at[target_rows, :],
            send_sem=send.at[number],
            recv_sem=recv.at[number],
            device_id=(z, y, xt, kt),
            device_id_type=MESH,
        )

    local = pltpu.make_async_copy(
        own_ref.at[:, pl.ds(pl.multiple_of((2 * x + k) * part, part), part)],
        out_ref.at[target_rows, :],
        recv.at[3],
    )
    return [copy(x, 1 - k, 0), copy(1 - x, k, 1), copy(1 - x, 1 - k, 2)], local


def pair_devices(me):
    z, y, x, k = me
    return [(z, y, x, 1 - k), (z, y, 1 - x, 1 - k)]


def row_scale(values):
    return lax.rsqrt(jnp.sum(values * values, axis=1, keepdims=True) / values.shape[1] + EPSILON)


def norm_back_strip(grad, values, gain):
    scale = row_scale(values)
    term = grad * values * scale
    weighted = grad * gain
    dot = jnp.sum(weighted * values, axis=1, keepdims=True)
    back = scale * weighted - values * (scale * scale * scale * dot / values.shape[1])
    return back, term[:8] + term[8:]


def comm_call(body, name, number, out_shape, in_specs, out_specs, scratch, cost=None):
    return pl.pallas_call(
        body,
        name=name,
        out_shape=out_shape,
        in_specs=in_specs,
        out_specs=out_specs,
        scratch_shapes=scratch,
        cost_estimate=cost,
        compiler_params=pltpu.CompilerParams(
            collective_id=number, has_side_effects=True, vmem_limit_bytes=BIG_VMEM
        ),
    )


def same_x_greet(me):
    z, y, x, k = me
    barrier = pltpu.get_barrier_semaphore()
    number = z * 4 + y * 2 + k

    def body(i, carry):
        other = lax.rem(number + i, 16)
        pl.semaphore_signal(
            barrier,
            inc=1,
            device_id=(other // 4, (other // 2) % 2, x, other % 2),
            device_id_type=MESH,
        )
        return carry

    lax.fori_loop(1, 16, body, 0)
    for kt in (k, 1 - k):
        pl.semaphore_signal(barrier, inc=1, device_id=(z, y, 1 - x, kt), device_id_type=MESH)
    pl.semaphore_wait(barrier, 17)


def masked_scores(q, keys, low, high, logical):
    raw = lax.dot_general(q, keys, (((1,), (1,)), ((), ())), preferred_element_type=F32)
    allowed = (logical >= low) & (logical <= high)
    return raw * (1.0 / math.sqrt(HD)), allowed


def open_layer(inputs, cotangent, w_query, w_key, w_value, w_out, w_gate, w_up, w_down, gains):
    rows, part = inputs.shape
    half = rows // 2
    quarter = half // 2
    tokens, width = 8 * half, 4 * part
    hidden = w_gate.shape[1]

    def body(*refs):
        (in_ref, cot_ref, wq_ref, wk_ref, wv_ref, wo_ref, wg_ref, wu_ref, wd_ref, gain_ref) = refs[:10]
        (full_out, own_out, own_cot_ref, wqkv_ref, wout_ref, gains_ref, gu_out, d_out) = refs[10:18]
        (q_ref, k_ref, v_ref) = refs[18:21]
        (full_ref, shard, cot_half, qkv_raw, out_raw, gu_raw, d_raw) = refs[21:28]
        (qkv_stage, out_stage, gu_stage, d_stage) = refs[28:32]
        (load_sem, pair_send, pair_recv, local_sem, deal_send, deal_recv) = refs[32:38]
        (share_send, share_recv, gain_send, gain_recv, cot_sems, keep_sem) = refs[38:44]
        gather_sems = refs[44:]
        me = z, y, x, k = place()
        ctx = own_tile(me)
        sibling = (z, y, x, 1 - k)

        loads = [
            pltpu.make_async_copy(src, dst, load_sem.at[i])
            for i, (src, dst) in enumerate(
                [
                    (wq_ref, qkv_raw.at[0]),
                    (wk_ref, qkv_raw.at[1]),
                    (wv_ref, qkv_raw.at[2]),
                    (wo_ref, out_raw),
                    (wg_ref, gu_raw.at[0]),
                    (wu_ref, gu_raw.at[1]),
                    (wd_ref, d_raw),
                ]
            )
        ]
        for load in loads:
            load.start()
        same_x_greet(me)

        def pair_copy(src, dst, number):
            columns = pl.ds(pl.multiple_of(k * part, part), part)
            remote = pltpu.make_async_remote_copy(
                src_ref=src.at[pl.ds(pl.multiple_of((1 - k) * half, half), half), :],
                dst_ref=dst.at[:, columns],
                send_sem=pair_send.at[number],
                recv_sem=pair_recv.at[number],
                device_id=sibling,
                device_id_type=MESH,
            )
            local = pltpu.make_async_copy(
                src.at[pl.ds(pl.multiple_of(k * half, half), half), :],
                dst.at[:, columns],
                local_sem.at[number],
            )
            remote.start()
            local.start()
            return remote, local

        first = pair_copy(in_ref, shard, 0)
        second = pair_copy(cot_ref, cot_half, 1)

        def gain_copy(xt, kt, number):
            return pltpu.make_async_remote_copy(
                src_ref=gain_ref,
                dst_ref=gains_ref.at[:, pl.ds(pl.multiple_of((2 * x + k) * part, part), part)],
                send_sem=gain_send.at[number],
                recv_sem=gain_recv.at[number],
                device_id=(z, y, xt, kt),
                device_id_type=MESH,
            )

        gain_copies = [gain_copy(x, 1 - k, 0), gain_copy(1 - x, k, 1), gain_copy(1 - x, 1 - k, 2)]
        for copy in gain_copies:
            copy.start()
        gain_local = pltpu.make_async_copy(
            gain_ref,
            gains_ref.at[:, pl.ds(pl.multiple_of((2 * x + k) * part, part), part)],
            local_sem.at[2],
        )
        gain_local.start()

        first[0].wait_recv()
        first[1].wait()

        def view(slot):
            return full_ref.at[
                pl.ds(pl.multiple_of((slot // 2) * half, half), half),
                pl.ds(pl.multiple_of((slot % 2) * 2 * part, 2 * part), 2 * part),
            ]

        own_slot = ctx * 2 + x
        own_local = pltpu.make_async_copy(shard, view(own_slot), local_sem.at[3])
        own_local.start()

        def deal(e):
            j, r = e // 2, e % 2
            return [
                pltpu.make_async_remote_copy(
                    src_ref=src,
                    dst_ref=dst,
                    send_sem=deal_send.at[i, e],
                    recv_sem=deal_recv.at[i, ctx],
                    device_id=(2 * k + e // 4, (e // 2) % 2, x, r),
                    device_id_type=MESH,
                )
                for i, (src, dst) in enumerate(deal_ends(j, r))
            ]

        def deal_ends(j, r):
            at = pl.ds(pl.multiple_of(ctx * 2 * HD + r * HD, HD), HD)
            return (
                (
                    qkv_stage.at[:, r * HD : (r + 1) * HD, j * HD : (j + 1) * HD],
                    wqkv_ref.at[:, at, :],
                ),
                (
                    out_stage.at[j * HD : (j + 1) * HD, r * HD : (r + 1) * HD],
                    wout_ref.at[:, at],
                ),
            )

        stays = k == z // 2
        own_e = (z % 2) * 4 + y * 2 + k

        def deal_all():
            for load in loads[:4]:
                load.wait()

            def round_qkv(s):
                for i in range(3):
                    qkv_stage[i, s] = qkv_raw[i, s].astype(BF)

            strips(rows, round_qkv)

            def round_out(s):
                out_stage[s] = out_raw[s].astype(BF)

            strips(2 * rows, round_out, 32)
            for e in range(8):

                @pl.when(jnp.logical_not(stays & (own_e == e)))
                def _(e=e):
                    for copy in deal(e):
                        copy.start()

                @pl.when(stays & (own_e == e))
                def _(e=e):
                    for i, (src, dst) in enumerate(deal_ends(e // 2, e % 2)):
                        pltpu.make_async_copy(src, dst, deal_recv.at[i, ctx]).start()

        def cot_begin():
            second[0].wait_recv()
            second[1].wait()
            cot_remote.start()
            cot_local.start()

        wide = pl.ds(pl.multiple_of(x * 2 * part, 2 * part), 2 * part)
        cot_remote = pltpu.make_async_remote_copy(
            src_ref=cot_half.at[pl.ds(pl.multiple_of((1 - x) * quarter, quarter), quarter), :],
            dst_ref=own_cot_ref.at[:, wide],
            send_sem=cot_sems.at[0],
            recv_sem=cot_sems.at[1],
            device_id=(z, y, 1 - x, k),
            device_id_type=MESH,
        )
        cot_local = pltpu.make_async_copy(
            cot_half.at[pl.ds(pl.multiple_of(x * quarter, quarter), quarter), :],
            own_cot_ref.at[:, wide],
            cot_sems.at[2],
        )

        keeps = [
            pltpu.make_async_copy(gu_stage.at[0], gu_out.at[0], keep_sem.at[0]),
            pltpu.make_async_copy(gu_stage.at[1], gu_out.at[1], keep_sem.at[1]),
            pltpu.make_async_copy(d_stage, d_out, keep_sem.at[2]),
        ]

        def round_up(i):
            loads[4 + i].wait()

            def work(s):
                gu_stage[i, s] = gu_raw[i, s].astype(BF)

            strips(rows, work)
            keeps[i].start()

        def round_down():
            loads[6].wait()

            def work(s):
                d_stage[s] = d_raw[s].astype(BF)

            strips(hidden, work, 128)
            keeps[2].start()

        between = [
            deal_all,
            lambda: (cot_begin(), round_up(0)),
            lambda: round_up(1),
            round_down,
            lambda: None,
        ]
        gather_plane(me, shard, view, gather_sems, lambda step: between[step]())

        def deal_wait(c):
            at = slice(c * 2 * HD, c * 2 * HD + HD)
            pltpu.make_async_copy(
                qkv_stage.at[:, :HD, :HD], wqkv_ref.at[:, at, :], deal_recv.at[0, c]
            ).wait()
            pltpu.make_async_copy(
                out_stage.at[:HD, :HD], wout_ref.at[:, at], deal_recv.at[1, c]
            ).wait()

        def share(c, r):
            at = pl.ds(pl.multiple_of(c * 2 * HD + r * HD, HD), HD)
            return [
                pltpu.make_async_remote_copy(
                    src_ref=ref,
                    dst_ref=ref,
                    send_sem=share_send.at[i, c],
                    recv_sem=share_recv.at[i, c],
                    device_id=sibling,
                    device_id_type=MESH,
                )
                for i, ref in enumerate((wqkv_ref.at[:, at, :], wout_ref.at[:, at]))
            ]

        for c in range(8):
            deal_wait(c)
            for copy in share(c, k):
                copy.start()
        own_local.wait()
        full_keep = pltpu.make_async_copy(full_ref, full_out, keep_sem.at[3])
        full_keep.start()
        own_rows = pl.ds(pl.multiple_of(own_slot * quarter, quarter), quarter)
        own_keep = pltpu.make_async_copy(full_ref.at[own_rows, :], own_out, keep_sem.at[4])
        own_keep.start()
        for c in range(8):
            for copy in share(c, 1 - k):
                copy.wait_recv()

        def project(s):
            tile = full_ref[s, :]
            q_ref[s, :] = jnp.dot(tile, wqkv_ref[0], preferred_element_type=F32)
            k_ref[s, :] = jnp.dot(tile, wqkv_ref[1], preferred_element_type=F32)
            v_ref[s, :] = jnp.dot(tile, wqkv_ref[2], preferred_element_type=F32).astype(BF)

        strips(tokens, project, 256)
        for e in range(8):

            @pl.when(jnp.logical_not(stays & (own_e == e)))
            def _(e=e):
                for copy in deal(e):
                    copy.wait_send()

        for c in range(8):
            for copy in share(c, k):
                copy.wait_send()
        first[0].wait_send()
        second[0].wait_send()
        for copy in gain_copies:
            copy.wait()
        gain_local.wait()
        cot_remote.wait()
        cot_local.wait()
        for keep in (*keeps, full_keep, own_keep):
            keep.wait()

    shape = jax.ShapeDtypeStruct
    return comm_call(
        body,
        "open_layer",
        0,
        (
            shape((tokens, width), BF),
            shape((quarter, width), BF),
            shape((quarter, width), BF),
            shape((3, width, HD), BF),
            shape((HD, width), BF),
            shape((4, width), F32),
            shape((2, rows, hidden), BF),
            shape((hidden, rows), BF),
            shape((tokens, HD), F32),
            shape((tokens, HD), F32),
            shape((tokens, HD), BF),
        ),
        [ANY] * 10,
        (ANY, ANY, ANY, VMEM, VMEM, ANY, ANY, ANY, VMEM, VMEM, VMEM),
        [
            pltpu.VMEM((tokens, width), BF),
            pltpu.VMEM((half, 2 * part), BF),
            pltpu.VMEM((half, 2 * part), BF),
            pltpu.VMEM((3, rows, part), F32),
            pltpu.VMEM((part, rows), F32),
            pltpu.VMEM((2, rows, hidden), F32),
            pltpu.VMEM((hidden, rows), F32),
            pltpu.VMEM((3, rows, part), BF),
            pltpu.VMEM((part, rows), BF),
            pltpu.VMEM((2, rows, hidden), BF),
            pltpu.VMEM((hidden, rows), BF),
            DMA((7,)),
            DMA((2,)),
            DMA((2,)),
            DMA((4,)),
            DMA((2, 8)),
            DMA((2, 8)),
            DMA((2, 8)),
            DMA((2, 8)),
            DMA((3,)),
            DMA((3,)),
            DMA((3,)),
            DMA((5,)),
            *GATHER_SEMS,
        ],
    )(inputs, cotangent, w_query, w_key, w_value, w_out, w_gate, w_up, w_down, gains)


def eye_mask():
    return lax.broadcasted_iota(jnp.int32, (HD, HD), 0) == lax.broadcasted_iota(
        jnp.int32, (HD, HD), 1
    )


def column_to_row(column, eye):
    return jnp.sum(jnp.where(eye, column, 0.0), axis=0, keepdims=True)


def row_to_column(row, eye):
    return jnp.sum(jnp.where(eye, row, 0.0), axis=1, keepdims=True)


def plane_peer(me, i):
    z, y, x, k = me
    other = lax.rem(z * 4 + y * 2 + x + i, 16)
    return other, (other // 4, (other // 2) % 2, other % 2, k)


def plane_greet_all(me, others):
    barrier = pltpu.get_barrier_semaphore()

    def call(i, carry):
        pl.semaphore_signal(barrier, inc=1, device_id=plane_peer(me, i)[1], device_id_type=MESH)
        return carry

    lax.fori_loop(1, 16, call, 0)
    for other in others:
        pl.semaphore_signal(barrier, inc=1, device_id=other, device_id_type=MESH)
    pl.semaphore_wait(barrier, 15 + len(others))


def sum_over_plane(me, slots, send, recv):
    own = me[0] * 4 + me[1] * 2 + me[2]

    def copy(i, slot):
        return pltpu.make_async_remote_copy(
            src_ref=slots.at[slot],
            dst_ref=slots.at[slot],
            send_sem=send.at[i],
            recv_sem=recv.at[slot],
            device_id=plane_peer(me, i)[1],
            device_id_type=MESH,
        )

    def begin(i, carry):
        copy(i, own).start()
        return carry

    lax.fori_loop(1, 16, begin, 0)

    def landed(i, carry):
        copy(i, plane_peer(me, i)[0]).wait_recv()
        return carry

    lax.fori_loop(1, 16, landed, 0)

    def sent(i, carry):
        copy(i, own).wait_send()
        return carry

    lax.fori_loop(1, 16, sent, 0)
    total = slots[0]
    for i in range(1, 16):
        total = total + slots[i]
    return total


def attention_forward(
    query, key, value, tables, bounds, logical, source, out_weight, gains, attn_gain, gu_stage, d_stage
):
    tokens, width = query.shape[0], source.shape[1]
    rows = tokens // 16
    group = tokens // 4
    hidden = gu_stage.shape[2] // 8
    part = width // 8

    def body(*refs):
        (q_in, k_in, v_in, cos_ref, sin_ref, low_ref, high_ref, log_ref, source_ref, wout_ref, gain_ref, attn_ref) = refs[:12]
        (gu_ref, d_ref) = refs[12:14]
        (full_ref, own_ref, branch_ref, wgu_ref, wd_ref, qrot_ref, keys_ref, values_ref, o_ref, lse_ref, scale_ref) = refs[14:25]
        (terms, shard, slots, tot_send, tot_recv, pair_send, pair_recv, local) = refs[25:33]
        (ffn_send, ffn_recv, share_send, share_recv, ffn_local) = refs[33:38]
        rest = refs[38:]
        me = z, y, x, k = place()
        ctx = own_tile(me)
        sibling = (z, y, x, 1 - k)
        barrier = pltpu.get_barrier_semaphore()
        plane_greet_all(me, [sibling])

        def pair(src, dst, n):
            return pltpu.make_async_remote_copy(
                src_ref=src,
                dst_ref=dst,
                send_sem=pair_send.at[n],
                recv_sem=pair_recv.at[n],
                device_id=sibling,
                device_id_type=MESH,
            )

        eye = eye_mask()
        own = z * 4 + y * 2 + x
        for i in range(8):
            piece = slice(i * HD, (i + 1) * HD)
            for side, ref in enumerate((q_in, k_in)):
                values = ref[piece, :]
                column = jnp.sum(values * values, axis=1, keepdims=True)
                slots[own, side * 8 + i : side * 8 + i + 1, :] = column_to_row(column, eye)
        values_ref[:tokens, :] = v_in[...]
        other_half = pl.ds(tokens, tokens)
        v_copy = pair(v_in, values_ref.at[other_half, :], 0)
        v_copy.start()

        def ffn_copy(t):
            to = ctx + t - 8 * ((ctx + t) // 8)
            device = (to // 2, to % 2, x, k)
            at = pl.ds(pl.multiple_of(to * hidden, hidden), hidden)
            from_at = pl.ds(pl.multiple_of(ctx * part, part), part)
            ends = (
                (gu_ref.at[:, :, at], wgu_ref.at[:, from_at, :hidden]),
                (d_ref.at[at, :], wd_ref.at[:hidden, from_at]),
            )
            return [
                pltpu.make_async_remote_copy(
                    src_ref=src,
                    dst_ref=dst,
                    send_sem=ffn_send.at[i, t],
                    recv_sem=ffn_recv.at[i, t],
                    device_id=device,
                    device_id_type=MESH,
                )
                for i, (src, dst) in enumerate(ends)
            ]

        def ffn_ends(c):
            at = pl.ds(pl.multiple_of(c * part, part), part)
            return (
                (wgu_ref.at[:, at, :hidden], wgu_ref.at[:, at, hidden:]),
                (wd_ref.at[:hidden, at], wd_ref.at[hidden:, at]),
            )

        own_at = pl.ds(pl.multiple_of(ctx * hidden, hidden), hidden)
        ffn_own = [
            pltpu.make_async_copy(src, dst[0], ffn_local.at[i])
            for i, (src, dst) in enumerate(
                zip((gu_ref.at[:, :, own_at], d_ref.at[own_at, :]), ffn_ends(ctx), strict=True)
            )
        ]
        for copy in ffn_own:
            copy.start()

        total = sum_over_plane(me, slots, tot_send, tot_recv)
        for t in range(1, 8):
            for copy in ffn_copy(t):
                copy.start()
        scales = lax.rsqrt(total / width + EPSILON)
        scale_ref[...] = scales

        def rotated(values, piece):
            return values * cos_ref[piece, :] + pltpu.roll(values, HD // 2, 1) * sin_ref[piece, :]

        for i in range(8):
            piece = slice(i * HD, (i + 1) * HD)
            factor = row_to_column(scales[8 + i : 9 + i, :], eye)
            keys_ref[piece, :] = rotated(k_in[piece, :] * factor * gain_ref[1:2, :], piece).astype(BF)
        k_copy = pair(keys_ref.at[:tokens, :], keys_ref.at[other_half, :], 1)
        k_copy.start()
        for i in range(8):
            piece = slice(i * HD, (i + 1) * HD)
            factor = row_to_column(scales[i : i + 1, :], eye)
            qrot_ref[piece, :] = rotated(q_in[piece, :] * factor * gain_ref[0:1, :], piece).astype(BF)
        v_copy.wait()
        k_copy.wait()

        def produce(zp):
            at = pl.ds(pl.multiple_of(zp * group, group), group)
            raw, allowed = masked_scores(
                qrot_ref[at, :], keys_ref[...], low_ref[at, :], high_ref[at, :], log_ref[...]
            )
            raw = jnp.where(allowed, raw, MASKED)
            top = jnp.max(raw, axis=1, keepdims=True)
            weights = jnp.where(allowed, jnp.exp(raw - top), 0.0)
            total_weight = jnp.sum(weights, axis=1, keepdims=True)
            weights = (weights / total_weight).astype(BF)
            out = jnp.dot(weights, values_ref[...], preferred_element_type=F32)
            o_ref[at, :] = out
            lse_ref[at, :] = top + jnp.log(total_weight)
            terms[at, :] = jnp.dot(
                out.astype(BF), wout_ref[...], preferred_element_type=F32
            ).astype(BF)

        def finish(strip, total):
            branch_ref[strip] = total
            h = source_ref[strip].astype(F32) + total * row_scale(total) * attn_ref[...]
            own_ref[strip] = h
            shard[strip] = h.astype(BF)

        settle = reduce_plane(me, terms, rows, rest[:N_REDUCE], produce, finish)
        view = gather_view(full_ref, rows)
        keep = pltpu.make_async_copy(shard, view(own), local)
        keep.start()

        def share(t):
            c = ctx + 8 - t - 8 * ((ctx + 8 - t) // 8)
            return [
                pltpu.make_async_remote_copy(
                    src_ref=src,
                    dst_ref=dst,
                    send_sem=share_send.at[i, t],
                    recv_sem=share_recv.at[i, t],
                    device_id=sibling,
                    device_id_type=MESH,
                )
                for i, (src, dst) in enumerate(ffn_ends(c))
            ]

        def ffn_landed(t):
            c = ctx + 8 - t - 8 * ((ctx + 8 - t) // 8)
            for i, ends in enumerate(ffn_ends(c)):
                pltpu.make_async_remote_copy(
                    src_ref=ends[0],
                    dst_ref=ends[0],
                    send_sem=ffn_send.at[i, t],
                    recv_sem=ffn_recv.at[i, t],
                    device_id=sibling,
                    device_id_type=MESH,
                ).wait_recv()

        def between(step):
            for t in (2 * step, 2 * step + 1):
                if t == 0:
                    for copy in ffn_own:
                        copy.wait()
                elif t < 8:
                    ffn_landed(t)
                if t < 8:
                    for copy in share(t):
                        copy.start()

        gather_plane(me, shard, view, rest[N_REDUCE:])
        for step in range(4):
            between(step)
        keep.wait()
        settle()
        for t in range(8):
            for copy in share(t):
                copy.wait()
            if t > 0:
                for copy in ffn_copy(t):
                    copy.wait_send()

    shape = jax.ShapeDtypeStruct
    return comm_call(
        body,
        "attention_forward",
        1,
        (
            shape((tokens, width), BF),
            shape((rows, width), F32),
            shape((rows, width), F32),
            shape((2, width, 2 * hidden), BF),
            shape((2 * hidden, width), BF),
            shape((tokens, HD), BF),
            shape((2 * tokens, HD), BF),
            shape((2 * tokens, HD), BF),
            shape((tokens, HD), F32),
            shape((tokens, 1), F32),
            shape((16, HD), F32),
        ),
        [VMEM] * 12 + [ANY, ANY],
        (ANY, VMEM, VMEM, ANY, ANY, VMEM, VMEM, VMEM, VMEM, VMEM, VMEM),
        [
            pltpu.VMEM((tokens, width), BF),
            pltpu.VMEM((rows, width), BF),
            pltpu.VMEM((16, 16, HD), F32),
            DMA((16,)),
            DMA((16,)),
            DMA((2,)),
            DMA((2,)),
            DMA,
            DMA((2, 8)),
            DMA((2, 8)),
            DMA((2, 8)),
            DMA((2, 8)),
            DMA((2,)),
            *reduce_scratch(rows, width),
            *GATHER_SEMS,
        ],
    )(query, key, value, *tables, *bounds, logical, source, out_weight, gains, attn_gain, gu_stage, d_stage)


def after_ffn(terms, residual, cotangent, gain):
    tokens, width = terms.shape
    rows = tokens // 16

    def body(term_ref, res_ref, cot_ref, gain_ref, full_ref, out_ref, gg_ref, shard, result, local, out_send, out_recv, *scratch):
        me = place()
        greet_plane(me, pair_devices(me))
        gg_ref[...] = jnp.zeros_like(gg_ref)

        def finish(strip, total):
            gain_row = gain_ref[...]
            out = res_ref[strip] + total * row_scale(total) * gain_row
            result[strip] = out.astype(BF)
            back, term = norm_back_strip(cot_ref[strip].astype(F32), total, gain_row)
            gg_ref[...] += term
            shard[strip] = back.astype(BF)

        settle = reduce_plane(me, term_ref, rows, scratch[:N_REDUCE], lambda zp: None, finish)
        view = gather_view(full_ref, rows)
        keep = pltpu.make_async_copy(shard, view(me[0] * 4 + me[1] * 2 + me[2]), local)
        keep.start()
        copies, own = hand_out_copies(me, result, out_ref, out_send, out_recv)
        for copy in copies:
            copy.start()
        own.start()
        gather_plane(me, shard, view, scratch[N_REDUCE:])
        keep.wait()
        settle()
        own.wait()
        for copy in copies:
            copy.wait()

    shape = jax.ShapeDtypeStruct
    return comm_call(
        body,
        "after_ffn",
        3,
        (shape((tokens, width), BF), shape((rows * 4, width // 4), BF), shape((8, width), F32)),
        [VMEM, VMEM, VMEM, VMEM],
        (ANY, ANY, VMEM),
        [
            pltpu.VMEM((rows, width), BF),
            pltpu.VMEM((rows, width), BF),
            DMA,
            DMA((3,)),
            DMA((4,)),
            *reduce_scratch(rows, width),
            *GATHER_SEMS,
        ],
    )(terms, residual, cotangent, gain)


def after_ffn_back(terms, cotangent, branch, gain):
    tokens, width = terms.shape
    rows = tokens // 16

    def body(term_ref, cot_ref, branch_ref, gain_ref, full_ref, own_ref, gg_ref, shard, local, *scratch):
        me = place()
        greet_plane(me)
        gg_ref[...] = jnp.zeros_like(gg_ref)

        def finish(strip, total):
            grad = cot_ref[strip].astype(F32) + total
            own_ref[strip] = grad
            back, term = norm_back_strip(grad, branch_ref[strip], gain_ref[...])
            gg_ref[...] += term
            shard[strip] = back.astype(BF)

        settle = reduce_plane(me, term_ref, rows, scratch[:N_REDUCE], lambda zp: None, finish)
        view = gather_view(full_ref, rows)
        keep = pltpu.make_async_copy(shard, view(me[0] * 4 + me[1] * 2 + me[2]), local)
        keep.start()
        gather_plane(me, shard, view, scratch[N_REDUCE:])
        keep.wait()
        settle()

    shape = jax.ShapeDtypeStruct
    return comm_call(
        body,
        "after_ffn_back",
        4,
        (shape((tokens, width), BF), shape((rows, width), F32), shape((8, width), F32)),
        [VMEM, VMEM, VMEM, VMEM],
        (ANY, VMEM, VMEM),
        [pltpu.VMEM((rows, width), BF), DMA, *reduce_scratch(rows, width), *GATHER_SEMS],
    )(terms, cotangent, branch, gain)


def close_greet(me):
    z, y, x, k = me
    barrier = pltpu.get_barrier_semaphore()

    def plane(i, carry):
        pl.semaphore_signal(barrier, inc=1, device_id=plane_peer(me, i)[1], device_id_type=MESH)
        return carry

    def others(i, carry):
        pl.semaphore_signal(
            barrier, inc=1, device_id=(i // 2, i % 2, x, 1 - k), device_id_type=MESH
        )
        return carry

    lax.fori_loop(1, 16, plane, 0)
    lax.fori_loop(0, 8, others, 0)
    pl.semaphore_signal(barrier, inc=1, device_id=(z, y, 1 - x, 1 - k), device_id_type=MESH)
    pl.semaphore_wait(barrier, 24)


def attention_backward(
    grad_attn,
    full_in,
    query,
    key,
    query_rot,
    keys,
    values,
    attended,
    lse,
    tables,
    bounds,
    logical,
    scales,
    head_gains,
    qkv_w,
    out_w,
    grad_own,
    attn_term,
    ffn_term,
):
    tokens, width = grad_attn.shape
    rows, group = tokens // 16, tokens // 4
    part = width // 4
    scaling = 1.0 / math.sqrt(HD)

    def body(*refs):
        (da_any, x_any) = refs[:2]
        (q_ref, k_ref, qrot_ref, keys_ref, values_ref, o_ref, lse_ref, cos_ref, sin_ref) = refs[2:11]
        (low_ref, high_ref, log_ref, scale_ref, gain_ref, wqkv_ref, wout_ref) = refs[11:18]
        (grad_ref, attn_ref, ffn_ref) = refs[18:21]
        (in_grad_ref, gq_ref, gk_ref, gv_ref, gout_ref, gains_ref) = refs[21:27]
        (da, xs, terms, do_ref, delta_ref, dq_ref, dk_ref, dv_ref) = refs[27:35]
        (pair_out, pair_in, dqkv, slots, result) = refs[35:40]
        (wall_grad, wall_out, wall_in, deal_out, deal_in) = refs[40:45]
        (gain_out, gain_in, gain_own, gain_slots) = refs[45:49]
        (load_sem, pair_send, pair_recv, tot_send, tot_recv, out_send, out_recv) = refs[49:56]
        (deal_send, deal_recv, gain_send, gain_recv) = refs[56:60]
        scratch = refs[60:]
        me = z, y, x, k = place()
        ctx = own_tile(me)
        own = ctx * 2 + x
        sibling = (z, y, x, 1 - k)

        da_loads = [
            pltpu.make_async_copy(
                da_any.at[g * group : (g + 1) * group, :],
                da.at[g * group : (g + 1) * group, :],
                load_sem.at[g],
            )
            for g in range(4)
        ]
        x_load = pltpu.make_async_copy(x_any, xs, load_sem.at[4])
        for load in (*da_loads, x_load):
            load.start()
        close_greet(me)

        def pair(n):
            return pltpu.make_async_remote_copy(
                src_ref=(pair_out.at[0], pair_out.at[1], wall_out, gain_out)[n],
                dst_ref=(pair_in.at[0], pair_in.at[1], wall_in, gain_in)[n],
                send_sem=pair_send.at[n],
                recv_sem=pair_recv.at[n],
                device_id=sibling,
                device_id_type=MESH,
            )

        for g in range(4):
            at = slice(g * group, (g + 1) * group)
            da_loads[g].wait()
            do = lax.dot_general(
                da[at, :], wout_ref[...], (((1,), (1,)), ((), ())), preferred_element_type=F32
            ).astype(BF)
            do_ref[at, :] = do
            delta_ref[at, :] = jnp.sum(do.astype(F32) * o_ref[at, :], axis=1, keepdims=True)

        across = (((0,), (0,)), ((), ()))
        for half in (1, 0):
            key_at = slice(half * tokens, (half + 1) * tokens)
            dk_ref[...] = jnp.zeros_like(dk_ref)
            dv_ref[...] = jnp.zeros_like(dv_ref)

            def work(at, half=half, key_at=key_at):
                q, g, key_part = qrot_ref[at, :], do_ref[at, :], keys_ref[key_at, :]
                raw, allowed = masked_scores(
                    q, key_part, low_ref[at, :], high_ref[at, :], log_ref[:, key_at]
                )
                weights = jnp.where(allowed, jnp.exp(raw - lse_ref[at, :]), 0.0)
                dp = lax.dot_general(
                    g, values_ref[key_at, :], (((1,), (1,)), ((), ())), preferred_element_type=F32
                )
                ds = (weights * (dp - delta_ref[at, :])).astype(BF)
                dq = jnp.dot(ds, key_part, preferred_element_type=F32) * scaling
                if half == 1:
                    dq_ref[at, :] = dq
                else:
                    dq_ref[at, :] += dq
                dk_ref[...] += (
                    lax.dot_general(ds, q, across, preferred_element_type=F32) * scaling
                )
                dv_ref[...] += lax.dot_general(
                    weights.astype(BF), g, across, preferred_element_type=F32
                )

            strips(tokens, work, group)
            if half == 1:
                pair_out[0] = dk_ref[...].astype(BF)
                pair_out[1] = dv_ref[...].astype(BF)
                pair(0).start()
                pair(1).start()

        eye = eye_mask()

        def normed_grad(values, piece):
            return values * cos_ref[piece, :] - pltpu.roll(values, HD // 2, 1) * sin_ref[piece, :]

        def side_dots(side, source, grads, proj):
            gain_sum = jnp.zeros((8, HD), F32)
            for i in range(8):
                piece = slice(i * HD, (i + 1) * HD)
                factor = row_to_column(scale_ref[side * 8 + i : side * 8 + i + 1, :], eye)
                back = normed_grad(source(piece), piece)
                term = back * proj[piece, :] * factor
                for j in range(0, HD, 8):
                    gain_sum = gain_sum + term[j : j + 8, :]
                weighted = back * gain_ref[side : side + 1, :]
                grads[piece, :] = weighted
                dot = jnp.sum(weighted * proj[piece, :], axis=1, keepdims=True)
                slots[own, side * 8 + i : side * 8 + i + 1, :] = column_to_row(dot, eye)
            return jnp.sum(gain_sum, axis=0, keepdims=True)

        query_gain = side_dots(0, lambda piece: dq_ref[piece, :], dq_ref, q_ref)
        pair(0).wait_recv()
        pair(1).wait_recv()
        key_gain = side_dots(
            1, lambda piece: dk_ref[piece, :] + pair_in[0, piece, :].astype(F32), dk_ref, k_ref
        )
        dqkv[:, 2 * HD :] = (dv_ref[...] + pair_in[1].astype(F32)).astype(BF)

        attn_sum = jnp.sum(attn_ref[...], axis=0, keepdims=True)
        ffn_sum = jnp.sum(ffn_ref[...], axis=0, keepdims=True)
        head_core = z // 2
        head_at = pl.ds(pl.multiple_of(((z % 2) * 2 + y) * HD, HD), HD)
        for mine, target in ((True, gain_own), (False, gain_out)):
            target[...] = jnp.zeros_like(target)
            for xt in range(2):
                for kt in range(2):

                    @pl.when((kt == k) if mine else (kt != k))
                    def _(xt=xt, kt=kt, target=target):
                        block = slice((2 * xt + kt) * part, (2 * xt + kt + 1) * part)
                        target[xt, 2:3, :] = attn_sum[:, block]
                        target[xt, 3:4, :] = ffn_sum[:, block]

            @pl.when((head_core == k) if mine else (head_core != k))
            def _(target=target):
                target[x, 0:1, head_at] = query_gain
                target[x, 1:2, head_at] = key_gain

        pair(3).start()

        total = sum_over_plane(me, slots, tot_send, tot_recv)
        for side, grads, proj in ((0, dq_ref, q_ref), (1, dk_ref, k_ref)):
            for i in range(8):
                piece = slice(i * HD, (i + 1) * HD)
                row = scale_ref[side * 8 + i : side * 8 + i + 1, :]
                factor = row_to_column(row, eye)
                cubed = row * row * row * total[side * 8 + i : side * 8 + i + 1, :] / width
                dqkv[piece, side * HD : (side + 1) * HD] = (
                    factor * grads[piece, :] - proj[piece, :] * row_to_column(cubed, eye)
                ).astype(BF)

        def produce(zp):
            at = pl.ds(pl.multiple_of(zp * group, group), group)
            term = jnp.zeros((group, width), F32)
            for i in range(3):
                term = term + lax.dot_general(
                    dqkv[at, i * HD : (i + 1) * HD],
                    wqkv_ref[i],
                    (((1,), (1,)), ((), ())),
                    preferred_element_type=F32,
                )
            terms[at, :] = term.astype(BF)

        gain_copies = []

        def gain_copy(i):
            other, device = plane_peer(me, i)
            return pltpu.make_async_remote_copy(
                src_ref=gain_own.at[other % 2],
                dst_ref=gain_slots.at[own],
                send_sem=gain_send.at[i],
                recv_sem=gain_recv.at[own],
                device_id=device,
                device_id_type=MESH,
            )

        number = ((z % 2) * 2 + y) * 2 + k

        def deal(c):
            return pltpu.make_async_remote_copy(
                src_ref=deal_out.at[c],
                dst_ref=deal_in.at[number],
                send_sem=deal_send.at[c],
                recv_sem=deal_recv.at[number],
                device_id=(c // 2, c % 2, x, head_core),
                device_id_type=MESH,
            )

        stays = k == head_core

        def after_terms():
            pair(3).wait_recv()
            gain_own[...] += gain_in[...]
            gain_slots[own] = gain_own[x]

            def begin(i, carry):
                gain_copy(i).start()
                return carry

            lax.fori_loop(1, 16, begin, 0)
            x_load.wait()
            for c in range(8):
                grads = lax.dot_general(
                    xs[:, c * 2 * HD : (c + 1) * 2 * HD],
                    dqkv[...],
                    across,
                    preferred_element_type=F32,
                )
                for i in range(3):
                    for r in range(2):
                        wall_grad[r, c, i] = grads[r * HD : (r + 1) * HD, i * HD : (i + 1) * HD]
                out_grad = lax.dot_general(
                    o_ref[...].astype(BF),
                    da[:, c * 2 * HD : (c + 1) * 2 * HD],
                    across,
                    preferred_element_type=F32,
                )
                for r in range(2):
                    wall_grad[r, c, 3] = out_grad[:, r * HD : (r + 1) * HD]

            def to_other(c, carry):
                wall_out[c] = wall_grad[1 - k, c].astype(BF)
                return carry

            lax.fori_loop(0, 8, to_other, 0)
            pair(2).start()
            pair(2).wait_recv()

            def to_owner(c, carry):
                deal_out[c] = (wall_grad[k, c] + wall_in[c].astype(F32)).astype(BF)
                return carry

            lax.fori_loop(0, 8, to_owner, 0)
            for c in range(8):

                @pl.when(jnp.logical_not(stays & (ctx == c)))
                def _(c=c):
                    deal(c).start()

                @pl.when(stays & (ctx == c))
                def _(c=c):
                    pltpu.make_async_copy(
                        deal_out.at[c], deal_in.at[number], deal_recv.at[number]
                    ).start()

        def finish(strip, total):
            result[strip] = (grad_ref[strip] + total).astype(BF)

        settle = reduce_plane(me, terms, rows, scratch, produce, finish, after_terms)
        copies, own_copy = hand_out_copies(me, result, in_grad_ref, out_send, out_recv)
        for copy in copies:
            copy.start()
        own_copy.start()
        for n in range(8):
            pltpu.make_async_copy(deal_out.at[n], deal_in.at[n], deal_recv.at[n]).wait()
            j, r = n // 2, n % 2
            for i, ref in enumerate((gq_ref, gk_ref, gv_ref)):
                ref[r * HD : (r + 1) * HD, j * HD : (j + 1) * HD] = deal_in[n, i].astype(F32)
            gout_ref[j * HD : (j + 1) * HD, r * HD : (r + 1) * HD] = deal_in[n, 3].astype(F32)

        def gain_landed(i, carry):
            other, device = plane_peer(me, i)
            pltpu.make_async_remote_copy(
                src_ref=gain_slots.at[other],
                dst_ref=gain_slots.at[other],
                send_sem=gain_send.at[i],
                recv_sem=gain_recv.at[other],
                device_id=device,
                device_id_type=MESH,
            ).wait_recv()
            gain_copy(i).wait_send()
            return carry

        lax.fori_loop(1, 16, gain_landed, 0)
        gain_total = gain_slots[0]
        for i in range(1, 16):
            gain_total = gain_total + gain_slots[i]
        gains_ref[...] = gain_total
        settle()
        own_copy.wait()
        for copy in copies:
            copy.wait()
        for c in range(8):

            @pl.when(jnp.logical_not(stays & (ctx == c)))
            def _(c=c):
                deal(c).wait_send()

        for n in range(4):
            pair(n).wait_send()

    shape = jax.ShapeDtypeStruct
    vmem = pltpu.VMEM
    return comm_call(
        body,
        "attention_backward",
        5,
        (
            shape((rows * 4, part), BF),
            shape((rows * 4, part), F32),
            shape((rows * 4, part), F32),
            shape((rows * 4, part), F32),
            shape((part, rows * 4), F32),
            shape((4, part), F32),
        ),
        [ANY, ANY, *[VMEM] * 19],
        (ANY, VMEM, VMEM, VMEM, VMEM, VMEM),
        [
            vmem((tokens, width), BF),
            vmem((tokens, width), BF),
            vmem((tokens, width), BF),
            vmem((tokens, HD), BF),
            vmem((tokens, 1), F32),
            vmem((tokens, HD), F32),
            vmem((tokens, HD), F32),
            vmem((tokens, HD), F32),
            vmem((2, tokens, HD), BF),
            vmem((2, tokens, HD), BF),
            vmem((tokens, 3 * HD), BF),
            vmem((16, 16, HD), F32),
            vmem((rows, width), BF),
            vmem((2, 8, 4, HD, HD), F32),
            vmem((8, 4, HD, HD), BF),
            vmem((8, 4, HD, HD), BF),
            vmem((8, 4, HD, HD), BF),
            vmem((8, 4, HD, HD), BF),
            vmem((2, 4, part), F32),
            vmem((2, 4, part), F32),
            vmem((2, 4, part), F32),
            vmem((16, 4, part), F32),
            DMA((5,)),
            DMA((4,)),
            DMA((4,)),
            DMA((16,)),
            DMA((16,)),
            DMA((3,)),
            DMA((4,)),
            DMA((8,)),
            DMA((8,)),
            DMA((16,)),
            DMA((16,)),
            *reduce_scratch(rows, width),
        ],
    )(
        grad_attn,
        full_in,
        query,
        key,
        query_rot,
        keys,
        values,
        attended,
        lse,
        *tables,
        *bounds,
        logical,
        scales,
        head_gains,
        qkv_w,
        out_w,
        grad_own,
        attn_term,
        ffn_term,
    )


def rotary_tables(offset):
    half_dim = HD // 2
    inverse = jnp.power(ROPE_THETA, -jnp.arange(half_dim, dtype=F32) * 2.0 / HD)
    angles = offset.astype(F32)[:, None] * inverse[None, :]
    cosine, sine_part = jnp.cos(angles), jnp.sin(angles)
    return (
        jnp.concatenate([cosine, cosine], axis=1),
        jnp.concatenate([-sine_part, sine_part], axis=1),
    )


def swap_cores(values):
    return lax.ppermute(values, "core", [(0, 1), (1, 0)])


def dotf(left, right, dims):
    return lax.dot_general(left, right, (dims, ((), ())), preferred_element_type=F32)


def plane_layer(
    inputs,
    cotangent,
    w_query,
    w_key,
    w_value,
    w_out,
    w_gate,
    w_up,
    w_down,
    query_gain,
    key_gain,
    attn_gain,
    ffn_gain,
    lengths,
    block_order,
):
    z, y, x, k = place()
    ctx = z * 2 + y
    tok_rows, width_part = inputs.shape
    plane_rows = tok_rows // 2
    tokens = 8 * plane_rows
    hidden = w_gate.shape[1] // 8

    order = block_order.reshape(8, 2, -1)
    block_rows = plane_rows // order.shape[2]

    def logical_of(core):
        blocks = lax.dynamic_index_in_dim(order, core, 1, keepdims=False).reshape(-1)
        return (
            blocks[:, None] * block_rows + jnp.arange(block_rows, dtype=jnp.int32)[None, :]
        ).reshape(-1)

    logical_own, logical_other = logical_of(k), logical_of(1 - k)
    offset_own = sequence_tables(logical_own, lengths)[1]
    tables = rotary_tables(offset_own)
    low = (logical_own - offset_own)[:, None]
    high = logical_own[:, None]
    logical_keys = jnp.concatenate([logical_own, logical_other])[None, :]

    gains = jnp.stack([query_gain, key_gain, attn_gain, ffn_gain])
    full_in, source_own, own_cot, qkv_w, out_w, gains_full, gu_stage, d_stage, query_proj, key_proj, value_low = open_layer(
        inputs, cotangent, w_query, w_key, w_value, w_out, w_gate, w_up, w_down, gains
    )
    head = x * 8 + ctx
    attn_gain_row, ffn_gain_row = gains_full[2:3], gains_full[3:4]
    head_gains = lax.dynamic_slice_in_dim(gains_full[:2], head * HD, HD, 1)
    (
        residual_full,
        residual_own,
        branch_own,
        gu_w,
        down_w,
        query_rot,
        keys_all,
        values_all,
        attended,
        lse,
        scales,
    ) = attention_forward(
        query_proj,
        key_proj,
        value_low,
        tables,
        (low, high),
        logical_keys,
        source_own,
        out_w,
        head_gains,
        attn_gain_row,
        gu_stage,
        d_stage,
    )
    gate_w, up_w = gu_w[0], gu_w[1]
    rows_dims = ((1,), (0,))

    gate_proj = dotf(residual_full, gate_w, rows_dims)
    up_proj = dotf(residual_full, up_w, rows_dims)
    gate_sigmoid = jax.nn.sigmoid(gate_proj)
    mixed = (gate_proj * gate_sigmoid * up_proj).astype(BF)
    grad_ffn, outputs, ffn_gain_term = after_ffn(
        dotf(mixed, down_w, rows_dims).astype(BF), residual_own, own_cot, ffn_gain_row
    )

    sum_rows = ((0,), (0,))
    turned = ((1,), (1,))
    grad_mixed = dotf(grad_ffn, down_w, turned)
    grad_gate = (
        grad_mixed * up_proj * gate_sigmoid * (1.0 + gate_proj * (1.0 - gate_sigmoid))
    ).astype(BF)
    grad_up = (grad_mixed * gate_proj * gate_sigmoid).astype(BF)
    resid_term = dotf(grad_gate, gate_w, turned) + dotf(grad_up, up_w, turned)
    grad_attn, grad_own, attn_gain_term = after_ffn_back(
        resid_term.astype(BF), own_cot, branch_own, attn_gain_row
    )
    gate_grad = dotf(residual_full, grad_gate, sum_rows)
    up_grad = dotf(residual_full, grad_up, sum_rows)
    down_grad = dotf(mixed, grad_ffn, sum_rows)
    mine_grads = (gate_grad[:, :hidden], up_grad[:, :hidden], down_grad[:hidden])
    other_grads = (gate_grad[:, hidden:], up_grad[:, hidden:], down_grad[hidden:])

    def ffn_stack(grads):
        return jnp.stack(
            [
                grads[0].reshape(8, -1, hidden),
                grads[1].reshape(8, -1, hidden),
                jnp.transpose(grads[2].reshape(hidden, 8, -1), (1, 0, 2)),
            ],
            axis=1,
        )

    from_other = swap_cores(ffn_stack(other_grads).astype(BF))
    ffn_sum = (ffn_stack(mine_grads) + from_other.astype(F32)).astype(BF)
    ffn_back = lax.all_to_all(ffn_sum, CTX, split_axis=0, concat_axis=0, tiled=True).astype(F32)
    grad_w_gate = jnp.transpose(ffn_back[:, 0], (1, 0, 2)).reshape(w_gate.shape)
    grad_w_up = jnp.transpose(ffn_back[:, 1], (1, 0, 2)).reshape(w_up.shape)
    grad_w_down = ffn_back[:, 2].reshape(w_down.shape)

    input_grad, grad_query, grad_key, grad_value, grad_w_out, gain_grads = attention_backward(
        grad_attn,
        full_in,
        query_proj,
        key_proj,
        query_rot,
        keys_all,
        values_all,
        attended,
        lse,
        tables,
        (low, high),
        logical_keys,
        scales,
        head_gains,
        qkv_w,
        out_w,
        grad_own,
        attn_gain_term,
        ffn_gain_term,
    )
    return (
        outputs,
        input_grad,
        grad_query,
        grad_key,
        grad_value,
        grad_w_out,
        grad_w_gate,
        grad_w_up,
        grad_w_down,
        gain_grads[0],
        gain_grads[1],
        gain_grads[2],
        gain_grads[3],
    )


def full_rows(piece):
    return lax.all_gather(piece, "head", axis=1, tiled=True)


def head_sums(term):
    return lax.psum_scatter(
        term.astype(jnp.bfloat16), "head", scatter_dimension=1, tiled=True
    ).astype(jnp.float32)


def row_single(term):
    return lax.psum(term, "head")


def row_pair(first, second):
    return lax.psum((first, second), "head")


def gather_weights(w_query, w_key, w_value, w_out, w_gate, w_up, w_down):
    row_parts = (
        lax.all_gather(w_query.astype(jnp.bfloat16), "ctx", axis=0, tiled=True),
        lax.all_gather(w_key.astype(jnp.bfloat16), "ctx", axis=0, tiled=True),
        lax.all_gather(w_value.astype(jnp.bfloat16), "ctx", axis=0, tiled=True),
        lax.all_gather(w_gate.astype(jnp.bfloat16), "ctx", axis=0, tiled=True),
        lax.all_gather(w_up.astype(jnp.bfloat16), "ctx", axis=0, tiled=True),
    )
    col_parts = (
        lax.all_gather(w_out.astype(jnp.bfloat16), "ctx", axis=1, tiled=True),
        lax.all_gather(w_down.astype(jnp.bfloat16), "ctx", axis=1, tiled=True),
    )
    return tuple(row_parts) + tuple(col_parts)


def sequence_tables(logical, lengths):
    seq_ends = jnp.cumsum(lengths)
    seq_starts = seq_ends - lengths
    number = jnp.sum((logical[:, None] >= seq_ends[None, :]).astype(jnp.int32), axis=1)
    member = number[:, None] == jnp.arange(lengths.shape[0], dtype=jnp.int32)[None, :]
    offset = logical - jnp.sum(jnp.where(member, seq_starts[None, :], 0), axis=1)
    return (number, offset)


def rotate(values, offset):
    half_dim = HD // 2
    inverse = jnp.power(ROPE_THETA, -jnp.arange(half_dim, dtype=jnp.float32) * 2.0 / HD)
    angles = offset.astype(jnp.float32)[:, None] * inverse[None, :]
    cosine = jnp.cos(angles)[:, None, :]
    sine_part = jnp.sin(angles)[:, None, :]
    first_half = values[..., :half_dim]
    second_half = values[..., half_dim:]
    return jnp.concatenate(
        [
            first_half * cosine - second_half * sine_part,
            second_half * cosine + first_half * sine_part,
        ],
        axis=-1,
    )


def norm_backward(grad_in, values, factor, gain):
    gain_term = jnp.sum(grad_in * values * factor[:, None], axis=0)
    weighted = grad_in * gain
    row_dot = row_single(jnp.sum(weighted * values, axis=1))
    grad_values = (
        factor[:, None] * weighted - values * (factor * factor * factor * row_dot / D)[:, None]
    )
    return (grad_values, gain_term)


def on_device(
    inputs,
    cotangent,
    w_query,
    w_key,
    w_value,
    w_out,
    w_gate,
    w_up,
    w_down,
    query_gain,
    key_gain,
    attn_gain,
    ffn_gain,
    lengths,
    block_order,
):
    shards = lax.axis_size("ctx")
    position = lax.axis_index("ctx")
    tok_rows, width_part = inputs.shape
    block_rows = tok_rows // shards
    total_tokens = tok_rows * shards
    local_heads = width_part // HD
    scaling = 1.0 / math.sqrt(HD)
    shard_range = jnp.arange(shards, dtype=jnp.int32)
    order_table = block_order.reshape(shards, shards)
    target = order_table % shards
    choose = target[:, :, None] == shard_range[None, None, :]
    stream = jnp.sum(jnp.where(choose, order_table[:, :, None], 0), axis=1)
    stream_blocks = jnp.transpose(stream).reshape(-1)
    logical = (
        stream_blocks[:, None] * block_rows + jnp.arange(block_rows, dtype=jnp.int32)[None, :]
    ).reshape(-1)
    own_target = lax.dynamic_index_in_dim(target, position, 0, keepdims=False)
    send_order = jnp.sum(
        jnp.where(own_target[:, None] == shard_range[None, :], shard_range[:, None], 0), axis=0
    )

    def deal_out(values):
        return values.reshape(shards, block_rows, width_part)[send_order].reshape(
            tok_rows, width_part
        )

    def undeal(values):
        return values.reshape(shards, block_rows, width_part)[own_target].reshape(
            tok_rows, width_part
        )

    local_in, local_cot = (
        lax.all_to_all(deal_out(inputs), "ctx", split_axis=0, concat_axis=0, tiled=True),
        lax.all_to_all(deal_out(cotangent), "ctx", split_axis=0, concat_axis=0, tiled=True),
    )
    number_all, offset_all = sequence_tables(logical, lengths)
    number_own = lax.dynamic_slice_in_dim(number_all, position * tok_rows, tok_rows)
    offset_own = lax.dynamic_slice_in_dim(offset_all, position * tok_rows, tok_rows)
    logical_own = lax.dynamic_slice_in_dim(logical, position * tok_rows, tok_rows)
    query_full, key_full, value_full, gate_full, up_full, out_full, down_full = gather_weights(
        w_query, w_key, w_value, w_out, w_gate, w_up, w_down
    )
    full_in = full_rows(local_in)
    query_proj = jnp.dot(full_in, query_full, preferred_element_type=jnp.float32)
    key_proj = jnp.dot(full_in, key_full, preferred_element_type=jnp.float32)
    value_proj = jnp.dot(full_in, value_full, preferred_element_type=jnp.float32)
    query_sq, key_sq = row_pair(
        jnp.sum(query_proj * query_proj, axis=1), jnp.sum(key_proj * key_proj, axis=1)
    )
    query_scale = lax.rsqrt(query_sq / D + EPSILON)
    key_scale = lax.rsqrt(key_sq / D + EPSILON)
    query_rot = rotate(
        (query_proj * query_scale[:, None] * query_gain).reshape(tok_rows, local_heads, HD),
        offset_own,
    ).astype(jnp.bfloat16)
    key_rot = rotate(
        (key_proj * key_scale[:, None] * key_gain).reshape(tok_rows, local_heads, HD), offset_own
    ).astype(jnp.bfloat16)
    value_low = value_proj.astype(jnp.bfloat16).reshape(tok_rows, local_heads, HD)
    keys_all, values_all = (
        lax.all_gather(key_rot, "ctx", axis=0, tiled=True),
        lax.all_gather(value_low, "ctx", axis=0, tiled=True),
    )
    key_span = math.gcd(total_tokens, 1024)
    key_turns = total_tokens // key_span
    pieces = (
        keys_all.reshape(key_turns, key_span, local_heads, HD),
        values_all.reshape(key_turns, key_span, local_heads, HD),
        number_all.reshape(key_turns, key_span),
        logical.reshape(key_turns, key_span),
    )

    def scores_of(key_piece, number_piece, logical_piece):
        raw_scores = (
            jnp.einsum("qhd,khd->hqk", query_rot, key_piece, preferred_element_type=jnp.float32)
            * scaling
        )
        allowed = (number_own[:, None] == number_piece[None, :]) & (
            logical_piece[None, :] <= logical_own[:, None]
        )
        return (raw_scores, allowed)

    def stat_turn(running, piece_set):
        running_max, running_sum = running
        raw_scores, allowed = scores_of(piece_set[0], piece_set[2], piece_set[3])
        masked_scores = jnp.where(allowed[None], raw_scores, MASKED)
        new_max = jnp.maximum(running_max, jnp.max(masked_scores, axis=2))
        fresh = jnp.sum(
            jnp.where(allowed[None], jnp.exp(masked_scores - new_max[..., None]), 0.0), axis=2
        )
        return ((new_max, running_sum * jnp.exp(running_max - new_max) + fresh), None)

    start_max = jnp.full((local_heads, tok_rows), MASKED, jnp.float32)
    start_sum = jnp.zeros((local_heads, tok_rows), jnp.float32)
    final_max, final_sum = lax.scan(stat_turn, (start_max, start_sum), pieces)[0]
    log_total = final_max + jnp.log(final_sum)

    def out_turn(accum, piece_set):
        raw_scores, allowed = scores_of(piece_set[0], piece_set[2], piece_set[3])
        weights_low = jnp.where(
            allowed[None], jnp.exp(raw_scores - log_total[..., None]), 0.0
        ).astype(jnp.bfloat16)
        return (
            accum
            + jnp.einsum(
                "hqk,khd->qhd", weights_low, piece_set[1], preferred_element_type=jnp.float32
            ),
            None,
        )

    attended = lax.scan(out_turn, jnp.zeros((tok_rows, local_heads, HD), jnp.float32), pieces)[0]
    attended_low = attended.reshape(tok_rows, width_part).astype(jnp.bfloat16)
    attn_part = head_sums(jnp.dot(attended_low, out_full, preferred_element_type=jnp.float32))
    attn_scale = lax.rsqrt(row_single(jnp.sum(attn_part * attn_part, axis=1)) / D + EPSILON)
    residual = local_in.astype(jnp.float32) + attn_part * attn_scale[:, None] * attn_gain
    residual_full = full_rows(residual.astype(jnp.bfloat16))
    gate_proj = jnp.dot(residual_full, gate_full, preferred_element_type=jnp.float32)
    up_proj = jnp.dot(residual_full, up_full, preferred_element_type=jnp.float32)
    gate_sigmoid = jax.nn.sigmoid(gate_proj)
    mixed_hidden = (gate_proj * gate_sigmoid * up_proj).astype(jnp.bfloat16)
    ffn_part = head_sums(jnp.dot(mixed_hidden, down_full, preferred_element_type=jnp.float32))
    ffn_scale = lax.rsqrt(row_single(jnp.sum(ffn_part * ffn_part, axis=1)) / D + EPSILON)
    result = residual + ffn_part * ffn_scale[:, None] * ffn_gain
    query_full, key_full, value_full, gate_full, up_full, out_full, down_full = gather_weights(
        w_query, w_key, w_value, w_out, w_gate, w_up, w_down
    )
    grad_result = local_cot.astype(jnp.float32)
    grad_ffn, ffn_gain_term = norm_backward(grad_result, ffn_part, ffn_scale, ffn_gain)
    grad_ffn_low = full_rows(grad_ffn.astype(jnp.bfloat16))
    down_grad = jnp.einsum(
        "tf,td->fd", mixed_hidden, grad_ffn_low, preferred_element_type=jnp.float32
    )
    grad_mixed = jnp.einsum(
        "td,fd->tf", grad_ffn_low, down_full, preferred_element_type=jnp.float32
    )
    grad_gate_low = (
        grad_mixed * up_proj * gate_sigmoid * (1.0 + gate_proj * (1.0 - gate_sigmoid))
    ).astype(jnp.bfloat16)
    grad_up_low = (grad_mixed * gate_proj * gate_sigmoid).astype(jnp.bfloat16)
    gate_grad = jnp.einsum(
        "td,tf->df", residual_full, grad_gate_low, preferred_element_type=jnp.float32
    )
    up_grad = jnp.einsum(
        "td,tf->df", residual_full, grad_up_low, preferred_element_type=jnp.float32
    )
    resid_term = jnp.einsum(
        "tf,df->td", grad_gate_low, gate_full, preferred_element_type=jnp.float32
    ) + jnp.einsum("tf,df->td", grad_up_low, up_full, preferred_element_type=jnp.float32)
    grad_residual = grad_result + head_sums(resid_term)
    grad_attn, attn_gain_term = norm_backward(grad_residual, attn_part, attn_scale, attn_gain)
    grad_attn_low = full_rows(grad_attn.astype(jnp.bfloat16))
    out_grad = jnp.einsum(
        "te,td->ed", attended_low, grad_attn_low, preferred_element_type=jnp.float32
    )
    grad_heads = (
        jnp.einsum("td,ed->te", grad_attn_low, out_full, preferred_element_type=jnp.float32)
        .astype(jnp.bfloat16)
        .reshape(tok_rows, local_heads, HD)
    )
    row_delta = jnp.transpose(jnp.sum(grad_heads.astype(jnp.float32) * attended, axis=2))

    def score_grads(key_piece, value_piece, number_piece, logical_piece):
        raw_scores, allowed = scores_of(key_piece, number_piece, logical_piece)
        probabilities = jnp.where(allowed[None], jnp.exp(raw_scores - log_total[..., None]), 0.0)
        grad_probs = jnp.einsum(
            "qhd,khd->hqk", grad_heads, value_piece, preferred_element_type=jnp.float32
        )
        grad_scores = (probabilities * (grad_probs - row_delta[..., None])).astype(jnp.bfloat16)
        return (probabilities, grad_scores)

    zero_heads = jnp.zeros((tok_rows, local_heads, HD), jnp.float32)

    def back_turn(grad_acc, piece_set):
        key_piece, value_piece, number_piece, logical_piece = piece_set
        probabilities, grad_scores = score_grads(
            key_piece, value_piece, number_piece, logical_piece
        )
        grad_acc = (
            grad_acc
            + jnp.einsum("hqk,khd->qhd", grad_scores, key_piece, preferred_element_type=jnp.float32)
            * scaling
        )
        key_term = (
            jnp.einsum("hqk,qhd->khd", grad_scores, query_rot, preferred_element_type=jnp.float32)
            * scaling
        )
        value_term = jnp.einsum(
            "hqk,qhd->khd",
            probabilities.astype(jnp.bfloat16),
            grad_heads,
            preferred_element_type=jnp.float32,
        )
        return (grad_acc, (key_term, value_term))

    grad_query_rot, key_value_terms = lax.scan(back_turn, zero_heads, pieces)
    key_terms = key_value_terms[0].reshape(total_tokens, local_heads, HD)
    value_terms = key_value_terms[1].reshape(total_tokens, local_heads, HD)
    grad_key_rot, grad_value_own = (
        lax.psum_scatter(
            key_terms.astype(jnp.bfloat16), "ctx", scatter_dimension=0, tiled=True
        ).astype(jnp.float32),
        lax.psum_scatter(
            value_terms.astype(jnp.bfloat16), "ctx", scatter_dimension=0, tiled=True
        ).astype(jnp.float32),
    )
    grad_query_normed = rotate(grad_query_rot, -offset_own).reshape(tok_rows, width_part)
    grad_key_normed = rotate(grad_key_rot, -offset_own).reshape(tok_rows, width_part)
    query_gain_term = jnp.sum(grad_query_normed * query_proj * query_scale[:, None], axis=0)
    key_gain_term = jnp.sum(grad_key_normed * key_proj * key_scale[:, None], axis=0)
    weighted_query = grad_query_normed * query_gain
    weighted_key = grad_key_normed * key_gain
    query_dot, key_dot = row_pair(
        jnp.sum(weighted_query * query_proj, axis=1), jnp.sum(weighted_key * key_proj, axis=1)
    )
    grad_query_low = (
        query_scale[:, None] * weighted_query
        - query_proj * (query_scale * query_scale * query_scale * query_dot / D)[:, None]
    ).astype(jnp.bfloat16)
    grad_key_low = (
        key_scale[:, None] * weighted_key
        - key_proj * (key_scale * key_scale * key_scale * key_dot / D)[:, None]
    ).astype(jnp.bfloat16)
    grad_value_low = grad_value_own.reshape(tok_rows, width_part).astype(jnp.bfloat16)
    query_grad = jnp.einsum(
        "td,te->de", full_in, grad_query_low, preferred_element_type=jnp.float32
    )
    key_grad = jnp.einsum("td,te->de", full_in, grad_key_low, preferred_element_type=jnp.float32)
    value_grad = jnp.einsum(
        "td,te->de", full_in, grad_value_low, preferred_element_type=jnp.float32
    )
    input_term = jnp.einsum(
        "te,de->td", grad_query_low, query_full, preferred_element_type=jnp.float32
    )
    input_term = input_term + jnp.einsum(
        "te,de->td", grad_key_low, key_full, preferred_element_type=jnp.float32
    )
    input_term = input_term + jnp.einsum(
        "te,de->td", grad_value_low, value_full, preferred_element_type=jnp.float32
    )
    grad_input = grad_residual + head_sums(input_term)
    row_grads = (
        lax.psum_scatter(
            query_grad.astype(jnp.bfloat16), "ctx", scatter_dimension=0, tiled=True
        ).astype(jnp.float32),
        lax.psum_scatter(
            key_grad.astype(jnp.bfloat16), "ctx", scatter_dimension=0, tiled=True
        ).astype(jnp.float32),
        lax.psum_scatter(
            value_grad.astype(jnp.bfloat16), "ctx", scatter_dimension=0, tiled=True
        ).astype(jnp.float32),
        lax.psum_scatter(
            gate_grad.astype(jnp.bfloat16), "ctx", scatter_dimension=0, tiled=True
        ).astype(jnp.float32),
        lax.psum_scatter(
            up_grad.astype(jnp.bfloat16), "ctx", scatter_dimension=0, tiled=True
        ).astype(jnp.float32),
    )
    col_grads = (
        lax.psum_scatter(
            out_grad.astype(jnp.bfloat16), "ctx", scatter_dimension=1, tiled=True
        ).astype(jnp.float32),
        lax.psum_scatter(
            down_grad.astype(jnp.bfloat16), "ctx", scatter_dimension=1, tiled=True
        ).astype(jnp.float32),
    )
    gain_totals = lax.psum((query_gain_term, key_gain_term, attn_gain_term, ffn_gain_term), "ctx")
    back_result, back_grad = (
        lax.all_to_all(result.astype(jnp.bfloat16), "ctx", split_axis=0, concat_axis=0, tiled=True),
        lax.all_to_all(
            grad_input.astype(jnp.bfloat16), "ctx", split_axis=0, concat_axis=0, tiled=True
        ),
    )
    return (
        undeal(back_result),
        undeal(back_grad),
        row_grads[0],
        row_grads[1],
        row_grads[2],
        col_grads[0],
        row_grads[3],
        row_grads[4],
        col_grads[1],
        gain_totals[0],
        gain_totals[1],
        gain_totals[2],
        gain_totals[3],
    )


def sharded(layer, mesh, ctx, head):
    wide, tall, line = P(ctx, head), P(head, ctx), P(head)
    return jax.shard_map(
        layer,
        mesh=mesh,
        in_specs=(
            *(wide,) * 5,
            tall,
            wide,
            wide,
            tall,
            *(line,) * 4,
            P(),
            P(),
        ),
        out_specs=(*(wide,) * 5, tall, wide, wide, tall, *(line,) * 4),
        check_vma=False,
    )


def solution(mesh):
    if dict(mesh.shape) == {"ctx": 8, "head": 4}:
        split = Mesh(mesh.devices.reshape(4, 2, 2, 2), AXES)
        return sharded(plane_layer, split, CTX, ("x", "core"))
    return sharded(on_device, mesh, "ctx", "head")
```

```python
import math

import jax
import jax.numpy as jnp
from jax import lax
from jax.experimental import pallas as pl
from jax.experimental.pallas import tpu as pltpu
from jax.sharding import Mesh
from jax.sharding import PartitionSpec as P

D = 2048
HD = 128


EPSILON = 1e-06
ROPE_THETA = 500000.0
MASKED = -1e30


BF = jnp.bfloat16
F32 = jnp.float32
MESH = pl.DeviceIdType.MESH
AXES = ("z", "y", "x", "core")
CTX = ("z", "y")
STRIP = 16
ANY = pl.BlockSpec(memory_space=pl.ANY)
VMEM = pl.BlockSpec(memory_space=pltpu.VMEM)
DMA = pltpu.SemaphoreType.DMA
BIG_VMEM = 56 * 1024 * 1024


def place():
    return tuple(lax.axis_index(name) for name in AXES)


def greet(targets):
    barrier = pltpu.get_barrier_semaphore()
    for target in targets:
        pl.semaphore_signal(barrier, inc=1, device_id=target, device_id_type=MESH)
    pl.semaphore_wait(barrier, len(targets))


def near_first(step, z):
    high = z // 2
    low = z + high * (3 - 2 * z)
    value = (low, 1 - low, 2, 3)[step]
    return value + high * (3 - 2 * value)


def plane_axes(me):
    z, y, x, k = me
    a = x * (1 - k) + y * k
    b = y * (1 - k) + x * k

    def slot(zp, ap, bp):
        yp = bp * (1 - k) + ap * k
        xp = ap * (1 - k) + bp * k
        return zp * 4 + yp * 2 + xp

    dev_a = (z, y * (1 - k) + (1 - y) * k, (1 - x) * (1 - k) + x * k, k)
    dev_b = (z, (1 - y) * (1 - k) + y * k, x * (1 - k) + (1 - x) * k, k)
    return a, b, slot, dev_a, dev_b


def plane_neighbours(me):
    z, y, x, k = me
    up = z + 1 - 2 * (z // 3)
    down = z - 1 + 2 * ((3 - z) // 3)
    return [(z, 1 - y, x, k), (z, y, 1 - x, k)], up, down


def greet_plane(me, others=()):
    z, y, x, k = me
    barrier = pltpu.get_barrier_semaphore()
    targets = [(z, 1 - y, x, k), (z, y, 1 - x, k), *others]
    for target in targets:
        pl.semaphore_signal(barrier, inc=1, device_id=target, device_id_type=MESH)

    @pl.when(z < 3)
    def _():
        pl.semaphore_signal(barrier, inc=1, device_id=(z + 1, y, x, k), device_id_type=MESH)

    @pl.when(z > 0)
    def _():
        pl.semaphore_signal(barrier, inc=1, device_id=(z - 1, y, x, k), device_id_type=MESH)

    inner = (z + 2) // 3 - z // 3
    pl.semaphore_wait(barrier, len(targets) + 1 + inner)


GATHER_SEMS = [DMA((16,)), DMA((4,)), DMA((4,)), DMA((4,)), DMA((8,))]


def gather_plane(me, own_ref, view, sems, between=lambda step: None):
    z, y, x, k = me
    recv, up_send, down_send, a_send, b_send = sems
    a, b, slot, dev_a, dev_b = plane_axes(me)
    own = slot(z, a, b)

    def copy(src, index, send_sem, device):
        return pltpu.make_async_remote_copy(
            src_ref=src,
            dst_ref=view(index),
            send_sem=send_sem,
            recv_sem=recv.at[index],
            device_id=device,
            device_id_type=MESH,
        )

    def landed(index):
        copy(view(index), index, a_send.at[0], dev_a).wait_recv()

    for step in range(5):
        if step < 4:
            zp = near_first(step, z)
            index = slot(zp, a, b)
            if step == 0:
                src = own_ref
            else:
                landed(index)
                src = view(index)

            @pl.when((zp <= z) & (z < 3))
            def _():
                copy(src, index, up_send.at[zp], (z + 1, y, x, k)).start()

            @pl.when((zp >= z) & (z > 0))
            def _():
                copy(src, index, down_send.at[zp], (z - 1, y, x, k)).start()

            copy(src, index, a_send.at[step], dev_a).start()
            copy(src, index, b_send.at[step], dev_b).start()
        if step > 0:
            index = slot(near_first(step - 1, z), 1 - a, b)
            landed(index)
            copy(view(index), index, b_send.at[3 + step], dev_b).start()
        between(step)
    for step in range(4):
        zp = near_first(step, z)
        landed(slot(zp, a, 1 - b))
        landed(slot(zp, 1 - a, 1 - b))
    for step in range(4):
        zp = near_first(step, z)
        for ap, number in ((a, step), (1 - a, 4 + step)):
            index = slot(zp, ap, b)
            copy(view(index), index, b_send.at[number], dev_b).wait_send()
        index = slot(zp, a, b)
        copy(view(index), index, a_send.at[step], dev_a).wait_send()

        @pl.when((zp <= z) & (z < 3))
        def _():
            copy(view(index), index, up_send.at[zp], (z + 1, y, x, k)).wait_send()

        @pl.when((zp >= z) & (z > 0))
        def _():
            copy(view(index), index, down_send.at[zp], (z - 1, y, x, k)).wait_send()


def reduce_scratch(rows, width):
    return [
        pltpu.VMEM((4, 2, rows, width), BF),
        pltpu.VMEM((4, rows, width), BF),
        pltpu.VMEM((4, rows, width), BF),
        pltpu.VMEM((4, rows, width), BF),
        pltpu.VMEM((4, rows, width), BF),
        pltpu.VMEM((4, rows, width), BF),
        DMA((8,)),
        DMA((8,)),
        DMA((4,)),
        DMA((4,)),
        DMA((4,)),
        DMA((4,)),
        DMA((4,)),
    ]


N_REDUCE = 13


def strips(rows, work, strip=STRIP):
    def body(i, carry):
        work(pl.ds(pl.multiple_of(i * strip, strip), strip))
        return carry

    lax.fori_loop(0, rows // strip, body, 0)


def reduce_plane(me, terms, rows, scratch, produce, finish, after_terms=lambda: None):
    z, y, x, k = me
    (from_b, to_a, from_a, to_z, from_low, from_high) = scratch[:6]
    (b_send, b_recv, a_send, a_recv, z_send, low_recv, high_recv) = scratch[6:]
    a, b, slot, dev_a, dev_b = plane_axes(me)
    order = [near_first(step, z) for step in (3, 2, 1, 0)]

    def start_of(zp, ap, bp):
        return pl.multiple_of(slot(zp, ap, bp) * rows, rows)

    def copy_b(zp, ap):
        return pltpu.make_async_remote_copy(
            src_ref=terms.at[pl.ds(start_of(zp, ap, 1 - b), rows), :],
            dst_ref=from_b.at[zp, ap],
            send_sem=b_send.at[zp * 2 + ap],
            recv_sem=b_recv.at[zp * 2 + ap],
            device_id=dev_b,
            device_id_type=MESH,
        )

    def copy_a(zp):
        return pltpu.make_async_remote_copy(
            src_ref=to_a.at[zp],
            dst_ref=from_a.at[zp],
            send_sem=a_send.at[zp],
            recv_sem=a_recv.at[zp],
            device_id=dev_a,
            device_id_type=MESH,
        )

    def copy_z(zp, target, recv, to):
        return pltpu.make_async_remote_copy(
            src_ref=to_z.at[zp],
            dst_ref=target.at[zp],
            send_sem=z_send.at[zp],
            recv_sem=recv.at[zp],
            device_id=(to, y, x, k),
            device_id_type=MESH,
        )

    def copy_up(zp):
        return copy_z(zp, from_low, low_recv, z + 1)

    def copy_down(zp):
        return copy_z(zp, from_high, high_recv, z - 1)

    def mine(zp, ap, strip):
        at = pl.ds(pl.multiple_of(start_of(zp, ap, b) + strip.start, STRIP), STRIP)
        return terms[at, :].astype(F32)

    for zp in order:
        produce(zp)
        for ap in (1 - a, a):
            copy_b(zp, ap).start()
    after_terms()

    for step in range(5):
        if step < 4:
            zp = order[step]
            copy_b(zp, 1 - a).wait_recv()

            def first(strip, zp=zp):
                to_a[zp, strip] = (
                    mine(zp, 1 - a, strip) + from_b[zp, 1 - a, strip].astype(F32)
                ).astype(BF)

            strips(rows, first)
            copy_a(zp).start()
        if step > 0:
            zp = order[step - 1]
            copy_b(zp, a).wait_recv()
            copy_a(zp).wait_recv()

            def own_sum(strip, zp=zp):
                return (
                    mine(zp, a, strip)
                    + from_b[zp, a, strip].astype(F32)
                    + from_a[zp, strip].astype(F32)
                )

            if step < 4:
                upward = zp > z

                @pl.when(upward & (z > 0))
                def _(zp=zp, own_sum=own_sum):
                    copy_up(zp).wait_recv()

                    def work(strip):
                        to_z[zp, strip] = (own_sum(strip) + from_low[zp, strip].astype(F32)).astype(BF)

                    strips(rows, work)

                @pl.when(jnp.logical_not(upward) & (z < 3))
                def _(zp=zp, own_sum=own_sum):
                    copy_down(zp).wait_recv()

                    def work(strip):
                        to_z[zp, strip] = (own_sum(strip) + from_high[zp, strip].astype(F32)).astype(BF)

                    strips(rows, work)

                @pl.when((z == 0) | (z == 3))
                def _(zp=zp, own_sum=own_sum):
                    def work(strip):
                        to_z[zp, strip] = own_sum(strip).astype(BF)

                    strips(rows, work)

                @pl.when(upward)
                def _(zp=zp):
                    copy_up(zp).start()

                @pl.when(jnp.logical_not(upward))
                def _(zp=zp):
                    copy_down(zp).start()

            else:

                @pl.when(z == 0)
                def _():
                    copy_down(z).wait_recv()
                    strips(rows, lambda s: finish(s, own_sum(s) + from_high[z, s].astype(F32)))

                @pl.when(z == 3)
                def _():
                    copy_up(z).wait_recv()
                    strips(rows, lambda s: finish(s, own_sum(s) + from_low[z, s].astype(F32)))

                @pl.when((z > 0) & (z < 3))
                def _():
                    copy_up(z).wait_recv()
                    copy_down(z).wait_recv()
                    strips(
                        rows,
                        lambda s: finish(
                            s,
                            own_sum(s) + from_low[z, s].astype(F32) + from_high[z, s].astype(F32),
                        ),
                    )

    def settle():
        for zp in order:
            copy_b(zp, 0).wait_send()
            copy_b(zp, 1).wait_send()
            copy_a(zp).wait_send()
        for zp in order[:3]:
            copy_up(zp).wait_send()

    return settle


def own_tile(me):
    z, y, x, k = me
    return z * 2 + y


def gather_view(out_ref, rows):
    def view(slot):
        return out_ref.at[pl.ds(pl.multiple_of(slot * rows, rows), rows), :]

    return view


def hand_out_copies(me, own_ref, out_ref, send, recv):
    z, y, x, k = me
    rows, width = own_ref.shape
    part = width // 4
    target_rows = pl.ds(pl.multiple_of(k * 2 * rows + x * rows, rows), rows)

    def copy(xt, kt, number):
        return pltpu.make_async_remote_copy(
            src_ref=own_ref.at[:, pl.ds(pl.multiple_of((2 * xt + kt) * part, part), part)],
            dst_ref=out_ref.at[target_rows, :],
            send_sem=send.at[number],
            recv_sem=recv.at[number],
            device_id=(z, y, xt, kt),
            device_id_type=MESH,
        )

    local = pltpu.make_async_copy(
        own_ref.at[:, pl.ds(pl.multiple_of((2 * x + k) * part, part), part)],
        out_ref.at[target_rows, :],
        recv.at[3],
    )
    return [copy(x, 1 - k, 0), copy(1 - x, k, 1), copy(1 - x, 1 - k, 2)], local


def pair_devices(me):
    z, y, x, k = me
    return [(z, y, x, 1 - k), (z, y, 1 - x, 1 - k)]


def row_scale(values):
    return lax.rsqrt(jnp.sum(values * values, axis=1, keepdims=True) / values.shape[1] + EPSILON)


def norm_back_strip(grad, values, gain):
    scale = row_scale(values)
    term = grad * values * scale
    weighted = grad * gain
    dot = jnp.sum(weighted * values, axis=1, keepdims=True)
    back = scale * weighted - values * (scale * scale * scale * dot / values.shape[1])
    return back, term[:8] + term[8:]


def comm_call(body, name, number, out_shape, in_specs, out_specs, scratch, cost=None):
    return pl.pallas_call(
        body,
        name=name,
        out_shape=out_shape,
        in_specs=in_specs,
        out_specs=out_specs,
        scratch_shapes=scratch,
        cost_estimate=cost,
        compiler_params=pltpu.CompilerParams(
            collective_id=number, has_side_effects=True, vmem_limit_bytes=BIG_VMEM
        ),
    )


def same_x_greet(me):
    z, y, x, k = me
    barrier = pltpu.get_barrier_semaphore()
    number = z * 4 + y * 2 + k

    def body(i, carry):
        other = lax.rem(number + i, 16)
        pl.semaphore_signal(
            barrier,
            inc=1,
            device_id=(other // 4, (other // 2) % 2, x, other % 2),
            device_id_type=MESH,
        )
        return carry

    lax.fori_loop(1, 16, body, 0)
    for kt in (k, 1 - k):
        pl.semaphore_signal(barrier, inc=1, device_id=(z, y, 1 - x, kt), device_id_type=MESH)
    pl.semaphore_wait(barrier, 17)


def masked_scores(q, keys, low, high, logical):
    raw = lax.dot_general(q, keys, (((1,), (1,)), ((), ())), preferred_element_type=F32)
    allowed = (logical >= low) & (logical <= high)
    return raw * (1.0 / math.sqrt(HD)), allowed


def open_layer(inputs, cotangent, w_query, w_key, w_value, w_out, w_gate, w_up, w_down, gains):
    rows, part = inputs.shape
    half = rows // 2
    quarter = half // 2
    tokens, width = 8 * half, 4 * part
    hidden = w_gate.shape[1]

    def body(*refs):
        (in_ref, cot_ref, wq_ref, wk_ref, wv_ref, wo_ref, wg_ref, wu_ref, wd_ref, gain_ref) = refs[:10]
        (full_out, own_out, own_cot_ref, wqkv_ref, wout_ref, gains_ref, gu_out, d_out) = refs[10:18]
        (q_ref, k_ref, v_ref) = refs[18:21]
        (full_ref, shard, cot_half, qkv_raw, out_raw, gu_raw, d_raw) = refs[21:28]
        (qkv_stage, out_stage, gu_stage, d_stage) = refs[28:32]
        (load_sem, pair_send, pair_recv, local_sem, deal_send, deal_recv) = refs[32:38]
        (share_send, share_recv, gain_send, gain_recv, cot_sems, keep_sem) = refs[38:44]
        gather_sems = refs[44:]
        me = z, y, x, k = place()
        ctx = own_tile(me)
        sibling = (z, y, x, 1 - k)

        loads = [
            pltpu.make_async_copy(src, dst, load_sem.at[i])
            for i, (src, dst) in enumerate(
                [
                    (wq_ref, qkv_raw.at[0]),
                    (wk_ref, qkv_raw.at[1]),
                    (wv_ref, qkv_raw.at[2]),
                    (wo_ref, out_raw),
                    (wg_ref, gu_raw.at[0]),
                    (wu_ref, gu_raw.at[1]),
                    (wd_ref, d_raw),
                ]
            )
        ]
        for load in loads:
            load.start()
        same_x_greet(me)

        def pair_copy(src, dst, number):
            columns = pl.ds(pl.multiple_of(k * part, part), part)
            remote = pltpu.make_async_remote_copy(
                src_ref=src.at[pl.ds(pl.multiple_of((1 - k) * half, half), half), :],
                dst_ref=dst.at[:, columns],
                send_sem=pair_send.at[number],
                recv_sem=pair_recv.at[number],
                device_id=sibling,
                device_id_type=MESH,
            )
            local = pltpu.make_async_copy(
                src.at[pl.ds(pl.multiple_of(k * half, half), half), :],
                dst.at[:, columns],
                local_sem.at[number],
            )
            remote.start()
            local.start()
            return remote, local

        first = pair_copy(in_ref, shard, 0)
        second = pair_copy(cot_ref, cot_half, 1)

        def gain_copy(xt, kt, number):
            return pltpu.make_async_remote_copy(
                src_ref=gain_ref,
                dst_ref=gains_ref.at[:, pl.ds(pl.multiple_of((2 * x + k) * part, part), part)],
                send_sem=gain_send.at[number],
                recv_sem=gain_recv.at[number],
                device_id=(z, y, xt, kt),
                device_id_type=MESH,
            )

        gain_copies = [gain_copy(x, 1 - k, 0), gain_copy(1 - x, k, 1), gain_copy(1 - x, 1 - k, 2)]
        for copy in gain_copies:
            copy.start()
        gain_local = pltpu.make_async_copy(
            gain_ref,
            gains_ref.at[:, pl.ds(pl.multiple_of((2 * x + k) * part, part), part)],
            local_sem.at[2],
        )
        gain_local.start()

        first[0].wait_recv()
        first[1].wait()

        def view(slot):
            return full_ref.at[
                pl.ds(pl.multiple_of((slot // 2) * half, half), half),
                pl.ds(pl.multiple_of((slot % 2) * 2 * part, 2 * part), 2 * part),
            ]

        own_slot = ctx * 2 + x
        own_local = pltpu.make_async_copy(shard, view(own_slot), local_sem.at[3])
        own_local.start()

        def deal(e):
            j, r = e // 2, e % 2
            return [
                pltpu.make_async_remote_copy(
                    src_ref=src,
                    dst_ref=dst,
                    send_sem=deal_send.at[i, e],
                    recv_sem=deal_recv.at[i, ctx],
                    device_id=(2 * k + e // 4, (e // 2) % 2, x, r),
                    device_id_type=MESH,
                )
                for i, (src, dst) in enumerate(deal_ends(j, r))
            ]

        def deal_ends(j, r):
            at = pl.ds(pl.multiple_of(ctx * 2 * HD + r * HD, HD), HD)
            return (
                (
                    qkv_stage.at[:, r * HD : (r + 1) * HD, j * HD : (j + 1) * HD],
                    wqkv_ref.at[:, at, :],
                ),
                (
                    out_stage.at[j * HD : (j + 1) * HD, r * HD : (r + 1) * HD],
                    wout_ref.at[:, at],
                ),
            )

        stays = k == z // 2
        own_e = (z % 2) * 4 + y * 2 + k

        def deal_all():
            for load in loads[:4]:
                load.wait()

            def round_qkv(s):
                for i in range(3):
                    qkv_stage[i, s] = qkv_raw[i, s].astype(BF)

            strips(rows, round_qkv)

            def round_out(s):
                out_stage[s] = out_raw[s].astype(BF)

            strips(2 * rows, round_out, 32)
            for e in range(8):

                @pl.when(jnp.logical_not(stays & (own_e == e)))
                def _(e=e):
                    for copy in deal(e):
                        copy.start()

                @pl.when(stays & (own_e == e))
                def _(e=e):
                    for i, (src, dst) in enumerate(deal_ends(e // 2, e % 2)):
                        pltpu.make_async_copy(src, dst, deal_recv.at[i, ctx]).start()

        def cot_begin():
            second[0].wait_recv()
            second[1].wait()
            cot_remote.start()
            cot_local.start()

        wide = pl.ds(pl.multiple_of(x * 2 * part, 2 * part), 2 * part)
        cot_remote = pltpu.make_async_remote_copy(
            src_ref=cot_half.at[pl.ds(pl.multiple_of((1 - x) * quarter, quarter), quarter), :],
            dst_ref=own_cot_ref.at[:, wide],
            send_sem=cot_sems.at[0],
            recv_sem=cot_sems.at[1],
            device_id=(z, y, 1 - x, k),
            device_id_type=MESH,
        )
        cot_local = pltpu.make_async_copy(
            cot_half.at[pl.ds(pl.multiple_of(x * quarter, quarter), quarter), :],
            own_cot_ref.at[:, wide],
            cot_sems.at[2],
        )

        keeps = [
            pltpu.make_async_copy(gu_stage.at[0], gu_out.at[0], keep_sem.at[0]),
            pltpu.make_async_copy(gu_stage.at[1], gu_out.at[1], keep_sem.at[1]),
            pltpu.make_async_copy(d_stage, d_out, keep_sem.at[2]),
        ]

        def round_up(i):
            loads[4 + i].wait()

            def work(s):
                gu_stage[i, s] = gu_raw[i, s].astype(BF)

            strips(rows, work)
            keeps[i].start()

        def round_down():
            loads[6].wait()

            def work(s):
                d_stage[s] = d_raw[s].astype(BF)

            strips(hidden, work, 128)
            keeps[2].start()

        between = [
            deal_all,
            lambda: (cot_begin(), round_up(0)),
            lambda: round_up(1),
            round_down,
            lambda: None,
        ]
        gather_plane(me, shard, view, gather_sems, lambda step: between[step]())

        def deal_wait(c):
            at = slice(c * 2 * HD, c * 2 * HD + HD)
            pltpu.make_async_copy(
                qkv_stage.at[:, :HD, :HD], wqkv_ref.at[:, at, :], deal_recv.at[0, c]
            ).wait()
            pltpu.make_async_copy(
                out_stage.at[:HD, :HD], wout_ref.at[:, at], deal_recv.at[1, c]
            ).wait()

        def share(c, r):
            at = pl.ds(pl.multiple_of(c * 2 * HD + r * HD, HD), HD)
            return [
                pltpu.make_async_remote_copy(
                    src_ref=ref,
                    dst_ref=ref,
                    send_sem=share_send.at[i, c],
                    recv_sem=share_recv.at[i, c],
                    device_id=sibling,
                    device_id_type=MESH,
                )
                for i, ref in enumerate((wqkv_ref.at[:, at, :], wout_ref.at[:, at]))
            ]

        for c in range(8):
            deal_wait(c)
            for copy in share(c, k):
                copy.start()
        own_local.wait()
        full_keep = pltpu.make_async_copy(full_ref, full_out, keep_sem.at[3])
        full_keep.start()
        own_rows = pl.ds(pl.multiple_of(own_slot * quarter, quarter), quarter)
        own_keep = pltpu.make_async_copy(full_ref.at[own_rows, :], own_out, keep_sem.at[4])
        own_keep.start()
        for c in range(8):
            for copy in share(c, 1 - k):
                copy.wait_recv()

        def project(s):
            tile = full_ref[s, :]
            q_ref[s, :] = jnp.dot(tile, wqkv_ref[0], preferred_element_type=F32)
            k_ref[s, :] = jnp.dot(tile, wqkv_ref[1], preferred_element_type=F32)
            v_ref[s, :] = jnp.dot(tile, wqkv_ref[2], preferred_element_type=F32).astype(BF)

        strips(tokens, project, 256)
        for e in range(8):

            @pl.when(jnp.logical_not(stays & (own_e == e)))
            def _(e=e):
                for copy in deal(e):
                    copy.wait_send()

        for c in range(8):
            for copy in share(c, k):
                copy.wait_send()
        first[0].wait_send()
        second[0].wait_send()
        for copy in gain_copies:
            copy.wait()
        gain_local.wait()
        cot_remote.wait()
        cot_local.wait()
        for keep in (*keeps, full_keep, own_keep):
            keep.wait()

    shape = jax.ShapeDtypeStruct
    return comm_call(
        body,
        "open_layer",
        0,
        (
            shape((tokens, width), BF),
            shape((quarter, width), BF),
            shape((quarter, width), BF),
            shape((3, width, HD), BF),
            shape((HD, width), BF),
            shape((4, width), F32),
            shape((2, rows, hidden), BF),
            shape((hidden, rows), BF),
            shape((tokens, HD), F32),
            shape((tokens, HD), F32),
            shape((tokens, HD), BF),
        ),
        [ANY] * 10,
        (ANY, ANY, ANY, VMEM, VMEM, ANY, ANY, ANY, VMEM, VMEM, VMEM),
        [
            pltpu.VMEM((tokens, width), BF),
            pltpu.VMEM((half, 2 * part), BF),
            pltpu.VMEM((half, 2 * part), BF),
            pltpu.VMEM((3, rows, part), F32),
            pltpu.VMEM((part, rows), F32),
            pltpu.VMEM((2, rows, hidden), F32),
            pltpu.VMEM((hidden, rows), F32),
            pltpu.VMEM((3, rows, part), BF),
            pltpu.VMEM((part, rows), BF),
            pltpu.VMEM((2, rows, hidden), BF),
            pltpu.VMEM((hidden, rows), BF),
            DMA((7,)),
            DMA((2,)),
            DMA((2,)),
            DMA((4,)),
            DMA((2, 8)),
            DMA((2, 8)),
            DMA((2, 8)),
            DMA((2, 8)),
            DMA((3,)),
            DMA((3,)),
            DMA((3,)),
            DMA((5,)),
            *GATHER_SEMS,
        ],
    )(inputs, cotangent, w_query, w_key, w_value, w_out, w_gate, w_up, w_down, gains)


def eye_mask():
    return lax.broadcasted_iota(jnp.int32, (HD, HD), 0) == lax.broadcasted_iota(
        jnp.int32, (HD, HD), 1
    )


def column_to_row(column, eye):
    return jnp.sum(jnp.where(eye, column, 0.0), axis=0, keepdims=True)


def row_to_column(row, eye):
    return jnp.sum(jnp.where(eye, row, 0.0), axis=1, keepdims=True)


def plane_peer(me, i):
    z, y, x, k = me
    other = lax.rem(z * 4 + y * 2 + x + i, 16)
    return other, (other // 4, (other // 2) % 2, other % 2, k)


def plane_greet_all(me, others):
    barrier = pltpu.get_barrier_semaphore()

    def call(i, carry):
        pl.semaphore_signal(barrier, inc=1, device_id=plane_peer(me, i)[1], device_id_type=MESH)
        return carry

    lax.fori_loop(1, 16, call, 0)
    for other in others:
        pl.semaphore_signal(barrier, inc=1, device_id=other, device_id_type=MESH)
    pl.semaphore_wait(barrier, 15 + len(others))


def sum_over_plane(me, slots, send, recv):
    own = me[0] * 4 + me[1] * 2 + me[2]

    def copy(i, slot):
        return pltpu.make_async_remote_copy(
            src_ref=slots.at[slot],
            dst_ref=slots.at[slot],
            send_sem=send.at[i],
            recv_sem=recv.at[slot],
            device_id=plane_peer(me, i)[1],
            device_id_type=MESH,
        )

    def begin(i, carry):
        copy(i, own).start()
        return carry

    lax.fori_loop(1, 16, begin, 0)

    def landed(i, carry):
        copy(i, plane_peer(me, i)[0]).wait_recv()
        return carry

    lax.fori_loop(1, 16, landed, 0)

    def sent(i, carry):
        copy(i, own).wait_send()
        return carry

    lax.fori_loop(1, 16, sent, 0)
    total = slots[0]
    for i in range(1, 16):
        total = total + slots[i]
    return total


def attention_forward(
    query, key, value, tables, bounds, logical, source, out_weight, gains, attn_gain, gu_stage, d_stage
):
    tokens, width = query.shape[0], source.shape[1]
    rows = tokens // 16
    group = tokens // 4
    hidden = gu_stage.shape[2] // 8
    part = width // 8

    def body(*refs):
        (q_in, k_in, v_in, cos_ref, sin_ref, low_ref, high_ref, log_ref, source_ref, wout_ref, gain_ref, attn_ref) = refs[:12]
        (gu_ref, d_ref) = refs[12:14]
        (full_ref, own_ref, branch_ref, wgu_ref, wd_ref, qrot_ref, keys_ref, values_ref, o_ref, lse_ref, scale_ref) = refs[14:25]
        (terms, shard, slots, tot_send, tot_recv, pair_send, pair_recv, local) = refs[25:33]
        (ffn_send, ffn_recv, share_send, share_recv, ffn_local) = refs[33:38]
        rest = refs[38:]
        me = z, y, x, k = place()
        ctx = own_tile(me)
        sibling = (z, y, x, 1 - k)
        barrier = pltpu.get_barrier_semaphore()
        plane_greet_all(me, [sibling])

        def pair(src, dst, n):
            return pltpu.make_async_remote_copy(
                src_ref=src,
                dst_ref=dst,
                send_sem=pair_send.at[n],
                recv_sem=pair_recv.at[n],
                device_id=sibling,
                device_id_type=MESH,
            )

        eye = eye_mask()
        own = z * 4 + y * 2 + x
        for i in range(8):
            piece = slice(i * HD, (i + 1) * HD)
            for side, ref in enumerate((q_in, k_in)):
                values = ref[piece, :]
                column = jnp.sum(values * values, axis=1, keepdims=True)
                slots[own, side * 8 + i : side * 8 + i + 1, :] = column_to_row(column, eye)
        values_ref[:tokens, :] = v_in[...]
        other_half = pl.ds(tokens, tokens)
        v_copy = pair(v_in, values_ref.at[other_half, :], 0)
        v_copy.start()

        def ffn_copy(t):
            to = ctx + t - 8 * ((ctx + t) // 8)
            device = (to // 2, to % 2, x, k)
            at = pl.ds(pl.multiple_of(to * hidden, hidden), hidden)
            from_at = pl.ds(pl.multiple_of(ctx * part, part), part)
            ends = (
                (gu_ref.at[:, :, at], wgu_ref.at[:, from_at, :hidden]),
                (d_ref.at[at, :], wd_ref.at[:hidden, from_at]),
            )
            return [
                pltpu.make_async_remote_copy(
                    src_ref=src,
                    dst_ref=dst,
                    send_sem=ffn_send.at[i, t],
                    recv_sem=ffn_recv.at[i, t],
                    device_id=device,
                    device_id_type=MESH,
                )
                for i, (src, dst) in enumerate(ends)
            ]

        def ffn_ends(c):
            at = pl.ds(pl.multiple_of(c * part, part), part)
            return (
                (wgu_ref.at[:, at, :hidden], wgu_ref.at[:, at, hidden:]),
                (wd_ref.at[:hidden, at], wd_ref.at[hidden:, at]),
            )

        own_at = pl.ds(pl.multiple_of(ctx * hidden, hidden), hidden)
        ffn_own = [
            pltpu.make_async_copy(src, dst[0], ffn_local.at[i])
            for i, (src, dst) in enumerate(
                zip((gu_ref.at[:, :, own_at], d_ref.at[own_at, :]), ffn_ends(ctx), strict=True)
            )
        ]
        for copy in ffn_own:
            copy.start()

        total = sum_over_plane(me, slots, tot_send, tot_recv)
        for t in range(1, 8):
            for copy in ffn_copy(t):
                copy.start()
        scales = lax.rsqrt(total / width + EPSILON)
        scale_ref[...] = scales

        def rotated(values, piece):
            return values * cos_ref[piece, :] + pltpu.roll(values, HD // 2, 1) * sin_ref[piece, :]

        for i in range(8):
            piece = slice(i * HD, (i + 1) * HD)
            factor = row_to_column(scales[8 + i : 9 + i, :], eye)
            keys_ref[piece, :] = rotated(k_in[piece, :] * factor * gain_ref[1:2, :], piece).astype(BF)
        k_copy = pair(keys_ref.at[:tokens, :], keys_ref.at[other_half, :], 1)
        k_copy.start()
        for i in range(8):
            piece = slice(i * HD, (i + 1) * HD)
            factor = row_to_column(scales[i : i + 1, :], eye)
            qrot_ref[piece, :] = rotated(q_in[piece, :] * factor * gain_ref[0:1, :], piece).astype(BF)
        v_copy.wait()
        k_copy.wait()

        def produce(zp):
            at = pl.ds(pl.multiple_of(zp * group, group), group)
            raw, allowed = masked_scores(
                qrot_ref[at, :], keys_ref[...], low_ref[at, :], high_ref[at, :], log_ref[...]
            )
            raw = jnp.where(allowed, raw, MASKED)
            top = jnp.max(raw, axis=1, keepdims=True)
            weights = jnp.where(allowed, jnp.exp(raw - top), 0.0)
            total_weight = jnp.sum(weights, axis=1, keepdims=True)
            weights = (weights / total_weight).astype(BF)
            out = jnp.dot(weights, values_ref[...], preferred_element_type=F32)
            o_ref[at, :] = out
            lse_ref[at, :] = top + jnp.log(total_weight)
            terms[at, :] = jnp.dot(
                out.astype(BF), wout_ref[...], preferred_element_type=F32
            ).astype(BF)

        def finish(strip, total):
            branch_ref[strip] = total
            h = source_ref[strip].astype(F32) + total * row_scale(total) * attn_ref[...]
            own_ref[strip] = h
            shard[strip] = h.astype(BF)

        settle = reduce_plane(me, terms, rows, rest[:N_REDUCE], produce, finish)
        view = gather_view(full_ref, rows)
        keep = pltpu.make_async_copy(shard, view(own), local)
        keep.start()

        def share(t):
            c = ctx + 8 - t - 8 * ((ctx + 8 - t) // 8)
            return [
                pltpu.make_async_remote_copy(
                    src_ref=src,
                    dst_ref=dst,
                    send_sem=share_send.at[i, t],
                    recv_sem=share_recv.at[i, t],
                    device_id=sibling,
                    device_id_type=MESH,
                )
                for i, (src, dst) in enumerate(ffn_ends(c))
            ]

        def ffn_landed(t):
            c = ctx + 8 - t - 8 * ((ctx + 8 - t) // 8)
            for i, ends in enumerate(ffn_ends(c)):
                pltpu.make_async_remote_copy(
                    src_ref=ends[0],
                    dst_ref=ends[0],
                    send_sem=ffn_send.at[i, t],
                    recv_sem=ffn_recv.at[i, t],
                    device_id=sibling,
                    device_id_type=MESH,
                ).wait_recv()

        def between(step):
            for t in (2 * step, 2 * step + 1):
                if t == 0:
                    for copy in ffn_own:
                        copy.wait()
                elif t < 8:
                    ffn_landed(t)
                if t < 8:
                    for copy in share(t):
                        copy.start()

        gather_plane(me, shard, view, rest[N_REDUCE:])
        for step in range(4):
            between(step)
        keep.wait()
        settle()
        for t in range(8):
            for copy in share(t):
                copy.wait()
            if t > 0:
                for copy in ffn_copy(t):
                    copy.wait_send()

    shape = jax.ShapeDtypeStruct
    return comm_call(
        body,
        "attention_forward",
        1,
        (
            shape((tokens, width), BF),
            shape((rows, width), F32),
            shape((rows, width), F32),
            shape((2, width, 2 * hidden), BF),
            shape((2 * hidden, width), BF),
            shape((tokens, HD), BF),
            shape((2 * tokens, HD), BF),
            shape((2 * tokens, HD), BF),
            shape((tokens, HD), F32),
            shape((tokens, 1), F32),
            shape((16, HD), F32),
        ),
        [VMEM] * 12 + [ANY, ANY],
        (ANY, VMEM, VMEM, ANY, ANY, VMEM, VMEM, VMEM, VMEM, VMEM, VMEM),
        [
            pltpu.VMEM((tokens, width), BF),
            pltpu.VMEM((rows, width), BF),
            pltpu.VMEM((16, 16, HD), F32),
            DMA((16,)),
            DMA((16,)),
            DMA((2,)),
            DMA((2,)),
            DMA,
            DMA((2, 8)),
            DMA((2, 8)),
            DMA((2, 8)),
            DMA((2, 8)),
            DMA((2,)),
            *reduce_scratch(rows, width),
            *GATHER_SEMS,
        ],
    )(query, key, value, *tables, *bounds, logical, source, out_weight, gains, attn_gain, gu_stage, d_stage)


def ffn_forward(source, gu_w, down_w, residual, cotangent, gain):
    tokens, width = source.shape
    rows, group = tokens // 16, tokens // 4
    hidden = down_w.shape[0]

    def body(*refs):
        (h_any, gu_any, d_any, res_ref, cot_ref, gain_ref) = refs[:6]
        (full_ref, out_ref, gg_ref, for_gate_ref, for_up_ref, m_ref) = refs[6:12]
        (hs, gu, dw, terms, shard, result, load_sem, local, out_send, out_recv) = refs[12:22]
        scratch = refs[22:]
        me = z, y, x, k = place()

        def h_load(zp):
            at = pl.ds(pl.multiple_of(zp * group, group), group)
            return pltpu.make_async_copy(h_any.at[at, :], hs.at[at, :], load_sem.at[zp])

        order = [near_first(step, z) for step in (3, 2, 1, 0)]
        gu_load = pltpu.make_async_copy(gu_any, gu, load_sem.at[4])
        d_load = pltpu.make_async_copy(d_any, dw, load_sem.at[5])
        h_load(order[0]).start()
        gu_load.start()
        d_load.start()
        for zp in order[1:]:
            h_load(zp).start()
        greet_plane(me, pair_devices(me))
        gg_ref[...] = jnp.zeros_like(gg_ref)
        gu_load.wait()

        def produce(zp):
            at = pl.ds(pl.multiple_of(zp * group, group), group)
            h_load(zp).wait()
            tile = hs[at, :]
            gate = jnp.dot(tile, gu[0], preferred_element_type=F32)
            up = jnp.dot(tile, gu[1], preferred_element_type=F32)
            sig = jax.nn.sigmoid(gate)
            silu = gate * sig
            mixed = (silu * up).astype(BF)
            for_gate_ref[at, :] = up * sig * (1.0 + gate * (1.0 - sig))
            for_up_ref[at, :] = silu
            m_ref[at, :] = mixed
            terms[at, :] = jnp.dot(mixed, dw[...], preferred_element_type=F32).astype(BF)

        def finish(strip, total):
            gain_row = gain_ref[...]
            out = res_ref[strip] + total * row_scale(total) * gain_row
            result[strip] = out.astype(BF)
            back, term = norm_back_strip(cot_ref[strip].astype(F32), total, gain_row)
            gg_ref[...] += term
            shard[strip] = back.astype(BF)

        d_load.wait()
        settle = reduce_plane(me, terms, rows, scratch[:N_REDUCE], produce, finish)
        view = gather_view(full_ref, rows)
        keep = pltpu.make_async_copy(shard, view(me[0] * 4 + me[1] * 2 + me[2]), local)
        keep.start()
        copies, own = hand_out_copies(me, result, out_ref, out_send, out_recv)
        for copy in copies:
            copy.start()
        own.start()
        gather_plane(me, shard, view, scratch[N_REDUCE:])
        keep.wait()
        settle()
        own.wait()
        for copy in copies:
            copy.wait()

    shape = jax.ShapeDtypeStruct
    return comm_call(
        body,
        "ffn_forward",
        3,
        (
            shape((tokens, width), BF),
            shape((rows * 4, width // 4), BF),
            shape((8, width), F32),
            shape((tokens, hidden), F32),
            shape((tokens, hidden), F32),
            shape((tokens, hidden), BF),
        ),
        [ANY, ANY, ANY, VMEM, VMEM, VMEM],
        (ANY, ANY, VMEM, VMEM, VMEM, VMEM),
        [
            pltpu.VMEM((tokens, width), BF),
            pltpu.VMEM((2, width, hidden), BF),
            pltpu.VMEM((hidden, width), BF),
            pltpu.VMEM((tokens, width), BF),
            pltpu.VMEM((rows, width), BF),
            pltpu.VMEM((rows, width), BF),
            DMA((6,)),
            DMA,
            DMA((3,)),
            DMA((4,)),
            *reduce_scratch(rows, width),
            *GATHER_SEMS,
        ],
    )(source, gu_w, down_w, residual, cotangent, gain)


EARLY = 4


def grad_copy(me, src, dst, send, recv, t):
    ctx = own_tile(me)
    to = ctx + t - 8 * ((ctx + t) // 8)
    return pltpu.make_async_remote_copy(
        src_ref=src,
        dst_ref=dst.at[ctx],
        send_sem=send.at[t],
        recv_sem=recv.at[t],
        device_id=(to // 2, to % 2, me[2], me[3]),
        device_id_type=MESH,
    )


def grad_landed(me, dst, send, recv, t):
    ctx = own_tile(me)
    c = ctx + 8 - t - 8 * ((ctx + 8 - t) // 8)
    pltpu.make_async_remote_copy(
        src_ref=dst.at[c],
        dst_ref=dst.at[c],
        send_sem=send.at[t],
        recv_sem=recv.at[t],
        device_id=(me[0], me[1], me[2], 1 - me[3]),
        device_id_type=MESH,
    ).wait_recv()


def ctx_greet(me, others):
    z, y, x, k = me
    barrier = pltpu.get_barrier_semaphore()

    def call(i, carry):
        to = lax.rem(z * 2 + y + i, 8)
        pl.semaphore_signal(
            barrier, inc=1, device_id=(to // 2, to % 2, x, k), device_id_type=MESH
        )
        return carry

    lax.fori_loop(1, 8, call, 0)
    for target in [(z, y, 1 - x, k), *others]:
        pl.semaphore_signal(barrier, inc=1, device_id=target, device_id_type=MESH)
    pl.semaphore_wait(barrier, 8 + len(others))


def ffn_backward(grad_ffn, source, gu_w, down_w, for_gate, for_up, mixed, cotangent, branch, gain):
    tokens, width = grad_ffn.shape
    rows, group = tokens // 16, tokens // 4
    hidden = down_w.shape[0]
    part = hidden // 2
    across = (((0,), (0,)), ((), ()))
    turned = (((1,), (1,)), ((), ()))

    def body(*refs):
        (df_any, h_any, gu_any, d_any, fg_any, fu_any, m_any, cot_ref, branch_ref, gain_ref) = refs[:10]
        (full_ref, own_ref, gg_ref, in_ref, rest_ref) = refs[10:15]
        (df, hs, gu, dw, fg, fu, ms, dgu, terms, shard) = refs[15:25]
        (mine, to_core, from_core, to_ctx) = refs[25:29]
        (load_sem, local, core_send, core_recv, grad_send, grad_recv, rest_sem) = refs[29:36]
        scratch = refs[36:]
        me = z, y, x, k = place()
        ctx = own_tile(me)
        order = [near_first(step, z) for step in (3, 2, 1, 0)]

        def group_load(zp):
            at = pl.ds(pl.multiple_of(zp * group, group), group)
            return [
                pltpu.make_async_copy(src.at[at, :], dst.at[at, :], load_sem.at[i, zp])
                for i, (src, dst) in enumerate(((df_any, df), (fg_any, fg), (fu_any, fu)))
            ]

        d_load = pltpu.make_async_copy(d_any, dw, load_sem.at[3, 0])
        gu_load = pltpu.make_async_copy(gu_any, gu, load_sem.at[3, 1])
        h_load = pltpu.make_async_copy(h_any, hs, load_sem.at[3, 2])
        m_load = pltpu.make_async_copy(m_any, ms, load_sem.at[3, 3])
        for load in (*group_load(order[0]), d_load, gu_load):
            load.start()
        for zp in order[1:]:
            for load in group_load(zp):
                load.start()
        h_load.start()
        m_load.start()
        sibling = (z, y, x, 1 - k)
        ctx_greet(me, [sibling])
        gg_ref[...] = jnp.zeros_like(gg_ref)
        d_load.wait()

        def produce(zp):
            at = pl.ds(pl.multiple_of(zp * group, group), group)
            for load in group_load(zp):
                load.wait()
            dm = lax.dot_general(df[at, :], dw[...], turned, preferred_element_type=F32)
            dg = (dm * fg[at, :]).astype(BF)
            du = (dm * fu[at, :]).astype(BF)
            dgu[at, :hidden] = dg
            dgu[at, hidden:] = du
            terms[at, :] = (
                lax.dot_general(dg, gu[0], turned, preferred_element_type=F32)
                + lax.dot_general(du, gu[1], turned, preferred_element_type=F32)
            ).astype(BF)

        def finish(strip, total):
            grad = cot_ref[strip].astype(F32) + total
            own_ref[strip] = grad
            back, term = norm_back_strip(grad, branch_ref[strip], gain_ref[...])
            gg_ref[...] += term
            shard[strip] = back.astype(BF)

        def core_copy(t):
            return pltpu.make_async_remote_copy(
                src_ref=to_core.at[t],
                dst_ref=from_core.at[t],
                send_sem=core_send.at[t],
                recv_sem=core_recv.at[t],
                device_id=sibling,
                device_id_type=MESH,
            )

        def compute(t):
            c = ctx + t - 8 * ((ctx + t) // 8)
            at = pl.ds(pl.multiple_of(c * part, part), part)
            up_like = lax.dot_general(hs[:, at], dgu[...], across, preferred_element_type=F32)
            down_like = lax.dot_general(ms[...], df[:, at], across, preferred_element_type=F32)
            slot = t % 2
            for i in range(2):
                mine[slot, i] = up_like[:, 2 * i * part : (2 * i + 1) * part]
                to_core[t, i] = up_like[:, (2 * i + 1) * part : (2 * i + 2) * part].astype(BF)
            mine[slot, 2] = down_like[:part]
            to_core[t, 2] = down_like[part:].astype(BF)
            core_copy(t).start()

        def send(t):
            core_copy(t).wait_recv()
            to_ctx[t] = (mine[t % 2] + from_core[t].astype(F32)).astype(BF)
            if t == 0:
                pltpu.make_async_copy(to_ctx.at[0], in_ref.at[ctx], rest_sem.at[0]).start()
            elif t <= EARLY:
                grad_copy(me, to_ctx.at[t], in_ref, grad_send, grad_recv, t).start()
            else:
                pltpu.make_async_copy(
                    to_ctx.at[t], rest_ref.at[t - EARLY - 1], rest_sem.at[t - EARLY]
                ).start()

        def grads(first, last):
            for t in range(first, last):
                compute(t)
                if t > 0:
                    send(t - 1)

        def after_terms():
            h_load.wait()
            m_load.wait()
            grads(0, 3)

        between = [
            lambda: grads(3, 5),
            lambda: grads(5, 6),
            lambda: grads(6, 7),
            lambda: grads(7, 8),
            lambda: send(7),
        ]
        gu_load.wait()
        settle = reduce_plane(me, terms, rows, scratch[:N_REDUCE], produce, finish, after_terms)
        view = gather_view(full_ref, rows)
        keep = pltpu.make_async_copy(shard, view(me[0] * 4 + me[1] * 2 + me[2]), local)
        keep.start()
        gather_plane(me, shard, view, scratch[N_REDUCE:], lambda step: between[step]())
        keep.wait()
        settle()
        for t in range(8):
            core_copy(t).wait_send()
        pltpu.make_async_copy(to_ctx.at[0], in_ref.at[ctx], rest_sem.at[0]).wait()
        for t in range(1, 8):
            if t <= EARLY:
                grad_landed(me, in_ref, grad_send, grad_recv, t)
                grad_copy(me, to_ctx.at[t], in_ref, grad_send, grad_recv, t).wait_send()
            else:
                pltpu.make_async_copy(
                    to_ctx.at[t], rest_ref.at[t - EARLY - 1], rest_sem.at[t - EARLY]
                ).wait()

    shape = jax.ShapeDtypeStruct
    vmem = pltpu.VMEM
    return comm_call(
        body,
        "ffn_backward",
        4,
        (
            shape((tokens, width), BF),
            shape((rows, width), F32),
            shape((8, width), F32),
            shape((8, 3, part, part), BF),
            shape((7 - EARLY, 3, part, part), BF),
        ),
        [*[ANY] * 7, VMEM, VMEM, VMEM],
        (ANY, VMEM, VMEM, ANY, ANY),
        [
            vmem((tokens, width), BF),
            vmem((tokens, width), BF),
            vmem((2, width, hidden), BF),
            vmem((hidden, width), BF),
            vmem((tokens, hidden), F32),
            vmem((tokens, hidden), F32),
            vmem((tokens, hidden), BF),
            vmem((tokens, 2 * hidden), BF),
            vmem((tokens, width), BF),
            vmem((rows, width), BF),
            vmem((2, 3, part, part), F32),
            vmem((8, 3, part, part), BF),
            vmem((8, 3, part, part), BF),
            vmem((8, 3, part, part), BF),
            DMA((4, 4)),
            DMA,
            DMA((8,)),
            DMA((8,)),
            DMA((8,)),
            DMA((8,)),
            DMA((8,)),
            *reduce_scratch(rows, width),
            *GATHER_SEMS,
        ],
    )(grad_ffn, source, gu_w, down_w, for_gate, for_up, mixed, cotangent, branch, gain)


def write_results(early, late, wall, outputs, input_grad, gains):
    part = early.shape[2]

    def body(early_ref, late_ref, wall_ref, out_ref, in_ref, gain_ref, *results):
        (out_to, in_to, gq, gk, gv, go, gg, gu, gd, gains_to) = results
        c = pl.program_id(0)
        ctx = lax.axis_index("z") * 2 + lax.axis_index("y")
        t = lax.rem(ctx + 8 - c, 8)

        @pl.when(c == 0)
        def _():
            out_to[...] = out_ref[...]
            in_to[...] = in_ref[...]
            gains_to[...] = gain_ref[...]

        for i, ref in enumerate((gq, gk, gv, go)):
            ref[...] = wall_ref[0, i].astype(F32)

        @pl.when(t <= EARLY)
        def _():
            for i, ref in enumerate((gg, gu, gd)):
                ref[...] = early_ref[0, i].astype(F32)

        @pl.when(t > EARLY)
        def _():
            for i, ref in enumerate((gg, gu, gd)):
                ref[...] = late_ref[0, i].astype(F32)

    shape = jax.ShapeDtypeStruct
    spec = pl.BlockSpec
    blob = spec((1, 3, part, part), lambda c: (c, 0, 0, 0))
    rows, columns = outputs.shape
    whole = spec((rows, columns), lambda c: (0, 0))
    in_row = spec((HD, HD), lambda c: (c % 2, c // 2))
    in_column = spec((HD, HD), lambda c: (c // 2, c % 2))
    side = spec((part, part), lambda c: (0, c))
    gain_spec = spec(gains.shape, lambda c: (0, 0))
    return pl.pallas_call(
        body,
        name="write_results",
        grid=(8,),
        out_shape=(
            shape((rows, columns), BF),
            shape((rows, columns), BF),
            shape((2 * HD, 4 * HD), F32),
            shape((2 * HD, 4 * HD), F32),
            shape((2 * HD, 4 * HD), F32),
            shape((4 * HD, 2 * HD), F32),
            shape((part, 8 * part), F32),
            shape((part, 8 * part), F32),
            shape((8 * part, part), F32),
            shape(gains.shape, F32),
        ),
        in_specs=[
            blob,
            blob,
            spec((1, 4, HD, HD), lambda c: (c, 0, 0, 0)),
            whole,
            whole,
            gain_spec,
        ],
        out_specs=(
            whole,
            whole,
            in_row,
            in_row,
            in_row,
            in_column,
            side,
            side,
            spec((part, part), lambda c: (c, 0)),
            gain_spec,
        ),
        compiler_params=pltpu.CompilerParams(vmem_limit_bytes=BIG_VMEM),
    )(early, late, wall, outputs, input_grad, gains)


def close_greet(me):
    z, y, x, k = me
    barrier = pltpu.get_barrier_semaphore()

    def plane(i, carry):
        pl.semaphore_signal(barrier, inc=1, device_id=plane_peer(me, i)[1], device_id_type=MESH)
        return carry

    def others(i, carry):
        pl.semaphore_signal(
            barrier, inc=1, device_id=(i // 2, i % 2, x, 1 - k), device_id_type=MESH
        )
        return carry

    lax.fori_loop(1, 16, plane, 0)
    lax.fori_loop(0, 8, others, 0)
    pl.semaphore_signal(barrier, inc=1, device_id=(z, y, 1 - x, 1 - k), device_id_type=MESH)
    pl.semaphore_wait(barrier, 24)


def attention_backward(
    grad_attn,
    full_in,
    query,
    key,
    query_rot,
    keys,
    values,
    attended,
    lse,
    tables,
    bounds,
    logical,
    scales,
    head_gains,
    qkv_w,
    out_w,
    grad_own,
    attn_term,
    ffn_term,
    grads_left,
):
    tokens, width = grad_attn.shape
    rows, group = tokens // 16, tokens // 4
    part = width // 4
    scaling = 1.0 / math.sqrt(HD)

    def body(*refs):
        (da_any, x_any) = refs[:2]
        (q_ref, k_ref, qrot_ref, keys_ref, values_ref, o_ref, lse_ref, cos_ref, sin_ref) = refs[2:11]
        (low_ref, high_ref, log_ref, scale_ref, gain_ref, wqkv_ref, wout_ref) = refs[11:18]
        (grad_ref, attn_ref, ffn_ref, left_ref) = refs[18:22]
        (in_grad_ref, deal_in, gains_ref, ffn_in) = refs[22:26]
        (da, xs, terms, do_ref, delta_ref, dq_ref, dk_ref, dv_ref) = refs[26:34]
        (pair_out, pair_in, dqkv, slots, result) = refs[34:39]
        (wall_grad, wall_out, wall_in, deal_out) = refs[39:43]
        (gain_out, gain_in, gain_own, gain_slots) = refs[43:47]
        (load_sem, pair_send, pair_recv, tot_send, tot_recv, out_send, out_recv) = refs[47:54]
        (deal_send, deal_recv, gain_send, gain_recv, grad_send, grad_recv) = refs[54:60]
        scratch = refs[60:]
        me = z, y, x, k = place()
        ctx = own_tile(me)
        own = ctx * 2 + x
        sibling = (z, y, x, 1 - k)

        da_loads = [
            pltpu.make_async_copy(
                da_any.at[g * group : (g + 1) * group, :],
                da.at[g * group : (g + 1) * group, :],
                load_sem.at[g],
            )
            for g in range(4)
        ]
        x_load = pltpu.make_async_copy(x_any, xs, load_sem.at[4])
        for load in (*da_loads, x_load):
            load.start()
        close_greet(me)
        for t in range(EARLY + 1, 8):
            grad_copy(me, left_ref.at[t - EARLY - 1], ffn_in, grad_send, grad_recv, t).start()

        def pair(n):
            return pltpu.make_async_remote_copy(
                src_ref=(pair_out.at[0], pair_out.at[1], wall_out, gain_out)[n],
                dst_ref=(pair_in.at[0], pair_in.at[1], wall_in, gain_in)[n],
                send_sem=pair_send.at[n],
                recv_sem=pair_recv.at[n],
                device_id=sibling,
                device_id_type=MESH,
            )

        for g in range(4):
            at = slice(g * group, (g + 1) * group)
            da_loads[g].wait()
            do = lax.dot_general(
                da[at, :], wout_ref[...], (((1,), (1,)), ((), ())), preferred_element_type=F32
            ).astype(BF)
            do_ref[at, :] = do
            delta_ref[at, :] = jnp.sum(do.astype(F32) * o_ref[at, :], axis=1, keepdims=True)

        across = (((0,), (0,)), ((), ()))
        for half in (1, 0):
            key_at = slice(half * tokens, (half + 1) * tokens)
            dk_ref[...] = jnp.zeros_like(dk_ref)
            dv_ref[...] = jnp.zeros_like(dv_ref)

            def work(at, half=half, key_at=key_at):
                q, g, key_part = qrot_ref[at, :], do_ref[at, :], keys_ref[key_at, :]
                raw, allowed = masked_scores(
                    q, key_part, low_ref[at, :], high_ref[at, :], log_ref[:, key_at]
                )
                weights = jnp.where(allowed, jnp.exp(raw - lse_ref[at, :]), 0.0)
                dp = lax.dot_general(
                    g, values_ref[key_at, :], (((1,), (1,)), ((), ())), preferred_element_type=F32
                )
                ds = (weights * (dp - delta_ref[at, :])).astype(BF)
                dq = jnp.dot(ds, key_part, preferred_element_type=F32) * scaling
                if half == 1:
                    dq_ref[at, :] = dq
                else:
                    dq_ref[at, :] += dq
                dk_ref[...] += (
                    lax.dot_general(ds, q, across, preferred_element_type=F32) * scaling
                )
                dv_ref[...] += lax.dot_general(
                    weights.astype(BF), g, across, preferred_element_type=F32
                )

            strips(tokens, work, group)
            if half == 1:
                pair_out[0] = dk_ref[...].astype(BF)
                pair_out[1] = dv_ref[...].astype(BF)
                pair(0).start()
                pair(1).start()

        eye = eye_mask()

        def normed_grad(values, piece):
            return values * cos_ref[piece, :] - pltpu.roll(values, HD // 2, 1) * sin_ref[piece, :]

        def side_dots(side, source, grads, proj):
            gain_sum = jnp.zeros((8, HD), F32)
            for i in range(8):
                piece = slice(i * HD, (i + 1) * HD)
                factor = row_to_column(scale_ref[side * 8 + i : side * 8 + i + 1, :], eye)
                back = normed_grad(source(piece), piece)
                term = back * proj[piece, :] * factor
                for j in range(0, HD, 8):
                    gain_sum = gain_sum + term[j : j + 8, :]
                weighted = back * gain_ref[side : side + 1, :]
                grads[piece, :] = weighted
                dot = jnp.sum(weighted * proj[piece, :], axis=1, keepdims=True)
                slots[own, side * 8 + i : side * 8 + i + 1, :] = column_to_row(dot, eye)
            return jnp.sum(gain_sum, axis=0, keepdims=True)

        query_gain = side_dots(0, lambda piece: dq_ref[piece, :], dq_ref, q_ref)
        pair(0).wait_recv()
        pair(1).wait_recv()
        key_gain = side_dots(
            1, lambda piece: dk_ref[piece, :] + pair_in[0, piece, :].astype(F32), dk_ref, k_ref
        )
        dqkv[:, 2 * HD :] = (dv_ref[...] + pair_in[1].astype(F32)).astype(BF)

        attn_sum = jnp.sum(attn_ref[...], axis=0, keepdims=True)
        ffn_sum = jnp.sum(ffn_ref[...], axis=0, keepdims=True)
        head_core = z // 2
        head_at = pl.ds(pl.multiple_of(((z % 2) * 2 + y) * HD, HD), HD)
        for mine, target in ((True, gain_own), (False, gain_out)):
            target[...] = jnp.zeros_like(target)
            for xt in range(2):
                for kt in range(2):

                    @pl.when((kt == k) if mine else (kt != k))
                    def _(xt=xt, kt=kt, target=target):
                        block = slice((2 * xt + kt) * part, (2 * xt + kt + 1) * part)
                        target[xt, 2:3, :] = attn_sum[:, block]
                        target[xt, 3:4, :] = ffn_sum[:, block]

            @pl.when((head_core == k) if mine else (head_core != k))
            def _(target=target):
                target[x, 0:1, head_at] = query_gain
                target[x, 1:2, head_at] = key_gain

        pair(3).start()

        total = sum_over_plane(me, slots, tot_send, tot_recv)
        for side, grads, proj in ((0, dq_ref, q_ref), (1, dk_ref, k_ref)):
            for i in range(8):
                piece = slice(i * HD, (i + 1) * HD)
                row = scale_ref[side * 8 + i : side * 8 + i + 1, :]
                factor = row_to_column(row, eye)
                cubed = row * row * row * total[side * 8 + i : side * 8 + i + 1, :] / width
                dqkv[piece, side * HD : (side + 1) * HD] = (
                    factor * grads[piece, :] - proj[piece, :] * row_to_column(cubed, eye)
                ).astype(BF)

        def produce(zp):
            at = pl.ds(pl.multiple_of(zp * group, group), group)
            term = jnp.zeros((group, width), F32)
            for i in range(3):
                term = term + lax.dot_general(
                    dqkv[at, i * HD : (i + 1) * HD],
                    wqkv_ref[i],
                    (((1,), (1,)), ((), ())),
                    preferred_element_type=F32,
                )
            terms[at, :] = term.astype(BF)

        gain_copies = []

        def gain_copy(i):
            other, device = plane_peer(me, i)
            return pltpu.make_async_remote_copy(
                src_ref=gain_own.at[other % 2],
                dst_ref=gain_slots.at[own],
                send_sem=gain_send.at[i],
                recv_sem=gain_recv.at[own],
                device_id=device,
                device_id_type=MESH,
            )

        number = ((z % 2) * 2 + y) * 2 + k

        def deal(c):
            return pltpu.make_async_remote_copy(
                src_ref=deal_out.at[c],
                dst_ref=deal_in.at[number],
                send_sem=deal_send.at[c],
                recv_sem=deal_recv.at[number],
                device_id=(c // 2, c % 2, x, head_core),
                device_id_type=MESH,
            )

        stays = k == head_core

        def after_terms():
            pair(3).wait_recv()
            gain_own[...] += gain_in[...]
            gain_slots[own] = gain_own[x]

            def begin(i, carry):
                gain_copy(i).start()
                return carry

            lax.fori_loop(1, 16, begin, 0)
            x_load.wait()
            for c in range(8):
                grads = lax.dot_general(
                    xs[:, c * 2 * HD : (c + 1) * 2 * HD],
                    dqkv[...],
                    across,
                    preferred_element_type=F32,
                )
                for i in range(3):
                    for r in range(2):
                        wall_grad[r, c, i] = grads[r * HD : (r + 1) * HD, i * HD : (i + 1) * HD]
                out_grad = lax.dot_general(
                    o_ref[...].astype(BF),
                    da[:, c * 2 * HD : (c + 1) * 2 * HD],
                    across,
                    preferred_element_type=F32,
                )
                for r in range(2):
                    wall_grad[r, c, 3] = out_grad[:, r * HD : (r + 1) * HD]

            def to_other(c, carry):
                wall_out[c] = wall_grad[1 - k, c].astype(BF)
                return carry

            lax.fori_loop(0, 8, to_other, 0)
            pair(2).start()
            pair(2).wait_recv()

            def to_owner(c, carry):
                deal_out[c] = (wall_grad[k, c] + wall_in[c].astype(F32)).astype(BF)
                return carry

            lax.fori_loop(0, 8, to_owner, 0)
            for c in range(8):

                @pl.when(jnp.logical_not(stays & (ctx == c)))
                def _(c=c):
                    deal(c).start()

                @pl.when(stays & (ctx == c))
                def _(c=c):
                    pltpu.make_async_copy(
                        deal_out.at[c], deal_in.at[number], deal_recv.at[number]
                    ).start()

        def finish(strip, total):
            result[strip] = (grad_ref[strip] + total).astype(BF)

        settle = reduce_plane(me, terms, rows, scratch, produce, finish, after_terms)
        copies, own_copy = hand_out_copies(me, result, in_grad_ref, out_send, out_recv)
        for copy in copies:
            copy.start()
        own_copy.start()
        for n in range(8):
            pltpu.make_async_copy(deal_out.at[n], deal_in.at[n], deal_recv.at[n]).wait()

        def gain_landed(i, carry):
            other, device = plane_peer(me, i)
            pltpu.make_async_remote_copy(
                src_ref=gain_slots.at[other],
                dst_ref=gain_slots.at[other],
                send_sem=gain_send.at[i],
                recv_sem=gain_recv.at[other],
                device_id=device,
                device_id_type=MESH,
            ).wait_recv()
            gain_copy(i).wait_send()
            return carry

        lax.fori_loop(1, 16, gain_landed, 0)
        gain_total = gain_slots[0]
        for i in range(1, 16):
            gain_total = gain_total + gain_slots[i]
        gains_ref[...] = gain_total
        settle()
        own_copy.wait()
        for copy in copies:
            copy.wait()
        for c in range(8):

            @pl.when(jnp.logical_not(stays & (ctx == c)))
            def _(c=c):
                deal(c).wait_send()

        for n in range(4):
            pair(n).wait_send()
        for t in range(EARLY + 1, 8):
            grad_landed(me, ffn_in, grad_send, grad_recv, t)
            grad_copy(
                me, left_ref.at[t - EARLY - 1], ffn_in, grad_send, grad_recv, t
            ).wait_send()

    shape = jax.ShapeDtypeStruct
    vmem = pltpu.VMEM
    return comm_call(
        body,
        "attention_backward",
        5,
        (
            shape((rows * 4, part), BF),
            shape((8, 4, HD, HD), BF),
            shape((4, part), F32),
            shape((8, *grads_left.shape[1:]), BF),
        ),
        [ANY, ANY, *[VMEM] * 19, ANY],
        (ANY, ANY, VMEM, ANY),
        [
            vmem((tokens, width), BF),
            vmem((tokens, width), BF),
            vmem((tokens, width), BF),
            vmem((tokens, HD), BF),
            vmem((tokens, 1), F32),
            vmem((tokens, HD), F32),
            vmem((tokens, HD), F32),
            vmem((tokens, HD), F32),
            vmem((2, tokens, HD), BF),
            vmem((2, tokens, HD), BF),
            vmem((tokens, 3 * HD), BF),
            vmem((16, 16, HD), F32),
            vmem((rows, width), BF),
            vmem((2, 8, 4, HD, HD), F32),
            vmem((8, 4, HD, HD), BF),
            vmem((8, 4, HD, HD), BF),
            vmem((8, 4, HD, HD), BF),
            vmem((2, 4, part), F32),
            vmem((2, 4, part), F32),
            vmem((2, 4, part), F32),
            vmem((16, 4, part), F32),
            DMA((5,)),
            DMA((4,)),
            DMA((4,)),
            DMA((16,)),
            DMA((16,)),
            DMA((3,)),
            DMA((4,)),
            DMA((8,)),
            DMA((8,)),
            DMA((16,)),
            DMA((16,)),
            DMA((8,)),
            DMA((8,)),
            *reduce_scratch(rows, width),
        ],
    )(
        grad_attn,
        full_in,
        query,
        key,
        query_rot,
        keys,
        values,
        attended,
        lse,
        *tables,
        *bounds,
        logical,
        scales,
        head_gains,
        qkv_w,
        out_w,
        grad_own,
        attn_term,
        ffn_term,
        grads_left,
    )


def rotary_tables(offset):
    half_dim = HD // 2
    inverse = jnp.power(ROPE_THETA, -jnp.arange(half_dim, dtype=F32) * 2.0 / HD)
    angles = offset.astype(F32)[:, None] * inverse[None, :]
    cosine, sine_part = jnp.cos(angles), jnp.sin(angles)
    return (
        jnp.concatenate([cosine, cosine], axis=1),
        jnp.concatenate([-sine_part, sine_part], axis=1),
    )


def plane_layer(
    inputs,
    cotangent,
    w_query,
    w_key,
    w_value,
    w_out,
    w_gate,
    w_up,
    w_down,
    query_gain,
    key_gain,
    attn_gain,
    ffn_gain,
    lengths,
    block_order,
):
    z, y, x, k = place()
    ctx = z * 2 + y
    tok_rows, width_part = inputs.shape
    plane_rows = tok_rows // 2
    tokens = 8 * plane_rows

    order = block_order.reshape(8, 2, -1)
    block_rows = plane_rows // order.shape[2]

    def logical_of(core):
        blocks = lax.dynamic_index_in_dim(order, core, 1, keepdims=False).reshape(-1)
        return (
            blocks[:, None] * block_rows + jnp.arange(block_rows, dtype=jnp.int32)[None, :]
        ).reshape(-1)

    logical_own, logical_other = logical_of(k), logical_of(1 - k)
    offset_own = sequence_tables(logical_own, lengths)[1]
    tables = rotary_tables(offset_own)
    low = (logical_own - offset_own)[:, None]
    high = logical_own[:, None]
    logical_keys = jnp.concatenate([logical_own, logical_other])[None, :]

    gains = jnp.stack([query_gain, key_gain, attn_gain, ffn_gain])
    full_in, source_own, own_cot, qkv_w, out_w, gains_full, gu_stage, d_stage, query_proj, key_proj, value_low = open_layer(
        inputs, cotangent, w_query, w_key, w_value, w_out, w_gate, w_up, w_down, gains
    )
    head = x * 8 + ctx
    attn_gain_row, ffn_gain_row = gains_full[2:3], gains_full[3:4]
    head_gains = lax.dynamic_slice_in_dim(gains_full[:2], head * HD, HD, 1)
    (
        residual_full,
        residual_own,
        branch_own,
        gu_w,
        down_w,
        query_rot,
        keys_all,
        values_all,
        attended,
        lse,
        scales,
    ) = attention_forward(
        query_proj,
        key_proj,
        value_low,
        tables,
        (low, high),
        logical_keys,
        source_own,
        out_w,
        head_gains,
        attn_gain_row,
        gu_stage,
        d_stage,
    )
    grad_ffn, outputs, ffn_gain_term, for_gate, for_up, mixed = ffn_forward(
        residual_full, gu_w, down_w, residual_own, own_cot, ffn_gain_row
    )
    grad_attn, grad_own, attn_gain_term, ffn_early, ffn_left = ffn_backward(
        grad_ffn,
        residual_full,
        gu_w,
        down_w,
        for_gate,
        for_up,
        mixed,
        own_cot,
        branch_own,
        attn_gain_row,
    )
    input_grad, wall_grads, gain_grads, ffn_late = attention_backward(
        grad_attn,
        full_in,
        query_proj,
        key_proj,
        query_rot,
        keys_all,
        values_all,
        attended,
        lse,
        tables,
        (low, high),
        logical_keys,
        scales,
        head_gains,
        qkv_w,
        out_w,
        grad_own,
        attn_gain_term,
        ffn_gain_term,
        ffn_left,
    )
    *results, gains_out = write_results(
        ffn_early, ffn_late, wall_grads, outputs, input_grad, gain_grads
    )
    return (*results, *gains_out)


def full_rows(piece):
    return lax.all_gather(piece, "head", axis=1, tiled=True)


def head_sums(term):
    return lax.psum_scatter(
        term.astype(jnp.bfloat16), "head", scatter_dimension=1, tiled=True
    ).astype(jnp.float32)


def row_single(term):
    return lax.psum(term, "head")


def row_pair(first, second):
    return lax.psum((first, second), "head")


def gather_weights(w_query, w_key, w_value, w_out, w_gate, w_up, w_down):
    row_parts = (
        lax.all_gather(w_query.astype(jnp.bfloat16), "ctx", axis=0, tiled=True),
        lax.all_gather(w_key.astype(jnp.bfloat16), "ctx", axis=0, tiled=True),
        lax.all_gather(w_value.astype(jnp.bfloat16), "ctx", axis=0, tiled=True),
        lax.all_gather(w_gate.astype(jnp.bfloat16), "ctx", axis=0, tiled=True),
        lax.all_gather(w_up.astype(jnp.bfloat16), "ctx", axis=0, tiled=True),
    )
    col_parts = (
        lax.all_gather(w_out.astype(jnp.bfloat16), "ctx", axis=1, tiled=True),
        lax.all_gather(w_down.astype(jnp.bfloat16), "ctx", axis=1, tiled=True),
    )
    return tuple(row_parts) + tuple(col_parts)


def sequence_tables(logical, lengths):
    seq_ends = jnp.cumsum(lengths)
    seq_starts = seq_ends - lengths
    number = jnp.sum((logical[:, None] >= seq_ends[None, :]).astype(jnp.int32), axis=1)
    member = number[:, None] == jnp.arange(lengths.shape[0], dtype=jnp.int32)[None, :]
    offset = logical - jnp.sum(jnp.where(member, seq_starts[None, :], 0), axis=1)
    return (number, offset)


def rotate(values, offset):
    half_dim = HD // 2
    inverse = jnp.power(ROPE_THETA, -jnp.arange(half_dim, dtype=jnp.float32) * 2.0 / HD)
    angles = offset.astype(jnp.float32)[:, None] * inverse[None, :]
    cosine = jnp.cos(angles)[:, None, :]
    sine_part = jnp.sin(angles)[:, None, :]
    first_half = values[..., :half_dim]
    second_half = values[..., half_dim:]
    return jnp.concatenate(
        [
            first_half * cosine - second_half * sine_part,
            second_half * cosine + first_half * sine_part,
        ],
        axis=-1,
    )


def norm_backward(grad_in, values, factor, gain):
    gain_term = jnp.sum(grad_in * values * factor[:, None], axis=0)
    weighted = grad_in * gain
    row_dot = row_single(jnp.sum(weighted * values, axis=1))
    grad_values = (
        factor[:, None] * weighted - values * (factor * factor * factor * row_dot / D)[:, None]
    )
    return (grad_values, gain_term)


def on_device(
    inputs,
    cotangent,
    w_query,
    w_key,
    w_value,
    w_out,
    w_gate,
    w_up,
    w_down,
    query_gain,
    key_gain,
    attn_gain,
    ffn_gain,
    lengths,
    block_order,
):
    shards = lax.axis_size("ctx")
    position = lax.axis_index("ctx")
    tok_rows, width_part = inputs.shape
    block_rows = tok_rows // shards
    total_tokens = tok_rows * shards
    local_heads = width_part // HD
    scaling = 1.0 / math.sqrt(HD)
    shard_range = jnp.arange(shards, dtype=jnp.int32)
    order_table = block_order.reshape(shards, shards)
    target = order_table % shards
    choose = target[:, :, None] == shard_range[None, None, :]
    stream = jnp.sum(jnp.where(choose, order_table[:, :, None], 0), axis=1)
    stream_blocks = jnp.transpose(stream).reshape(-1)
    logical = (
        stream_blocks[:, None] * block_rows + jnp.arange(block_rows, dtype=jnp.int32)[None, :]
    ).reshape(-1)
    own_target = lax.dynamic_index_in_dim(target, position, 0, keepdims=False)
    send_order = jnp.sum(
        jnp.where(own_target[:, None] == shard_range[None, :], shard_range[:, None], 0), axis=0
    )

    def deal_out(values):
        return values.reshape(shards, block_rows, width_part)[send_order].reshape(
            tok_rows, width_part
        )

    def undeal(values):
        return values.reshape(shards, block_rows, width_part)[own_target].reshape(
            tok_rows, width_part
        )

    local_in, local_cot = (
        lax.all_to_all(deal_out(inputs), "ctx", split_axis=0, concat_axis=0, tiled=True),
        lax.all_to_all(deal_out(cotangent), "ctx", split_axis=0, concat_axis=0, tiled=True),
    )
    number_all, offset_all = sequence_tables(logical, lengths)
    number_own = lax.dynamic_slice_in_dim(number_all, position * tok_rows, tok_rows)
    offset_own = lax.dynamic_slice_in_dim(offset_all, position * tok_rows, tok_rows)
    logical_own = lax.dynamic_slice_in_dim(logical, position * tok_rows, tok_rows)
    query_full, key_full, value_full, gate_full, up_full, out_full, down_full = gather_weights(
        w_query, w_key, w_value, w_out, w_gate, w_up, w_down
    )
    full_in = full_rows(local_in)
    query_proj = jnp.dot(full_in, query_full, preferred_element_type=jnp.float32)
    key_proj = jnp.dot(full_in, key_full, preferred_element_type=jnp.float32)
    value_proj = jnp.dot(full_in, value_full, preferred_element_type=jnp.float32)
    query_sq, key_sq = row_pair(
        jnp.sum(query_proj * query_proj, axis=1), jnp.sum(key_proj * key_proj, axis=1)
    )
    query_scale = lax.rsqrt(query_sq / D + EPSILON)
    key_scale = lax.rsqrt(key_sq / D + EPSILON)
    query_rot = rotate(
        (query_proj * query_scale[:, None] * query_gain).reshape(tok_rows, local_heads, HD),
        offset_own,
    ).astype(jnp.bfloat16)
    key_rot = rotate(
        (key_proj * key_scale[:, None] * key_gain).reshape(tok_rows, local_heads, HD), offset_own
    ).astype(jnp.bfloat16)
    value_low = value_proj.astype(jnp.bfloat16).reshape(tok_rows, local_heads, HD)
    keys_all, values_all = (
        lax.all_gather(key_rot, "ctx", axis=0, tiled=True),
        lax.all_gather(value_low, "ctx", axis=0, tiled=True),
    )
    key_span = math.gcd(total_tokens, 1024)
    key_turns = total_tokens // key_span
    pieces = (
        keys_all.reshape(key_turns, key_span, local_heads, HD),
        values_all.reshape(key_turns, key_span, local_heads, HD),
        number_all.reshape(key_turns, key_span),
        logical.reshape(key_turns, key_span),
    )

    def scores_of(key_piece, number_piece, logical_piece):
        raw_scores = (
            jnp.einsum("qhd,khd->hqk", query_rot, key_piece, preferred_element_type=jnp.float32)
            * scaling
        )
        allowed = (number_own[:, None] == number_piece[None, :]) & (
            logical_piece[None, :] <= logical_own[:, None]
        )
        return (raw_scores, allowed)

    def stat_turn(running, piece_set):
        running_max, running_sum = running
        raw_scores, allowed = scores_of(piece_set[0], piece_set[2], piece_set[3])
        masked_scores = jnp.where(allowed[None], raw_scores, MASKED)
        new_max = jnp.maximum(running_max, jnp.max(masked_scores, axis=2))
        fresh = jnp.sum(
            jnp.where(allowed[None], jnp.exp(masked_scores - new_max[..., None]), 0.0), axis=2
        )
        return ((new_max, running_sum * jnp.exp(running_max - new_max) + fresh), None)

    start_max = jnp.full((local_heads, tok_rows), MASKED, jnp.float32)
    start_sum = jnp.zeros((local_heads, tok_rows), jnp.float32)
    final_max, final_sum = lax.scan(stat_turn, (start_max, start_sum), pieces)[0]
    log_total = final_max + jnp.log(final_sum)

    def out_turn(accum, piece_set):
        raw_scores, allowed = scores_of(piece_set[0], piece_set[2], piece_set[3])
        weights_low = jnp.where(
            allowed[None], jnp.exp(raw_scores - log_total[..., None]), 0.0
        ).astype(jnp.bfloat16)
        return (
            accum
            + jnp.einsum(
                "hqk,khd->qhd", weights_low, piece_set[1], preferred_element_type=jnp.float32
            ),
            None,
        )

    attended = lax.scan(out_turn, jnp.zeros((tok_rows, local_heads, HD), jnp.float32), pieces)[0]
    attended_low = attended.reshape(tok_rows, width_part).astype(jnp.bfloat16)
    attn_part = head_sums(jnp.dot(attended_low, out_full, preferred_element_type=jnp.float32))
    attn_scale = lax.rsqrt(row_single(jnp.sum(attn_part * attn_part, axis=1)) / D + EPSILON)
    residual = local_in.astype(jnp.float32) + attn_part * attn_scale[:, None] * attn_gain
    residual_full = full_rows(residual.astype(jnp.bfloat16))
    gate_proj = jnp.dot(residual_full, gate_full, preferred_element_type=jnp.float32)
    up_proj = jnp.dot(residual_full, up_full, preferred_element_type=jnp.float32)
    gate_sigmoid = jax.nn.sigmoid(gate_proj)
    mixed_hidden = (gate_proj * gate_sigmoid * up_proj).astype(jnp.bfloat16)
    ffn_part = head_sums(jnp.dot(mixed_hidden, down_full, preferred_element_type=jnp.float32))
    ffn_scale = lax.rsqrt(row_single(jnp.sum(ffn_part * ffn_part, axis=1)) / D + EPSILON)
    result = residual + ffn_part * ffn_scale[:, None] * ffn_gain
    query_full, key_full, value_full, gate_full, up_full, out_full, down_full = gather_weights(
        w_query, w_key, w_value, w_out, w_gate, w_up, w_down
    )
    grad_result = local_cot.astype(jnp.float32)
    grad_ffn, ffn_gain_term = norm_backward(grad_result, ffn_part, ffn_scale, ffn_gain)
    grad_ffn_low = full_rows(grad_ffn.astype(jnp.bfloat16))
    down_grad = jnp.einsum(
        "tf,td->fd", mixed_hidden, grad_ffn_low, preferred_element_type=jnp.float32
    )
    grad_mixed = jnp.einsum(
        "td,fd->tf", grad_ffn_low, down_full, preferred_element_type=jnp.float32
    )
    grad_gate_low = (
        grad_mixed * up_proj * gate_sigmoid * (1.0 + gate_proj * (1.0 - gate_sigmoid))
    ).astype(jnp.bfloat16)
    grad_up_low = (grad_mixed * gate_proj * gate_sigmoid).astype(jnp.bfloat16)
    gate_grad = jnp.einsum(
        "td,tf->df", residual_full, grad_gate_low, preferred_element_type=jnp.float32
    )
    up_grad = jnp.einsum(
        "td,tf->df", residual_full, grad_up_low, preferred_element_type=jnp.float32
    )
    resid_term = jnp.einsum(
        "tf,df->td", grad_gate_low, gate_full, preferred_element_type=jnp.float32
    ) + jnp.einsum("tf,df->td", grad_up_low, up_full, preferred_element_type=jnp.float32)
    grad_residual = grad_result + head_sums(resid_term)
    grad_attn, attn_gain_term = norm_backward(grad_residual, attn_part, attn_scale, attn_gain)
    grad_attn_low = full_rows(grad_attn.astype(jnp.bfloat16))
    out_grad = jnp.einsum(
        "te,td->ed", attended_low, grad_attn_low, preferred_element_type=jnp.float32
    )
    grad_heads = (
        jnp.einsum("td,ed->te", grad_attn_low, out_full, preferred_element_type=jnp.float32)
        .astype(jnp.bfloat16)
        .reshape(tok_rows, local_heads, HD)
    )
    row_delta = jnp.transpose(jnp.sum(grad_heads.astype(jnp.float32) * attended, axis=2))

    def score_grads(key_piece, value_piece, number_piece, logical_piece):
        raw_scores, allowed = scores_of(key_piece, number_piece, logical_piece)
        probabilities = jnp.where(allowed[None], jnp.exp(raw_scores - log_total[..., None]), 0.0)
        grad_probs = jnp.einsum(
            "qhd,khd->hqk", grad_heads, value_piece, preferred_element_type=jnp.float32
        )
        grad_scores = (probabilities * (grad_probs - row_delta[..., None])).astype(jnp.bfloat16)
        return (probabilities, grad_scores)

    zero_heads = jnp.zeros((tok_rows, local_heads, HD), jnp.float32)

    def back_turn(grad_acc, piece_set):
        key_piece, value_piece, number_piece, logical_piece = piece_set
        probabilities, grad_scores = score_grads(
            key_piece, value_piece, number_piece, logical_piece
        )
        grad_acc = (
            grad_acc
            + jnp.einsum("hqk,khd->qhd", grad_scores, key_piece, preferred_element_type=jnp.float32)
            * scaling
        )
        key_term = (
            jnp.einsum("hqk,qhd->khd", grad_scores, query_rot, preferred_element_type=jnp.float32)
            * scaling
        )
        value_term = jnp.einsum(
            "hqk,qhd->khd",
            probabilities.astype(jnp.bfloat16),
            grad_heads,
            preferred_element_type=jnp.float32,
        )
        return (grad_acc, (key_term, value_term))

    grad_query_rot, key_value_terms = lax.scan(back_turn, zero_heads, pieces)
    key_terms = key_value_terms[0].reshape(total_tokens, local_heads, HD)
    value_terms = key_value_terms[1].reshape(total_tokens, local_heads, HD)
    grad_key_rot, grad_value_own = (
        lax.psum_scatter(
            key_terms.astype(jnp.bfloat16), "ctx", scatter_dimension=0, tiled=True
        ).astype(jnp.float32),
        lax.psum_scatter(
            value_terms.astype(jnp.bfloat16), "ctx", scatter_dimension=0, tiled=True
        ).astype(jnp.float32),
    )
    grad_query_normed = rotate(grad_query_rot, -offset_own).reshape(tok_rows, width_part)
    grad_key_normed = rotate(grad_key_rot, -offset_own).reshape(tok_rows, width_part)
    query_gain_term = jnp.sum(grad_query_normed * query_proj * query_scale[:, None], axis=0)
    key_gain_term = jnp.sum(grad_key_normed * key_proj * key_scale[:, None], axis=0)
    weighted_query = grad_query_normed * query_gain
    weighted_key = grad_key_normed * key_gain
    query_dot, key_dot = row_pair(
        jnp.sum(weighted_query * query_proj, axis=1), jnp.sum(weighted_key * key_proj, axis=1)
    )
    grad_query_low = (
        query_scale[:, None] * weighted_query
        - query_proj * (query_scale * query_scale * query_scale * query_dot / D)[:, None]
    ).astype(jnp.bfloat16)
    grad_key_low = (
        key_scale[:, None] * weighted_key
        - key_proj * (key_scale * key_scale * key_scale * key_dot / D)[:, None]
    ).astype(jnp.bfloat16)
    grad_value_low = grad_value_own.reshape(tok_rows, width_part).astype(jnp.bfloat16)
    query_grad = jnp.einsum(
        "td,te->de", full_in, grad_query_low, preferred_element_type=jnp.float32
    )
    key_grad = jnp.einsum("td,te->de", full_in, grad_key_low, preferred_element_type=jnp.float32)
    value_grad = jnp.einsum(
        "td,te->de", full_in, grad_value_low, preferred_element_type=jnp.float32
    )
    input_term = jnp.einsum(
        "te,de->td", grad_query_low, query_full, preferred_element_type=jnp.float32
    )
    input_term = input_term + jnp.einsum(
        "te,de->td", grad_key_low, key_full, preferred_element_type=jnp.float32
    )
    input_term = input_term + jnp.einsum(
        "te,de->td", grad_value_low, value_full, preferred_element_type=jnp.float32
    )
    grad_input = grad_residual + head_sums(input_term)
    row_grads = (
        lax.psum_scatter(
            query_grad.astype(jnp.bfloat16), "ctx", scatter_dimension=0, tiled=True
        ).astype(jnp.float32),
        lax.psum_scatter(
            key_grad.astype(jnp.bfloat16), "ctx", scatter_dimension=0, tiled=True
        ).astype(jnp.float32),
        lax.psum_scatter(
            value_grad.astype(jnp.bfloat16), "ctx", scatter_dimension=0, tiled=True
        ).astype(jnp.float32),
        lax.psum_scatter(
            gate_grad.astype(jnp.bfloat16), "ctx", scatter_dimension=0, tiled=True
        ).astype(jnp.float32),
        lax.psum_scatter(
            up_grad.astype(jnp.bfloat16), "ctx", scatter_dimension=0, tiled=True
        ).astype(jnp.float32),
    )
    col_grads = (
        lax.psum_scatter(
            out_grad.astype(jnp.bfloat16), "ctx", scatter_dimension=1, tiled=True
        ).astype(jnp.float32),
        lax.psum_scatter(
            down_grad.astype(jnp.bfloat16), "ctx", scatter_dimension=1, tiled=True
        ).astype(jnp.float32),
    )
    gain_totals = lax.psum((query_gain_term, key_gain_term, attn_gain_term, ffn_gain_term), "ctx")
    back_result, back_grad = (
        lax.all_to_all(result.astype(jnp.bfloat16), "ctx", split_axis=0, concat_axis=0, tiled=True),
        lax.all_to_all(
            grad_input.astype(jnp.bfloat16), "ctx", split_axis=0, concat_axis=0, tiled=True
        ),
    )
    return (
        undeal(back_result),
        undeal(back_grad),
        row_grads[0],
        row_grads[1],
        row_grads[2],
        col_grads[0],
        row_grads[3],
        row_grads[4],
        col_grads[1],
        gain_totals[0],
        gain_totals[1],
        gain_totals[2],
        gain_totals[3],
    )


def sharded(layer, mesh, ctx, head):
    wide, tall, line = P(ctx, head), P(head, ctx), P(head)
    return jax.shard_map(
        layer,
        mesh=mesh,
        in_specs=(
            *(wide,) * 5,
            tall,
            wide,
            wide,
            tall,
            *(line,) * 4,
            P(),
            P(),
        ),
        out_specs=(*(wide,) * 5, tall, wide, wide, tall, *(line,) * 4),
        check_vma=False,
    )


def solution(mesh):
    if dict(mesh.shape) == {"ctx": 8, "head": 4}:
        split = Mesh(mesh.devices.reshape(4, 2, 2, 2), AXES)
        return sharded(plane_layer, split, CTX, ("x", "core"))
    return sharded(on_device, mesh, "ctx", "head")
```

```python
import math

import jax
import jax.numpy as jnp
import numpy as np
from jax import lax
from jax.experimental import pallas as pl
from jax.experimental.pallas import tpu as pltpu
from jax.sharding import Mesh
from jax.sharding import PartitionSpec as P

D = 2048
HD = 128


EPSILON = 1e-06
ROPE_THETA = 500000.0
MASKED = -1e30


BF = jnp.bfloat16
F32 = jnp.float32
MESH = pl.DeviceIdType.MESH
AXES = ("z", "y", "x", "core")
CTX = ("z", "y")
STRIP = 16
ANY = pl.BlockSpec(memory_space=pl.ANY)
VMEM = pl.BlockSpec(memory_space=pltpu.VMEM)
DMA = pltpu.SemaphoreType.DMA
BIG_VMEM = 60 * 1024 * 1024


def place():
    return tuple(lax.axis_index(name) for name in AXES)


def greet(targets):
    barrier = pltpu.get_barrier_semaphore()
    for target in targets:
        pl.semaphore_signal(barrier, inc=1, device_id=target, device_id_type=MESH)
    pl.semaphore_wait(barrier, len(targets))


def near_first(step, z):
    high = z // 2
    low = z + high * (3 - 2 * z)
    value = (low, 1 - low, 2, 3)[step]
    return value + high * (3 - 2 * value)


def plane_axes(me, turn):
    z, y, x, k = me
    a = x * (1 - turn) + y * turn
    b = y * (1 - turn) + x * turn

    def slot(zp, ap, bp):
        yp = bp * (1 - turn) + ap * turn
        xp = ap * (1 - turn) + bp * turn
        return zp * 4 + yp * 2 + xp

    dev_a = (z, y * (1 - turn) + (1 - y) * turn, (1 - x) * (1 - turn) + x * turn, k)
    dev_b = (z, (1 - y) * (1 - turn) + y * turn, x * (1 - turn) + (1 - x) * turn, k)
    return a, b, slot, dev_a, dev_b


EVEN = ((0, 1),) * 4
MORE_X = ((0, 1), (1, 1)) * 2
ALL_X = ((1, 1),) * 4
TURNS_OPEN = ALL_X
TURNS_ATTENTION = (MORE_X, EVEN)
TURNS_FFN_BACK = (EVEN, EVEN)
TURNS_CLOSE = ALL_X


def layer_axes(me, turns):
    return [plane_axes(me, t0 + me[3] * (t1 - t0)) for t0, t1 in turns]


def greet_plane(me, others=()):
    z, y, x, k = me
    barrier = pltpu.get_barrier_semaphore()
    targets = [(z, 1 - y, x, k), (z, y, 1 - x, k), *others]
    for target in targets:
        pl.semaphore_signal(barrier, inc=1, device_id=target, device_id_type=MESH)

    @pl.when(z < 3)
    def _():
        pl.semaphore_signal(barrier, inc=1, device_id=(z + 1, y, x, k), device_id_type=MESH)

    @pl.when(z > 0)
    def _():
        pl.semaphore_signal(barrier, inc=1, device_id=(z - 1, y, x, k), device_id_type=MESH)

    inner = (z + 2) // 3 - z // 3
    pl.semaphore_wait(barrier, len(targets) + 1 + inner)


GATHER_SEMS = [DMA((16,)), DMA((4,)), DMA((4,)), DMA((4,)), DMA((8,))]


DEAL_ORDER = (4, 1, 5, 2, 6, 3, 7)
OPEN_RATE = 2
DEALT_FIRST = 5
FORWARD_RATE = 1
BACK_RATE = 1
CLOSE_FIRST = 0
CLOSE_NEXT = 4
SUM_LAG = 1
BACK_LAG = 1
CLOSE_LAG = 3
CLOSE_RATE = 1


class Trickle:
    def __init__(self):
        self.waiting = []

    def add(self, copies):
        self.waiting.extend(copies)

    def tick(self, count=1):
        for start in self.waiting[:count]:
            start()
        self.waiting = self.waiting[count:]

    def flush(self):
        self.tick(len(self.waiting))


def gather_plane(
    me,
    own_ref,
    view,
    sems,
    turns,
    between=lambda step: None,
    arrived=lambda step: None,
    tick=lambda: None,
):
    z, y, x, k = me
    recv, up_send, down_send, a_send, b_send = sems
    axes = layer_axes(me, turns)

    def copy(src, index, send_sem, device):
        return pltpu.make_async_remote_copy(
            src_ref=src,
            dst_ref=view(index),
            send_sem=send_sem,
            recv_sem=recv.at[index],
            device_id=device,
            device_id_type=MESH,
        )

    def landed(index):
        copy(view(index), index, a_send.at[0], axes[0][3]).wait_recv()

    def layer_landed(step):
        tick()
        a, b, slot, dev_a, dev_b = axes[step]
        zp = near_first(step, z)
        landed(slot(zp, a, 1 - b))
        landed(slot(zp, 1 - a, 1 - b))
        arrived(step)

    for step in range(5):
        if step < 4:
            a, b, slot, dev_a, dev_b = axes[step]
            zp = near_first(step, z)
            index = slot(zp, a, b)
            if step == 0:
                src = own_ref
            else:
                landed(index)
                src = view(index)

            @pl.when((zp <= z) & (z < 3))
            def _():
                copy(src, index, up_send.at[zp], (z + 1, y, x, k)).start()

            @pl.when((zp >= z) & (z > 0))
            def _():
                copy(src, index, down_send.at[zp], (z - 1, y, x, k)).start()

            copy(src, index, a_send.at[step], dev_a).start()
            copy(src, index, b_send.at[step], dev_b).start()
            tick()
        if step > 0:
            a, b, slot, dev_a, dev_b = axes[step - 1]
            index = slot(near_first(step - 1, z), 1 - a, b)
            landed(index)
            copy(view(index), index, b_send.at[3 + step], dev_b).start()
            tick()
        between(step)
        if step >= 2:
            layer_landed(step - 2)
    layer_landed(3)
    for step in range(4):
        a, b, slot, dev_a, dev_b = axes[step]
        zp = near_first(step, z)
        for ap, number in ((a, step), (1 - a, 4 + step)):
            index = slot(zp, ap, b)
            copy(view(index), index, b_send.at[number], dev_b).wait_send()
        index = slot(zp, a, b)
        copy(view(index), index, a_send.at[step], dev_a).wait_send()

        @pl.when((zp <= z) & (z < 3))
        def _():
            copy(view(index), index, up_send.at[zp], (z + 1, y, x, k)).wait_send()

        @pl.when((zp >= z) & (z > 0))
        def _():
            copy(view(index), index, down_send.at[zp], (z - 1, y, x, k)).wait_send()


def reduce_scratch(rows, width):
    return [
        pltpu.VMEM((4, 2, rows, width), BF),
        pltpu.VMEM((4, rows, width), BF),
        pltpu.VMEM((4, rows, width), BF),
        pltpu.VMEM((4, rows, width), BF),
        pltpu.VMEM((4, rows, width), BF),
        pltpu.VMEM((4, rows, width), BF),
        DMA((8,)),
        DMA((8,)),
        DMA((4,)),
        DMA((4,)),
        DMA((4,)),
        DMA((4,)),
        DMA((4,)),
    ]


N_REDUCE = 13


def strips(rows, work, strip=STRIP):
    def body(i, carry):
        work(pl.ds(pl.multiple_of(i * strip, strip), strip))
        return carry

    lax.fori_loop(0, rows // strip, body, 0)


def reduce_plane(
    me,
    terms,
    rows,
    scratch,
    turns,
    produce,
    finish,
    after_terms=lambda: None,
    tick=lambda: None,
):
    z, y, x, k = me
    (from_b, to_a, from_a, to_z, from_low, from_high) = scratch[:6]
    (b_send, b_recv, a_send, a_recv, z_send, low_recv, high_recv) = scratch[6:]
    axes = layer_axes(me, turns)[::-1]
    order = [near_first(step, z) for step in (3, 2, 1, 0)]

    def start_of(step, ap, bp):
        return pl.multiple_of(axes[step][2](order[step], ap, bp) * rows, rows)

    def copy_b(step, flip):
        a, b, slot, dev_a, dev_b = axes[step]
        zp, ap = order[step], (1 - a if flip else a)
        return pltpu.make_async_remote_copy(
            src_ref=terms.at[pl.ds(start_of(step, ap, 1 - b), rows), :],
            dst_ref=from_b.at[zp, ap],
            send_sem=b_send.at[zp * 2 + ap],
            recv_sem=b_recv.at[zp * 2 + ap],
            device_id=dev_b,
            device_id_type=MESH,
        )

    def copy_a(step):
        zp, dev_a = order[step], axes[step][3]
        return pltpu.make_async_remote_copy(
            src_ref=to_a.at[zp],
            dst_ref=from_a.at[zp],
            send_sem=a_send.at[zp],
            recv_sem=a_recv.at[zp],
            device_id=dev_a,
            device_id_type=MESH,
        )

    def copy_z(zp, target, recv, to):
        return pltpu.make_async_remote_copy(
            src_ref=to_z.at[zp],
            dst_ref=target.at[zp],
            send_sem=z_send.at[zp],
            recv_sem=recv.at[zp],
            device_id=(to, y, x, k),
            device_id_type=MESH,
        )

    def copy_up(zp):
        return copy_z(zp, from_low, low_recv, z + 1)

    def copy_down(zp):
        return copy_z(zp, from_high, high_recv, z - 1)

    def mine(step, flip, strip):
        a, b = axes[step][:2]
        at = start_of(step, 1 - a if flip else a, b) + strip.start
        return terms[pl.ds(pl.multiple_of(at, STRIP), STRIP), :].astype(F32)

    for step in range(4):
        produce(order[step])
        for flip in (True, False):
            copy_b(step, flip).start()
        tick()
    after_terms()

    for step in range(4 + SUM_LAG):
        if step < 4:
            copy_b(step, True).wait_recv()

            def first(strip, step=step):
                zp, ap = order[step], 1 - axes[step][0]
                to_a[zp, strip] = (
                    mine(step, True, strip) + from_b[zp, ap, strip].astype(F32)
                ).astype(BF)

            strips(rows, first)
            copy_a(step).start()
            tick()
        if step >= SUM_LAG:
            done = step - SUM_LAG
            tick()
            copy_b(done, False).wait_recv()
            copy_a(done).wait_recv()

            def own_sum(strip, last=done):
                zp, ap = order[last], axes[last][0]
                return (
                    mine(last, False, strip)
                    + from_b[zp, ap, strip].astype(F32)
                    + from_a[zp, strip].astype(F32)
                )

            if done < 3:
                zp = order[done]
                upward = zp > z

                @pl.when(upward & (z > 0))
                def _(zp=zp, own_sum=own_sum):
                    copy_up(zp).wait_recv()

                    def work(strip):
                        to_z[zp, strip] = (own_sum(strip) + from_low[zp, strip].astype(F32)).astype(BF)

                    strips(rows, work)

                @pl.when(jnp.logical_not(upward) & (z < 3))
                def _(zp=zp, own_sum=own_sum):
                    copy_down(zp).wait_recv()

                    def work(strip):
                        to_z[zp, strip] = (own_sum(strip) + from_high[zp, strip].astype(F32)).astype(BF)

                    strips(rows, work)

                @pl.when((z == 0) | (z == 3))
                def _(zp=zp, own_sum=own_sum):
                    def work(strip):
                        to_z[zp, strip] = own_sum(strip).astype(BF)

                    strips(rows, work)

                @pl.when(upward)
                def _(zp=zp):
                    copy_up(zp).start()

                @pl.when(jnp.logical_not(upward))
                def _(zp=zp):
                    copy_down(zp).start()

            else:

                @pl.when(z == 0)
                def _():
                    copy_down(z).wait_recv()
                    strips(rows, lambda s: finish(s, own_sum(s) + from_high[z, s].astype(F32)))

                @pl.when(z == 3)
                def _():
                    copy_up(z).wait_recv()
                    strips(rows, lambda s: finish(s, own_sum(s) + from_low[z, s].astype(F32)))

                @pl.when((z > 0) & (z < 3))
                def _():
                    copy_up(z).wait_recv()
                    copy_down(z).wait_recv()
                    strips(
                        rows,
                        lambda s: finish(
                            s,
                            own_sum(s) + from_low[z, s].astype(F32) + from_high[z, s].astype(F32),
                        ),
                    )

    def settle():
        for step in range(4):
            copy_b(step, True).wait_send()
            copy_b(step, False).wait_send()
            copy_a(step).wait_send()
        for zp in order[:3]:
            copy_up(zp).wait_send()

    return settle


def own_tile(me):
    z, y, x, k = me
    return z * 2 + y


def gather_view(out_ref, rows):
    def view(slot):
        return out_ref.at[pl.ds(pl.multiple_of(slot * rows, rows), rows), :]

    return view


def hand_out_copies(me, own_ref, out_ref, send, recv):
    z, y, x, k = me
    rows, width = own_ref.shape
    part = width // 4
    target_rows = pl.ds(pl.multiple_of(k * 2 * rows + x * rows, rows), rows)

    def copy(xt, kt, number):
        return pltpu.make_async_remote_copy(
            src_ref=own_ref.at[:, pl.ds(pl.multiple_of((2 * xt + kt) * part, part), part)],
            dst_ref=out_ref.at[target_rows, :],
            send_sem=send.at[number],
            recv_sem=recv.at[number],
            device_id=(z, y, xt, kt),
            device_id_type=MESH,
        )

    local = pltpu.make_async_copy(
        own_ref.at[:, pl.ds(pl.multiple_of((2 * x + k) * part, part), part)],
        out_ref.at[target_rows, :],
        recv.at[3],
    )
    return [copy(x, 1 - k, 0), copy(1 - x, k, 1), copy(1 - x, 1 - k, 2)], local


def pair_devices(me):
    z, y, x, k = me
    return [(z, y, x, 1 - k), (z, y, 1 - x, 1 - k)]


def row_scale(values):
    return lax.rsqrt(jnp.sum(values * values, axis=1, keepdims=True) / values.shape[1] + EPSILON)


def norm_back_strip(grad, values, gain):
    scale = row_scale(values)
    term = grad * values * scale
    weighted = grad * gain
    dot = jnp.sum(weighted * values, axis=1, keepdims=True)
    back = scale * weighted - values * (scale * scale * scale * dot / values.shape[1])
    return back, term[:8] + term[8:]


def comm_call(body, name, number, out_shape, in_specs, out_specs, scratch, cost=None):
    return pl.pallas_call(
        body,
        name=name,
        out_shape=out_shape,
        in_specs=in_specs,
        out_specs=out_specs,
        scratch_shapes=scratch,
        cost_estimate=cost,
        compiler_params=pltpu.CompilerParams(
            collective_id=number, has_side_effects=True, vmem_limit_bytes=BIG_VMEM
        ),
    )


def same_x_greet(me):
    z, y, x, k = me
    barrier = pltpu.get_barrier_semaphore()
    number = z * 4 + y * 2 + k

    def body(i, carry):
        other = lax.rem(number + i, 16)
        pl.semaphore_signal(
            barrier,
            inc=1,
            device_id=(other // 4, (other // 2) % 2, x, other % 2),
            device_id_type=MESH,
        )
        return carry

    lax.fori_loop(1, 16, body, 0)
    for kt in (k, 1 - k):
        pl.semaphore_signal(barrier, inc=1, device_id=(z, y, 1 - x, kt), device_id_type=MESH)
    pl.semaphore_wait(barrier, 17)


def masked_scores(q, keys, low, high, logical):
    raw = lax.dot_general(q, keys, (((1,), (1,)), ((), ())), preferred_element_type=F32)
    allowed = (logical >= low) & (logical <= high)
    return raw * (1.0 / math.sqrt(HD)), allowed


def eye_mask():
    return lax.broadcasted_iota(jnp.int32, (HD, HD), 0) == lax.broadcasted_iota(
        jnp.int32, (HD, HD), 1
    )


def column_to_row(column, eye):
    return jnp.sum(jnp.where(eye, column, 0.0), axis=0, keepdims=True)


def row_to_column(row, eye):
    return jnp.sum(jnp.where(eye, row, 0.0), axis=1, keepdims=True)


def open_layer(
    inputs,
    cotangent,
    w_query,
    w_key,
    w_value,
    w_out,
    w_gate,
    w_up,
    w_down,
    query_gain,
    key_gain,
    attn_gain,
    ffn_gain,
    order,
    lengths,
    frequency,
):
    rows, part = inputs.shape
    half = rows // 2
    quarter = half // 2
    tokens, width = 8 * half, 4 * part
    hidden = w_gate.shape[1]
    down = hidden // 8

    def body(*refs):
        (in_ref, cot_ref, wq_ref, wk_ref, wv_ref, wo_ref, wg_ref, wu_ref, wd_ref) = refs[:9]
        gain_parts = refs[9:13]
        (order_ref, lengths_ref, frequency_ref) = refs[13:16]
        (cos_ref, sin_ref, low_ref, high_ref, log_ref) = refs[27:32]
        gain_ref = refs[-1]
        refs = refs[:10] + refs[16:27] + refs[32:-1]
        (full_out, own_out, own_cot_ref, wqkv_ref, wout_ref, gains_ref, gu_out, down_ref) = refs[10:18]
        (q_ref, k_ref, v_ref) = refs[18:21]
        (full_ref, shard, cot_half, qkv_raw, out_raw, gu_raw, d_raw) = refs[21:28]
        (qkv_stage, out_stage, gu_stage, d_stage) = refs[28:32]
        (load_sem, pair_send, pair_recv, local_sem, deal_send, deal_recv) = refs[32:38]
        (share_send, share_recv, gain_send, gain_recv, cot_sems, keep_sem) = refs[38:44]
        (down_send, down_recv) = refs[44:46]
        gather_sems = refs[46:]
        me = z, y, x, k = place()
        ctx = own_tile(me)
        sibling = (z, y, x, 1 - k)

        loads = [
            pltpu.make_async_copy(src, dst, load_sem.at[i])
            for i, (src, dst) in enumerate(
                [
                    (wq_ref, qkv_raw.at[0]),
                    (wk_ref, qkv_raw.at[1]),
                    (wv_ref, qkv_raw.at[2]),
                    (wo_ref, out_raw),
                    (wg_ref, gu_raw.at[0]),
                    (wu_ref, gu_raw.at[1]),
                    (wd_ref, d_raw),
                ]
            )
        ]
        for load in loads:
            load.start()
        same_x_greet(me)

        def pair_copy(src, dst, number):
            columns = pl.ds(pl.multiple_of(k * part, part), part)
            remote = pltpu.make_async_remote_copy(
                src_ref=src.at[pl.ds(pl.multiple_of((1 - k) * half, half), half), :],
                dst_ref=dst.at[:, columns],
                send_sem=pair_send.at[number],
                recv_sem=pair_recv.at[number],
                device_id=sibling,
                device_id_type=MESH,
            )
            local = pltpu.make_async_copy(
                src.at[pl.ds(pl.multiple_of(k * half, half), half), :],
                dst.at[:, columns],
                local_sem.at[number],
            )
            remote.start()
            local.start()
            return remote, local

        first = pair_copy(in_ref, shard, 0)
        second = pair_copy(cot_ref, cot_half, 1)

        for i, gain_part in enumerate(gain_parts):
            gain_ref[i : i + 1, :] = gain_part[...]

        def gain_copy(xt, kt, number):
            return pltpu.make_async_remote_copy(
                src_ref=gain_ref,
                dst_ref=gains_ref.at[:, pl.ds(pl.multiple_of((2 * x + k) * part, part), part)],
                send_sem=gain_send.at[number],
                recv_sem=gain_recv.at[number],
                device_id=(z, y, xt, kt),
                device_id_type=MESH,
            )

        gain_copies = [gain_copy(x, 1 - k, 0), gain_copy(1 - x, k, 1), gain_copy(1 - x, 1 - k, 2)]
        for copy in gain_copies:
            copy.start()
        gain_local = pltpu.make_async_copy(
            gain_ref,
            gains_ref.at[:, pl.ds(pl.multiple_of((2 * x + k) * part, part), part)],
            local_sem.at[2],
        )
        gain_local.start()

        first[0].wait_recv()
        first[1].wait()

        def view(slot):
            return full_ref.at[
                pl.ds(pl.multiple_of((slot // 2) * half, half), half),
                pl.ds(pl.multiple_of((slot % 2) * 2 * part, 2 * part), 2 * part),
            ]

        own_slot = ctx * 2 + x
        own_local = pltpu.make_async_copy(shard, view(own_slot), local_sem.at[3])
        own_local.start()

        def deal(e):
            j, r = e // 2, e % 2
            return [
                pltpu.make_async_remote_copy(
                    src_ref=src,
                    dst_ref=dst,
                    send_sem=deal_send.at[i, e],
                    recv_sem=deal_recv.at[i, ctx],
                    device_id=(2 * k + e // 4, (e // 2) % 2, x, r),
                    device_id_type=MESH,
                )
                for i, (src, dst) in enumerate(deal_ends(j, r))
            ]

        def deal_ends(j, r):
            at = pl.ds(pl.multiple_of(ctx * 2 * HD + r * HD, HD), HD)
            return (
                (
                    qkv_stage.at[:, r * HD : (r + 1) * HD, j * HD : (j + 1) * HD],
                    wqkv_ref.at[:, at, :],
                ),
                (
                    out_stage.at[j * HD : (j + 1) * HD, r * HD : (r + 1) * HD],
                    wout_ref.at[:, at],
                ),
            )

        trickle = Trickle()
        stays = k == z // 2
        own_e = (z % 2) * 4 + y * 2 + k

        def deal_all():
            for load in loads[:4]:
                load.wait()

            def round_qkv(s):
                for i in range(3):
                    qkv_stage[i, s] = qkv_raw[i, s].astype(BF)

            strips(rows, round_qkv)

            def round_out(s):
                out_stage[s] = out_raw[s].astype(BF)

            strips(2 * rows, round_out, 32)
            trickle.add([lambda e=e: deal_start(e) for e in range(8)])

        def deal_start(e):
            @pl.when(jnp.logical_not(stays & (own_e == e)))
            def _():
                for copy in deal(e):
                    copy.start()

            @pl.when(stays & (own_e == e))
            def _():
                for i, (src, dst) in enumerate(deal_ends(e // 2, e % 2)):
                    pltpu.make_async_copy(src, dst, deal_recv.at[i, ctx]).start()

        def cot_begin():
            second[0].wait_recv()
            second[1].wait()
            cot_remote.start()
            cot_local.start()

        wide = pl.ds(pl.multiple_of(x * 2 * part, 2 * part), 2 * part)
        cot_remote = pltpu.make_async_remote_copy(
            src_ref=cot_half.at[pl.ds(pl.multiple_of((1 - x) * quarter, quarter), quarter), :],
            dst_ref=own_cot_ref.at[:, wide],
            send_sem=cot_sems.at[0],
            recv_sem=cot_sems.at[1],
            device_id=(z, y, 1 - x, k),
            device_id_type=MESH,
        )
        cot_local = pltpu.make_async_copy(
            cot_half.at[pl.ds(pl.multiple_of(x * quarter, quarter), quarter), :],
            own_cot_ref.at[:, wide],
            cot_sems.at[2],
        )

        keeps = [
            pltpu.make_async_copy(gu_stage.at[0], gu_out.at[0], keep_sem.at[0]),
            pltpu.make_async_copy(gu_stage.at[1], gu_out.at[1], keep_sem.at[1]),
            pltpu.make_async_copy(
                d_stage.at[pl.ds(pl.multiple_of(ctx * down, down), down), :],
                down_ref.at[:, pl.ds(pl.multiple_of(ctx * rows, rows), rows)],
                keep_sem.at[2],
            ),
        ]

        def down_copy(t):
            to = ctx + t - 8 * ((ctx + t) // 8)
            return pltpu.make_async_remote_copy(
                src_ref=d_stage.at[pl.ds(pl.multiple_of(to * down, down), down), :],
                dst_ref=down_ref.at[:, pl.ds(pl.multiple_of(ctx * rows, rows), rows)],
                send_sem=down_send.at[t],
                recv_sem=down_recv.at[t],
                device_id=(to // 2, to % 2, x, k),
                device_id_type=MESH,
            )

        def down_landed(t):
            c = ctx + 8 - t - 8 * ((ctx + 8 - t) // 8)
            part_of = down_ref.at[:, pl.ds(pl.multiple_of(c * rows, rows), rows)]
            pltpu.make_async_remote_copy(
                src_ref=part_of,
                dst_ref=part_of,
                send_sem=down_send.at[t],
                recv_sem=down_recv.at[t],
                device_id=sibling,
                device_id_type=MESH,
            ).wait_recv()

        def deal_down():
            trickle.add([lambda t=t: down_copy(t).start() for t in DEAL_ORDER])

        def round_up(i):
            loads[4 + i].wait()

            def work(s):
                gu_stage[i, s] = gu_raw[i, s].astype(BF)

            strips(rows, work)
            keeps[i].start()

        def round_down():
            loads[6].wait()

            def work(s):
                d_stage[s] = d_raw[s].astype(BF)

            strips(hidden, work, 128)
            keeps[2].start()

        def positions():
            blocks = order_ref.shape[1]
            square = lax.broadcasted_iota(jnp.int32, (blocks, blocks), 0)
            square = square == lax.broadcasted_iota(jnp.int32, (blocks, blocks), 1)
            column = row_to_column(order_ref[...].astype(F32), square)
            lane = lax.broadcasted_iota(jnp.int32, (1, 2 * tokens), 1)
            other = (lane >= tokens).astype(jnp.int32)
            core = k + other - 2 * k * other
            lane = lane - tokens * other
            in_half = lane & (half - 1)
            block_rows = 2 * tokens // blocks
            block = (lane - in_half) // half * (2 * half // block_rows)
            block = block + core * (half // block_rows)
            block = block + (in_half - (in_half & (block_rows - 1))) // block_rows
            match = lax.broadcasted_iota(jnp.int32, (blocks, 2 * tokens), 0) == block
            first_of = jnp.sum(jnp.where(match, column, 0.0), axis=0, keepdims=True) * block_rows
            logical = first_of + (in_half & (block_rows - 1)).astype(F32)
            log_ref[...] = logical
            own = logical[:, :tokens]
            begin = jnp.zeros_like(own)
            end = jnp.zeros((1, 1), F32)
            for j in range(lengths_ref.shape[1]):
                length = lengths_ref[:, j : j + 1].astype(F32)
                end = end + length
                begin = begin + jnp.where(own >= end, length, 0.0)
            eye = eye_mask()
            for i in range(tokens // HD):
                piece = slice(i * HD, (i + 1) * HD)
                low = row_to_column(begin[:, piece], eye)
                high = row_to_column(own[:, piece], eye)
                low_ref[piece, :] = low
                high_ref[piece, :] = high
                angles = (high - low) * frequency_ref[...]
                cos_ref[piece, :] = jnp.cos(angles)
                sine = jnp.sin(angles)
                left = lax.broadcasted_iota(jnp.int32, (HD, HD), 1) < HD // 2
                sin_ref[piece, :] = jnp.where(left, -sine, sine)

        between = [
            deal_all,
            lambda: (cot_begin(), round_down(), deal_down()),
            lambda: (round_up(0), round_up(1)),
            positions,
            lambda: None,
        ]
        gather_plane(
            me,
            shard,
            view,
            gather_sems,
            TURNS_OPEN,
            lambda step: between[step](),
            tick=lambda: trickle.tick(OPEN_RATE),
        )
        trickle.flush()

        def deal_wait(c):
            at = slice(c * 2 * HD, c * 2 * HD + HD)
            pltpu.make_async_copy(
                qkv_stage.at[:, :HD, :HD], wqkv_ref.at[:, at, :], deal_recv.at[0, c]
            ).wait()
            pltpu.make_async_copy(
                out_stage.at[:HD, :HD], wout_ref.at[:, at], deal_recv.at[1, c]
            ).wait()

        def share(c, r):
            at = pl.ds(pl.multiple_of(c * 2 * HD + r * HD, HD), HD)
            return [
                pltpu.make_async_remote_copy(
                    src_ref=ref,
                    dst_ref=ref,
                    send_sem=share_send.at[i, c],
                    recv_sem=share_recv.at[i, c],
                    device_id=sibling,
                    device_id_type=MESH,
                )
                for i, ref in enumerate((wqkv_ref.at[:, at, :], wout_ref.at[:, at]))
            ]

        for c in range(8):
            deal_wait(c)
            for copy in share(c, k):
                copy.start()
        own_local.wait()
        full_keep = pltpu.make_async_copy(full_ref, full_out, keep_sem.at[3])
        full_keep.start()
        own_rows = pl.ds(pl.multiple_of(own_slot * quarter, quarter), quarter)
        own_keep = pltpu.make_async_copy(full_ref.at[own_rows, :], own_out, keep_sem.at[4])
        own_keep.start()
        for c in range(8):
            for copy in share(c, 1 - k):
                copy.wait_recv()

        def project(s):
            tile = full_ref[s, :]
            q_ref[s, :] = jnp.dot(tile, wqkv_ref[0], preferred_element_type=F32)
            k_ref[s, :] = jnp.dot(tile, wqkv_ref[1], preferred_element_type=F32)
            v_ref[s, :] = jnp.dot(tile, wqkv_ref[2], preferred_element_type=F32).astype(BF)

        strips(tokens, project, 256)
        for e in range(8):

            @pl.when(jnp.logical_not(stays & (own_e == e)))
            def _(e=e):
                for copy in deal(e):
                    copy.wait_send()

        for c in range(8):
            for copy in share(c, k):
                copy.wait_send()
        first[0].wait_send()
        second[0].wait_send()
        for copy in gain_copies:
            copy.wait()
        gain_local.wait()
        cot_remote.wait()
        cot_local.wait()
        for keep in (*keeps, full_keep, own_keep):
            keep.wait()
        for t in range(1, 8):
            down_landed(t)
            down_copy(t).wait_send()

    shape = jax.ShapeDtypeStruct
    return comm_call(
        body,
        "open_layer",
        0,
        (
            shape((tokens, width), BF),
            shape((quarter, width), BF),
            shape((quarter, width), BF),
            shape((3, width, HD), BF),
            shape((HD, width), BF),
            shape((4, width), F32),
            shape((2, rows, hidden), BF),
            shape((down, width), BF),
            shape((tokens, HD), F32),
            shape((tokens, HD), F32),
            shape((tokens, HD), BF),
            shape((tokens, HD), F32),
            shape((tokens, HD), F32),
            shape((tokens, 1), F32),
            shape((tokens, 1), F32),
            shape((1, 2 * tokens), F32),
        ),
        [*[ANY] * 9, *[VMEM] * 7],
        (ANY, ANY, ANY, VMEM, VMEM, ANY, ANY, ANY, VMEM, VMEM, VMEM, *[VMEM] * 5),
        [
            pltpu.VMEM((tokens, width), BF),
            pltpu.VMEM((half, 2 * part), BF),
            pltpu.VMEM((half, 2 * part), BF),
            pltpu.VMEM((3, rows, part), F32),
            pltpu.VMEM((part, rows), F32),
            pltpu.VMEM((2, rows, hidden), F32),
            pltpu.VMEM((hidden, rows), F32),
            pltpu.VMEM((3, rows, part), BF),
            pltpu.VMEM((part, rows), BF),
            pltpu.VMEM((2, rows, hidden), BF),
            pltpu.VMEM((hidden, rows), BF),
            DMA((7,)),
            DMA((2,)),
            DMA((2,)),
            DMA((4,)),
            DMA((2, 8)),
            DMA((2, 8)),
            DMA((2, 8)),
            DMA((2, 8)),
            DMA((3,)),
            DMA((3,)),
            DMA((3,)),
            DMA((5,)),
            DMA((8,)),
            DMA((8,)),
            *GATHER_SEMS,
            pltpu.VMEM((4, part), F32),
        ],
    )(
        inputs,
        cotangent,
        w_query,
        w_key,
        w_value,
        w_out,
        w_gate,
        w_up,
        w_down,
        query_gain,
        key_gain,
        attn_gain,
        ffn_gain,
        order,
        lengths,
        frequency,
    )


def plane_peer(me, i):
    z, y, x, k = me
    other = lax.rem(z * 4 + y * 2 + x + i, 16)
    return other, (other // 4, (other // 2) % 2, other % 2, k)


def plane_greet_all(me, others):
    barrier = pltpu.get_barrier_semaphore()

    def call(i, carry):
        pl.semaphore_signal(barrier, inc=1, device_id=plane_peer(me, i)[1], device_id_type=MESH)
        return carry

    lax.fori_loop(1, 16, call, 0)
    for other in others:
        pl.semaphore_signal(barrier, inc=1, device_id=other, device_id_type=MESH)
    pl.semaphore_wait(barrier, 15 + len(others))


def sum_begin(me, slots, send, recv):
    own = me[0] * 4 + me[1] * 2 + me[2]

    def copy(i, slot):
        return pltpu.make_async_remote_copy(
            src_ref=slots.at[slot],
            dst_ref=slots.at[slot],
            send_sem=send.at[i],
            recv_sem=recv.at[slot],
            device_id=plane_peer(me, i)[1],
            device_id_type=MESH,
        )

    def begin(i, carry):
        copy(i, own).start()
        return carry

    def landed(i, carry):
        copy(i, plane_peer(me, i)[0]).wait_recv()
        return carry

    def sent(i, carry):
        copy(i, own).wait_send()
        return carry

    lax.fori_loop(1, 16, begin, 0)

    def end():
        lax.fori_loop(1, 16, landed, 0)
        lax.fori_loop(1, 16, sent, 0)
        total = slots[0]
        for i in range(1, 16):
            total = total + slots[i]
        return total

    return end


def attention_forward(
    query, key, value, tables, bounds, logical, source, out_weight, gains, gu_stage, down_own
):
    tokens, width = query.shape[0], source.shape[1]
    rows = tokens // 16
    group = tokens // 4
    hidden = gu_stage.shape[2] // 8
    part = width // 8

    def body(*refs):
        (q_in, k_in, v_in, cos_ref, sin_ref, low_ref, high_ref, log_ref, source_ref, wout_ref, gain_ref) = refs[:11]
        (gu_ref, d_ref) = refs[11:13]
        (full_ref, own_ref, branch_ref, wgu_ref, d_other_ref, qrot_ref, keys_ref, values_ref, o_ref, lse_ref, scale_ref) = refs[13:24]
        (terms, shard, slots, tot_send, tot_recv, pair_send, pair_recv, local) = refs[24:32]
        (ffn_send, ffn_recv, share_send, share_recv, ffn_local) = refs[32:37]
        rest = refs[37:]
        me = z, y, x, k = place()
        ctx = own_tile(me)
        head_at = pl.ds(pl.multiple_of((x * 8 + ctx) * HD, HD), HD)
        query_gain, key_gain = gain_ref[0:1, head_at], gain_ref[1:2, head_at]
        sibling = (z, y, x, 1 - k)
        barrier = pltpu.get_barrier_semaphore()
        plane_greet_all(me, [sibling])

        def pair(src, dst, n):
            return pltpu.make_async_remote_copy(
                src_ref=src,
                dst_ref=dst,
                send_sem=pair_send.at[n],
                recv_sem=pair_recv.at[n],
                device_id=sibling,
                device_id_type=MESH,
            )

        eye = eye_mask()
        own = z * 4 + y * 2 + x
        for i in range(8):
            piece = slice(i * HD, (i + 1) * HD)
            for side, ref in enumerate((q_in, k_in)):
                values = ref[piece, :]
                column = jnp.sum(values * values, axis=1, keepdims=True)
                slots[own, side * 8 + i : side * 8 + i + 1, :] = column_to_row(column, eye)
        values_ref[:tokens, :] = v_in[...]
        other_half = pl.ds(tokens, tokens)
        v_copy = pair(v_in, values_ref.at[other_half, :], 0)
        v_copy.start()

        def ffn_copy(t, i):
            to = ctx + t - 8 * ((ctx + t) // 8)
            at = pl.ds(pl.multiple_of(to * hidden, hidden), hidden)
            from_at = pl.ds(pl.multiple_of(ctx * part, part), part)
            return pltpu.make_async_remote_copy(
                src_ref=gu_ref.at[i, :, at],
                dst_ref=wgu_ref.at[i, from_at, :hidden],
                send_sem=ffn_send.at[i, t],
                recv_sem=ffn_recv.at[i, t],
                device_id=(to // 2, to % 2, x, k),
                device_id_type=MESH,
            )

        def ffn_ends(t):
            c = ctx + 8 - t - 8 * ((ctx + 8 - t) // 8)
            at = pl.ds(pl.multiple_of(c * part, part), part)
            return wgu_ref.at[:, at, :hidden], wgu_ref.at[:, at, hidden:]

        own_at = pl.ds(pl.multiple_of(ctx * hidden, hidden), hidden)
        ffn_own = pltpu.make_async_copy(gu_ref.at[:, :, own_at], ffn_ends(0)[0], ffn_local)
        ffn_own.start()
        down_copy = pair(d_ref, d_other_ref, 2)
        down_copy.start()

        total = sum_begin(me, slots, tot_send, tot_recv)()
        trickle = Trickle()
        trickle.add([lambda t=t, i=i: ffn_copy(t, i).start() for t in DEAL_ORDER for i in range(2)])
        trickle.tick(DEALT_FIRST)
        scales = lax.rsqrt(total / width + EPSILON)
        scale_ref[...] = scales

        def rotated(values, piece):
            return values * cos_ref[piece, :] + pltpu.roll(values, HD // 2, 1) * sin_ref[piece, :]

        for i in range(8):
            piece = slice(i * HD, (i + 1) * HD)
            factor = row_to_column(scales[8 + i : 9 + i, :], eye)
            keys_ref[piece, :] = rotated(k_in[piece, :] * factor * key_gain, piece).astype(BF)
        k_copy = pair(keys_ref.at[:tokens, :], keys_ref.at[other_half, :], 1)
        k_copy.start()
        for i in range(8):
            piece = slice(i * HD, (i + 1) * HD)
            factor = row_to_column(scales[i : i + 1, :], eye)
            qrot_ref[piece, :] = rotated(q_in[piece, :] * factor * query_gain, piece).astype(BF)
        v_copy.wait()
        k_copy.wait()

        def produce(zp):
            at = pl.ds(pl.multiple_of(zp * group, group), group)
            raw, allowed = masked_scores(
                qrot_ref[at, :], keys_ref[...], low_ref[at, :], high_ref[at, :], log_ref[...]
            )
            raw = jnp.where(allowed, raw, MASKED)
            top = jnp.max(raw, axis=1, keepdims=True)
            weights = jnp.where(allowed, jnp.exp(raw - top), 0.0)
            total_weight = jnp.sum(weights, axis=1, keepdims=True)
            weights = (weights / total_weight).astype(BF)
            out = jnp.dot(weights, values_ref[...], preferred_element_type=F32)
            o_ref[at, :] = out
            lse_ref[at, :] = top + jnp.log(total_weight)
            terms[at, :] = jnp.dot(
                out.astype(BF), wout_ref[...], preferred_element_type=F32
            ).astype(BF)

        def finish(strip, total):
            branch_ref[strip] = total
            h = source_ref[strip].astype(F32) + total * row_scale(total) * gain_ref[2:3, :]
            own_ref[strip] = h
            shard[strip] = h.astype(BF)

        settle = reduce_plane(
            me,
            terms,
            rows,
            rest[:N_REDUCE],
            TURNS_ATTENTION[0],
            produce,
            finish,
            tick=lambda: trickle.tick(FORWARD_RATE),
        )
        view = gather_view(full_ref, rows)
        keep = pltpu.make_async_copy(shard, view(own), local)
        keep.start()

        def share(t):
            src, dst = ffn_ends(t)
            return pltpu.make_async_remote_copy(
                src_ref=src,
                dst_ref=dst,
                send_sem=share_send.at[t],
                recv_sem=share_recv.at[t],
                device_id=sibling,
                device_id_type=MESH,
            )

        def ffn_landed(t):
            for i in range(2):
                src = ffn_ends(t)[0].at[i]
                pltpu.make_async_remote_copy(
                    src_ref=src,
                    dst_ref=src,
                    send_sem=ffn_send.at[i, t],
                    recv_sem=ffn_recv.at[i, t],
                    device_id=sibling,
                    device_id_type=MESH,
                ).wait_recv()

        gather_plane(
            me,
            shard,
            view,
            rest[N_REDUCE:],
            TURNS_ATTENTION[1],
            tick=lambda: trickle.tick(FORWARD_RATE),
        )
        trickle.flush()
        ffn_own.wait()
        share(0).start()
        for t in DEAL_ORDER:
            ffn_landed(t)
            share(t).start()
        keep.wait()
        settle()
        for t in range(8):
            share(t).wait()
            for i in range(2):
                if t > 0:
                    ffn_copy(t, i).wait_send()
        down_copy.wait()

    shape = jax.ShapeDtypeStruct
    return comm_call(
        body,
        "attention_forward",
        1,
        (
            shape((tokens, width), BF),
            shape((rows, width), F32),
            shape((rows, width), F32),
            shape((2, width, 2 * hidden), BF),
            shape((hidden, width), BF),
            shape((tokens, HD), BF),
            shape((2 * tokens, HD), BF),
            shape((2 * tokens, HD), BF),
            shape((tokens, HD), F32),
            shape((tokens, 1), F32),
            shape((16, HD), F32),
        ),
        [VMEM] * 11 + [ANY, ANY],
        (ANY, VMEM, VMEM, ANY, ANY, VMEM, VMEM, VMEM, VMEM, VMEM, VMEM),
        [
            pltpu.VMEM((tokens, width), BF),
            pltpu.VMEM((rows, width), BF),
            pltpu.VMEM((16, 16, HD), F32),
            DMA((16,)),
            DMA((16,)),
            DMA((3,)),
            DMA((3,)),
            DMA,
            DMA((2, 8)),
            DMA((2, 8)),
            DMA((8,)),
            DMA((8,)),
            DMA,
            *reduce_scratch(rows, width),
            *GATHER_SEMS,
        ],
    )(query, key, value, *tables, *bounds, logical, source, out_weight, gains, gu_stage, down_own)


def ffn_forward(source, gu_w, down_w, residual, cotangent, gain):
    tokens, width = source.shape
    rows, group = tokens // 16, tokens // 4
    hidden = 2 * down_w[0].shape[0]

    def body(*refs):
        (h_any, gu_any, d_any, d_any2, res_ref, cot_ref, gain_ref) = refs[:7]
        (full_ref, out_ref, gg_ref, for_gate_ref, for_up_ref, m_ref) = refs[7:13]
        (hs, gu, dw, terms, shard, result, load_sem, local, out_send, out_recv) = refs[13:23]
        scratch = refs[23:]
        me = z, y, x, k = place()

        def h_load(zp):
            at = pl.ds(pl.multiple_of(zp * group, group), group)
            return pltpu.make_async_copy(h_any.at[at, :], hs.at[at, :], load_sem.at[zp])

        order = [near_first(step, z) for step in (3, 2, 1, 0)]
        gu_load = pltpu.make_async_copy(gu_any, gu, load_sem.at[4])
        d_loads = [
            pltpu.make_async_copy(d_any, dw.at[: hidden // 2, :], load_sem.at[5]),
            pltpu.make_async_copy(d_any2, dw.at[hidden // 2 :, :], load_sem.at[6]),
        ]
        for load in (h_load(order[0]), gu_load, *d_loads):
            load.start()
        for zp in order[1:]:
            h_load(zp).start()
        greet_plane(me, pair_devices(me))
        gg_ref[...] = jnp.zeros_like(gg_ref)
        gu_load.wait()

        def produce(zp):
            at = pl.ds(pl.multiple_of(zp * group, group), group)
            h_load(zp).wait()
            tile = hs[at, :]
            gate = jnp.dot(tile, gu[0], preferred_element_type=F32)
            up = jnp.dot(tile, gu[1], preferred_element_type=F32)
            sig = jax.nn.sigmoid(gate)
            silu = gate * sig
            mixed = (silu * up).astype(BF)
            for_gate_ref[at, :] = up * sig * (1.0 + gate * (1.0 - sig))
            for_up_ref[at, :] = silu
            m_ref[at, :] = mixed
            terms[at, :] = jnp.dot(mixed, dw[...], preferred_element_type=F32).astype(BF)

        def finish(strip, total):
            gain_row = gain_ref[3:4, :]
            out = res_ref[strip] + total * row_scale(total) * gain_row
            result[strip] = out.astype(BF)
            back, term = norm_back_strip(cot_ref[strip].astype(F32), total, gain_row)
            gg_ref[...] += term
            shard[strip] = back.astype(BF)

        for load in d_loads:
            load.wait()
        settle = reduce_plane(me, terms, rows, scratch[:N_REDUCE], EVEN, produce, finish)
        view = gather_view(full_ref, rows)
        keep = pltpu.make_async_copy(shard, view(me[0] * 4 + me[1] * 2 + me[2]), local)
        keep.start()
        copies, own = hand_out_copies(me, result, out_ref, out_send, out_recv)
        for copy in copies:
            copy.start()
        own.start()
        gather_plane(me, shard, view, scratch[N_REDUCE:], EVEN)
        keep.wait()
        settle()
        own.wait()
        for copy in copies:
            copy.wait()

    shape = jax.ShapeDtypeStruct
    return comm_call(
        body,
        "ffn_forward",
        3,
        (
            shape((tokens, width), BF),
            shape((rows * 4, width // 4), BF),
            shape((8, width), F32),
            shape((tokens, hidden), F32),
            shape((tokens, hidden), F32),
            shape((tokens, hidden), BF),
        ),
        [ANY, ANY, ANY, ANY, VMEM, VMEM, VMEM],
        (ANY, ANY, VMEM, VMEM, VMEM, VMEM),
        [
            pltpu.VMEM((tokens, width), BF),
            pltpu.VMEM((2, width, hidden), BF),
            pltpu.VMEM((hidden, width), BF),
            pltpu.VMEM((tokens, width), BF),
            pltpu.VMEM((rows, width), BF),
            pltpu.VMEM((rows, width), BF),
            DMA((7,)),
            DMA,
            DMA((3,)),
            DMA((4,)),
            *reduce_scratch(rows, width),
            *GATHER_SEMS,
        ],
    )(source, gu_w, *down_w, residual, cotangent, gain)


EARLY = 5
GRADS_FIRST = 6


def grad_copies(me, src, dst, send, recv, t):
    ctx = own_tile(me)
    to = ctx + t - 8 * ((ctx + t) // 8)
    return [
        pltpu.make_async_remote_copy(
            src_ref=src.at[i],
            dst_ref=dst.at[ctx, i],
            send_sem=send.at[t, i],
            recv_sem=recv.at[t, i],
            device_id=(to // 2, to % 2, me[2], me[3]),
            device_id_type=MESH,
        )
        for i in range(3)
    ]


def grad_landed(me, dst, send, recv, t):
    ctx = own_tile(me)
    c = ctx + 8 - t - 8 * ((ctx + 8 - t) // 8)
    for i in range(3):
        pltpu.make_async_remote_copy(
            src_ref=dst.at[c, i],
            dst_ref=dst.at[c, i],
            send_sem=send.at[t, i],
            recv_sem=recv.at[t, i],
            device_id=(me[0], me[1], me[2], 1 - me[3]),
            device_id_type=MESH,
        ).wait_recv()


def ctx_greet(me, others):
    z, y, x, k = me
    barrier = pltpu.get_barrier_semaphore()

    def call(i, carry):
        to = lax.rem(z * 2 + y + i, 8)
        pl.semaphore_signal(
            barrier, inc=1, device_id=(to // 2, to % 2, x, k), device_id_type=MESH
        )
        return carry

    lax.fori_loop(1, 8, call, 0)
    for target in [(z, y, 1 - x, k), *others]:
        pl.semaphore_signal(barrier, inc=1, device_id=target, device_id_type=MESH)
    pl.semaphore_wait(barrier, 8 + len(others))


def ffn_backward(
    grad_ffn, source, gu_w, down_w, for_gate, for_up, mixed, cotangent, branch, gain, attention
):
    tokens, width = grad_ffn.shape
    rows, group = tokens // 16, tokens // 4
    hidden = 2 * down_w[0].shape[0]
    part = hidden // 2
    across = (((0,), (0,)), ((), ()))
    turned = (((1,), (1,)), ((), ()))
    scaling = 1.0 / math.sqrt(HD)

    def body(*refs):
        (df_any, h_any, gu_any, d_any, d_any2, fg_any, fu_any, m_any, cot_ref, branch_ref, gain_ref) = refs[:11]
        (wout_ref, qrot_ref, keys_ref, values_ref, o_ref, lse_ref, low_ref, high_ref, log_ref) = refs[11:20]
        (full_ref, own_ref, gg_ref, in_ref, rest_ref, dq_ref, dk_ref, dv_ref) = refs[20:28]
        (df, hs, gu, dw, fg, fu, ms, dgu, terms, shard) = refs[28:38]
        (to_core, from_core, to_ctx) = refs[38:41]
        (da, dk_all, dv_all, pair_out, pair_in) = refs[41:46]
        (load_sem, local, core_send, core_recv, grad_send, grad_recv, rest_sem) = refs[46:53]
        (da_sem, pair_send, pair_recv) = refs[53:56]
        scratch = refs[56:]
        me = z, y, x, k = place()
        ctx = own_tile(me)
        order = [near_first(step, z) for step in (3, 2, 1, 0)]

        def group_load(zp):
            at = pl.ds(pl.multiple_of(zp * group, group), group)
            return [
                pltpu.make_async_copy(src.at[at, :], dst.at[at, :], load_sem.at[i, zp])
                for i, (src, dst) in enumerate(((df_any, df), (fg_any, fg), (fu_any, fu)))
            ]

        d_load = pltpu.make_async_copy(d_any, dw.at[:part, :], load_sem.at[3, 0])
        d_load2 = pltpu.make_async_copy(d_any2, dw.at[part:, :], load_sem.at[4, 0])
        gu_load = pltpu.make_async_copy(gu_any, gu, load_sem.at[3, 1])
        h_load = pltpu.make_async_copy(h_any, hs, load_sem.at[3, 2])
        m_load = pltpu.make_async_copy(m_any, ms, load_sem.at[3, 3])
        for load in (*group_load(order[0]), d_load, d_load2, gu_load):
            load.start()
        for zp in order[1:]:
            for load in group_load(zp):
                load.start()
        h_load.start()
        m_load.start()
        sibling = (z, y, x, 1 - k)
        ctx_greet(me, [sibling])
        gg_ref[...] = jnp.zeros_like(gg_ref)
        d_load.wait()
        d_load2.wait()

        def produce(zp):
            at = pl.ds(pl.multiple_of(zp * group, group), group)
            for load in group_load(zp):
                load.wait()
            dm = lax.dot_general(df[at, :], dw[...], turned, preferred_element_type=F32)
            dg = (dm * fg[at, :]).astype(BF)
            du = (dm * fu[at, :]).astype(BF)
            dgu[at, :hidden] = dg
            dgu[at, hidden:] = du
            terms[at, :] = (
                lax.dot_general(dg, gu[0], turned, preferred_element_type=F32)
                + lax.dot_general(du, gu[1], turned, preferred_element_type=F32)
            ).astype(BF)

        def finish(strip, total):
            grad = cot_ref[strip].astype(F32) + total
            own_ref[strip] = grad
            back, term = norm_back_strip(grad, branch_ref[strip], gain_ref[2:3, :])
            gg_ref[...] += term
            shard[strip] = back.astype(BF)

        def core_copy(t):
            return pltpu.make_async_remote_copy(
                src_ref=to_core.at[t],
                dst_ref=from_core.at[t],
                send_sem=core_send.at[t],
                recv_sem=core_recv.at[t],
                device_id=sibling,
                device_id_type=MESH,
            )

        parts = (*DEAL_ORDER, 0)

        def compute(n):
            t = parts[n]
            c = ctx + t - 8 * ((ctx + t) // 8)
            at = pl.ds(pl.multiple_of(c * part, part), part)
            up_like = lax.dot_general(hs[:, at], dgu[...], across, preferred_element_type=F32)
            down_like = lax.dot_general(ms[...], df[:, at], across, preferred_element_type=F32)
            for i in range(2):
                to_ctx[t, i] = up_like[:, 2 * i * part : (2 * i + 1) * part].astype(BF)
                to_core[t, i] = up_like[:, (2 * i + 1) * part : (2 * i + 2) * part].astype(BF)
            to_ctx[t, 2] = down_like[:part].astype(BF)
            to_core[t, 2] = down_like[part:].astype(BF)
            core_copy(t).start()

        trickle = Trickle()

        def send(n):
            t = parts[n]
            core_copy(t).wait_recv()
            to_ctx[t] = (to_ctx[t].astype(F32) + from_core[t].astype(F32)).astype(BF)
            if t == 0:
                pltpu.make_async_copy(to_ctx.at[0], in_ref.at[ctx], rest_sem.at[0]).start()
            elif n < EARLY:
                trickle.add(
                    [
                        copy.start
                        for copy in grad_copies(me, to_ctx.at[t], in_ref, grad_send, grad_recv, t)
                    ]
                )
            else:
                pltpu.make_async_copy(
                    to_ctx.at[t], rest_ref.at[n - EARLY], rest_sem.at[n - EARLY + 1]
                ).start()

        begun = []

        def next_part():
            n = len(begun)
            begun.append(n)
            if n < 8:
                compute(n)
            if BACK_LAG <= n < 8 + BACK_LAG:
                send(n - BACK_LAG)

        def tick():
            if begun:
                next_part()
            trickle.tick(BACK_RATE)

        def da_load(step):
            at = pl.ds(pl.multiple_of(near_first(step, z) * group, group), group)
            return pltpu.make_async_copy(full_ref.at[at, :], da.at[step % 2], da_sem.at[step % 2])

        def attend_back(step):
            at = pl.ds(pl.multiple_of(near_first(step, z) * group, group), group)
            da_load(step).wait()
            grad = lax.dot_general(
                da[step % 2], wout_ref[...], turned, preferred_element_type=F32
            ).astype(BF)
            delta = jnp.sum(grad.astype(F32) * o_ref[at, :], axis=1, keepdims=True)
            q, low, high, lse = qrot_ref[at, :], low_ref[at, :], high_ref[at, :], lse_ref[at, :]
            dq_ref[at, :] = jnp.zeros((group, HD), F32)

            def work(key_at):
                key_part = keys_ref[key_at, :]
                raw, allowed = masked_scores(q, key_part, low, high, log_ref[:, key_at])
                weights = jnp.where(allowed, jnp.exp(raw - lse), 0.0)
                dp = lax.dot_general(
                    grad, values_ref[key_at, :], turned, preferred_element_type=F32
                )
                ds = (weights * (dp - delta)).astype(BF)
                dq_ref[at, :] += jnp.dot(ds, key_part, preferred_element_type=F32) * scaling
                dk_all[key_at, :] += (
                    lax.dot_general(ds, q, across, preferred_element_type=F32) * scaling
                )
                dv_all[key_at, :] += lax.dot_general(
                    weights.astype(BF), grad, across, preferred_element_type=F32
                )

            strips(2 * tokens, work, tokens)

        def arrived(step):
            if step == 0:
                keep.wait()
                dk_all[...] = jnp.zeros_like(dk_all)
                dv_all[...] = jnp.zeros_like(dv_all)
            da_load(step).start()
            if step > 0:
                attend_back(step - 1)

        def pair(n):
            return pltpu.make_async_remote_copy(
                src_ref=pair_out.at[n],
                dst_ref=pair_in.at[n],
                send_sem=pair_send.at[n],
                recv_sem=pair_recv.at[n],
                device_id=sibling,
                device_id_type=MESH,
            )

        def after_terms():
            h_load.wait()
            m_load.wait()
            for _ in range(GRADS_FIRST):
                next_part()

        gu_load.wait()
        settle = reduce_plane(
            me,
            terms,
            rows,
            scratch[:N_REDUCE],
            TURNS_FFN_BACK[0],
            produce,
            finish,
            after_terms,
            tick,
        )
        view = gather_view(full_ref, rows)
        keep = pltpu.make_async_copy(shard, view(me[0] * 4 + me[1] * 2 + me[2]), local)
        keep.start()
        gather_plane(
            me,
            shard,
            view,
            scratch[N_REDUCE:],
            TURNS_FFN_BACK[1],
            arrived=arrived,
            tick=tick,
        )
        while len(begun) < 8 + BACK_LAG:
            next_part()
        trickle.flush()
        attend_back(3)
        pair_out[0] = dk_all[tokens:, :].astype(BF)
        pair_out[1] = dv_all[tokens:, :].astype(BF)
        pair(0).start()
        pair(1).start()
        settle()
        for n, (ref, source_ref) in enumerate(((dk_ref, dk_all), (dv_ref, dv_all))):
            pair(n).wait()
            ref[...] = source_ref[:tokens, :] + pair_in[n].astype(F32)
        for t in range(8):
            core_copy(t).wait_send()
        pltpu.make_async_copy(to_ctx.at[0], in_ref.at[ctx], rest_sem.at[0]).wait()
        for n, t in enumerate(DEAL_ORDER):
            if n < EARLY:
                grad_landed(me, in_ref, grad_send, grad_recv, t)
                for copy in grad_copies(me, to_ctx.at[t], in_ref, grad_send, grad_recv, t):
                    copy.wait_send()
            else:
                pltpu.make_async_copy(
                    to_ctx.at[t], rest_ref.at[n - EARLY], rest_sem.at[n - EARLY + 1]
                ).wait()

    shape = jax.ShapeDtypeStruct
    vmem = pltpu.VMEM
    return comm_call(
        body,
        "ffn_backward",
        4,
        (
            shape((tokens, width), BF),
            shape((rows, width), F32),
            shape((8, width), F32),
            shape((8, 3, part, part), BF),
            shape((7 - EARLY, 3, part, part), BF),
            shape((tokens, HD), F32),
            shape((tokens, HD), F32),
            shape((tokens, HD), F32),
        ),
        [*[ANY] * 8, *[VMEM] * 12],
        (ANY, VMEM, VMEM, ANY, ANY, VMEM, VMEM, VMEM),
        [
            vmem((tokens, width), BF),
            vmem((tokens, width), BF),
            vmem((2, width, hidden), BF),
            vmem((hidden, width), BF),
            vmem((tokens, hidden), F32),
            vmem((tokens, hidden), F32),
            vmem((tokens, hidden), BF),
            vmem((tokens, 2 * hidden), BF),
            vmem((tokens, width), BF),
            vmem((rows, width), BF),
            vmem((8, 3, part, part), BF),
            vmem((8, 3, part, part), BF),
            vmem((8, 3, part, part), BF),
            vmem((2, group, width), BF),
            vmem((2 * tokens, HD), F32),
            vmem((2 * tokens, HD), F32),
            vmem((2, tokens, HD), BF),
            vmem((2, tokens, HD), BF),
            DMA((5, 4)),
            DMA,
            DMA((8,)),
            DMA((8,)),
            DMA((8, 3)),
            DMA((8, 3)),
            DMA((8,)),
            DMA((2,)),
            DMA((2,)),
            DMA((2,)),
            *reduce_scratch(rows, width),
            *GATHER_SEMS,
        ],
    )(
        grad_ffn,
        source,
        gu_w,
        *down_w,
        for_gate,
        for_up,
        mixed,
        cotangent,
        branch,
        gain,
        *attention,
    )


def write_results(early, late, wall, outputs, input_grad, gains):
    part = early.shape[2]

    def body(early_ref, late_ref, wall_ref, out_ref, in_ref, gain_ref, *results):
        (out_to, in_to, gq, gk, gv, go, gg, gu, gd, *gains_to) = results
        n = pl.program_id(0)

        @pl.when(n == 0)
        def _():
            out_to[...] = out_ref[...]
            in_to[...] = in_ref[...]
            for i, ref in enumerate(gains_to):
                ref[...] = gain_ref[i : i + 1, :]

        for i, ref in enumerate((gq, gk, gv, go)):
            ref[...] = wall_ref[0, i].astype(F32)

        @pl.when(n <= EARLY)
        def _():
            for i, ref in enumerate((gg, gu, gd)):
                ref[...] = early_ref[0, i].astype(F32)

        @pl.when(n > EARLY)
        def _():
            for i, ref in enumerate((gg, gu, gd)):
                ref[...] = late_ref[0, i].astype(F32)

    shape = jax.ShapeDtypeStruct
    spec = pl.BlockSpec

    def source(n):
        ctx = lax.axis_index("z") * 2 + lax.axis_index("y")
        odd = lax.rem(n, 2)
        t = odd * (4 + n // 2) + (1 - odd) * (n // 2)
        return lax.rem(ctx + 8 - t, 8)

    rows, columns = outputs.shape
    whole = spec((rows, columns), lambda n: (0, 0))
    in_row = spec((HD, HD), lambda n: (source(n) % 2, source(n) // 2))
    in_column = spec((HD, HD), lambda n: (source(n) // 2, source(n) % 2))
    side = spec((part, part), lambda n: (0, source(n)))
    gain_spec = spec(gains.shape, lambda n: (0, 0))
    gain_row = spec((1, gains.shape[1]), lambda n: (0, 0))
    blob = (1, 3, part, part)
    return pl.pallas_call(
        body,
        name="write_results",
        grid=(8,),
        out_shape=(
            shape((rows, columns), BF),
            shape((rows, columns), BF),
            shape((2 * HD, 4 * HD), F32),
            shape((2 * HD, 4 * HD), F32),
            shape((2 * HD, 4 * HD), F32),
            shape((4 * HD, 2 * HD), F32),
            shape((part, 8 * part), F32),
            shape((part, 8 * part), F32),
            shape((8 * part, part), F32),
            *[shape((1, gains.shape[1]), F32)] * 4,
        ),
        in_specs=[
            spec(blob, lambda n: (source(jnp.minimum(n, EARLY)), 0, 0, 0)),
            spec(blob, lambda n: (source(jnp.maximum(n, EARLY + 1)), 0, 0, 0)),
            spec((1, 4, HD, HD), lambda n: (source(n), 0, 0, 0)),
            whole,
            whole,
            gain_spec,
        ],
        out_specs=(
            whole,
            whole,
            in_row,
            in_row,
            in_row,
            in_column,
            side,
            side,
            spec((part, part), lambda n: (source(n), 0)),
            *[gain_row] * 4,
        ),
        compiler_params=pltpu.CompilerParams(vmem_limit_bytes=BIG_VMEM),
    )(early, late, wall, outputs, input_grad, gains)


def close_greet(me):
    z, y, x, k = me
    barrier = pltpu.get_barrier_semaphore()

    def plane(i, carry):
        pl.semaphore_signal(barrier, inc=1, device_id=plane_peer(me, i)[1], device_id_type=MESH)
        return carry

    def others(i, carry):
        pl.semaphore_signal(
            barrier, inc=1, device_id=(i // 2, i % 2, x, 1 - k), device_id_type=MESH
        )
        return carry

    lax.fori_loop(1, 16, plane, 0)
    lax.fori_loop(0, 8, others, 0)
    pl.semaphore_signal(barrier, inc=1, device_id=(z, y, 1 - x, 1 - k), device_id_type=MESH)
    pl.semaphore_wait(barrier, 24)


def attention_backward(
    grad_attn,
    full_in,
    query,
    key,
    attended,
    grads_rotated,
    tables,
    scales,
    gains,
    qkv_w,
    grad_own,
    attn_term,
    ffn_term,
    grads_left,
):
    tokens, width = grad_attn.shape
    rows, group = tokens // 16, tokens // 4
    part = width // 4

    def body(*refs):
        (da_any, x_any) = refs[:2]
        (q_ref, k_ref, o_ref, dq_in, dk_in, dv_in, cos_ref, sin_ref) = refs[2:10]
        (scale_ref, gain_ref, wqkv_ref) = refs[10:13]
        (grad_ref, attn_ref, ffn_ref, left_ref) = refs[13:17]
        (in_grad_ref, deal_in, gains_ref, ffn_in) = refs[17:21]
        (da, xs, terms, dq_ref, dk_ref) = refs[21:26]
        (dqkv, slots, result) = refs[26:29]
        (qkv_grads, out_grads, wall_out, wall_in, deal_out) = refs[29:34]
        (gain_out, gain_in, gain_own, gain_slots) = refs[34:38]
        (load_sem, pair_send, pair_recv, tot_send, tot_recv, out_send, out_recv) = refs[38:45]
        (deal_send, deal_recv, gain_send, gain_recv, grad_send, grad_recv) = refs[45:51]
        scratch = refs[51:]
        me = z, y, x, k = place()
        ctx = own_tile(me)
        own = ctx * 2 + x
        own_head = pl.ds(pl.multiple_of((x * 8 + ctx) * HD, HD), HD)
        sibling = (z, y, x, 1 - k)

        da_load = pltpu.make_async_copy(da_any, da, load_sem.at[0])
        x_load = pltpu.make_async_copy(x_any, xs, load_sem.at[1])
        x_load.start()
        da_load.start()
        close_greet(me)

        trickle = Trickle()

        def left_copies(n):
            return grad_copies(me, left_ref.at[n - EARLY], ffn_in, grad_send, grad_recv, DEAL_ORDER[n])

        for n in range(EARLY, 7):
            trickle.add([copy.start for copy in left_copies(n)])
        trickle.tick(CLOSE_FIRST)

        def pair(n):
            return pltpu.make_async_remote_copy(
                src_ref=wall_out.at[n] if n < 8 else gain_out,
                dst_ref=wall_in.at[n] if n < 8 else gain_in,
                send_sem=pair_send.at[n],
                recv_sem=pair_recv.at[n],
                device_id=sibling,
                device_id_type=MESH,
            )

        across = (((0,), (0,)), ((), ()))
        eye = eye_mask()

        def normed_grad(values, piece):
            return values * cos_ref[piece, :] - pltpu.roll(values, HD // 2, 1) * sin_ref[piece, :]

        def side_dots(side, source, grads, proj):
            gain_sum = jnp.zeros((8, HD), F32)
            for i in range(8):
                piece = slice(i * HD, (i + 1) * HD)
                factor = row_to_column(scale_ref[side * 8 + i : side * 8 + i + 1, :], eye)
                back = normed_grad(source[piece, :], piece)
                term = back * proj[piece, :] * factor
                for j in range(0, HD, 8):
                    gain_sum = gain_sum + term[j : j + 8, :]
                weighted = back * gain_ref[side : side + 1, own_head]
                grads[piece, :] = weighted
                dot = jnp.sum(weighted * proj[piece, :], axis=1, keepdims=True)
                slots[own, side * 8 + i : side * 8 + i + 1, :] = column_to_row(dot, eye)
            return jnp.sum(gain_sum, axis=0, keepdims=True)

        query_gain = side_dots(0, dq_in, dq_ref, q_ref)
        key_gain = side_dots(1, dk_in, dk_ref, k_ref)
        sum_end = sum_begin(me, slots, tot_send, tot_recv)
        dqkv[:, 2 * HD :] = dv_in[...].astype(BF)

        attn_sum = jnp.sum(attn_ref[...], axis=0, keepdims=True)
        ffn_sum = jnp.sum(ffn_ref[...], axis=0, keepdims=True)
        head_core = z // 2
        head_at = pl.ds(pl.multiple_of(((z % 2) * 2 + y) * HD, HD), HD)
        for mine, target in ((True, gain_own), (False, gain_out)):
            target[...] = jnp.zeros_like(target)
            for xt in range(2):
                for kt in range(2):

                    @pl.when((kt == k) if mine else (kt != k))
                    def _(xt=xt, kt=kt, target=target):
                        block = slice((2 * xt + kt) * part, (2 * xt + kt + 1) * part)
                        target[xt, 2:3, :] = attn_sum[:, block]
                        target[xt, 3:4, :] = ffn_sum[:, block]

            @pl.when((head_core == k) if mine else (head_core != k))
            def _(target=target):
                target[x, 0:1, head_at] = query_gain
                target[x, 1:2, head_at] = key_gain

        pair(8).start()

        parts = (*DEAL_ORDER, 0)

        def columns_of(n):
            c = ctx + parts[n] - 8 * ((ctx + parts[n]) // 8)
            return pl.ds(pl.multiple_of(c * 2 * HD, 2 * HD), 2 * HD)

        attended_low = o_ref[...].astype(BF)
        da_load.wait()
        for n in range(8):
            out_grads[n] = lax.dot_general(
                attended_low, da[:, columns_of(n)], across, preferred_element_type=F32
            )
        total = sum_end()
        trickle.tick(CLOSE_NEXT)
        for side, grads, proj in ((0, dq_ref, q_ref), (1, dk_ref, k_ref)):
            for i in range(8):
                piece = slice(i * HD, (i + 1) * HD)
                row = scale_ref[side * 8 + i : side * 8 + i + 1, :]
                factor = row_to_column(row, eye)
                cubed = row * row * row * total[side * 8 + i : side * 8 + i + 1, :] / width
                dqkv[piece, side * HD : (side + 1) * HD] = (
                    factor * grads[piece, :] - proj[piece, :] * row_to_column(cubed, eye)
                ).astype(BF)

        def produce(zp):
            at = pl.ds(pl.multiple_of(zp * group, group), group)
            term = jnp.zeros((group, width), F32)
            for i in range(3):
                term = term + lax.dot_general(
                    dqkv[at, i * HD : (i + 1) * HD],
                    wqkv_ref[i],
                    (((1,), (1,)), ((), ())),
                    preferred_element_type=F32,
                )
            terms[at, :] = term.astype(BF)

        gain_copies = []

        def gain_copy(i):
            other, device = plane_peer(me, i)
            return pltpu.make_async_remote_copy(
                src_ref=gain_own.at[other % 2],
                dst_ref=gain_slots.at[own],
                send_sem=gain_send.at[i],
                recv_sem=gain_recv.at[own],
                device_id=device,
                device_id_type=MESH,
            )

        number = ((z % 2) * 2 + y) * 2 + k

        def deal(n):
            c = ctx + parts[n] - 8 * ((ctx + parts[n]) // 8)
            return pltpu.make_async_remote_copy(
                src_ref=deal_out.at[n],
                dst_ref=deal_in.at[number],
                send_sem=deal_send.at[n],
                recv_sem=deal_recv.at[number],
                device_id=(c // 2, c % 2, x, head_core),
                device_id_type=MESH,
            )

        stays = k == head_core

        def deal_start(n):
            if n < 7:
                deal(n).start()
                return

            @pl.when(jnp.logical_not(stays))
            def _():
                deal(n).start()

            @pl.when(stays)
            def _():
                pltpu.make_async_copy(
                    deal_out.at[n], deal_in.at[number], deal_recv.at[number]
                ).start()

        def after_terms():
            pair(8).wait_recv()
            gain_own[...] += gain_in[...]
            gain_slots[own] = gain_own[x]

            def begin(i, carry):
                gain_copy(i).start()
                return carry

            lax.fori_loop(1, 16, begin, 0)

        x_load.wait()
        begun = []

        def halves(n, r):
            rows_at = pl.ds(pl.multiple_of(r * HD, HD), HD)
            for i in range(3):
                yield i, qkv_grads[rows_at, i * HD : (i + 1) * HD]
            yield 3, out_grads[n, :, rows_at]

        def tick():
            n = len(begun)
            begun.append(n)
            if n < 8:
                qkv_grads[...] = lax.dot_general(
                    xs[:, columns_of(n)], dqkv[...], across, preferred_element_type=F32
                )
                for i, value in halves(n, 1 - k):
                    wall_out[n, i] = value.astype(BF)
                for i, value in halves(n, k):
                    deal_out[n, i] = value.astype(BF)
                pair(n).start()
            if CLOSE_LAG <= n < 8 + CLOSE_LAG:
                last = n - CLOSE_LAG
                pair(last).wait_recv()
                deal_out[last] = (deal_out[last].astype(F32) + wall_in[last].astype(F32)).astype(BF)
                deals.add([lambda: deal_start(last)])
            deals.tick()
            trickle.tick(CLOSE_RATE)

        deals = Trickle()

        def finish(strip, total):
            result[strip] = (grad_ref[strip] + total).astype(BF)

        settle = reduce_plane(
            me,
            terms,
            rows,
            scratch,
            TURNS_CLOSE,
            produce,
            finish,
            after_terms,
            tick,
        )
        while len(begun) < 8 + CLOSE_LAG:
            tick()
        deals.flush()
        trickle.flush()
        copies, own_copy = hand_out_copies(me, result, in_grad_ref, out_send, out_recv)
        for copy in copies:
            copy.start()
        own_copy.start()
        for n in range(8):
            pltpu.make_async_copy(deal_out.at[n], deal_in.at[n], deal_recv.at[n]).wait()

        def gain_landed(i, carry):
            other, device = plane_peer(me, i)
            pltpu.make_async_remote_copy(
                src_ref=gain_slots.at[other],
                dst_ref=gain_slots.at[other],
                send_sem=gain_send.at[i],
                recv_sem=gain_recv.at[other],
                device_id=device,
                device_id_type=MESH,
            ).wait_recv()
            gain_copy(i).wait_send()
            return carry

        lax.fori_loop(1, 16, gain_landed, 0)
        gain_total = gain_slots[0]
        for i in range(1, 16):
            gain_total = gain_total + gain_slots[i]
        gains_ref[...] = gain_total
        settle()
        own_copy.wait()
        for copy in copies:
            copy.wait()
        for n in range(7):
            deal(n).wait_send()

        @pl.when(jnp.logical_not(stays))
        def _():
            deal(7).wait_send()

        for n in range(9):
            pair(n).wait_send()
        for n in range(EARLY, 7):
            grad_landed(me, ffn_in, grad_send, grad_recv, DEAL_ORDER[n])
            for copy in left_copies(n):
                copy.wait_send()

    shape = jax.ShapeDtypeStruct
    vmem = pltpu.VMEM
    return comm_call(
        body,
        "attention_backward",
        5,
        (
            shape((rows * 4, part), BF),
            shape((8, 4, HD, HD), BF),
            shape((4, part), F32),
            shape((8, *grads_left.shape[1:]), BF),
        ),
        [ANY, ANY, *[VMEM] * 14, ANY],
        (ANY, ANY, VMEM, ANY),
        [
            vmem((tokens, width), BF),
            vmem((tokens, width), BF),
            vmem((tokens, width), BF),
            vmem((tokens, HD), F32),
            vmem((tokens, HD), F32),
            vmem((tokens, 3 * HD), BF),
            vmem((16, 16, HD), F32),
            vmem((rows, width), BF),
            vmem((2 * HD, 3 * HD), F32),
            vmem((8, HD, 2 * HD), F32),
            vmem((8, 4, HD, HD), BF),
            vmem((8, 4, HD, HD), BF),
            vmem((8, 4, HD, HD), BF),
            vmem((2, 4, part), F32),
            vmem((2, 4, part), F32),
            vmem((2, 4, part), F32),
            vmem((16, 4, part), F32),
            DMA((2,)),
            DMA((9,)),
            DMA((9,)),
            DMA((16,)),
            DMA((16,)),
            DMA((3,)),
            DMA((4,)),
            DMA((8,)),
            DMA((8,)),
            DMA((16,)),
            DMA((16,)),
            DMA((8, 3)),
            DMA((8, 3)),
            *reduce_scratch(rows, width),
        ],
    )(
        grad_attn,
        full_in,
        query,
        key,
        attended,
        *grads_rotated,
        *tables,
        scales,
        gains,
        qkv_w,
        grad_own,
        attn_term,
        ffn_term,
        grads_left,
    )


def plane_layer(
    inputs,
    cotangent,
    w_query,
    w_key,
    w_value,
    w_out,
    w_gate,
    w_up,
    w_down,
    query_gain,
    key_gain,
    attn_gain,
    ffn_gain,
    lengths,
    block_order,
):
    steps = np.arange(HD // 2, dtype=np.float64) * 2.0 / HD
    frequency = np.tile(np.power(ROPE_THETA, -steps), 2)[None, :].astype(np.float32)
    full_in, source_own, own_cot, qkv_w, out_w, gains_full, gu_stage, down_own, query_proj, key_proj, value_low, cosine, sine, low, high, logical_keys = open_layer(
        inputs,
        cotangent,
        w_query,
        w_key,
        w_value,
        w_out,
        w_gate,
        w_up,
        w_down,
        query_gain[None, :],
        key_gain[None, :],
        attn_gain[None, :],
        ffn_gain[None, :],
        block_order[None, :],
        lengths[None, :],
        jnp.asarray(frequency),
    )
    tables = (cosine, sine)
    (
        residual_full,
        residual_own,
        branch_own,
        gu_w,
        down_other,
        query_rot,
        keys_all,
        values_all,
        attended,
        lse,
        scales,
    ) = attention_forward(
        query_proj,
        key_proj,
        value_low,
        tables,
        (low, high),
        logical_keys,
        source_own,
        out_w,
        gains_full,
        gu_stage,
        down_own,
    )
    grad_ffn, outputs, ffn_gain_term, for_gate, for_up, mixed = ffn_forward(
        residual_full, gu_w, (down_own, down_other), residual_own, own_cot, gains_full
    )
    grad_attn, grad_own, attn_gain_term, ffn_early, ffn_left, *grads_rotated = ffn_backward(
        grad_ffn,
        residual_full,
        gu_w,
        (down_own, down_other),
        for_gate,
        for_up,
        mixed,
        own_cot,
        branch_own,
        gains_full,
        (out_w, query_rot, keys_all, values_all, attended, lse, low, high, logical_keys),
    )
    input_grad, wall_grads, gain_grads, ffn_late = attention_backward(
        grad_attn,
        full_in,
        query_proj,
        key_proj,
        attended,
        grads_rotated,
        tables,
        scales,
        gains_full,
        qkv_w,
        grad_own,
        attn_gain_term,
        ffn_gain_term,
        ffn_left,
    )
    results = write_results(ffn_early, ffn_late, wall_grads, outputs, input_grad, gain_grads)
    return (*results[:9], *[row[0] for row in results[9:]])


def full_rows(piece):
    return lax.all_gather(piece, "head", axis=1, tiled=True)


def head_sums(term):
    return lax.psum_scatter(
        term.astype(jnp.bfloat16), "head", scatter_dimension=1, tiled=True
    ).astype(jnp.float32)


def row_single(term):
    return lax.psum(term, "head")


def row_pair(first, second):
    return lax.psum((first, second), "head")


def gather_weights(w_query, w_key, w_value, w_out, w_gate, w_up, w_down):
    row_parts = (
        lax.all_gather(w_query.astype(jnp.bfloat16), "ctx", axis=0, tiled=True),
        lax.all_gather(w_key.astype(jnp.bfloat16), "ctx", axis=0, tiled=True),
        lax.all_gather(w_value.astype(jnp.bfloat16), "ctx", axis=0, tiled=True),
        lax.all_gather(w_gate.astype(jnp.bfloat16), "ctx", axis=0, tiled=True),
        lax.all_gather(w_up.astype(jnp.bfloat16), "ctx", axis=0, tiled=True),
    )
    col_parts = (
        lax.all_gather(w_out.astype(jnp.bfloat16), "ctx", axis=1, tiled=True),
        lax.all_gather(w_down.astype(jnp.bfloat16), "ctx", axis=1, tiled=True),
    )
    return tuple(row_parts) + tuple(col_parts)


def sequence_tables(logical, lengths):
    seq_ends = jnp.cumsum(lengths)
    seq_starts = seq_ends - lengths
    number = jnp.sum((logical[:, None] >= seq_ends[None, :]).astype(jnp.int32), axis=1)
    member = number[:, None] == jnp.arange(lengths.shape[0], dtype=jnp.int32)[None, :]
    offset = logical - jnp.sum(jnp.where(member, seq_starts[None, :], 0), axis=1)
    return (number, offset)


def rotate(values, offset):
    half_dim = HD // 2
    inverse = jnp.power(ROPE_THETA, -jnp.arange(half_dim, dtype=jnp.float32) * 2.0 / HD)
    angles = offset.astype(jnp.float32)[:, None] * inverse[None, :]
    cosine = jnp.cos(angles)[:, None, :]
    sine_part = jnp.sin(angles)[:, None, :]
    first_half = values[..., :half_dim]
    second_half = values[..., half_dim:]
    return jnp.concatenate(
        [
            first_half * cosine - second_half * sine_part,
            second_half * cosine + first_half * sine_part,
        ],
        axis=-1,
    )


def norm_backward(grad_in, values, factor, gain):
    gain_term = jnp.sum(grad_in * values * factor[:, None], axis=0)
    weighted = grad_in * gain
    row_dot = row_single(jnp.sum(weighted * values, axis=1))
    grad_values = (
        factor[:, None] * weighted - values * (factor * factor * factor * row_dot / D)[:, None]
    )
    return (grad_values, gain_term)


def on_device(
    inputs,
    cotangent,
    w_query,
    w_key,
    w_value,
    w_out,
    w_gate,
    w_up,
    w_down,
    query_gain,
    key_gain,
    attn_gain,
    ffn_gain,
    lengths,
    block_order,
):
    shards = lax.axis_size("ctx")
    position = lax.axis_index("ctx")
    tok_rows, width_part = inputs.shape
    block_rows = tok_rows // shards
    total_tokens = tok_rows * shards
    local_heads = width_part // HD
    scaling = 1.0 / math.sqrt(HD)
    shard_range = jnp.arange(shards, dtype=jnp.int32)
    order_table = block_order.reshape(shards, shards)
    target = order_table % shards
    choose = target[:, :, None] == shard_range[None, None, :]
    stream = jnp.sum(jnp.where(choose, order_table[:, :, None], 0), axis=1)
    stream_blocks = jnp.transpose(stream).reshape(-1)
    logical = (
        stream_blocks[:, None] * block_rows + jnp.arange(block_rows, dtype=jnp.int32)[None, :]
    ).reshape(-1)
    own_target = lax.dynamic_index_in_dim(target, position, 0, keepdims=False)
    send_order = jnp.sum(
        jnp.where(own_target[:, None] == shard_range[None, :], shard_range[:, None], 0), axis=0
    )

    def deal_out(values):
        return values.reshape(shards, block_rows, width_part)[send_order].reshape(
            tok_rows, width_part
        )

    def undeal(values):
        return values.reshape(shards, block_rows, width_part)[own_target].reshape(
            tok_rows, width_part
        )

    local_in, local_cot = (
        lax.all_to_all(deal_out(inputs), "ctx", split_axis=0, concat_axis=0, tiled=True),
        lax.all_to_all(deal_out(cotangent), "ctx", split_axis=0, concat_axis=0, tiled=True),
    )
    number_all, offset_all = sequence_tables(logical, lengths)
    number_own = lax.dynamic_slice_in_dim(number_all, position * tok_rows, tok_rows)
    offset_own = lax.dynamic_slice_in_dim(offset_all, position * tok_rows, tok_rows)
    logical_own = lax.dynamic_slice_in_dim(logical, position * tok_rows, tok_rows)
    query_full, key_full, value_full, gate_full, up_full, out_full, down_full = gather_weights(
        w_query, w_key, w_value, w_out, w_gate, w_up, w_down
    )
    full_in = full_rows(local_in)
    query_proj = jnp.dot(full_in, query_full, preferred_element_type=jnp.float32)
    key_proj = jnp.dot(full_in, key_full, preferred_element_type=jnp.float32)
    value_proj = jnp.dot(full_in, value_full, preferred_element_type=jnp.float32)
    query_sq, key_sq = row_pair(
        jnp.sum(query_proj * query_proj, axis=1), jnp.sum(key_proj * key_proj, axis=1)
    )
    query_scale = lax.rsqrt(query_sq / D + EPSILON)
    key_scale = lax.rsqrt(key_sq / D + EPSILON)
    query_rot = rotate(
        (query_proj * query_scale[:, None] * query_gain).reshape(tok_rows, local_heads, HD),
        offset_own,
    ).astype(jnp.bfloat16)
    key_rot = rotate(
        (key_proj * key_scale[:, None] * key_gain).reshape(tok_rows, local_heads, HD), offset_own
    ).astype(jnp.bfloat16)
    value_low = value_proj.astype(jnp.bfloat16).reshape(tok_rows, local_heads, HD)
    keys_all, values_all = (
        lax.all_gather(key_rot, "ctx", axis=0, tiled=True),
        lax.all_gather(value_low, "ctx", axis=0, tiled=True),
    )
    key_span = math.gcd(total_tokens, 1024)
    key_turns = total_tokens // key_span
    pieces = (
        keys_all.reshape(key_turns, key_span, local_heads, HD),
        values_all.reshape(key_turns, key_span, local_heads, HD),
        number_all.reshape(key_turns, key_span),
        logical.reshape(key_turns, key_span),
    )

    def scores_of(key_piece, number_piece, logical_piece):
        raw_scores = (
            jnp.einsum("qhd,khd->hqk", query_rot, key_piece, preferred_element_type=jnp.float32)
            * scaling
        )
        allowed = (number_own[:, None] == number_piece[None, :]) & (
            logical_piece[None, :] <= logical_own[:, None]
        )
        return (raw_scores, allowed)

    def stat_turn(running, piece_set):
        running_max, running_sum = running
        raw_scores, allowed = scores_of(piece_set[0], piece_set[2], piece_set[3])
        masked_scores = jnp.where(allowed[None], raw_scores, MASKED)
        new_max = jnp.maximum(running_max, jnp.max(masked_scores, axis=2))
        fresh = jnp.sum(
            jnp.where(allowed[None], jnp.exp(masked_scores - new_max[..., None]), 0.0), axis=2
        )
        return ((new_max, running_sum * jnp.exp(running_max - new_max) + fresh), None)

    start_max = jnp.full((local_heads, tok_rows), MASKED, jnp.float32)
    start_sum = jnp.zeros((local_heads, tok_rows), jnp.float32)
    final_max, final_sum = lax.scan(stat_turn, (start_max, start_sum), pieces)[0]
    log_total = final_max + jnp.log(final_sum)

    def out_turn(accum, piece_set):
        raw_scores, allowed = scores_of(piece_set[0], piece_set[2], piece_set[3])
        weights_low = jnp.where(
            allowed[None], jnp.exp(raw_scores - log_total[..., None]), 0.0
        ).astype(jnp.bfloat16)
        return (
            accum
            + jnp.einsum(
                "hqk,khd->qhd", weights_low, piece_set[1], preferred_element_type=jnp.float32
            ),
            None,
        )

    attended = lax.scan(out_turn, jnp.zeros((tok_rows, local_heads, HD), jnp.float32), pieces)[0]
    attended_low = attended.reshape(tok_rows, width_part).astype(jnp.bfloat16)
    attn_part = head_sums(jnp.dot(attended_low, out_full, preferred_element_type=jnp.float32))
    attn_scale = lax.rsqrt(row_single(jnp.sum(attn_part * attn_part, axis=1)) / D + EPSILON)
    residual = local_in.astype(jnp.float32) + attn_part * attn_scale[:, None] * attn_gain
    residual_full = full_rows(residual.astype(jnp.bfloat16))
    gate_proj = jnp.dot(residual_full, gate_full, preferred_element_type=jnp.float32)
    up_proj = jnp.dot(residual_full, up_full, preferred_element_type=jnp.float32)
    gate_sigmoid = jax.nn.sigmoid(gate_proj)
    mixed_hidden = (gate_proj * gate_sigmoid * up_proj).astype(jnp.bfloat16)
    ffn_part = head_sums(jnp.dot(mixed_hidden, down_full, preferred_element_type=jnp.float32))
    ffn_scale = lax.rsqrt(row_single(jnp.sum(ffn_part * ffn_part, axis=1)) / D + EPSILON)
    result = residual + ffn_part * ffn_scale[:, None] * ffn_gain
    query_full, key_full, value_full, gate_full, up_full, out_full, down_full = gather_weights(
        w_query, w_key, w_value, w_out, w_gate, w_up, w_down
    )
    grad_result = local_cot.astype(jnp.float32)
    grad_ffn, ffn_gain_term = norm_backward(grad_result, ffn_part, ffn_scale, ffn_gain)
    grad_ffn_low = full_rows(grad_ffn.astype(jnp.bfloat16))
    down_grad = jnp.einsum(
        "tf,td->fd", mixed_hidden, grad_ffn_low, preferred_element_type=jnp.float32
    )
    grad_mixed = jnp.einsum(
        "td,fd->tf", grad_ffn_low, down_full, preferred_element_type=jnp.float32
    )
    grad_gate_low = (
        grad_mixed * up_proj * gate_sigmoid * (1.0 + gate_proj * (1.0 - gate_sigmoid))
    ).astype(jnp.bfloat16)
    grad_up_low = (grad_mixed * gate_proj * gate_sigmoid).astype(jnp.bfloat16)
    gate_grad = jnp.einsum(
        "td,tf->df", residual_full, grad_gate_low, preferred_element_type=jnp.float32
    )
    up_grad = jnp.einsum(
        "td,tf->df", residual_full, grad_up_low, preferred_element_type=jnp.float32
    )
    resid_term = jnp.einsum(
        "tf,df->td", grad_gate_low, gate_full, preferred_element_type=jnp.float32
    ) + jnp.einsum("tf,df->td", grad_up_low, up_full, preferred_element_type=jnp.float32)
    grad_residual = grad_result + head_sums(resid_term)
    grad_attn, attn_gain_term = norm_backward(grad_residual, attn_part, attn_scale, attn_gain)
    grad_attn_low = full_rows(grad_attn.astype(jnp.bfloat16))
    out_grad = jnp.einsum(
        "te,td->ed", attended_low, grad_attn_low, preferred_element_type=jnp.float32
    )
    grad_heads = (
        jnp.einsum("td,ed->te", grad_attn_low, out_full, preferred_element_type=jnp.float32)
        .astype(jnp.bfloat16)
        .reshape(tok_rows, local_heads, HD)
    )
    row_delta = jnp.transpose(jnp.sum(grad_heads.astype(jnp.float32) * attended, axis=2))

    def score_grads(key_piece, value_piece, number_piece, logical_piece):
        raw_scores, allowed = scores_of(key_piece, number_piece, logical_piece)
        probabilities = jnp.where(allowed[None], jnp.exp(raw_scores - log_total[..., None]), 0.0)
        grad_probs = jnp.einsum(
            "qhd,khd->hqk", grad_heads, value_piece, preferred_element_type=jnp.float32
        )
        grad_scores = (probabilities * (grad_probs - row_delta[..., None])).astype(jnp.bfloat16)
        return (probabilities, grad_scores)

    zero_heads = jnp.zeros((tok_rows, local_heads, HD), jnp.float32)

    def back_turn(grad_acc, piece_set):
        key_piece, value_piece, number_piece, logical_piece = piece_set
        probabilities, grad_scores = score_grads(
            key_piece, value_piece, number_piece, logical_piece
        )
        grad_acc = (
            grad_acc
            + jnp.einsum("hqk,khd->qhd", grad_scores, key_piece, preferred_element_type=jnp.float32)
            * scaling
        )
        key_term = (
            jnp.einsum("hqk,qhd->khd", grad_scores, query_rot, preferred_element_type=jnp.float32)
            * scaling
        )
        value_term = jnp.einsum(
            "hqk,qhd->khd",
            probabilities.astype(jnp.bfloat16),
            grad_heads,
            preferred_element_type=jnp.float32,
        )
        return (grad_acc, (key_term, value_term))

    grad_query_rot, key_value_terms = lax.scan(back_turn, zero_heads, pieces)
    key_terms = key_value_terms[0].reshape(total_tokens, local_heads, HD)
    value_terms = key_value_terms[1].reshape(total_tokens, local_heads, HD)
    grad_key_rot, grad_value_own = (
        lax.psum_scatter(
            key_terms.astype(jnp.bfloat16), "ctx", scatter_dimension=0, tiled=True
        ).astype(jnp.float32),
        lax.psum_scatter(
            value_terms.astype(jnp.bfloat16), "ctx", scatter_dimension=0, tiled=True
        ).astype(jnp.float32),
    )
    grad_query_normed = rotate(grad_query_rot, -offset_own).reshape(tok_rows, width_part)
    grad_key_normed = rotate(grad_key_rot, -offset_own).reshape(tok_rows, width_part)
    query_gain_term = jnp.sum(grad_query_normed * query_proj * query_scale[:, None], axis=0)
    key_gain_term = jnp.sum(grad_key_normed * key_proj * key_scale[:, None], axis=0)
    weighted_query = grad_query_normed * query_gain
    weighted_key = grad_key_normed * key_gain
    query_dot, key_dot = row_pair(
        jnp.sum(weighted_query * query_proj, axis=1), jnp.sum(weighted_key * key_proj, axis=1)
    )
    grad_query_low = (
        query_scale[:, None] * weighted_query
        - query_proj * (query_scale * query_scale * query_scale * query_dot / D)[:, None]
    ).astype(jnp.bfloat16)
    grad_key_low = (
        key_scale[:, None] * weighted_key
        - key_proj * (key_scale * key_scale * key_scale * key_dot / D)[:, None]
    ).astype(jnp.bfloat16)
    grad_value_low = grad_value_own.reshape(tok_rows, width_part).astype(jnp.bfloat16)
    query_grad = jnp.einsum(
        "td,te->de", full_in, grad_query_low, preferred_element_type=jnp.float32
    )
    key_grad = jnp.einsum("td,te->de", full_in, grad_key_low, preferred_element_type=jnp.float32)
    value_grad = jnp.einsum(
        "td,te->de", full_in, grad_value_low, preferred_element_type=jnp.float32
    )
    input_term = jnp.einsum(
        "te,de->td", grad_query_low, query_full, preferred_element_type=jnp.float32
    )
    input_term = input_term + jnp.einsum(
        "te,de->td", grad_key_low, key_full, preferred_element_type=jnp.float32
    )
    input_term = input_term + jnp.einsum(
        "te,de->td", grad_value_low, value_full, preferred_element_type=jnp.float32
    )
    grad_input = grad_residual + head_sums(input_term)
    row_grads = (
        lax.psum_scatter(
            query_grad.astype(jnp.bfloat16), "ctx", scatter_dimension=0, tiled=True
        ).astype(jnp.float32),
        lax.psum_scatter(
            key_grad.astype(jnp.bfloat16), "ctx", scatter_dimension=0, tiled=True
        ).astype(jnp.float32),
        lax.psum_scatter(
            value_grad.astype(jnp.bfloat16), "ctx", scatter_dimension=0, tiled=True
        ).astype(jnp.float32),
        lax.psum_scatter(
            gate_grad.astype(jnp.bfloat16), "ctx", scatter_dimension=0, tiled=True
        ).astype(jnp.float32),
        lax.psum_scatter(
            up_grad.astype(jnp.bfloat16), "ctx", scatter_dimension=0, tiled=True
        ).astype(jnp.float32),
    )
    col_grads = (
        lax.psum_scatter(
            out_grad.astype(jnp.bfloat16), "ctx", scatter_dimension=1, tiled=True
        ).astype(jnp.float32),
        lax.psum_scatter(
            down_grad.astype(jnp.bfloat16), "ctx", scatter_dimension=1, tiled=True
        ).astype(jnp.float32),
    )
    gain_totals = lax.psum((query_gain_term, key_gain_term, attn_gain_term, ffn_gain_term), "ctx")
    back_result, back_grad = (
        lax.all_to_all(result.astype(jnp.bfloat16), "ctx", split_axis=0, concat_axis=0, tiled=True),
        lax.all_to_all(
            grad_input.astype(jnp.bfloat16), "ctx", split_axis=0, concat_axis=0, tiled=True
        ),
    )
    return (
        undeal(back_result),
        undeal(back_grad),
        row_grads[0],
        row_grads[1],
        row_grads[2],
        col_grads[0],
        row_grads[3],
        row_grads[4],
        col_grads[1],
        gain_totals[0],
        gain_totals[1],
        gain_totals[2],
        gain_totals[3],
    )


def sharded(layer, mesh, ctx, head):
    wide, tall, line = P(ctx, head), P(head, ctx), P(head)
    return jax.shard_map(
        layer,
        mesh=mesh,
        in_specs=(
            *(wide,) * 5,
            tall,
            wide,
            wide,
            tall,
            *(line,) * 4,
            P(),
            P(),
        ),
        out_specs=(*(wide,) * 5, tall, wide, wide, tall, *(line,) * 4),
        check_vma=False,
    )


def solution(mesh):
    if dict(mesh.shape) == {"ctx": 8, "head": 4}:
        split = Mesh(mesh.devices.reshape(4, 2, 2, 2), AXES)
        return sharded(plane_layer, split, CTX, ("x", "core"))
    return sharded(on_device, mesh, "ctx", "head")
```

```python
import math

import jax
import jax.numpy as jnp
import numpy as np
from jax import lax
from jax.experimental import pallas as pl
from jax.experimental.pallas import tpu as pltpu
from jax.sharding import Mesh
from jax.sharding import PartitionSpec as P

D = 2048
HD = 128


EPSILON = 1e-06
ROPE_THETA = 500000.0
MASKED = -1e30


BF = jnp.bfloat16
F32 = jnp.float32
MESH = pl.DeviceIdType.MESH
AXES = ("z", "y", "x", "core")
CTX = ("z", "y")
STRIP = 16
ANY = pl.BlockSpec(memory_space=pl.ANY)
VMEM = pl.BlockSpec(memory_space=pltpu.VMEM)
DMA = pltpu.SemaphoreType.DMA
BIG_VMEM = 60 * 1024 * 1024


def place():
    return tuple(lax.axis_index(name) for name in AXES)


def greet(targets):
    barrier = pltpu.get_barrier_semaphore()
    for target in targets:
        pl.semaphore_signal(barrier, inc=1, device_id=target, device_id_type=MESH)
    pl.semaphore_wait(barrier, len(targets))


def near_first(step, z):
    high = z // 2
    low = z + high * (3 - 2 * z)
    value = (low, 1 - low, 2, 3)[step]
    return value + high * (3 - 2 * value)


def plane_axes(me, turn):
    z, y, x, k = me
    a = x * (1 - turn) + y * turn
    b = y * (1 - turn) + x * turn

    def slot(zp, ap, bp):
        yp = bp * (1 - turn) + ap * turn
        xp = ap * (1 - turn) + bp * turn
        return zp * 4 + yp * 2 + xp

    dev_a = (z, y * (1 - turn) + (1 - y) * turn, (1 - x) * (1 - turn) + x * turn, k)
    dev_b = (z, (1 - y) * (1 - turn) + y * turn, x * (1 - turn) + (1 - x) * turn, k)
    return a, b, slot, dev_a, dev_b


EVEN = ((0, 1),) * 4
MORE_X = ((0, 1), (1, 1)) * 2
ALL_X = ((1, 1),) * 4
TURNS_OPEN = ALL_X
TURNS_ATTENTION = (MORE_X, EVEN)
TURNS_FFN_BACK = (EVEN, EVEN)
TURNS_CLOSE = ALL_X


def layer_axes(me, turns):
    return [plane_axes(me, t0 + me[3] * (t1 - t0)) for t0, t1 in turns]


def greet_plane(me, others=()):
    z, y, x, k = me
    barrier = pltpu.get_barrier_semaphore()
    targets = [(z, 1 - y, x, k), (z, y, 1 - x, k), *others]
    for target in targets:
        pl.semaphore_signal(barrier, inc=1, device_id=target, device_id_type=MESH)

    @pl.when(z < 3)
    def _():
        pl.semaphore_signal(barrier, inc=1, device_id=(z + 1, y, x, k), device_id_type=MESH)

    @pl.when(z > 0)
    def _():
        pl.semaphore_signal(barrier, inc=1, device_id=(z - 1, y, x, k), device_id_type=MESH)

    inner = (z + 2) // 3 - z // 3
    pl.semaphore_wait(barrier, len(targets) + 1 + inner)


GATHER_SEMS = [DMA((16,)), DMA((4,)), DMA((4,)), DMA((4,)), DMA((8,))]


DEAL_ORDER = (4, 1, 5, 2, 6, 3, 7)
OPEN_DEAL = 0
OPEN_RATE = 2
DEALT_FIRST = 5
FORWARD_RATE = 1
BACK_RATE = 1
CLOSE_FIRST = 0
CLOSE_NEXT = 4
SUM_LAG = 1
EARLY_LAYERS = True
BACK_LAG = 1
CLOSE_LAG = 2
CLOSE_RATE = 1


class Trickle:
    def __init__(self):
        self.waiting = []

    def add(self, copies):
        self.waiting.extend(copies)

    def tick(self, count=1):
        for start in self.waiting[:count]:
            start()
        self.waiting = self.waiting[count:]

    def flush(self):
        self.tick(len(self.waiting))


def gather_plane(
    me,
    own_ref,
    view,
    sems,
    turns,
    between=lambda step: None,
    arrived=None,
    tick=lambda: None,
    early=False,
):
    z, y, x, k = me
    recv, up_send, down_send, a_send, b_send = sems
    axes = layer_axes(me, turns)

    def copy(src, index, send_sem, device):
        return pltpu.make_async_remote_copy(
            src_ref=src,
            dst_ref=view(index),
            send_sem=send_sem,
            recv_sem=recv.at[index],
            device_id=device,
            device_id_type=MESH,
        )

    def landed(index):
        copy(view(index), index, a_send.at[0], axes[0][3]).wait_recv()

    def layer_landed(step):
        tick()
        a, b, slot, dev_a, dev_b = axes[step]
        zp = near_first(step, z)
        landed(slot(zp, a, 1 - b))
        landed(slot(zp, 1 - a, 1 - b))
        if arrived is not None:
            arrived(step)

    for step in range(5):
        if step < 4:
            a, b, slot, dev_a, dev_b = axes[step]
            zp = near_first(step, z)
            index = slot(zp, a, b)
            if step == 0:
                src = own_ref
            else:
                landed(index)
                src = view(index)

            @pl.when((zp <= z) & (z < 3))
            def _():
                copy(src, index, up_send.at[zp], (z + 1, y, x, k)).start()

            @pl.when((zp >= z) & (z > 0))
            def _():
                copy(src, index, down_send.at[zp], (z - 1, y, x, k)).start()

            copy(src, index, a_send.at[step], dev_a).start()
            copy(src, index, b_send.at[step], dev_b).start()
            tick()
        if step > 0:
            a, b, slot, dev_a, dev_b = axes[step - 1]
            index = slot(near_first(step - 1, z), 1 - a, b)
            landed(index)
            copy(view(index), index, b_send.at[3 + step], dev_b).start()
            tick()
        between(step)
        if step >= 2 and early:
            layer_landed(step - 2)
    for step in ((3,) if early else range(4)):
        layer_landed(step)
    for step in range(4):
        a, b, slot, dev_a, dev_b = axes[step]
        zp = near_first(step, z)
        for ap, number in ((a, step), (1 - a, 4 + step)):
            index = slot(zp, ap, b)
            copy(view(index), index, b_send.at[number], dev_b).wait_send()
        index = slot(zp, a, b)
        copy(view(index), index, a_send.at[step], dev_a).wait_send()

        @pl.when((zp <= z) & (z < 3))
        def _():
            copy(view(index), index, up_send.at[zp], (z + 1, y, x, k)).wait_send()

        @pl.when((zp >= z) & (z > 0))
        def _():
            copy(view(index), index, down_send.at[zp], (z - 1, y, x, k)).wait_send()


def reduce_scratch(rows, width):
    return [
        pltpu.VMEM((4, 2, rows, width), BF),
        pltpu.VMEM((4, rows, width), BF),
        pltpu.VMEM((4, rows, width), BF),
        pltpu.VMEM((4, rows, width), BF),
        pltpu.VMEM((4, rows, width), BF),
        pltpu.VMEM((4, rows, width), BF),
        DMA((8,)),
        DMA((8,)),
        DMA((4,)),
        DMA((4,)),
        DMA((4,)),
        DMA((4,)),
        DMA((4,)),
    ]


N_REDUCE = 13


def strips(rows, work, strip=STRIP):
    def body(i, carry):
        work(pl.ds(pl.multiple_of(i * strip, strip), strip))
        return carry

    lax.fori_loop(0, rows // strip, body, 0)


def reduce_plane(
    me,
    terms,
    rows,
    scratch,
    turns,
    produce,
    finish,
    after_terms=lambda: None,
    tick=lambda: None,
):
    z, y, x, k = me
    (from_b, to_a, from_a, to_z, from_low, from_high) = scratch[:6]
    (b_send, b_recv, a_send, a_recv, z_send, low_recv, high_recv) = scratch[6:]
    axes = layer_axes(me, turns)[::-1]
    order = [near_first(step, z) for step in (3, 2, 1, 0)]

    def start_of(step, ap, bp):
        return pl.multiple_of(axes[step][2](order[step], ap, bp) * rows, rows)

    def copy_b(step, flip):
        a, b, slot, dev_a, dev_b = axes[step]
        zp, ap = order[step], (1 - a if flip else a)
        return pltpu.make_async_remote_copy(
            src_ref=terms.at[pl.ds(start_of(step, ap, 1 - b), rows), :],
            dst_ref=from_b.at[zp, ap],
            send_sem=b_send.at[zp * 2 + ap],
            recv_sem=b_recv.at[zp * 2 + ap],
            device_id=dev_b,
            device_id_type=MESH,
        )

    def copy_a(step):
        zp, dev_a = order[step], axes[step][3]
        return pltpu.make_async_remote_copy(
            src_ref=to_a.at[zp],
            dst_ref=from_a.at[zp],
            send_sem=a_send.at[zp],
            recv_sem=a_recv.at[zp],
            device_id=dev_a,
            device_id_type=MESH,
        )

    def copy_z(zp, target, recv, to):
        return pltpu.make_async_remote_copy(
            src_ref=to_z.at[zp],
            dst_ref=target.at[zp],
            send_sem=z_send.at[zp],
            recv_sem=recv.at[zp],
            device_id=(to, y, x, k),
            device_id_type=MESH,
        )

    def copy_up(zp):
        return copy_z(zp, from_low, low_recv, z + 1)

    def copy_down(zp):
        return copy_z(zp, from_high, high_recv, z - 1)

    def mine(step, flip, strip):
        a, b = axes[step][:2]
        at = start_of(step, 1 - a if flip else a, b) + strip.start
        return terms[pl.ds(pl.multiple_of(at, STRIP), STRIP), :].astype(F32)

    for step in range(4):
        produce(order[step])
        for flip in (True, False):
            copy_b(step, flip).start()
        tick()
    after_terms()

    for step in range(4 + SUM_LAG):
        if step < 4:
            copy_b(step, True).wait_recv()

            def first(strip, step=step):
                zp, ap = order[step], 1 - axes[step][0]
                to_a[zp, strip] = (
                    mine(step, True, strip) + from_b[zp, ap, strip].astype(F32)
                ).astype(BF)

            strips(rows, first)
            copy_a(step).start()
            tick()
        if step >= SUM_LAG:
            done = step - SUM_LAG
            tick()
            copy_b(done, False).wait_recv()
            copy_a(done).wait_recv()

            def own_sum(strip, last=done):
                zp, ap = order[last], axes[last][0]
                return (
                    mine(last, False, strip)
                    + from_b[zp, ap, strip].astype(F32)
                    + from_a[zp, strip].astype(F32)
                )

            if done < 3:
                zp = order[done]
                upward = zp > z

                @pl.when(upward & (z > 0))
                def _(zp=zp, own_sum=own_sum):
                    copy_up(zp).wait_recv()

                    def work(strip):
                        to_z[zp, strip] = (own_sum(strip) + from_low[zp, strip].astype(F32)).astype(BF)

                    strips(rows, work)

                @pl.when(jnp.logical_not(upward) & (z < 3))
                def _(zp=zp, own_sum=own_sum):
                    copy_down(zp).wait_recv()

                    def work(strip):
                        to_z[zp, strip] = (own_sum(strip) + from_high[zp, strip].astype(F32)).astype(BF)

                    strips(rows, work)

                @pl.when((z == 0) | (z == 3))
                def _(zp=zp, own_sum=own_sum):
                    def work(strip):
                        to_z[zp, strip] = own_sum(strip).astype(BF)

                    strips(rows, work)

                @pl.when(upward)
                def _(zp=zp):
                    copy_up(zp).start()

                @pl.when(jnp.logical_not(upward))
                def _(zp=zp):
                    copy_down(zp).start()

            else:

                @pl.when(z == 0)
                def _():
                    copy_down(z).wait_recv()
                    strips(rows, lambda s: finish(s, own_sum(s) + from_high[z, s].astype(F32)))

                @pl.when(z == 3)
                def _():
                    copy_up(z).wait_recv()
                    strips(rows, lambda s: finish(s, own_sum(s) + from_low[z, s].astype(F32)))

                @pl.when((z > 0) & (z < 3))
                def _():
                    copy_up(z).wait_recv()
                    copy_down(z).wait_recv()
                    strips(
                        rows,
                        lambda s: finish(
                            s,
                            own_sum(s) + from_low[z, s].astype(F32) + from_high[z, s].astype(F32),
                        ),
                    )

    def settle():
        for step in range(4):
            copy_b(step, True).wait_send()
            copy_b(step, False).wait_send()
            copy_a(step).wait_send()
        for zp in order[:3]:
            copy_up(zp).wait_send()

    return settle


def own_tile(me):
    z, y, x, k = me
    return z * 2 + y


def gather_view(out_ref, rows):
    def view(slot):
        return out_ref.at[pl.ds(pl.multiple_of(slot * rows, rows), rows), :]

    return view


def hand_out_copies(me, own_ref, out_ref, send, recv):
    z, y, x, k = me
    rows, width = own_ref.shape
    part = width // 4
    target_rows = pl.ds(pl.multiple_of(k * 2 * rows + x * rows, rows), rows)

    def copy(xt, kt, number):
        return pltpu.make_async_remote_copy(
            src_ref=own_ref.at[:, pl.ds(pl.multiple_of((2 * xt + kt) * part, part), part)],
            dst_ref=out_ref.at[target_rows, :],
            send_sem=send.at[number],
            recv_sem=recv.at[number],
            device_id=(z, y, xt, kt),
            device_id_type=MESH,
        )

    local = pltpu.make_async_copy(
        own_ref.at[:, pl.ds(pl.multiple_of((2 * x + k) * part, part), part)],
        out_ref.at[target_rows, :],
        recv.at[3],
    )
    return [copy(x, 1 - k, 0), copy(1 - x, k, 1), copy(1 - x, 1 - k, 2)], local


def pair_devices(me):
    z, y, x, k = me
    return [(z, y, x, 1 - k), (z, y, 1 - x, 1 - k)]


def row_scale(values):
    return lax.rsqrt(jnp.sum(values * values, axis=1, keepdims=True) / values.shape[1] + EPSILON)


def norm_back_strip(grad, values, gain):
    scale = row_scale(values)
    term = grad * values * scale
    weighted = grad * gain
    dot = jnp.sum(weighted * values, axis=1, keepdims=True)
    back = scale * weighted - values * (scale * scale * scale * dot / values.shape[1])
    return back, term[:8] + term[8:]


def comm_call(body, name, number, out_shape, in_specs, out_specs, scratch, lift=True):
    lifted = [i for i, spec in enumerate(in_specs) if spec is VMEM] if lift else []

    def with_loads(*refs):
        refs = list(refs)
        sems = refs.pop() if lifted else None
        held = refs[len(refs) - len(lifted) :]
        refs = refs[: len(refs) - len(lifted)]
        copies = []
        for n, i in enumerate(lifted):
            copies.append(pltpu.make_async_copy(refs[i], held[n], sems.at[n]))
            refs[i] = held[n]
        for copy in copies:
            copy.start()

        def loaded():
            for copy in copies:
                copy.wait()

        body(*refs, loaded=loaded)

    def call(*args):
        extra = [pltpu.VMEM(args[i].shape, args[i].dtype) for i in lifted]
        return pl.pallas_call(
            with_loads,
            name=name,
            out_shape=out_shape,
            in_specs=[ANY if i in lifted else spec for i, spec in enumerate(in_specs)],
            out_specs=out_specs,
            scratch_shapes=[*scratch, *extra, *([DMA((len(lifted),))] if lifted else [])],
            compiler_params=pltpu.CompilerParams(
                collective_id=number, has_side_effects=True, vmem_limit_bytes=BIG_VMEM
            ),
        )(*args)

    return call


def same_x_greet(me):
    z, y, x, k = me
    barrier = pltpu.get_barrier_semaphore()
    number = z * 4 + y * 2 + k

    def body(i, carry):
        other = lax.rem(number + i, 16)
        pl.semaphore_signal(
            barrier,
            inc=1,
            device_id=(other // 4, (other // 2) % 2, x, other % 2),
            device_id_type=MESH,
        )
        return carry

    lax.fori_loop(1, 16, body, 0)
    for kt in (k, 1 - k):
        pl.semaphore_signal(barrier, inc=1, device_id=(z, y, 1 - x, kt), device_id_type=MESH)
    pl.semaphore_wait(barrier, 17)


def masked_scores(q, keys, low, high, logical):
    raw = lax.dot_general(q, keys, (((1,), (1,)), ((), ())), preferred_element_type=F32)
    allowed = (logical >= low) & (logical <= high)
    return raw * (1.0 / math.sqrt(HD)), allowed


def eye_mask():
    return lax.broadcasted_iota(jnp.int32, (HD, HD), 0) == lax.broadcasted_iota(
        jnp.int32, (HD, HD), 1
    )


def column_to_row(column, eye):
    return jnp.sum(jnp.where(eye, column, 0.0), axis=0, keepdims=True)


def row_to_column(row, eye):
    return jnp.sum(jnp.where(eye, row, 0.0), axis=1, keepdims=True)


def open_layer(
    inputs,
    cotangent,
    w_query,
    w_key,
    w_value,
    w_out,
    w_gate,
    w_up,
    w_down,
    query_gain,
    key_gain,
    attn_gain,
    ffn_gain,
    order,
    lengths,
    frequency,
):
    rows, part = inputs.shape
    half = rows // 2
    quarter = half // 2
    tokens, width = 8 * half, 4 * part
    hidden = w_gate.shape[1]
    down = hidden // 8

    def body(*refs, loaded):
        (in_ref, cot_ref, wq_ref, wk_ref, wv_ref, wo_ref, wg_ref, wu_ref, wd_ref) = refs[:9]
        gain_parts = refs[9:13]
        (order_ref, lengths_ref, frequency_ref) = refs[13:16]
        (cos_ref, sin_ref, low_ref, high_ref, log_ref) = refs[27:32]
        gain_ref = refs[-1]
        refs = refs[:10] + refs[16:27] + refs[32:-1]
        (full_out, own_out, own_cot_ref, wqkv_ref, wout_ref, gains_ref, gu_out, down_ref) = refs[10:18]
        (q_ref, k_ref, v_ref) = refs[18:21]
        (full_ref, shard, cot_half, qkv_raw, out_raw, gu_raw, d_raw) = refs[21:28]
        (qkv_stage, out_stage, gu_stage, d_stage) = refs[28:32]
        (load_sem, pair_send, pair_recv, local_sem, deal_send, deal_recv) = refs[32:38]
        (share_send, share_recv, gain_send, gain_recv, cot_sems, keep_sem) = refs[38:44]
        (down_send, down_recv) = refs[44:46]
        gather_sems = refs[46:]
        me = z, y, x, k = place()
        ctx = own_tile(me)
        sibling = (z, y, x, 1 - k)

        loads = [
            pltpu.make_async_copy(src, dst, load_sem.at[i])
            for i, (src, dst) in enumerate(
                [
                    (wq_ref, qkv_raw.at[0]),
                    (wk_ref, qkv_raw.at[1]),
                    (wv_ref, qkv_raw.at[2]),
                    (wo_ref, out_raw),
                    (wg_ref, gu_raw.at[0]),
                    (wu_ref, gu_raw.at[1]),
                    (wd_ref, d_raw),
                ]
            )
        ]
        for load in loads:
            load.start()
        same_x_greet(me)
        loaded()

        def pair_copy(src, dst, number):
            columns = pl.ds(pl.multiple_of(k * part, part), part)
            remote = pltpu.make_async_remote_copy(
                src_ref=src.at[pl.ds(pl.multiple_of((1 - k) * half, half), half), :],
                dst_ref=dst.at[:, columns],
                send_sem=pair_send.at[number],
                recv_sem=pair_recv.at[number],
                device_id=sibling,
                device_id_type=MESH,
            )
            local = pltpu.make_async_copy(
                src.at[pl.ds(pl.multiple_of(k * half, half), half), :],
                dst.at[:, columns],
                local_sem.at[number],
            )
            remote.start()
            local.start()
            return remote, local

        first = pair_copy(in_ref, shard, 0)
        second = pair_copy(cot_ref, cot_half, 1)

        for i, gain_part in enumerate(gain_parts):
            gain_ref[i : i + 1, :] = gain_part[...]

        def gain_copy(xt, kt, number):
            return pltpu.make_async_remote_copy(
                src_ref=gain_ref,
                dst_ref=gains_ref.at[:, pl.ds(pl.multiple_of((2 * x + k) * part, part), part)],
                send_sem=gain_send.at[number],
                recv_sem=gain_recv.at[number],
                device_id=(z, y, xt, kt),
                device_id_type=MESH,
            )

        gain_copies = [gain_copy(x, 1 - k, 0), gain_copy(1 - x, k, 1), gain_copy(1 - x, 1 - k, 2)]
        for copy in gain_copies:
            copy.start()
        gain_local = pltpu.make_async_copy(
            gain_ref,
            gains_ref.at[:, pl.ds(pl.multiple_of((2 * x + k) * part, part), part)],
            local_sem.at[2],
        )
        gain_local.start()

        first[0].wait_recv()
        first[1].wait()

        def view(slot):
            return full_ref.at[
                pl.ds(pl.multiple_of((slot // 2) * half, half), half),
                pl.ds(pl.multiple_of((slot % 2) * 2 * part, 2 * part), 2 * part),
            ]

        own_slot = ctx * 2 + x
        own_local = pltpu.make_async_copy(shard, view(own_slot), local_sem.at[3])
        own_local.start()

        def deal(e):
            j, r = e // 2, e % 2
            return [
                pltpu.make_async_remote_copy(
                    src_ref=src,
                    dst_ref=dst,
                    send_sem=deal_send.at[i, e],
                    recv_sem=deal_recv.at[i, ctx],
                    device_id=(2 * k + e // 4, (e // 2) % 2, x, r),
                    device_id_type=MESH,
                )
                for i, (src, dst) in enumerate(deal_ends(j, r))
            ]

        def deal_ends(j, r):
            at = pl.ds(pl.multiple_of(ctx * 2 * HD + r * HD, HD), HD)
            return (
                (
                    qkv_stage.at[:, r * HD : (r + 1) * HD, j * HD : (j + 1) * HD],
                    wqkv_ref.at[:, at, :],
                ),
                (
                    out_stage.at[j * HD : (j + 1) * HD, r * HD : (r + 1) * HD],
                    wout_ref.at[:, at],
                ),
            )

        trickle = Trickle()
        stays = k == z // 2
        own_e = (z % 2) * 4 + y * 2 + k

        def deal_all():
            for load in loads[:4]:
                load.wait()

            def round_qkv(s):
                for i in range(3):
                    qkv_stage[i, s] = qkv_raw[i, s].astype(BF)

            strips(rows, round_qkv)

            def round_out(s):
                out_stage[s] = out_raw[s].astype(BF)

            strips(2 * rows, round_out, 32)
            if OPEN_DEAL == 0:
                begin_deal()

        def begin_deal():
            trickle.add([lambda e=e: deal_start(e) for e in range(8)])

        def deal_start(e):
            @pl.when(jnp.logical_not(stays & (own_e == e)))
            def _():
                for copy in deal(e):
                    copy.start()

            @pl.when(stays & (own_e == e))
            def _():
                for i, (src, dst) in enumerate(deal_ends(e // 2, e % 2)):
                    pltpu.make_async_copy(src, dst, deal_recv.at[i, ctx]).start()

        def cot_begin():
            second[0].wait_recv()
            second[1].wait()
            cot_remote.start()
            cot_local.start()

        wide = pl.ds(pl.multiple_of(x * 2 * part, 2 * part), 2 * part)
        cot_remote = pltpu.make_async_remote_copy(
            src_ref=cot_half.at[pl.ds(pl.multiple_of((1 - x) * quarter, quarter), quarter), :],
            dst_ref=own_cot_ref.at[:, wide],
            send_sem=cot_sems.at[0],
            recv_sem=cot_sems.at[1],
            device_id=(z, y, 1 - x, k),
            device_id_type=MESH,
        )
        cot_local = pltpu.make_async_copy(
            cot_half.at[pl.ds(pl.multiple_of(x * quarter, quarter), quarter), :],
            own_cot_ref.at[:, wide],
            cot_sems.at[2],
        )

        keeps = [
            pltpu.make_async_copy(gu_stage.at[0], gu_out.at[0], keep_sem.at[0]),
            pltpu.make_async_copy(gu_stage.at[1], gu_out.at[1], keep_sem.at[1]),
            pltpu.make_async_copy(
                d_stage.at[pl.ds(pl.multiple_of(ctx * down, down), down), :],
                down_ref.at[:, pl.ds(pl.multiple_of(ctx * rows, rows), rows)],
                keep_sem.at[2],
            ),
        ]

        def down_copy(t):
            to = ctx + t - 8 * ((ctx + t) // 8)
            return pltpu.make_async_remote_copy(
                src_ref=d_stage.at[pl.ds(pl.multiple_of(to * down, down), down), :],
                dst_ref=down_ref.at[:, pl.ds(pl.multiple_of(ctx * rows, rows), rows)],
                send_sem=down_send.at[t],
                recv_sem=down_recv.at[t],
                device_id=(to // 2, to % 2, x, k),
                device_id_type=MESH,
            )

        def down_landed(t):
            c = ctx + 8 - t - 8 * ((ctx + 8 - t) // 8)
            part_of = down_ref.at[:, pl.ds(pl.multiple_of(c * rows, rows), rows)]
            pltpu.make_async_remote_copy(
                src_ref=part_of,
                dst_ref=part_of,
                send_sem=down_send.at[t],
                recv_sem=down_recv.at[t],
                device_id=sibling,
                device_id_type=MESH,
            ).wait_recv()

        def deal_down():
            trickle.add([lambda t=t: down_copy(t).start() for t in DEAL_ORDER])

        def round_up(i):
            loads[4 + i].wait()

            def work(s):
                gu_stage[i, s] = gu_raw[i, s].astype(BF)

            strips(rows, work)
            keeps[i].start()

        def round_down():
            loads[6].wait()

            def work(s):
                d_stage[s] = d_raw[s].astype(BF)

            strips(hidden, work, 128)
            keeps[2].start()

        def positions():
            blocks = order_ref.shape[1]
            square = lax.broadcasted_iota(jnp.int32, (blocks, blocks), 0)
            square = square == lax.broadcasted_iota(jnp.int32, (blocks, blocks), 1)
            column = row_to_column(order_ref[...].astype(F32), square)
            lane = lax.broadcasted_iota(jnp.int32, (1, 2 * tokens), 1)
            other = (lane >= tokens).astype(jnp.int32)
            core = k + other - 2 * k * other
            lane = lane - tokens * other
            in_half = lane & (half - 1)
            block_rows = 2 * tokens // blocks
            block = (lane - in_half) // half * (2 * half // block_rows)
            block = block + core * (half // block_rows)
            block = block + (in_half - (in_half & (block_rows - 1))) // block_rows
            match = lax.broadcasted_iota(jnp.int32, (blocks, 2 * tokens), 0) == block
            first_of = jnp.sum(jnp.where(match, column, 0.0), axis=0, keepdims=True) * block_rows
            logical = first_of + (in_half & (block_rows - 1)).astype(F32)
            log_ref[...] = logical
            own = logical[:, :tokens]
            begin = jnp.zeros_like(own)
            end = jnp.zeros((1, 1), F32)
            for j in range(lengths_ref.shape[1]):
                length = lengths_ref[:, j : j + 1].astype(F32)
                end = end + length
                begin = begin + jnp.where(own >= end, length, 0.0)
            eye = eye_mask()
            for i in range(tokens // HD):
                piece = slice(i * HD, (i + 1) * HD)
                low = row_to_column(begin[:, piece], eye)
                high = row_to_column(own[:, piece], eye)
                low_ref[piece, :] = low
                high_ref[piece, :] = high
                angles = (high - low) * frequency_ref[...]
                cos_ref[piece, :] = jnp.cos(angles)
                sine = jnp.sin(angles)
                left = lax.broadcasted_iota(jnp.int32, (HD, HD), 1) < HD // 2
                sin_ref[piece, :] = jnp.where(left, -sine, sine)

        between = [
            deal_all,
            lambda: (cot_begin(), round_down()),
            lambda: (round_up(0), round_up(1)),
            positions,
            lambda: None,
        ]

        def open_between(step):
            if 0 < step == OPEN_DEAL:
                begin_deal()
            if step == max(OPEN_DEAL, 1):
                if step == 1:
                    between[1]()
                deal_down()
                if step == 1:
                    return
            between[step]()

        def deal_wait(c):
            at = slice(c * 2 * HD, c * 2 * HD + HD)
            pltpu.make_async_copy(
                qkv_stage.at[:, :HD, :HD], wqkv_ref.at[:, at, :], deal_recv.at[0, c]
            ).wait()
            pltpu.make_async_copy(
                out_stage.at[:HD, :HD], wout_ref.at[:, at], deal_recv.at[1, c]
            ).wait()

        def share(c, r):
            at = pl.ds(pl.multiple_of(c * 2 * HD + r * HD, HD), HD)
            return [
                pltpu.make_async_remote_copy(
                    src_ref=ref,
                    dst_ref=ref,
                    send_sem=share_send.at[i, c],
                    recv_sem=share_recv.at[i, c],
                    device_id=sibling,
                    device_id_type=MESH,
                )
                for i, ref in enumerate((wqkv_ref.at[:, at, :], wout_ref.at[:, at]))
            ]

        def project_layer(step):
            if step == 0:
                trickle.flush()
                own_local.wait()
                for c in range(8):
                    deal_wait(c)
                    for copy in share(c, k):
                        copy.start()
                for c in range(8):
                    for copy in share(c, 1 - k):
                        copy.wait_recv()
            at = pl.ds(pl.multiple_of(near_first(step, z) * 2 * half, 2 * half), 2 * half)
            tile = full_ref[at, :]
            q_ref[at, :] = jnp.dot(tile, wqkv_ref[0], preferred_element_type=F32)
            k_ref[at, :] = jnp.dot(tile, wqkv_ref[1], preferred_element_type=F32)
            v_ref[at, :] = jnp.dot(tile, wqkv_ref[2], preferred_element_type=F32).astype(BF)

        gather_plane(
            me,
            shard,
            view,
            gather_sems,
            TURNS_OPEN,
            open_between,
            project_layer,
            lambda: trickle.tick(OPEN_RATE),
        )

        full_keep = pltpu.make_async_copy(full_ref, full_out, keep_sem.at[3])
        full_keep.start()
        own_rows = pl.ds(pl.multiple_of(own_slot * quarter, quarter), quarter)
        own_keep = pltpu.make_async_copy(full_ref.at[own_rows, :], own_out, keep_sem.at[4])
        own_keep.start()
        for e in range(8):

            @pl.when(jnp.logical_not(stays & (own_e == e)))
            def _(e=e):
                for copy in deal(e):
                    copy.wait_send()

        for c in range(8):
            for copy in share(c, k):
                copy.wait_send()
        first[0].wait_send()
        second[0].wait_send()
        for copy in gain_copies:
            copy.wait()
        gain_local.wait()
        cot_remote.wait()
        cot_local.wait()
        for keep in (*keeps, full_keep, own_keep):
            keep.wait()
        for t in range(1, 8):
            down_landed(t)
            down_copy(t).wait_send()

    shape = jax.ShapeDtypeStruct
    return comm_call(
        body,
        "open_layer",
        0,
        (
            shape((tokens, width), BF),
            shape((quarter, width), BF),
            shape((quarter, width), BF),
            shape((3, width, HD), BF),
            shape((HD, width), BF),
            shape((4, width), F32),
            shape((2, rows, hidden), BF),
            shape((down, width), BF),
            shape((tokens, HD), F32),
            shape((tokens, HD), F32),
            shape((tokens, HD), BF),
            shape((tokens, HD), F32),
            shape((tokens, HD), F32),
            shape((tokens, 1), F32),
            shape((tokens, 1), F32),
            shape((1, 2 * tokens), F32),
        ),
        [*[ANY] * 9, *[VMEM] * 7],
        (ANY, ANY, ANY, VMEM, VMEM, ANY, ANY, ANY, VMEM, VMEM, VMEM, *[VMEM] * 5),
        [
            pltpu.VMEM((tokens, width), BF),
            pltpu.VMEM((half, 2 * part), BF),
            pltpu.VMEM((half, 2 * part), BF),
            pltpu.VMEM((3, rows, part), F32),
            pltpu.VMEM((part, rows), F32),
            pltpu.VMEM((2, rows, hidden), F32),
            pltpu.VMEM((hidden, rows), F32),
            pltpu.VMEM((3, rows, part), BF),
            pltpu.VMEM((part, rows), BF),
            pltpu.VMEM((2, rows, hidden), BF),
            pltpu.VMEM((hidden, rows), BF),
            DMA((7,)),
            DMA((2,)),
            DMA((2,)),
            DMA((4,)),
            DMA((2, 8)),
            DMA((2, 8)),
            DMA((2, 8)),
            DMA((2, 8)),
            DMA((3,)),
            DMA((3,)),
            DMA((3,)),
            DMA((5,)),
            DMA((8,)),
            DMA((8,)),
            *GATHER_SEMS,
            pltpu.VMEM((4, part), F32),
        ],
        lift=False,
    )(
        inputs,
        cotangent,
        w_query,
        w_key,
        w_value,
        w_out,
        w_gate,
        w_up,
        w_down,
        query_gain,
        key_gain,
        attn_gain,
        ffn_gain,
        order,
        lengths,
        frequency,
    )


def plane_peer(me, i):
    z, y, x, k = me
    other = lax.rem(z * 4 + y * 2 + x + i, 16)
    return other, (other // 4, (other // 2) % 2, other % 2, k)


def plane_greet_all(me, others):
    barrier = pltpu.get_barrier_semaphore()

    def call(i, carry):
        pl.semaphore_signal(barrier, inc=1, device_id=plane_peer(me, i)[1], device_id_type=MESH)
        return carry

    lax.fori_loop(1, 16, call, 0)
    for other in others:
        pl.semaphore_signal(barrier, inc=1, device_id=other, device_id_type=MESH)
    pl.semaphore_wait(barrier, 15 + len(others))


def sum_begin(me, slots, send, recv):
    own = me[0] * 4 + me[1] * 2 + me[2]

    def copy(i, slot):
        return pltpu.make_async_remote_copy(
            src_ref=slots.at[slot],
            dst_ref=slots.at[slot],
            send_sem=send.at[i],
            recv_sem=recv.at[slot],
            device_id=plane_peer(me, i)[1],
            device_id_type=MESH,
        )

    def begin(i, carry):
        copy(i, own).start()
        return carry

    def landed(i, carry):
        copy(i, plane_peer(me, i)[0]).wait_recv()
        return carry

    def sent(i, carry):
        copy(i, own).wait_send()
        return carry

    lax.fori_loop(1, 16, begin, 0)

    def end():
        lax.fori_loop(1, 16, landed, 0)
        lax.fori_loop(1, 16, sent, 0)
        total = slots[0]
        for i in range(1, 16):
            total = total + slots[i]
        return total

    return end


def attention_forward(
    query, key, value, tables, bounds, logical, source, out_weight, gains, gu_stage, down_own
):
    tokens, width = query.shape[0], source.shape[1]
    rows = tokens // 16
    group = tokens // 4
    hidden = gu_stage.shape[2] // 8
    part = width // 8

    def body(*refs, loaded):
        (q_in, k_in, v_in, cos_ref, sin_ref, low_ref, high_ref, log_ref, source_ref, wout_ref, gain_ref) = refs[:11]
        (gu_ref, d_ref) = refs[11:13]
        (full_ref, own_ref, branch_ref, wgu_ref, d_other_ref, qrot_ref, keys_ref, values_ref, o_ref, lse_ref, scale_ref) = refs[13:24]
        (terms, shard, slots, tot_send, tot_recv, pair_send, pair_recv, local) = refs[24:32]
        (ffn_send, ffn_recv, share_send, share_recv, ffn_local) = refs[32:37]
        rest = refs[37:]
        me = z, y, x, k = place()
        ctx = own_tile(me)
        head_at = pl.ds(pl.multiple_of((x * 8 + ctx) * HD, HD), HD)
        sibling = (z, y, x, 1 - k)
        barrier = pltpu.get_barrier_semaphore()
        plane_greet_all(me, [sibling])
        loaded()
        query_gain, key_gain = gain_ref[0:1, head_at], gain_ref[1:2, head_at]

        def pair(src, dst, n):
            return pltpu.make_async_remote_copy(
                src_ref=src,
                dst_ref=dst,
                send_sem=pair_send.at[n],
                recv_sem=pair_recv.at[n],
                device_id=sibling,
                device_id_type=MESH,
            )

        eye = eye_mask()
        own = z * 4 + y * 2 + x
        for i in range(8):
            piece = slice(i * HD, (i + 1) * HD)
            for side, ref in enumerate((q_in, k_in)):
                values = ref[piece, :]
                column = jnp.sum(values * values, axis=1, keepdims=True)
                slots[own, side * 8 + i : side * 8 + i + 1, :] = column_to_row(column, eye)
        values_ref[:tokens, :] = v_in[...]
        other_half = pl.ds(tokens, tokens)
        v_copy = pair(v_in, values_ref.at[other_half, :], 0)
        v_copy.start()

        def ffn_copy(t, i):
            to = ctx + t - 8 * ((ctx + t) // 8)
            at = pl.ds(pl.multiple_of(to * hidden, hidden), hidden)
            from_at = pl.ds(pl.multiple_of(ctx * part, part), part)
            return pltpu.make_async_remote_copy(
                src_ref=gu_ref.at[i, :, at],
                dst_ref=wgu_ref.at[i, from_at, :hidden],
                send_sem=ffn_send.at[i, t],
                recv_sem=ffn_recv.at[i, t],
                device_id=(to // 2, to % 2, x, k),
                device_id_type=MESH,
            )

        def ffn_ends(t):
            c = ctx + 8 - t - 8 * ((ctx + 8 - t) // 8)
            at = pl.ds(pl.multiple_of(c * part, part), part)
            return wgu_ref.at[:, at, :hidden], wgu_ref.at[:, at, hidden:]

        own_at = pl.ds(pl.multiple_of(ctx * hidden, hidden), hidden)
        ffn_own = pltpu.make_async_copy(gu_ref.at[:, :, own_at], ffn_ends(0)[0], ffn_local)
        ffn_own.start()
        down_copy = pair(d_ref, d_other_ref, 2)
        down_copy.start()

        total = sum_begin(me, slots, tot_send, tot_recv)()
        trickle = Trickle()
        trickle.add([lambda t=t, i=i: ffn_copy(t, i).start() for t in DEAL_ORDER for i in range(2)])
        trickle.tick(DEALT_FIRST)
        scales = lax.rsqrt(total / width + EPSILON)
        scale_ref[...] = scales

        def rotated(values, piece):
            return values * cos_ref[piece, :] + pltpu.roll(values, HD // 2, 1) * sin_ref[piece, :]

        for i in range(8):
            piece = slice(i * HD, (i + 1) * HD)
            factor = row_to_column(scales[8 + i : 9 + i, :], eye)
            keys_ref[piece, :] = rotated(k_in[piece, :] * factor * key_gain, piece).astype(BF)
        k_copy = pair(keys_ref.at[:tokens, :], keys_ref.at[other_half, :], 1)
        k_copy.start()
        for i in range(8):
            piece = slice(i * HD, (i + 1) * HD)
            factor = row_to_column(scales[i : i + 1, :], eye)
            qrot_ref[piece, :] = rotated(q_in[piece, :] * factor * query_gain, piece).astype(BF)
        v_copy.wait()
        k_copy.wait()

        def produce(zp):
            at = pl.ds(pl.multiple_of(zp * group, group), group)
            raw, allowed = masked_scores(
                qrot_ref[at, :], keys_ref[...], low_ref[at, :], high_ref[at, :], log_ref[...]
            )
            raw = jnp.where(allowed, raw, MASKED)
            top = jnp.max(raw, axis=1, keepdims=True)
            weights = jnp.exp(raw - top)
            total_weight = jnp.sum(weights, axis=1, keepdims=True)
            out = jnp.dot(weights.astype(BF), values_ref[...], preferred_element_type=F32)
            out = out * (1.0 / total_weight)
            o_ref[at, :] = out
            lse_ref[at, :] = top + jnp.log(total_weight)
            terms[at, :] = jnp.dot(
                out.astype(BF), wout_ref[...], preferred_element_type=F32
            ).astype(BF)

        def finish(strip, total):
            branch_ref[strip] = total
            h = source_ref[strip].astype(F32) + total * row_scale(total) * gain_ref[2:3, :]
            own_ref[strip] = h
            shard[strip] = h.astype(BF)

        settle = reduce_plane(
            me,
            terms,
            rows,
            rest[:N_REDUCE],
            TURNS_ATTENTION[0],
            produce,
            finish,
            tick=lambda: trickle.tick(FORWARD_RATE),
        )
        view = gather_view(full_ref, rows)
        keep = pltpu.make_async_copy(shard, view(own), local)
        keep.start()

        def share(t):
            src, dst = ffn_ends(t)
            return pltpu.make_async_remote_copy(
                src_ref=src,
                dst_ref=dst,
                send_sem=share_send.at[t],
                recv_sem=share_recv.at[t],
                device_id=sibling,
                device_id_type=MESH,
            )

        def ffn_landed(t):
            for i in range(2):
                src = ffn_ends(t)[0].at[i]
                pltpu.make_async_remote_copy(
                    src_ref=src,
                    dst_ref=src,
                    send_sem=ffn_send.at[i, t],
                    recv_sem=ffn_recv.at[i, t],
                    device_id=sibling,
                    device_id_type=MESH,
                ).wait_recv()

        gather_plane(
            me,
            shard,
            view,
            rest[N_REDUCE:],
            TURNS_ATTENTION[1],
            tick=lambda: trickle.tick(FORWARD_RATE),
        )
        trickle.flush()
        ffn_own.wait()
        share(0).start()
        for t in DEAL_ORDER:
            ffn_landed(t)
            share(t).start()
        keep.wait()
        settle()
        for t in range(8):
            share(t).wait()
            for i in range(2):
                if t > 0:
                    ffn_copy(t, i).wait_send()
        down_copy.wait()

    shape = jax.ShapeDtypeStruct
    return comm_call(
        body,
        "attention_forward",
        1,
        (
            shape((tokens, width), BF),
            shape((rows, width), F32),
            shape((rows, width), F32),
            shape((2, width, 2 * hidden), BF),
            shape((hidden, width), BF),
            shape((tokens, HD), BF),
            shape((2 * tokens, HD), BF),
            shape((2 * tokens, HD), BF),
            shape((tokens, HD), F32),
            shape((tokens, 1), F32),
            shape((16, HD), F32),
        ),
        [VMEM] * 11 + [ANY, ANY],
        (ANY, VMEM, VMEM, ANY, ANY, VMEM, VMEM, VMEM, VMEM, VMEM, VMEM),
        [
            pltpu.VMEM((tokens, width), BF),
            pltpu.VMEM((rows, width), BF),
            pltpu.VMEM((16, 16, HD), F32),
            DMA((16,)),
            DMA((16,)),
            DMA((3,)),
            DMA((3,)),
            DMA,
            DMA((2, 8)),
            DMA((2, 8)),
            DMA((8,)),
            DMA((8,)),
            DMA,
            *reduce_scratch(rows, width),
            *GATHER_SEMS,
        ],
    )(query, key, value, *tables, *bounds, logical, source, out_weight, gains, gu_stage, down_own)


def ffn_forward(source, gu_w, down_w, residual, cotangent, gain):
    tokens, width = source.shape
    rows, group = tokens // 16, tokens // 4
    hidden = 2 * down_w[0].shape[0]

    def body(*refs, loaded):
        (h_any, gu_any, d_any, d_any2, res_ref, cot_ref, gain_ref) = refs[:7]
        (full_ref, out_ref, gg_ref, for_gate_out, for_up_out, m_out) = refs[7:13]
        (hs, gu, dw, terms, shard, result, load_sem, local, out_send, out_recv) = refs[13:23]
        (for_gate_ref, for_up_ref, m_ref, leave_sem) = refs[23:27]
        scratch = refs[27:]
        me = z, y, x, k = place()

        def h_load(zp):
            at = pl.ds(pl.multiple_of(zp * group, group), group)
            return pltpu.make_async_copy(h_any.at[at, :], hs.at[at, :], load_sem.at[zp])

        order = [near_first(step, z) for step in (3, 2, 1, 0)]
        gu_load = pltpu.make_async_copy(gu_any, gu, load_sem.at[4])
        d_loads = [
            pltpu.make_async_copy(d_any, dw.at[: hidden // 2, :], load_sem.at[5]),
            pltpu.make_async_copy(d_any2, dw.at[hidden // 2 :, :], load_sem.at[6]),
        ]
        for load in (h_load(order[0]), gu_load, *d_loads):
            load.start()
        for zp in order[1:]:
            h_load(zp).start()
        greet_plane(me, pair_devices(me))
        loaded()
        gg_ref[...] = jnp.zeros_like(gg_ref)
        gu_load.wait()

        def leave(zp):
            at = pl.ds(pl.multiple_of(zp * group, group), group)
            pairs = ((for_gate_ref, for_gate_out), (for_up_ref, for_up_out), (m_ref, m_out))
            return [
                pltpu.make_async_copy(src.at[at, :], dst.at[at, :], leave_sem.at[i, zp])
                for i, (src, dst) in enumerate(pairs)
            ]

        def produce(zp):
            at = pl.ds(pl.multiple_of(zp * group, group), group)
            h_load(zp).wait()
            tile = hs[at, :]
            gate = jnp.dot(tile, gu[0], preferred_element_type=F32)
            up = jnp.dot(tile, gu[1], preferred_element_type=F32)
            sig = jax.nn.sigmoid(gate)
            silu = gate * sig
            mixed = (silu * up).astype(BF)
            for_gate_ref[at, :] = up * sig * (1.0 + gate * (1.0 - sig))
            for_up_ref[at, :] = silu
            m_ref[at, :] = mixed
            for copy in leave(zp):
                copy.start()
            terms[at, :] = jnp.dot(mixed, dw[...], preferred_element_type=F32).astype(BF)

        def finish(strip, total):
            gain_row = gain_ref[3:4, :]
            out = res_ref[strip] + total * row_scale(total) * gain_row
            result[strip] = out.astype(BF)
            back, term = norm_back_strip(cot_ref[strip].astype(F32), total, gain_row)
            gg_ref[...] += term
            shard[strip] = back.astype(BF)

        for load in d_loads:
            load.wait()
        settle = reduce_plane(me, terms, rows, scratch[:N_REDUCE], EVEN, produce, finish)
        view = gather_view(full_ref, rows)
        keep = pltpu.make_async_copy(shard, view(me[0] * 4 + me[1] * 2 + me[2]), local)
        keep.start()
        copies, own = hand_out_copies(me, result, out_ref, out_send, out_recv)
        for copy in copies:
            copy.start()
        own.start()
        gather_plane(me, shard, view, scratch[N_REDUCE:], EVEN)
        keep.wait()
        settle()
        for zp in range(4):
            for copy in leave(zp):
                copy.wait()
        own.wait()
        for copy in copies:
            copy.wait()

    shape = jax.ShapeDtypeStruct
    return comm_call(
        body,
        "ffn_forward",
        3,
        (
            shape((tokens, width), BF),
            shape((rows * 4, width // 4), BF),
            shape((8, width), F32),
            shape((tokens, hidden), F32),
            shape((tokens, hidden), F32),
            shape((tokens, hidden), BF),
        ),
        [ANY, ANY, ANY, ANY, VMEM, VMEM, VMEM],
        (ANY, ANY, VMEM, ANY, ANY, ANY),
        [
            pltpu.VMEM((tokens, width), BF),
            pltpu.VMEM((2, width, hidden), BF),
            pltpu.VMEM((hidden, width), BF),
            pltpu.VMEM((tokens, width), BF),
            pltpu.VMEM((rows, width), BF),
            pltpu.VMEM((rows, width), BF),
            DMA((7,)),
            DMA,
            DMA((3,)),
            DMA((4,)),
            pltpu.VMEM((tokens, hidden), F32),
            pltpu.VMEM((tokens, hidden), F32),
            pltpu.VMEM((tokens, hidden), BF),
            DMA((3, 4)),
            *reduce_scratch(rows, width),
            *GATHER_SEMS,
        ],
    )(source, gu_w, *down_w, residual, cotangent, gain)


EARLY = 5
GRADS_FIRST = 3


def grad_copies(me, src, dst, send, recv, t):
    ctx = own_tile(me)
    to = ctx + t - 8 * ((ctx + t) // 8)
    return [
        pltpu.make_async_remote_copy(
            src_ref=src.at[i],
            dst_ref=dst.at[ctx, i],
            send_sem=send.at[t, i],
            recv_sem=recv.at[t, i],
            device_id=(to // 2, to % 2, me[2], me[3]),
            device_id_type=MESH,
        )
        for i in range(3)
    ]


def grad_landed(me, dst, send, recv, t):
    ctx = own_tile(me)
    c = ctx + 8 - t - 8 * ((ctx + 8 - t) // 8)
    for i in range(3):
        pltpu.make_async_remote_copy(
            src_ref=dst.at[c, i],
            dst_ref=dst.at[c, i],
            send_sem=send.at[t, i],
            recv_sem=recv.at[t, i],
            device_id=(me[0], me[1], me[2], 1 - me[3]),
            device_id_type=MESH,
        ).wait_recv()


def ctx_greet(me, others):
    z, y, x, k = me
    barrier = pltpu.get_barrier_semaphore()

    def call(i, carry):
        to = lax.rem(z * 2 + y + i, 8)
        pl.semaphore_signal(
            barrier, inc=1, device_id=(to // 2, to % 2, x, k), device_id_type=MESH
        )
        return carry

    lax.fori_loop(1, 8, call, 0)
    for target in [(z, y, 1 - x, k), *others]:
        pl.semaphore_signal(barrier, inc=1, device_id=target, device_id_type=MESH)
    pl.semaphore_wait(barrier, 8 + len(others))


def ffn_backward(
    grad_ffn, source, gu_w, down_w, for_gate, for_up, mixed, cotangent, branch, gain, attention
):
    tokens, width = grad_ffn.shape
    rows, group = tokens // 16, tokens // 4
    hidden = 2 * down_w[0].shape[0]
    part = hidden // 2
    across = (((0,), (0,)), ((), ()))
    turned = (((1,), (1,)), ((), ()))
    scaling = 1.0 / math.sqrt(HD)

    def body(*refs, loaded):
        (df_any, h_any, gu_any, d_any, d_any2, fg_any, fu_any, m_any, cot_ref, branch_ref, gain_ref) = refs[:11]
        (wout_ref, qrot_ref, keys_ref, values_ref, o_ref, lse_ref, low_ref, high_ref, log_ref) = refs[11:20]
        (full_ref, own_ref, gg_ref, in_ref, rest_ref, dq_ref, dk_ref, dv_ref) = refs[20:28]
        (df, hs, gu, dw, fg, fu, ms, dgu, terms, shard) = refs[28:38]
        (to_core, from_core, to_ctx) = refs[38:41]
        (da, dk_all, dv_all, pair_out, pair_in) = refs[41:46]
        (load_sem, local, core_send, core_recv, grad_send, grad_recv, rest_sem) = refs[46:53]
        (da_sem, pair_send, pair_recv) = refs[53:56]
        scratch = refs[56:]
        me = z, y, x, k = place()
        ctx = own_tile(me)
        order = [near_first(step, z) for step in (3, 2, 1, 0)]

        def group_load(zp):
            at = pl.ds(pl.multiple_of(zp * group, group), group)
            return [
                pltpu.make_async_copy(src.at[at, :], dst.at[at, :], load_sem.at[i, zp])
                for i, (src, dst) in enumerate(((df_any, df), (fg_any, fg), (fu_any, fu)))
            ]

        d_load = pltpu.make_async_copy(d_any, dw.at[:part, :], load_sem.at[3, 0])
        d_load2 = pltpu.make_async_copy(d_any2, dw.at[part:, :], load_sem.at[4, 0])
        gu_load = pltpu.make_async_copy(gu_any, gu, load_sem.at[3, 1])
        h_load = pltpu.make_async_copy(h_any, hs, load_sem.at[3, 2])
        m_load = pltpu.make_async_copy(m_any, ms, load_sem.at[3, 3])
        for load in (*group_load(order[0]), d_load, d_load2, gu_load):
            load.start()
        for zp in order[1:]:
            for load in group_load(zp):
                load.start()
        h_load.start()
        m_load.start()
        sibling = (z, y, x, 1 - k)
        ctx_greet(me, [sibling])
        loaded()
        gg_ref[...] = jnp.zeros_like(gg_ref)
        d_load.wait()
        d_load2.wait()

        def produce(zp):
            at = pl.ds(pl.multiple_of(zp * group, group), group)
            for load in group_load(zp):
                load.wait()
            dm = lax.dot_general(df[at, :], dw[...], turned, preferred_element_type=F32)
            dg = (dm * fg[at, :]).astype(BF)
            du = (dm * fu[at, :]).astype(BF)
            dgu[at, :hidden] = dg
            dgu[at, hidden:] = du
            terms[at, :] = (
                lax.dot_general(dg, gu[0], turned, preferred_element_type=F32)
                + lax.dot_general(du, gu[1], turned, preferred_element_type=F32)
            ).astype(BF)

        def finish(strip, total):
            grad = cot_ref[strip].astype(F32) + total
            own_ref[strip] = grad
            back, term = norm_back_strip(grad, branch_ref[strip], gain_ref[2:3, :])
            gg_ref[...] += term
            shard[strip] = back.astype(BF)

        def core_copy(t):
            return pltpu.make_async_remote_copy(
                src_ref=to_core.at[t],
                dst_ref=from_core.at[t],
                send_sem=core_send.at[t],
                recv_sem=core_recv.at[t],
                device_id=sibling,
                device_id_type=MESH,
            )

        parts = (*DEAL_ORDER, 0)

        def compute(n):
            t = parts[n]
            c = ctx + t - 8 * ((ctx + t) // 8)
            at = pl.ds(pl.multiple_of(c * part, part), part)
            up_like = lax.dot_general(hs[:, at], dgu[...], across, preferred_element_type=F32)
            down_like = lax.dot_general(ms[...], df[:, at], across, preferred_element_type=F32)
            for i in range(2):
                to_ctx[t, i] = up_like[:, 2 * i * part : (2 * i + 1) * part].astype(BF)
                to_core[t, i] = up_like[:, (2 * i + 1) * part : (2 * i + 2) * part].astype(BF)
            to_ctx[t, 2] = down_like[:part].astype(BF)
            to_core[t, 2] = down_like[part:].astype(BF)
            core_copy(t).start()

        trickle = Trickle()

        def send(n):
            t = parts[n]
            core_copy(t).wait_recv()
            to_ctx[t] = (to_ctx[t].astype(F32) + from_core[t].astype(F32)).astype(BF)
            if t == 0:
                pltpu.make_async_copy(to_ctx.at[0], in_ref.at[ctx], rest_sem.at[0]).start()
            elif n < EARLY:
                trickle.add(
                    [
                        copy.start
                        for copy in grad_copies(me, to_ctx.at[t], in_ref, grad_send, grad_recv, t)
                    ]
                )
            else:
                pltpu.make_async_copy(
                    to_ctx.at[t], rest_ref.at[n - EARLY], rest_sem.at[n - EARLY + 1]
                ).start()

        begun = []

        def next_part():
            n = len(begun)
            begun.append(n)
            if n < 8:
                compute(n)
            if BACK_LAG <= n < 8 + BACK_LAG:
                send(n - BACK_LAG)

        def tick():
            if begun:
                next_part()
            trickle.tick(BACK_RATE)

        def da_load(step):
            at = pl.ds(pl.multiple_of(near_first(step, z) * group, group), group)
            return pltpu.make_async_copy(full_ref.at[at, :], da.at[step % 2], da_sem.at[step % 2])

        def attend_back(step):
            at = pl.ds(pl.multiple_of(near_first(step, z) * group, group), group)
            da_load(step).wait()
            grad = lax.dot_general(
                da[step % 2], wout_ref[...], turned, preferred_element_type=F32
            ).astype(BF)
            delta = jnp.sum(grad.astype(F32) * o_ref[at, :], axis=1, keepdims=True)
            q, low, high, lse = qrot_ref[at, :], low_ref[at, :], high_ref[at, :], lse_ref[at, :]
            dq_ref[at, :] = jnp.zeros((group, HD), F32)

            def work(key_at):
                key_part = keys_ref[key_at, :]
                raw, allowed = masked_scores(q, key_part, low, high, log_ref[:, key_at])
                weights = jnp.where(allowed, jnp.exp(raw - lse), 0.0)
                dp = lax.dot_general(
                    grad, values_ref[key_at, :], turned, preferred_element_type=F32
                )
                ds = (weights * (dp - delta)).astype(BF)
                dq_ref[at, :] += jnp.dot(ds, key_part, preferred_element_type=F32) * scaling
                dk_all[key_at, :] += (
                    lax.dot_general(ds, q, across, preferred_element_type=F32) * scaling
                )
                dv_all[key_at, :] += lax.dot_general(
                    weights.astype(BF), grad, across, preferred_element_type=F32
                )

            strips(2 * tokens, work, tokens)

        def arrived(step):
            if step == 0:
                keep.wait()
                dk_all[...] = jnp.zeros_like(dk_all)
                dv_all[...] = jnp.zeros_like(dv_all)
            da_load(step).start()
            if step > 0:
                attend_back(step - 1)

        def pair(n):
            return pltpu.make_async_remote_copy(
                src_ref=pair_out.at[n],
                dst_ref=pair_in.at[n],
                send_sem=pair_send.at[n],
                recv_sem=pair_recv.at[n],
                device_id=sibling,
                device_id_type=MESH,
            )

        def after_terms():
            h_load.wait()
            m_load.wait()
            for _ in range(GRADS_FIRST):
                next_part()

        gu_load.wait()
        settle = reduce_plane(
            me,
            terms,
            rows,
            scratch[:N_REDUCE],
            TURNS_FFN_BACK[0],
            produce,
            finish,
            after_terms,
            tick,
        )
        view = gather_view(full_ref, rows)
        keep = pltpu.make_async_copy(shard, view(me[0] * 4 + me[1] * 2 + me[2]), local)
        keep.start()
        gather_plane(
            me,
            shard,
            view,
            scratch[N_REDUCE:],
            TURNS_FFN_BACK[1],
            arrived=arrived,
            tick=tick,
            early=EARLY_LAYERS,
        )
        while len(begun) < 8 + BACK_LAG:
            next_part()
        trickle.flush()
        attend_back(3)
        pair_out[0] = dk_all[tokens:, :].astype(BF)
        pair_out[1] = dv_all[tokens:, :].astype(BF)
        pair(0).start()
        pair(1).start()
        settle()
        for n, (ref, source_ref) in enumerate(((dk_ref, dk_all), (dv_ref, dv_all))):
            pair(n).wait()
            ref[...] = source_ref[:tokens, :] + pair_in[n].astype(F32)
        for t in range(8):
            core_copy(t).wait_send()
        pltpu.make_async_copy(to_ctx.at[0], in_ref.at[ctx], rest_sem.at[0]).wait()
        for n, t in enumerate(DEAL_ORDER):
            if n < EARLY:
                grad_landed(me, in_ref, grad_send, grad_recv, t)
                for copy in grad_copies(me, to_ctx.at[t], in_ref, grad_send, grad_recv, t):
                    copy.wait_send()
            else:
                pltpu.make_async_copy(
                    to_ctx.at[t], rest_ref.at[n - EARLY], rest_sem.at[n - EARLY + 1]
                ).wait()

    shape = jax.ShapeDtypeStruct
    vmem = pltpu.VMEM
    return comm_call(
        body,
        "ffn_backward",
        4,
        (
            shape((tokens, width), BF),
            shape((rows, width), F32),
            shape((8, width), F32),
            shape((8, 3, part, part), BF),
            shape((7 - EARLY, 3, part, part), BF),
            shape((tokens, HD), F32),
            shape((tokens, HD), F32),
            shape((tokens, HD), F32),
        ),
        [*[ANY] * 8, *[VMEM] * 12],
        (ANY, VMEM, VMEM, ANY, ANY, VMEM, VMEM, VMEM),
        [
            vmem((tokens, width), BF),
            vmem((tokens, width), BF),
            vmem((2, width, hidden), BF),
            vmem((hidden, width), BF),
            vmem((tokens, hidden), F32),
            vmem((tokens, hidden), F32),
            vmem((tokens, hidden), BF),
            vmem((tokens, 2 * hidden), BF),
            vmem((tokens, width), BF),
            vmem((rows, width), BF),
            vmem((8, 3, part, part), BF),
            vmem((8, 3, part, part), BF),
            vmem((8, 3, part, part), BF),
            vmem((2, group, width), BF),
            vmem((2 * tokens, HD), F32),
            vmem((2 * tokens, HD), F32),
            vmem((2, tokens, HD), BF),
            vmem((2, tokens, HD), BF),
            DMA((5, 4)),
            DMA,
            DMA((8,)),
            DMA((8,)),
            DMA((8, 3)),
            DMA((8, 3)),
            DMA((8,)),
            DMA((2,)),
            DMA((2,)),
            DMA((2,)),
            *reduce_scratch(rows, width),
            *GATHER_SEMS,
        ],
    )(
        grad_ffn,
        source,
        gu_w,
        *down_w,
        for_gate,
        for_up,
        mixed,
        cotangent,
        branch,
        gain,
        *attention,
    )


def write_results(early, late, wall, outputs, input_grad, gains):
    part = early.shape[2]

    def body(early_ref, late_ref, wall_ref, out_ref, in_ref, gain_ref, *results):
        (out_to, in_to, gq, gk, gv, go, gg, gu, gd, *gains_to) = results
        n = pl.program_id(0)

        @pl.when(n == 0)
        def _():
            out_to[...] = out_ref[...]
            in_to[...] = in_ref[...]
            for i, ref in enumerate(gains_to):
                ref[...] = gain_ref[i : i + 1, :]

        for i, ref in enumerate((gq, gk, gv, go)):
            ref[...] = wall_ref[0, i].astype(F32)

        @pl.when(n <= EARLY)
        def _():
            for i, ref in enumerate((gg, gu, gd)):
                ref[...] = early_ref[0, i].astype(F32)

        @pl.when(n > EARLY)
        def _():
            for i, ref in enumerate((gg, gu, gd)):
                ref[...] = late_ref[0, i].astype(F32)

    shape = jax.ShapeDtypeStruct
    spec = pl.BlockSpec

    def source(n):
        ctx = lax.axis_index("z") * 2 + lax.axis_index("y")
        odd = lax.rem(n, 2)
        t = odd * (4 + n // 2) + (1 - odd) * (n // 2)
        return lax.rem(ctx + 8 - t, 8)

    rows, columns = outputs.shape
    whole = spec((rows, columns), lambda n: (0, 0))
    in_row = spec((HD, HD), lambda n: (source(n) % 2, source(n) // 2))
    in_column = spec((HD, HD), lambda n: (source(n) // 2, source(n) % 2))
    side = spec((part, part), lambda n: (0, source(n)))
    gain_spec = spec(gains.shape, lambda n: (0, 0))
    gain_row = spec((1, gains.shape[1]), lambda n: (0, 0))
    blob = (1, 3, part, part)
    return pl.pallas_call(
        body,
        name="write_results",
        grid=(8,),
        out_shape=(
            shape((rows, columns), BF),
            shape((rows, columns), BF),
            shape((2 * HD, 4 * HD), F32),
            shape((2 * HD, 4 * HD), F32),
            shape((2 * HD, 4 * HD), F32),
            shape((4 * HD, 2 * HD), F32),
            shape((part, 8 * part), F32),
            shape((part, 8 * part), F32),
            shape((8 * part, part), F32),
            *[shape((1, gains.shape[1]), F32)] * 4,
        ),
        in_specs=[
            spec(blob, lambda n: (source(jnp.minimum(n, EARLY)), 0, 0, 0)),
            spec(blob, lambda n: (source(jnp.maximum(n, EARLY + 1)), 0, 0, 0)),
            spec((1, 4, HD, HD), lambda n: (source(n), 0, 0, 0)),
            whole,
            whole,
            gain_spec,
        ],
        out_specs=(
            whole,
            whole,
            in_row,
            in_row,
            in_row,
            in_column,
            side,
            side,
            spec((part, part), lambda n: (source(n), 0)),
            *[gain_row] * 4,
        ),
        compiler_params=pltpu.CompilerParams(vmem_limit_bytes=BIG_VMEM),
    )(early, late, wall, outputs, input_grad, gains)


def close_greet(me):
    z, y, x, k = me
    barrier = pltpu.get_barrier_semaphore()

    def plane(i, carry):
        pl.semaphore_signal(barrier, inc=1, device_id=plane_peer(me, i)[1], device_id_type=MESH)
        return carry

    def others(i, carry):
        pl.semaphore_signal(
            barrier, inc=1, device_id=(i // 2, i % 2, x, 1 - k), device_id_type=MESH
        )
        return carry

    lax.fori_loop(1, 16, plane, 0)
    lax.fori_loop(0, 8, others, 0)
    pl.semaphore_signal(barrier, inc=1, device_id=(z, y, 1 - x, 1 - k), device_id_type=MESH)
    pl.semaphore_wait(barrier, 24)


def attention_backward(
    grad_attn,
    full_in,
    query,
    key,
    attended,
    grads_rotated,
    tables,
    scales,
    gains,
    qkv_w,
    grad_own,
    attn_term,
    ffn_term,
    grads_left,
):
    tokens, width = grad_attn.shape
    rows, group = tokens // 16, tokens // 4
    part = width // 4

    def body(*refs, loaded):
        (da_any, x_any) = refs[:2]
        (q_ref, k_ref, o_ref, dq_in, dk_in, dv_in, cos_ref, sin_ref) = refs[2:10]
        (scale_ref, gain_ref, wqkv_ref) = refs[10:13]
        (grad_ref, attn_ref, ffn_ref, left_ref) = refs[13:17]
        (in_grad_ref, deal_in, gains_ref, ffn_in) = refs[17:21]
        (da, xs, terms, dq_ref, dk_ref) = refs[21:26]
        (dqkv, slots, result) = refs[26:29]
        (qkv_grads, out_grads, wall_out, wall_in, deal_out) = refs[29:34]
        (gain_out, gain_in, gain_own, gain_slots) = refs[34:38]
        (load_sem, pair_send, pair_recv, tot_send, tot_recv, out_send, out_recv) = refs[38:45]
        (deal_send, deal_recv, gain_send, gain_recv, grad_send, grad_recv) = refs[45:51]
        scratch = refs[51:]
        me = z, y, x, k = place()
        ctx = own_tile(me)
        own = ctx * 2 + x
        own_head = pl.ds(pl.multiple_of((x * 8 + ctx) * HD, HD), HD)
        sibling = (z, y, x, 1 - k)

        da_load = pltpu.make_async_copy(da_any, da, load_sem.at[0])
        x_load = pltpu.make_async_copy(x_any, xs, load_sem.at[1])
        x_load.start()
        da_load.start()
        close_greet(me)
        loaded()

        trickle = Trickle()

        def left_copies(n):
            return grad_copies(me, left_ref.at[n - EARLY], ffn_in, grad_send, grad_recv, DEAL_ORDER[n])

        for n in range(EARLY, 7):
            trickle.add([copy.start for copy in left_copies(n)])
        trickle.tick(CLOSE_FIRST)

        def pair(n):
            return pltpu.make_async_remote_copy(
                src_ref=wall_out.at[n] if n < 8 else gain_out,
                dst_ref=wall_in.at[n] if n < 8 else gain_in,
                send_sem=pair_send.at[n],
                recv_sem=pair_recv.at[n],
                device_id=sibling,
                device_id_type=MESH,
            )

        across = (((0,), (0,)), ((), ()))
        eye = eye_mask()

        def normed_grad(values, piece):
            return values * cos_ref[piece, :] - pltpu.roll(values, HD // 2, 1) * sin_ref[piece, :]

        def side_dots(side, source, grads, proj):
            gain_sum = jnp.zeros((8, HD), F32)
            for i in range(8):
                piece = slice(i * HD, (i + 1) * HD)
                factor = row_to_column(scale_ref[side * 8 + i : side * 8 + i + 1, :], eye)
                back = normed_grad(source[piece, :], piece)
                term = back * proj[piece, :] * factor
                for j in range(0, HD, 8):
                    gain_sum = gain_sum + term[j : j + 8, :]
                weighted = back * gain_ref[side : side + 1, own_head]
                grads[piece, :] = weighted
                dot = jnp.sum(weighted * proj[piece, :], axis=1, keepdims=True)
                slots[own, side * 8 + i : side * 8 + i + 1, :] = column_to_row(dot, eye)
            return jnp.sum(gain_sum, axis=0, keepdims=True)

        query_gain = side_dots(0, dq_in, dq_ref, q_ref)
        key_gain = side_dots(1, dk_in, dk_ref, k_ref)
        sum_end = sum_begin(me, slots, tot_send, tot_recv)
        dqkv[:, 2 * HD :] = dv_in[...].astype(BF)

        attn_sum = jnp.sum(attn_ref[...], axis=0, keepdims=True)
        ffn_sum = jnp.sum(ffn_ref[...], axis=0, keepdims=True)
        head_core = z // 2
        head_at = pl.ds(pl.multiple_of(((z % 2) * 2 + y) * HD, HD), HD)
        for mine, target in ((True, gain_own), (False, gain_out)):
            target[...] = jnp.zeros_like(target)
            for xt in range(2):
                for kt in range(2):

                    @pl.when((kt == k) if mine else (kt != k))
                    def _(xt=xt, kt=kt, target=target):
                        block = slice((2 * xt + kt) * part, (2 * xt + kt + 1) * part)
                        target[xt, 2:3, :] = attn_sum[:, block]
                        target[xt, 3:4, :] = ffn_sum[:, block]

            @pl.when((head_core == k) if mine else (head_core != k))
            def _(target=target):
                target[x, 0:1, head_at] = query_gain
                target[x, 1:2, head_at] = key_gain

        pair(8).start()

        parts = (*DEAL_ORDER, 0)

        def columns_of(n):
            c = ctx + parts[n] - 8 * ((ctx + parts[n]) // 8)
            return pl.ds(pl.multiple_of(c * 2 * HD, 2 * HD), 2 * HD)

        attended_low = o_ref[...].astype(BF)
        da_load.wait()
        for n in range(8):
            out_grads[n] = lax.dot_general(
                attended_low, da[:, columns_of(n)], across, preferred_element_type=F32
            )
        total = sum_end()
        trickle.tick(CLOSE_NEXT)
        for side, grads, proj in ((0, dq_ref, q_ref), (1, dk_ref, k_ref)):
            for i in range(8):
                piece = slice(i * HD, (i + 1) * HD)
                row = scale_ref[side * 8 + i : side * 8 + i + 1, :]
                factor = row_to_column(row, eye)
                cubed = row * row * row * total[side * 8 + i : side * 8 + i + 1, :] / width
                dqkv[piece, side * HD : (side + 1) * HD] = (
                    factor * grads[piece, :] - proj[piece, :] * row_to_column(cubed, eye)
                ).astype(BF)

        def produce(zp):
            at = pl.ds(pl.multiple_of(zp * group, group), group)
            term = jnp.zeros((group, width), F32)
            for i in range(3):
                term = term + lax.dot_general(
                    dqkv[at, i * HD : (i + 1) * HD],
                    wqkv_ref[i],
                    (((1,), (1,)), ((), ())),
                    preferred_element_type=F32,
                )
            terms[at, :] = term.astype(BF)

        gain_copies = []

        def gain_copy(i):
            other, device = plane_peer(me, i)
            return pltpu.make_async_remote_copy(
                src_ref=gain_own.at[other % 2],
                dst_ref=gain_slots.at[own],
                send_sem=gain_send.at[i],
                recv_sem=gain_recv.at[own],
                device_id=device,
                device_id_type=MESH,
            )

        number = ((z % 2) * 2 + y) * 2 + k

        def deal(n):
            c = ctx + parts[n] - 8 * ((ctx + parts[n]) // 8)
            return pltpu.make_async_remote_copy(
                src_ref=deal_out.at[n],
                dst_ref=deal_in.at[number],
                send_sem=deal_send.at[n],
                recv_sem=deal_recv.at[number],
                device_id=(c // 2, c % 2, x, head_core),
                device_id_type=MESH,
            )

        stays = k == head_core

        def deal_start(n):
            if n < 7:
                deal(n).start()
                return

            @pl.when(jnp.logical_not(stays))
            def _():
                deal(n).start()

            @pl.when(stays)
            def _():
                pltpu.make_async_copy(
                    deal_out.at[n], deal_in.at[number], deal_recv.at[number]
                ).start()

        def after_terms():
            pair(8).wait_recv()
            gain_own[...] += gain_in[...]
            gain_slots[own] = gain_own[x]

            def begin(i, carry):
                gain_copy(i).start()
                return carry

            lax.fori_loop(1, 16, begin, 0)

        x_load.wait()
        begun = []

        def halves(n, r):
            rows_at = pl.ds(pl.multiple_of(r * HD, HD), HD)
            for i in range(3):
                yield i, qkv_grads[rows_at, i * HD : (i + 1) * HD]
            yield 3, out_grads[n, :, rows_at]

        def tick():
            n = len(begun)
            begun.append(n)
            if n < 8:
                qkv_grads[...] = lax.dot_general(
                    xs[:, columns_of(n)], dqkv[...], across, preferred_element_type=F32
                )
                for i, value in halves(n, 1 - k):
                    wall_out[n, i] = value.astype(BF)
                for i, value in halves(n, k):
                    deal_out[n, i] = value.astype(BF)
                pair(n).start()
            if CLOSE_LAG <= n < 8 + CLOSE_LAG:
                last = n - CLOSE_LAG
                pair(last).wait_recv()
                deal_out[last] = (deal_out[last].astype(F32) + wall_in[last].astype(F32)).astype(BF)
                deals.add([lambda: deal_start(last)])
            deals.tick()
            trickle.tick(CLOSE_RATE)

        deals = Trickle()

        def finish(strip, total):
            result[strip] = (grad_ref[strip] + total).astype(BF)

        settle = reduce_plane(
            me,
            terms,
            rows,
            scratch,
            TURNS_CLOSE,
            produce,
            finish,
            after_terms,
            tick,
        )
        while len(begun) < 8 + CLOSE_LAG:
            tick()
        deals.flush()
        trickle.flush()
        copies, own_copy = hand_out_copies(me, result, in_grad_ref, out_send, out_recv)
        for copy in copies:
            copy.start()
        own_copy.start()
        for n in range(8):
            pltpu.make_async_copy(deal_out.at[n], deal_in.at[n], deal_recv.at[n]).wait()

        def gain_landed(i, carry):
            other, device = plane_peer(me, i)
            pltpu.make_async_remote_copy(
                src_ref=gain_slots.at[other],
                dst_ref=gain_slots.at[other],
                send_sem=gain_send.at[i],
                recv_sem=gain_recv.at[other],
                device_id=device,
                device_id_type=MESH,
            ).wait_recv()
            gain_copy(i).wait_send()
            return carry

        lax.fori_loop(1, 16, gain_landed, 0)
        gain_total = gain_slots[0]
        for i in range(1, 16):
            gain_total = gain_total + gain_slots[i]
        gains_ref[...] = gain_total
        settle()
        own_copy.wait()
        for copy in copies:
            copy.wait()
        for n in range(7):
            deal(n).wait_send()

        @pl.when(jnp.logical_not(stays))
        def _():
            deal(7).wait_send()

        for n in range(9):
            pair(n).wait_send()
        for n in range(EARLY, 7):
            grad_landed(me, ffn_in, grad_send, grad_recv, DEAL_ORDER[n])
            for copy in left_copies(n):
                copy.wait_send()

    shape = jax.ShapeDtypeStruct
    vmem = pltpu.VMEM
    return comm_call(
        body,
        "attention_backward",
        5,
        (
            shape((rows * 4, part), BF),
            shape((8, 4, HD, HD), BF),
            shape((4, part), F32),
            shape((8, *grads_left.shape[1:]), BF),
        ),
        [ANY, ANY, *[VMEM] * 14, ANY],
        (ANY, ANY, VMEM, ANY),
        [
            vmem((tokens, width), BF),
            vmem((tokens, width), BF),
            vmem((tokens, width), BF),
            vmem((tokens, HD), F32),
            vmem((tokens, HD), F32),
            vmem((tokens, 3 * HD), BF),
            vmem((16, 16, HD), F32),
            vmem((rows, width), BF),
            vmem((2 * HD, 3 * HD), F32),
            vmem((8, HD, 2 * HD), F32),
            vmem((8, 4, HD, HD), BF),
            vmem((8, 4, HD, HD), BF),
            vmem((8, 4, HD, HD), BF),
            vmem((2, 4, part), F32),
            vmem((2, 4, part), F32),
            vmem((2, 4, part), F32),
            vmem((16, 4, part), F32),
            DMA((2,)),
            DMA((9,)),
            DMA((9,)),
            DMA((16,)),
            DMA((16,)),
            DMA((3,)),
            DMA((4,)),
            DMA((8,)),
            DMA((8,)),
            DMA((16,)),
            DMA((16,)),
            DMA((8, 3)),
            DMA((8, 3)),
            *reduce_scratch(rows, width),
        ],
    )(
        grad_attn,
        full_in,
        query,
        key,
        attended,
        *grads_rotated,
        *tables,
        scales,
        gains,
        qkv_w,
        grad_own,
        attn_term,
        ffn_term,
        grads_left,
    )


def plane_layer(
    inputs,
    cotangent,
    w_query,
    w_key,
    w_value,
    w_out,
    w_gate,
    w_up,
    w_down,
    query_gain,
    key_gain,
    attn_gain,
    ffn_gain,
    lengths,
    block_order,
):
    steps = np.arange(HD // 2, dtype=np.float64) * 2.0 / HD
    frequency = np.tile(np.power(ROPE_THETA, -steps), 2)[None, :].astype(np.float32)
    full_in, source_own, own_cot, qkv_w, out_w, gains_full, gu_stage, down_own, query_proj, key_proj, value_low, cosine, sine, low, high, logical_keys = open_layer(
        inputs,
        cotangent,
        w_query,
        w_key,
        w_value,
        w_out,
        w_gate,
        w_up,
        w_down,
        query_gain[None, :],
        key_gain[None, :],
        attn_gain[None, :],
        ffn_gain[None, :],
        block_order[None, :],
        lengths[None, :],
        jnp.asarray(frequency),
    )
    tables = (cosine, sine)
    (
        residual_full,
        residual_own,
        branch_own,
        gu_w,
        down_other,
        query_rot,
        keys_all,
        values_all,
        attended,
        lse,
        scales,
    ) = attention_forward(
        query_proj,
        key_proj,
        value_low,
        tables,
        (low, high),
        logical_keys,
        source_own,
        out_w,
        gains_full,
        gu_stage,
        down_own,
    )
    grad_ffn, outputs, ffn_gain_term, for_gate, for_up, mixed = ffn_forward(
        residual_full, gu_w, (down_own, down_other), residual_own, own_cot, gains_full
    )
    grad_attn, grad_own, attn_gain_term, ffn_early, ffn_left, *grads_rotated = ffn_backward(
        grad_ffn,
        residual_full,
        gu_w,
        (down_own, down_other),
        for_gate,
        for_up,
        mixed,
        own_cot,
        branch_own,
        gains_full,
        (out_w, query_rot, keys_all, values_all, attended, lse, low, high, logical_keys),
    )
    input_grad, wall_grads, gain_grads, ffn_late = attention_backward(
        grad_attn,
        full_in,
        query_proj,
        key_proj,
        attended,
        grads_rotated,
        tables,
        scales,
        gains_full,
        qkv_w,
        grad_own,
        attn_gain_term,
        ffn_gain_term,
        ffn_left,
    )
    results = write_results(ffn_early, ffn_late, wall_grads, outputs, input_grad, gain_grads)
    return (*results[:9], *[row[0] for row in results[9:]])


def full_rows(piece):
    return lax.all_gather(piece, "head", axis=1, tiled=True)


def head_sums(term):
    return lax.psum_scatter(
        term.astype(jnp.bfloat16), "head", scatter_dimension=1, tiled=True
    ).astype(jnp.float32)


def row_single(term):
    return lax.psum(term, "head")


def row_pair(first, second):
    return lax.psum((first, second), "head")


def gather_weights(w_query, w_key, w_value, w_out, w_gate, w_up, w_down):
    row_parts = (
        lax.all_gather(w_query.astype(jnp.bfloat16), "ctx", axis=0, tiled=True),
        lax.all_gather(w_key.astype(jnp.bfloat16), "ctx", axis=0, tiled=True),
        lax.all_gather(w_value.astype(jnp.bfloat16), "ctx", axis=0, tiled=True),
        lax.all_gather(w_gate.astype(jnp.bfloat16), "ctx", axis=0, tiled=True),
        lax.all_gather(w_up.astype(jnp.bfloat16), "ctx", axis=0, tiled=True),
    )
    col_parts = (
        lax.all_gather(w_out.astype(jnp.bfloat16), "ctx", axis=1, tiled=True),
        lax.all_gather(w_down.astype(jnp.bfloat16), "ctx", axis=1, tiled=True),
    )
    return tuple(row_parts) + tuple(col_parts)


def sequence_tables(logical, lengths):
    seq_ends = jnp.cumsum(lengths)
    seq_starts = seq_ends - lengths
    number = jnp.sum((logical[:, None] >= seq_ends[None, :]).astype(jnp.int32), axis=1)
    member = number[:, None] == jnp.arange(lengths.shape[0], dtype=jnp.int32)[None, :]
    offset = logical - jnp.sum(jnp.where(member, seq_starts[None, :], 0), axis=1)
    return (number, offset)


def rotate(values, offset):
    half_dim = HD // 2
    inverse = jnp.power(ROPE_THETA, -jnp.arange(half_dim, dtype=jnp.float32) * 2.0 / HD)
    angles = offset.astype(jnp.float32)[:, None] * inverse[None, :]
    cosine = jnp.cos(angles)[:, None, :]
    sine_part = jnp.sin(angles)[:, None, :]
    first_half = values[..., :half_dim]
    second_half = values[..., half_dim:]
    return jnp.concatenate(
        [
            first_half * cosine - second_half * sine_part,
            second_half * cosine + first_half * sine_part,
        ],
        axis=-1,
    )


def norm_backward(grad_in, values, factor, gain):
    gain_term = jnp.sum(grad_in * values * factor[:, None], axis=0)
    weighted = grad_in * gain
    row_dot = row_single(jnp.sum(weighted * values, axis=1))
    grad_values = (
        factor[:, None] * weighted - values * (factor * factor * factor * row_dot / D)[:, None]
    )
    return (grad_values, gain_term)


def on_device(
    inputs,
    cotangent,
    w_query,
    w_key,
    w_value,
    w_out,
    w_gate,
    w_up,
    w_down,
    query_gain,
    key_gain,
    attn_gain,
    ffn_gain,
    lengths,
    block_order,
):
    shards = lax.axis_size("ctx")
    position = lax.axis_index("ctx")
    tok_rows, width_part = inputs.shape
    block_rows = tok_rows // shards
    total_tokens = tok_rows * shards
    local_heads = width_part // HD
    scaling = 1.0 / math.sqrt(HD)
    shard_range = jnp.arange(shards, dtype=jnp.int32)
    order_table = block_order.reshape(shards, shards)
    target = order_table % shards
    choose = target[:, :, None] == shard_range[None, None, :]
    stream = jnp.sum(jnp.where(choose, order_table[:, :, None], 0), axis=1)
    stream_blocks = jnp.transpose(stream).reshape(-1)
    logical = (
        stream_blocks[:, None] * block_rows + jnp.arange(block_rows, dtype=jnp.int32)[None, :]
    ).reshape(-1)
    own_target = lax.dynamic_index_in_dim(target, position, 0, keepdims=False)
    send_order = jnp.sum(
        jnp.where(own_target[:, None] == shard_range[None, :], shard_range[:, None], 0), axis=0
    )

    def deal_out(values):
        return values.reshape(shards, block_rows, width_part)[send_order].reshape(
            tok_rows, width_part
        )

    def undeal(values):
        return values.reshape(shards, block_rows, width_part)[own_target].reshape(
            tok_rows, width_part
        )

    local_in, local_cot = (
        lax.all_to_all(deal_out(inputs), "ctx", split_axis=0, concat_axis=0, tiled=True),
        lax.all_to_all(deal_out(cotangent), "ctx", split_axis=0, concat_axis=0, tiled=True),
    )
    number_all, offset_all = sequence_tables(logical, lengths)
    number_own = lax.dynamic_slice_in_dim(number_all, position * tok_rows, tok_rows)
    offset_own = lax.dynamic_slice_in_dim(offset_all, position * tok_rows, tok_rows)
    logical_own = lax.dynamic_slice_in_dim(logical, position * tok_rows, tok_rows)
    query_full, key_full, value_full, gate_full, up_full, out_full, down_full = gather_weights(
        w_query, w_key, w_value, w_out, w_gate, w_up, w_down
    )
    full_in = full_rows(local_in)
    query_proj = jnp.dot(full_in, query_full, preferred_element_type=jnp.float32)
    key_proj = jnp.dot(full_in, key_full, preferred_element_type=jnp.float32)
    value_proj = jnp.dot(full_in, value_full, preferred_element_type=jnp.float32)
    query_sq, key_sq = row_pair(
        jnp.sum(query_proj * query_proj, axis=1), jnp.sum(key_proj * key_proj, axis=1)
    )
    query_scale = lax.rsqrt(query_sq / D + EPSILON)
    key_scale = lax.rsqrt(key_sq / D + EPSILON)
    query_rot = rotate(
        (query_proj * query_scale[:, None] * query_gain).reshape(tok_rows, local_heads, HD),
        offset_own,
    ).astype(jnp.bfloat16)
    key_rot = rotate(
        (key_proj * key_scale[:, None] * key_gain).reshape(tok_rows, local_heads, HD), offset_own
    ).astype(jnp.bfloat16)
    value_low = value_proj.astype(jnp.bfloat16).reshape(tok_rows, local_heads, HD)
    keys_all, values_all = (
        lax.all_gather(key_rot, "ctx", axis=0, tiled=True),
        lax.all_gather(value_low, "ctx", axis=0, tiled=True),
    )
    key_span = math.gcd(total_tokens, 1024)
    key_turns = total_tokens // key_span
    pieces = (
        keys_all.reshape(key_turns, key_span, local_heads, HD),
        values_all.reshape(key_turns, key_span, local_heads, HD),
        number_all.reshape(key_turns, key_span),
        logical.reshape(key_turns, key_span),
    )

    def scores_of(key_piece, number_piece, logical_piece):
        raw_scores = (
            jnp.einsum("qhd,khd->hqk", query_rot, key_piece, preferred_element_type=jnp.float32)
            * scaling
        )
        allowed = (number_own[:, None] == number_piece[None, :]) & (
            logical_piece[None, :] <= logical_own[:, None]
        )
        return (raw_scores, allowed)

    def stat_turn(running, piece_set):
        running_max, running_sum = running
        raw_scores, allowed = scores_of(piece_set[0], piece_set[2], piece_set[3])
        masked_scores = jnp.where(allowed[None], raw_scores, MASKED)
        new_max = jnp.maximum(running_max, jnp.max(masked_scores, axis=2))
        fresh = jnp.sum(
            jnp.where(allowed[None], jnp.exp(masked_scores - new_max[..., None]), 0.0), axis=2
        )
        return ((new_max, running_sum * jnp.exp(running_max - new_max) + fresh), None)

    start_max = jnp.full((local_heads, tok_rows), MASKED, jnp.float32)
    start_sum = jnp.zeros((local_heads, tok_rows), jnp.float32)
    final_max, final_sum = lax.scan(stat_turn, (start_max, start_sum), pieces)[0]
    log_total = final_max + jnp.log(final_sum)

    def out_turn(accum, piece_set):
        raw_scores, allowed = scores_of(piece_set[0], piece_set[2], piece_set[3])
        weights_low = jnp.where(
            allowed[None], jnp.exp(raw_scores - log_total[..., None]), 0.0
        ).astype(jnp.bfloat16)
        return (
            accum
            + jnp.einsum(
                "hqk,khd->qhd", weights_low, piece_set[1], preferred_element_type=jnp.float32
            ),
            None,
        )

    attended = lax.scan(out_turn, jnp.zeros((tok_rows, local_heads, HD), jnp.float32), pieces)[0]
    attended_low = attended.reshape(tok_rows, width_part).astype(jnp.bfloat16)
    attn_part = head_sums(jnp.dot(attended_low, out_full, preferred_element_type=jnp.float32))
    attn_scale = lax.rsqrt(row_single(jnp.sum(attn_part * attn_part, axis=1)) / D + EPSILON)
    residual = local_in.astype(jnp.float32) + attn_part * attn_scale[:, None] * attn_gain
    residual_full = full_rows(residual.astype(jnp.bfloat16))
    gate_proj = jnp.dot(residual_full, gate_full, preferred_element_type=jnp.float32)
    up_proj = jnp.dot(residual_full, up_full, preferred_element_type=jnp.float32)
    gate_sigmoid = jax.nn.sigmoid(gate_proj)
    mixed_hidden = (gate_proj * gate_sigmoid * up_proj).astype(jnp.bfloat16)
    ffn_part = head_sums(jnp.dot(mixed_hidden, down_full, preferred_element_type=jnp.float32))
    ffn_scale = lax.rsqrt(row_single(jnp.sum(ffn_part * ffn_part, axis=1)) / D + EPSILON)
    result = residual + ffn_part * ffn_scale[:, None] * ffn_gain
    query_full, key_full, value_full, gate_full, up_full, out_full, down_full = gather_weights(
        w_query, w_key, w_value, w_out, w_gate, w_up, w_down
    )
    grad_result = local_cot.astype(jnp.float32)
    grad_ffn, ffn_gain_term = norm_backward(grad_result, ffn_part, ffn_scale, ffn_gain)
    grad_ffn_low = full_rows(grad_ffn.astype(jnp.bfloat16))
    down_grad = jnp.einsum(
        "tf,td->fd", mixed_hidden, grad_ffn_low, preferred_element_type=jnp.float32
    )
    grad_mixed = jnp.einsum(
        "td,fd->tf", grad_ffn_low, down_full, preferred_element_type=jnp.float32
    )
    grad_gate_low = (
        grad_mixed * up_proj * gate_sigmoid * (1.0 + gate_proj * (1.0 - gate_sigmoid))
    ).astype(jnp.bfloat16)
    grad_up_low = (grad_mixed * gate_proj * gate_sigmoid).astype(jnp.bfloat16)
    gate_grad = jnp.einsum(
        "td,tf->df", residual_full, grad_gate_low, preferred_element_type=jnp.float32
    )
    up_grad = jnp.einsum(
        "td,tf->df", residual_full, grad_up_low, preferred_element_type=jnp.float32
    )
    resid_term = jnp.einsum(
        "tf,df->td", grad_gate_low, gate_full, preferred_element_type=jnp.float32
    ) + jnp.einsum("tf,df->td", grad_up_low, up_full, preferred_element_type=jnp.float32)
    grad_residual = grad_result + head_sums(resid_term)
    grad_attn, attn_gain_term = norm_backward(grad_residual, attn_part, attn_scale, attn_gain)
    grad_attn_low = full_rows(grad_attn.astype(jnp.bfloat16))
    out_grad = jnp.einsum(
        "te,td->ed", attended_low, grad_attn_low, preferred_element_type=jnp.float32
    )
    grad_heads = (
        jnp.einsum("td,ed->te", grad_attn_low, out_full, preferred_element_type=jnp.float32)
        .astype(jnp.bfloat16)
        .reshape(tok_rows, local_heads, HD)
    )
    row_delta = jnp.transpose(jnp.sum(grad_heads.astype(jnp.float32) * attended, axis=2))

    def score_grads(key_piece, value_piece, number_piece, logical_piece):
        raw_scores, allowed = scores_of(key_piece, number_piece, logical_piece)
        probabilities = jnp.where(allowed[None], jnp.exp(raw_scores - log_total[..., None]), 0.0)
        grad_probs = jnp.einsum(
            "qhd,khd->hqk", grad_heads, value_piece, preferred_element_type=jnp.float32
        )
        grad_scores = (probabilities * (grad_probs - row_delta[..., None])).astype(jnp.bfloat16)
        return (probabilities, grad_scores)

    zero_heads = jnp.zeros((tok_rows, local_heads, HD), jnp.float32)

    def back_turn(grad_acc, piece_set):
        key_piece, value_piece, number_piece, logical_piece = piece_set
        probabilities, grad_scores = score_grads(
            key_piece, value_piece, number_piece, logical_piece
        )
        grad_acc = (
            grad_acc
            + jnp.einsum("hqk,khd->qhd", grad_scores, key_piece, preferred_element_type=jnp.float32)
            * scaling
        )
        key_term = (
            jnp.einsum("hqk,qhd->khd", grad_scores, query_rot, preferred_element_type=jnp.float32)
            * scaling
        )
        value_term = jnp.einsum(
            "hqk,qhd->khd",
            probabilities.astype(jnp.bfloat16),
            grad_heads,
            preferred_element_type=jnp.float32,
        )
        return (grad_acc, (key_term, value_term))

    grad_query_rot, key_value_terms = lax.scan(back_turn, zero_heads, pieces)
    key_terms = key_value_terms[0].reshape(total_tokens, local_heads, HD)
    value_terms = key_value_terms[1].reshape(total_tokens, local_heads, HD)
    grad_key_rot, grad_value_own = (
        lax.psum_scatter(
            key_terms.astype(jnp.bfloat16), "ctx", scatter_dimension=0, tiled=True
        ).astype(jnp.float32),
        lax.psum_scatter(
            value_terms.astype(jnp.bfloat16), "ctx", scatter_dimension=0, tiled=True
        ).astype(jnp.float32),
    )
    grad_query_normed = rotate(grad_query_rot, -offset_own).reshape(tok_rows, width_part)
    grad_key_normed = rotate(grad_key_rot, -offset_own).reshape(tok_rows, width_part)
    query_gain_term = jnp.sum(grad_query_normed * query_proj * query_scale[:, None], axis=0)
    key_gain_term = jnp.sum(grad_key_normed * key_proj * key_scale[:, None], axis=0)
    weighted_query = grad_query_normed * query_gain
    weighted_key = grad_key_normed * key_gain
    query_dot, key_dot = row_pair(
        jnp.sum(weighted_query * query_proj, axis=1), jnp.sum(weighted_key * key_proj, axis=1)
    )
    grad_query_low = (
        query_scale[:, None] * weighted_query
        - query_proj * (query_scale * query_scale * query_scale * query_dot / D)[:, None]
    ).astype(jnp.bfloat16)
    grad_key_low = (
        key_scale[:, None] * weighted_key
        - key_proj * (key_scale * key_scale * key_scale * key_dot / D)[:, None]
    ).astype(jnp.bfloat16)
    grad_value_low = grad_value_own.reshape(tok_rows, width_part).astype(jnp.bfloat16)
    query_grad = jnp.einsum(
        "td,te->de", full_in, grad_query_low, preferred_element_type=jnp.float32
    )
    key_grad = jnp.einsum("td,te->de", full_in, grad_key_low, preferred_element_type=jnp.float32)
    value_grad = jnp.einsum(
        "td,te->de", full_in, grad_value_low, preferred_element_type=jnp.float32
    )
    input_term = jnp.einsum(
        "te,de->td", grad_query_low, query_full, preferred_element_type=jnp.float32
    )
    input_term = input_term + jnp.einsum(
        "te,de->td", grad_key_low, key_full, preferred_element_type=jnp.float32
    )
    input_term = input_term + jnp.einsum(
        "te,de->td", grad_value_low, value_full, preferred_element_type=jnp.float32
    )
    grad_input = grad_residual + head_sums(input_term)
    row_grads = (
        lax.psum_scatter(
            query_grad.astype(jnp.bfloat16), "ctx", scatter_dimension=0, tiled=True
        ).astype(jnp.float32),
        lax.psum_scatter(
            key_grad.astype(jnp.bfloat16), "ctx", scatter_dimension=0, tiled=True
        ).astype(jnp.float32),
        lax.psum_scatter(
            value_grad.astype(jnp.bfloat16), "ctx", scatter_dimension=0, tiled=True
        ).astype(jnp.float32),
        lax.psum_scatter(
            gate_grad.astype(jnp.bfloat16), "ctx", scatter_dimension=0, tiled=True
        ).astype(jnp.float32),
        lax.psum_scatter(
            up_grad.astype(jnp.bfloat16), "ctx", scatter_dimension=0, tiled=True
        ).astype(jnp.float32),
    )
    col_grads = (
        lax.psum_scatter(
            out_grad.astype(jnp.bfloat16), "ctx", scatter_dimension=1, tiled=True
        ).astype(jnp.float32),
        lax.psum_scatter(
            down_grad.astype(jnp.bfloat16), "ctx", scatter_dimension=1, tiled=True
        ).astype(jnp.float32),
    )
    gain_totals = lax.psum((query_gain_term, key_gain_term, attn_gain_term, ffn_gain_term), "ctx")
    back_result, back_grad = (
        lax.all_to_all(result.astype(jnp.bfloat16), "ctx", split_axis=0, concat_axis=0, tiled=True),
        lax.all_to_all(
            grad_input.astype(jnp.bfloat16), "ctx", split_axis=0, concat_axis=0, tiled=True
        ),
    )
    return (
        undeal(back_result),
        undeal(back_grad),
        row_grads[0],
        row_grads[1],
        row_grads[2],
        col_grads[0],
        row_grads[3],
        row_grads[4],
        col_grads[1],
        gain_totals[0],
        gain_totals[1],
        gain_totals[2],
        gain_totals[3],
    )


def sharded(layer, mesh, ctx, head):
    wide, tall, line = P(ctx, head), P(head, ctx), P(head)
    return jax.shard_map(
        layer,
        mesh=mesh,
        in_specs=(
            *(wide,) * 5,
            tall,
            wide,
            wide,
            tall,
            *(line,) * 4,
            P(),
            P(),
        ),
        out_specs=(*(wide,) * 5, tall, wide, wide, tall, *(line,) * 4),
        check_vma=False,
    )


def solution(mesh):
    if dict(mesh.shape) == {"ctx": 8, "head": 4}:
        split = Mesh(mesh.devices.reshape(4, 2, 2, 2), AXES)
        return sharded(plane_layer, split, CTX, ("x", "core"))
    return sharded(on_device, mesh, "ctx", "head")
```

```python
import math

import jax
import jax.numpy as jnp
import numpy as np
from jax import lax
from jax.experimental import pallas as pl
from jax.experimental.pallas import tpu as pltpu
from jax.sharding import Mesh
from jax.sharding import PartitionSpec as P

D = 2048
HD = 128


EPSILON = 1e-06
ROPE_THETA = 500000.0
MASKED = -1e30


BF = jnp.bfloat16
F32 = jnp.float32
MESH = pl.DeviceIdType.MESH
AXES = ("z", "y", "x", "core")
CTX = ("z", "y")
STRIP = 16
ANY = pl.BlockSpec(memory_space=pl.ANY)
VMEM = pl.BlockSpec(memory_space=pltpu.VMEM)
DMA = pltpu.SemaphoreType.DMA
BIG_VMEM = 60 * 1024 * 1024


def place():
    return tuple(lax.axis_index(name) for name in AXES)


def greet(targets):
    barrier = pltpu.get_barrier_semaphore()
    for target in targets:
        pl.semaphore_signal(barrier, inc=1, device_id=target, device_id_type=MESH)
    pl.semaphore_wait(barrier, len(targets))


def near_first(step, z):
    high = z // 2
    low = z + high * (3 - 2 * z)
    value = (low, 1 - low, 2, 3)[step]
    return value + high * (3 - 2 * value)


def plane_axes(me, turn):
    z, y, x, k = me
    a = x * (1 - turn) + y * turn
    b = y * (1 - turn) + x * turn

    def slot(zp, ap, bp):
        yp = bp * (1 - turn) + ap * turn
        xp = ap * (1 - turn) + bp * turn
        return zp * 4 + yp * 2 + xp

    dev_a = (z, y * (1 - turn) + (1 - y) * turn, (1 - x) * (1 - turn) + x * turn, k)
    dev_b = (z, (1 - y) * (1 - turn) + y * turn, x * (1 - turn) + (1 - x) * turn, k)
    return a, b, slot, dev_a, dev_b


EVEN = ((0, 1),) * 4
MORE_X = ((0, 1), (1, 1)) * 2
ALL_X = ((1, 1),) * 4
TURNS_OPEN = ALL_X
TURNS_ATTENTION = (MORE_X, EVEN)
TURNS_FFN_BACK = (EVEN, EVEN)
TURNS_CLOSE = ALL_X


def layer_axes(me, turns):
    return [plane_axes(me, t0 + me[3] * (t1 - t0)) for t0, t1 in turns]


def greet_plane(me, others=()):
    z, y, x, k = me
    barrier = pltpu.get_barrier_semaphore()
    targets = [(z, 1 - y, x, k), (z, y, 1 - x, k), *others]
    for target in targets:
        pl.semaphore_signal(barrier, inc=1, device_id=target, device_id_type=MESH)

    @pl.when(z < 3)
    def _():
        pl.semaphore_signal(barrier, inc=1, device_id=(z + 1, y, x, k), device_id_type=MESH)

    @pl.when(z > 0)
    def _():
        pl.semaphore_signal(barrier, inc=1, device_id=(z - 1, y, x, k), device_id_type=MESH)

    inner = (z + 2) // 3 - z // 3
    pl.semaphore_wait(barrier, len(targets) + 1 + inner)


GATHER_SEMS = [DMA((16,)), DMA((4,)), DMA((4,)), DMA((4,)), DMA((8,))]


DEAL_ORDER = (4, 1, 5, 2, 6, 3, 7)
OPEN_DEAL = 0
OPEN_RATE = 2
DEALT_FIRST = 5
FORWARD_RATE = 1
FORWARD_EVERY = 1
BACK_EVERY = 1
BACK_RATE = 1
CLOSE_FIRST = 0
CLOSE_NEXT = 4
SUM_LAG = 1
EARLY_LAYERS = True
BACK_LAG = 1
CLOSE_LAG = 2
CLOSE_RATE = 1


class Trickle:
    def __init__(self):
        self.waiting = []
        self.calls = 0

    def add(self, copies):
        self.waiting.extend(copies)

    def tick(self, count=1, every=1):
        self.calls += 1
        if self.calls % every:
            return
        for start in self.waiting[:count]:
            start()
        self.waiting = self.waiting[count:]

    def flush(self):
        self.tick(len(self.waiting))


def gather_plane(
    me,
    own_ref,
    view,
    sems,
    turns,
    between=lambda step: None,
    arrived=None,
    tick=lambda: None,
    early=False,
):
    z, y, x, k = me
    recv, up_send, down_send, a_send, b_send = sems
    axes = layer_axes(me, turns)

    def copy(src, index, send_sem, device):
        return pltpu.make_async_remote_copy(
            src_ref=src,
            dst_ref=view(index),
            send_sem=send_sem,
            recv_sem=recv.at[index],
            device_id=device,
            device_id_type=MESH,
        )

    def landed(index):
        copy(view(index), index, a_send.at[0], axes[0][3]).wait_recv()

    def layer_landed(step):
        tick()
        a, b, slot, dev_a, dev_b = axes[step]
        zp = near_first(step, z)
        landed(slot(zp, a, 1 - b))
        landed(slot(zp, 1 - a, 1 - b))
        if arrived is not None:
            arrived(step)

    for step in range(5):
        if step < 4:
            a, b, slot, dev_a, dev_b = axes[step]
            zp = near_first(step, z)
            index = slot(zp, a, b)
            if step == 0:
                src = own_ref
            else:
                landed(index)
                src = view(index)

            @pl.when((zp <= z) & (z < 3))
            def _():
                copy(src, index, up_send.at[zp], (z + 1, y, x, k)).start()

            @pl.when((zp >= z) & (z > 0))
            def _():
                copy(src, index, down_send.at[zp], (z - 1, y, x, k)).start()

            copy(src, index, a_send.at[step], dev_a).start()
            copy(src, index, b_send.at[step], dev_b).start()
            tick()
        if step > 0:
            a, b, slot, dev_a, dev_b = axes[step - 1]
            index = slot(near_first(step - 1, z), 1 - a, b)
            landed(index)
            copy(view(index), index, b_send.at[3 + step], dev_b).start()
            tick()
        between(step)
        if step >= 2 and early:
            layer_landed(step - 2)
    for step in ((3,) if early else range(4)):
        layer_landed(step)
    for step in range(4):
        a, b, slot, dev_a, dev_b = axes[step]
        zp = near_first(step, z)
        for ap, number in ((a, step), (1 - a, 4 + step)):
            index = slot(zp, ap, b)
            copy(view(index), index, b_send.at[number], dev_b).wait_send()
        index = slot(zp, a, b)
        copy(view(index), index, a_send.at[step], dev_a).wait_send()

        @pl.when((zp <= z) & (z < 3))
        def _():
            copy(view(index), index, up_send.at[zp], (z + 1, y, x, k)).wait_send()

        @pl.when((zp >= z) & (z > 0))
        def _():
            copy(view(index), index, down_send.at[zp], (z - 1, y, x, k)).wait_send()


def reduce_scratch(rows, width):
    return [
        pltpu.VMEM((4, 2, rows, width), BF),
        pltpu.VMEM((4, rows, width), BF),
        pltpu.VMEM((4, rows, width), BF),
        pltpu.VMEM((4, rows, width), BF),
        pltpu.VMEM((4, rows, width), BF),
        pltpu.VMEM((4, rows, width), BF),
        DMA((8,)),
        DMA((8,)),
        DMA((4,)),
        DMA((4,)),
        DMA((4,)),
        DMA((4,)),
        DMA((4,)),
    ]


N_REDUCE = 13


def strips(rows, work, strip=STRIP):
    def body(i, carry):
        work(pl.ds(pl.multiple_of(i * strip, strip), strip))
        return carry

    lax.fori_loop(0, rows // strip, body, 0)


def reduce_plane(
    me,
    terms,
    rows,
    scratch,
    turns,
    produce,
    finish,
    after_terms=lambda: None,
    tick=lambda: None,
):
    z, y, x, k = me
    (from_b, to_a, from_a, to_z, from_low, from_high) = scratch[:6]
    (b_send, b_recv, a_send, a_recv, z_send, low_recv, high_recv) = scratch[6:]
    axes = layer_axes(me, turns)[::-1]
    order = [near_first(step, z) for step in (3, 2, 1, 0)]

    def start_of(step, ap, bp):
        return pl.multiple_of(axes[step][2](order[step], ap, bp) * rows, rows)

    def copy_b(step, flip):
        a, b, slot, dev_a, dev_b = axes[step]
        zp, ap = order[step], (1 - a if flip else a)
        return pltpu.make_async_remote_copy(
            src_ref=terms.at[pl.ds(start_of(step, ap, 1 - b), rows), :],
            dst_ref=from_b.at[zp, ap],
            send_sem=b_send.at[zp * 2 + ap],
            recv_sem=b_recv.at[zp * 2 + ap],
            device_id=dev_b,
            device_id_type=MESH,
        )

    def copy_a(step):
        zp, dev_a = order[step], axes[step][3]
        return pltpu.make_async_remote_copy(
            src_ref=to_a.at[zp],
            dst_ref=from_a.at[zp],
            send_sem=a_send.at[zp],
            recv_sem=a_recv.at[zp],
            device_id=dev_a,
            device_id_type=MESH,
        )

    def copy_z(zp, target, recv, to):
        return pltpu.make_async_remote_copy(
            src_ref=to_z.at[zp],
            dst_ref=target.at[zp],
            send_sem=z_send.at[zp],
            recv_sem=recv.at[zp],
            device_id=(to, y, x, k),
            device_id_type=MESH,
        )

    def copy_up(zp):
        return copy_z(zp, from_low, low_recv, z + 1)

    def copy_down(zp):
        return copy_z(zp, from_high, high_recv, z - 1)

    def mine(step, flip, strip):
        a, b = axes[step][:2]
        at = start_of(step, 1 - a if flip else a, b) + strip.start
        return terms[pl.ds(pl.multiple_of(at, STRIP), STRIP), :].astype(F32)

    for step in range(4):
        produce(order[step])
        for flip in (True, False):
            copy_b(step, flip).start()
        tick()
    after_terms()

    for step in range(4 + SUM_LAG):
        if step < 4:
            copy_b(step, True).wait_recv()

            def first(strip, step=step):
                zp, ap = order[step], 1 - axes[step][0]
                to_a[zp, strip] = (
                    mine(step, True, strip) + from_b[zp, ap, strip].astype(F32)
                ).astype(BF)

            strips(rows, first)
            copy_a(step).start()
            tick()
        if step >= SUM_LAG:
            done = step - SUM_LAG
            tick()
            copy_b(done, False).wait_recv()
            copy_a(done).wait_recv()

            def own_sum(strip, last=done):
                zp, ap = order[last], axes[last][0]
                return (
                    mine(last, False, strip)
                    + from_b[zp, ap, strip].astype(F32)
                    + from_a[zp, strip].astype(F32)
                )

            if done < 3:
                zp = order[done]
                upward = zp > z

                @pl.when(upward & (z > 0))
                def _(zp=zp, own_sum=own_sum):
                    copy_up(zp).wait_recv()

                    def work(strip):
                        to_z[zp, strip] = (own_sum(strip) + from_low[zp, strip].astype(F32)).astype(BF)

                    strips(rows, work)

                @pl.when(jnp.logical_not(upward) & (z < 3))
                def _(zp=zp, own_sum=own_sum):
                    copy_down(zp).wait_recv()

                    def work(strip):
                        to_z[zp, strip] = (own_sum(strip) + from_high[zp, strip].astype(F32)).astype(BF)

                    strips(rows, work)

                @pl.when((z == 0) | (z == 3))
                def _(zp=zp, own_sum=own_sum):
                    def work(strip):
                        to_z[zp, strip] = own_sum(strip).astype(BF)

                    strips(rows, work)

                @pl.when(upward)
                def _(zp=zp):
                    copy_up(zp).start()

                @pl.when(jnp.logical_not(upward))
                def _(zp=zp):
                    copy_down(zp).start()

            else:

                @pl.when(z == 0)
                def _():
                    copy_down(z).wait_recv()
                    strips(rows, lambda s: finish(s, own_sum(s) + from_high[z, s].astype(F32)))

                @pl.when(z == 3)
                def _():
                    copy_up(z).wait_recv()
                    strips(rows, lambda s: finish(s, own_sum(s) + from_low[z, s].astype(F32)))

                @pl.when((z > 0) & (z < 3))
                def _():
                    copy_up(z).wait_recv()
                    copy_down(z).wait_recv()
                    strips(
                        rows,
                        lambda s: finish(
                            s,
                            own_sum(s) + from_low[z, s].astype(F32) + from_high[z, s].astype(F32),
                        ),
                    )

    def settle():
        for step in range(4):
            copy_b(step, True).wait_send()
            copy_b(step, False).wait_send()
            copy_a(step).wait_send()
        for zp in order[:3]:
            copy_up(zp).wait_send()

    return settle


def own_tile(me):
    z, y, x, k = me
    return z * 2 + y


def gather_view(out_ref, rows):
    def view(slot):
        return out_ref.at[pl.ds(pl.multiple_of(slot * rows, rows), rows), :]

    return view


def hand_out_copies(me, own_ref, out_ref, send, recv):
    z, y, x, k = me
    rows, width = own_ref.shape
    part = width // 4
    target_rows = pl.ds(pl.multiple_of(k * 2 * rows + x * rows, rows), rows)

    def copy(xt, kt, number):
        return pltpu.make_async_remote_copy(
            src_ref=own_ref.at[:, pl.ds(pl.multiple_of((2 * xt + kt) * part, part), part)],
            dst_ref=out_ref.at[target_rows, :],
            send_sem=send.at[number],
            recv_sem=recv.at[number],
            device_id=(z, y, xt, kt),
            device_id_type=MESH,
        )

    local = pltpu.make_async_copy(
        own_ref.at[:, pl.ds(pl.multiple_of((2 * x + k) * part, part), part)],
        out_ref.at[target_rows, :],
        recv.at[3],
    )
    return [copy(x, 1 - k, 0), copy(1 - x, k, 1), copy(1 - x, 1 - k, 2)], local


def pair_devices(me):
    z, y, x, k = me
    return [(z, y, x, 1 - k), (z, y, 1 - x, 1 - k)]


def row_scale(values):
    return lax.rsqrt(jnp.sum(values * values, axis=1, keepdims=True) / values.shape[1] + EPSILON)


def norm_back_strip(grad, values, gain):
    scale = row_scale(values)
    term = grad * values * scale
    weighted = grad * gain
    dot = jnp.sum(weighted * values, axis=1, keepdims=True)
    back = scale * weighted - values * (scale * scale * scale * dot / values.shape[1])
    return back, term[:8] + term[8:]


def comm_call(body, name, number, out_shape, in_specs, out_specs, scratch, lift=True):
    lifted = [i for i, spec in enumerate(in_specs) if spec is VMEM] if lift else []
    leaving = [i for i, spec in enumerate(out_specs) if spec is VMEM]
    first_out = len(in_specs)

    def with_copies(*refs):
        refs = list(refs)
        sems = refs.pop()
        count = len(lifted) + len(leaving)
        held = refs[len(refs) - count :]
        refs = refs[: len(refs) - count]
        loads, stores, begun = [], [], []
        for n, i in enumerate(lifted):
            loads.append(pltpu.make_async_copy(refs[i], held[n], sems.at[n]))
            refs[i] = held[n]
        for n, i in enumerate(leaving, len(lifted)):
            stores.append((held[n], pltpu.make_async_copy(held[n], refs[first_out + i], sems.at[n])))
            refs[first_out + i] = held[n]
        for copy in loads:
            copy.start()

        def loaded():
            for copy in loads:
                copy.wait()

        def leave(*done):
            for ref, copy in stores:
                if any(ref is other for other in done):
                    copy.start()
                    begun.append(ref)

        body(*refs, loaded=loaded, leave=leave)
        leave(*[ref for ref, _ in stores if not any(ref is other for other in begun)])
        for _, copy in stores:
            copy.wait()

    def call(*args):
        extra = [pltpu.VMEM(args[i].shape, args[i].dtype) for i in lifted]
        extra += [pltpu.VMEM(out_shape[i].shape, out_shape[i].dtype) for i in leaving]
        return pl.pallas_call(
            with_copies,
            name=name,
            out_shape=out_shape,
            in_specs=[ANY if i in lifted else spec for i, spec in enumerate(in_specs)],
            out_specs=tuple(ANY for _ in out_specs),
            scratch_shapes=[*scratch, *extra, DMA((len(extra),))],
            compiler_params=pltpu.CompilerParams(
                collective_id=number, has_side_effects=True, vmem_limit_bytes=BIG_VMEM
            ),
        )(*args)

    return call


def same_x_greet(me):
    z, y, x, k = me
    barrier = pltpu.get_barrier_semaphore()
    number = z * 4 + y * 2 + k

    def body(i, carry):
        other = lax.rem(number + i, 16)
        pl.semaphore_signal(
            barrier,
            inc=1,
            device_id=(other // 4, (other // 2) % 2, x, other % 2),
            device_id_type=MESH,
        )
        return carry

    lax.fori_loop(1, 16, body, 0)
    for kt in (k, 1 - k):
        pl.semaphore_signal(barrier, inc=1, device_id=(z, y, 1 - x, kt), device_id_type=MESH)
    pl.semaphore_wait(barrier, 17)


def masked_scores(q, keys, low, high, logical):
    raw = lax.dot_general(q, keys, (((1,), (1,)), ((), ())), preferred_element_type=F32)
    allowed = (logical >= low) & (logical <= high)
    return raw * (1.0 / math.sqrt(HD)), allowed


def eye_mask():
    return lax.broadcasted_iota(jnp.int32, (HD, HD), 0) == lax.broadcasted_iota(
        jnp.int32, (HD, HD), 1
    )


def column_to_row(column, eye):
    return jnp.sum(jnp.where(eye, column, 0.0), axis=0, keepdims=True)


def row_to_column(row, eye):
    return jnp.sum(jnp.where(eye, row, 0.0), axis=1, keepdims=True)


def open_layer(
    inputs,
    cotangent,
    w_query,
    w_key,
    w_value,
    w_out,
    w_gate,
    w_up,
    w_down,
    query_gain,
    key_gain,
    attn_gain,
    ffn_gain,
    order,
    lengths,
    frequency,
):
    rows, part = inputs.shape
    half = rows // 2
    quarter = half // 2
    tokens, width = 8 * half, 4 * part
    hidden = w_gate.shape[1]
    down = hidden // 8

    def body(*refs, loaded, leave):
        (in_ref, cot_ref, wq_ref, wk_ref, wv_ref, wo_ref, wg_ref, wu_ref, wd_ref) = refs[:9]
        gain_parts = refs[9:13]
        (order_ref, lengths_ref, frequency_ref) = refs[13:16]
        (cos_ref, sin_ref, low_ref, high_ref, log_ref) = refs[27:32]
        gain_ref = refs[-1]
        refs = refs[:10] + refs[16:27] + refs[32:-1]
        (full_out, own_out, own_cot_ref, wqkv_ref, wout_ref, gains_ref, gu_out, down_ref) = refs[10:18]
        (q_ref, k_ref, v_ref) = refs[18:21]
        (full_ref, shard, cot_half, qkv_raw, out_raw, gu_raw, d_raw) = refs[21:28]
        (qkv_stage, out_stage, gu_stage, d_stage) = refs[28:32]
        (load_sem, pair_send, pair_recv, local_sem, deal_send, deal_recv) = refs[32:38]
        (share_send, share_recv, gain_send, gain_recv, cot_sems, keep_sem) = refs[38:44]
        (down_send, down_recv) = refs[44:46]
        gather_sems = refs[46:]
        me = z, y, x, k = place()
        ctx = own_tile(me)
        sibling = (z, y, x, 1 - k)

        loads = [
            pltpu.make_async_copy(src, dst, load_sem.at[i])
            for i, (src, dst) in enumerate(
                [
                    (wq_ref, qkv_raw.at[0]),
                    (wk_ref, qkv_raw.at[1]),
                    (wv_ref, qkv_raw.at[2]),
                    (wo_ref, out_raw),
                    (wg_ref, gu_raw.at[0]),
                    (wu_ref, gu_raw.at[1]),
                    (wd_ref, d_raw),
                ]
            )
        ]
        for load in loads:
            load.start()
        same_x_greet(me)
        loaded()

        def pair_copy(src, dst, number):
            columns = pl.ds(pl.multiple_of(k * part, part), part)
            remote = pltpu.make_async_remote_copy(
                src_ref=src.at[pl.ds(pl.multiple_of((1 - k) * half, half), half), :],
                dst_ref=dst.at[:, columns],
                send_sem=pair_send.at[number],
                recv_sem=pair_recv.at[number],
                device_id=sibling,
                device_id_type=MESH,
            )
            local = pltpu.make_async_copy(
                src.at[pl.ds(pl.multiple_of(k * half, half), half), :],
                dst.at[:, columns],
                local_sem.at[number],
            )
            remote.start()
            local.start()
            return remote, local

        first = pair_copy(in_ref, shard, 0)
        second = pair_copy(cot_ref, cot_half, 1)

        for i, gain_part in enumerate(gain_parts):
            gain_ref[i : i + 1, :] = gain_part[...]

        def gain_copy(xt, kt, number):
            return pltpu.make_async_remote_copy(
                src_ref=gain_ref,
                dst_ref=gains_ref.at[:, pl.ds(pl.multiple_of((2 * x + k) * part, part), part)],
                send_sem=gain_send.at[number],
                recv_sem=gain_recv.at[number],
                device_id=(z, y, xt, kt),
                device_id_type=MESH,
            )

        gain_copies = [gain_copy(x, 1 - k, 0), gain_copy(1 - x, k, 1), gain_copy(1 - x, 1 - k, 2)]
        for copy in gain_copies:
            copy.start()
        gain_local = pltpu.make_async_copy(
            gain_ref,
            gains_ref.at[:, pl.ds(pl.multiple_of((2 * x + k) * part, part), part)],
            local_sem.at[2],
        )
        gain_local.start()

        first[0].wait_recv()
        first[1].wait()

        def view(slot):
            return full_ref.at[
                pl.ds(pl.multiple_of((slot // 2) * half, half), half),
                pl.ds(pl.multiple_of((slot % 2) * 2 * part, 2 * part), 2 * part),
            ]

        own_slot = ctx * 2 + x
        own_local = pltpu.make_async_copy(shard, view(own_slot), local_sem.at[3])
        own_local.start()

        def deal(e):
            j, r = e // 2, e % 2
            return [
                pltpu.make_async_remote_copy(
                    src_ref=src,
                    dst_ref=dst,
                    send_sem=deal_send.at[i, e],
                    recv_sem=deal_recv.at[i, ctx],
                    device_id=(2 * k + e // 4, (e // 2) % 2, x, r),
                    device_id_type=MESH,
                )
                for i, (src, dst) in enumerate(deal_ends(j, r))
            ]

        def deal_ends(j, r):
            at = pl.ds(pl.multiple_of(ctx * 2 * HD + r * HD, HD), HD)
            return (
                (
                    qkv_stage.at[:, r * HD : (r + 1) * HD, j * HD : (j + 1) * HD],
                    wqkv_ref.at[:, at, :],
                ),
                (
                    out_stage.at[j * HD : (j + 1) * HD, r * HD : (r + 1) * HD],
                    wout_ref.at[:, at],
                ),
            )

        trickle = Trickle()
        stays = k == z // 2
        own_e = (z % 2) * 4 + y * 2 + k

        def deal_all():
            for load in loads[:4]:
                load.wait()

            def round_qkv(s):
                for i in range(3):
                    qkv_stage[i, s] = qkv_raw[i, s].astype(BF)

            strips(rows, round_qkv)

            def round_out(s):
                out_stage[s] = out_raw[s].astype(BF)

            strips(2 * rows, round_out, 32)
            if OPEN_DEAL == 0:
                begin_deal()

        def begin_deal():
            trickle.add([lambda e=e: deal_start(e) for e in range(8)])

        def deal_start(e):
            @pl.when(jnp.logical_not(stays & (own_e == e)))
            def _():
                for copy in deal(e):
                    copy.start()

            @pl.when(stays & (own_e == e))
            def _():
                for i, (src, dst) in enumerate(deal_ends(e // 2, e % 2)):
                    pltpu.make_async_copy(src, dst, deal_recv.at[i, ctx]).start()

        def cot_begin():
            second[0].wait_recv()
            second[1].wait()
            cot_remote.start()
            cot_local.start()

        wide = pl.ds(pl.multiple_of(x * 2 * part, 2 * part), 2 * part)
        cot_remote = pltpu.make_async_remote_copy(
            src_ref=cot_half.at[pl.ds(pl.multiple_of((1 - x) * quarter, quarter), quarter), :],
            dst_ref=own_cot_ref.at[:, wide],
            send_sem=cot_sems.at[0],
            recv_sem=cot_sems.at[1],
            device_id=(z, y, 1 - x, k),
            device_id_type=MESH,
        )
        cot_local = pltpu.make_async_copy(
            cot_half.at[pl.ds(pl.multiple_of(x * quarter, quarter), quarter), :],
            own_cot_ref.at[:, wide],
            cot_sems.at[2],
        )

        keeps = [
            pltpu.make_async_copy(gu_stage.at[0], gu_out.at[0], keep_sem.at[0]),
            pltpu.make_async_copy(gu_stage.at[1], gu_out.at[1], keep_sem.at[1]),
            pltpu.make_async_copy(
                d_stage.at[pl.ds(pl.multiple_of(ctx * down, down), down), :],
                down_ref.at[:, pl.ds(pl.multiple_of(ctx * rows, rows), rows)],
                keep_sem.at[2],
            ),
        ]

        def down_copy(t):
            to = ctx + t - 8 * ((ctx + t) // 8)
            return pltpu.make_async_remote_copy(
                src_ref=d_stage.at[pl.ds(pl.multiple_of(to * down, down), down), :],
                dst_ref=down_ref.at[:, pl.ds(pl.multiple_of(ctx * rows, rows), rows)],
                send_sem=down_send.at[t],
                recv_sem=down_recv.at[t],
                device_id=(to // 2, to % 2, x, k),
                device_id_type=MESH,
            )

        def down_landed(t):
            c = ctx + 8 - t - 8 * ((ctx + 8 - t) // 8)
            part_of = down_ref.at[:, pl.ds(pl.multiple_of(c * rows, rows), rows)]
            pltpu.make_async_remote_copy(
                src_ref=part_of,
                dst_ref=part_of,
                send_sem=down_send.at[t],
                recv_sem=down_recv.at[t],
                device_id=sibling,
                device_id_type=MESH,
            ).wait_recv()

        def deal_down():
            trickle.add([lambda t=t: down_copy(t).start() for t in DEAL_ORDER])

        def round_up(i):
            loads[4 + i].wait()

            def work(s):
                gu_stage[i, s] = gu_raw[i, s].astype(BF)

            strips(rows, work)
            keeps[i].start()

        def round_down():
            loads[6].wait()

            def work(s):
                d_stage[s] = d_raw[s].astype(BF)

            strips(hidden, work, 128)
            keeps[2].start()

        def positions():
            blocks = order_ref.shape[1]
            square = lax.broadcasted_iota(jnp.int32, (blocks, blocks), 0)
            square = square == lax.broadcasted_iota(jnp.int32, (blocks, blocks), 1)
            column = row_to_column(order_ref[...].astype(F32), square)
            lane = lax.broadcasted_iota(jnp.int32, (1, 2 * tokens), 1)
            other = (lane >= tokens).astype(jnp.int32)
            core = k + other - 2 * k * other
            lane = lane - tokens * other
            in_half = lane & (half - 1)
            block_rows = 2 * tokens // blocks
            block = (lane - in_half) // half * (2 * half // block_rows)
            block = block + core * (half // block_rows)
            block = block + (in_half - (in_half & (block_rows - 1))) // block_rows
            match = lax.broadcasted_iota(jnp.int32, (blocks, 2 * tokens), 0) == block
            first_of = jnp.sum(jnp.where(match, column, 0.0), axis=0, keepdims=True) * block_rows
            logical = first_of + (in_half & (block_rows - 1)).astype(F32)
            log_ref[...] = logical
            own = logical[:, :tokens]
            begin = jnp.zeros_like(own)
            end = jnp.zeros((1, 1), F32)
            for j in range(lengths_ref.shape[1]):
                length = lengths_ref[:, j : j + 1].astype(F32)
                end = end + length
                begin = begin + jnp.where(own >= end, length, 0.0)
            eye = eye_mask()
            for i in range(tokens // HD):
                piece = slice(i * HD, (i + 1) * HD)
                low = row_to_column(begin[:, piece], eye)
                high = row_to_column(own[:, piece], eye)
                low_ref[piece, :] = low
                high_ref[piece, :] = high
                angles = (high - low) * frequency_ref[...]
                cos_ref[piece, :] = jnp.cos(angles)
                sine = jnp.sin(angles)
                left = lax.broadcasted_iota(jnp.int32, (HD, HD), 1) < HD // 2
                sin_ref[piece, :] = jnp.where(left, -sine, sine)
            leave(cos_ref, sin_ref, low_ref, high_ref, log_ref)

        between = [
            deal_all,
            lambda: (cot_begin(), round_down()),
            lambda: (round_up(0), round_up(1)),
            positions,
            lambda: None,
        ]

        def open_between(step):
            if 0 < step == OPEN_DEAL:
                begin_deal()
            if step == max(OPEN_DEAL, 1):
                if step == 1:
                    between[1]()
                deal_down()
                if step == 1:
                    return
            between[step]()

        def deal_wait(c):
            at = slice(c * 2 * HD, c * 2 * HD + HD)
            pltpu.make_async_copy(
                qkv_stage.at[:, :HD, :HD], wqkv_ref.at[:, at, :], deal_recv.at[0, c]
            ).wait()
            pltpu.make_async_copy(
                out_stage.at[:HD, :HD], wout_ref.at[:, at], deal_recv.at[1, c]
            ).wait()

        def share(c, r):
            at = pl.ds(pl.multiple_of(c * 2 * HD + r * HD, HD), HD)
            return [
                pltpu.make_async_remote_copy(
                    src_ref=ref,
                    dst_ref=ref,
                    send_sem=share_send.at[i, c],
                    recv_sem=share_recv.at[i, c],
                    device_id=sibling,
                    device_id_type=MESH,
                )
                for i, ref in enumerate((wqkv_ref.at[:, at, :], wout_ref.at[:, at]))
            ]

        def project_layer(step):
            if step == 0:
                trickle.flush()
                own_local.wait()
                for c in range(8):
                    deal_wait(c)
                    for copy in share(c, k):
                        copy.start()
                for c in range(8):
                    for copy in share(c, 1 - k):
                        copy.wait_recv()
                leave(wqkv_ref, wout_ref)
            at = pl.ds(pl.multiple_of(near_first(step, z) * 2 * half, 2 * half), 2 * half)
            tile = full_ref[at, :]
            q_ref[at, :] = jnp.dot(tile, wqkv_ref[0], preferred_element_type=F32)
            k_ref[at, :] = jnp.dot(tile, wqkv_ref[1], preferred_element_type=F32)
            v_ref[at, :] = jnp.dot(tile, wqkv_ref[2], preferred_element_type=F32).astype(BF)

        gather_plane(
            me,
            shard,
            view,
            gather_sems,
            TURNS_OPEN,
            open_between,
            project_layer,
            lambda: trickle.tick(OPEN_RATE),
        )

        full_keep = pltpu.make_async_copy(full_ref, full_out, keep_sem.at[3])
        full_keep.start()
        own_rows = pl.ds(pl.multiple_of(own_slot * quarter, quarter), quarter)
        own_keep = pltpu.make_async_copy(full_ref.at[own_rows, :], own_out, keep_sem.at[4])
        own_keep.start()
        for e in range(8):

            @pl.when(jnp.logical_not(stays & (own_e == e)))
            def _(e=e):
                for copy in deal(e):
                    copy.wait_send()

        for c in range(8):
            for copy in share(c, k):
                copy.wait_send()
        first[0].wait_send()
        second[0].wait_send()
        for copy in gain_copies:
            copy.wait()
        gain_local.wait()
        cot_remote.wait()
        cot_local.wait()
        for keep in (*keeps, full_keep, own_keep):
            keep.wait()
        for t in range(1, 8):
            down_landed(t)
            down_copy(t).wait_send()

    shape = jax.ShapeDtypeStruct
    return comm_call(
        body,
        "open_layer",
        0,
        (
            shape((tokens, width), BF),
            shape((quarter, width), BF),
            shape((quarter, width), BF),
            shape((3, width, HD), BF),
            shape((HD, width), BF),
            shape((4, width), F32),
            shape((2, rows, hidden), BF),
            shape((down, width), BF),
            shape((tokens, HD), F32),
            shape((tokens, HD), F32),
            shape((tokens, HD), BF),
            shape((tokens, HD), F32),
            shape((tokens, HD), F32),
            shape((tokens, 1), F32),
            shape((tokens, 1), F32),
            shape((1, 2 * tokens), F32),
        ),
        [*[ANY] * 9, *[VMEM] * 7],
        (ANY, ANY, ANY, VMEM, VMEM, ANY, ANY, ANY, VMEM, VMEM, VMEM, *[VMEM] * 5),
        [
            pltpu.VMEM((tokens, width), BF),
            pltpu.VMEM((half, 2 * part), BF),
            pltpu.VMEM((half, 2 * part), BF),
            pltpu.VMEM((3, rows, part), F32),
            pltpu.VMEM((part, rows), F32),
            pltpu.VMEM((2, rows, hidden), F32),
            pltpu.VMEM((hidden, rows), F32),
            pltpu.VMEM((3, rows, part), BF),
            pltpu.VMEM((part, rows), BF),
            pltpu.VMEM((2, rows, hidden), BF),
            pltpu.VMEM((hidden, rows), BF),
            DMA((7,)),
            DMA((2,)),
            DMA((2,)),
            DMA((4,)),
            DMA((2, 8)),
            DMA((2, 8)),
            DMA((2, 8)),
            DMA((2, 8)),
            DMA((3,)),
            DMA((3,)),
            DMA((3,)),
            DMA((5,)),
            DMA((8,)),
            DMA((8,)),
            *GATHER_SEMS,
            pltpu.VMEM((4, part), F32),
        ],
        lift=False,
    )(
        inputs,
        cotangent,
        w_query,
        w_key,
        w_value,
        w_out,
        w_gate,
        w_up,
        w_down,
        query_gain,
        key_gain,
        attn_gain,
        ffn_gain,
        order,
        lengths,
        frequency,
    )


def plane_peer(me, i):
    z, y, x, k = me
    other = lax.rem(z * 4 + y * 2 + x + i, 16)
    return other, (other // 4, (other // 2) % 2, other % 2, k)


def plane_greet_all(me, others):
    barrier = pltpu.get_barrier_semaphore()

    def call(i, carry):
        pl.semaphore_signal(barrier, inc=1, device_id=plane_peer(me, i)[1], device_id_type=MESH)
        return carry

    lax.fori_loop(1, 16, call, 0)
    for other in others:
        pl.semaphore_signal(barrier, inc=1, device_id=other, device_id_type=MESH)
    pl.semaphore_wait(barrier, 15 + len(others))


def sum_begin(me, slots, send, recv):
    own = me[0] * 4 + me[1] * 2 + me[2]

    def copy(i, slot):
        return pltpu.make_async_remote_copy(
            src_ref=slots.at[slot],
            dst_ref=slots.at[slot],
            send_sem=send.at[i],
            recv_sem=recv.at[slot],
            device_id=plane_peer(me, i)[1],
            device_id_type=MESH,
        )

    def begin(i, carry):
        copy(i, own).start()
        return carry

    def landed(i, carry):
        copy(i, plane_peer(me, i)[0]).wait_recv()
        return carry

    def sent(i, carry):
        copy(i, own).wait_send()
        return carry

    lax.fori_loop(1, 16, begin, 0)

    def end():
        lax.fori_loop(1, 16, landed, 0)
        lax.fori_loop(1, 16, sent, 0)
        total = slots[0]
        for i in range(1, 16):
            total = total + slots[i]
        return total

    return end


def attention_forward(
    query, key, value, tables, bounds, logical, source, out_weight, gains, gu_stage, down_own
):
    tokens, width = query.shape[0], source.shape[1]
    rows = tokens // 16
    group = tokens // 4
    hidden = gu_stage.shape[2] // 8
    part = width // 8

    def body(*refs, loaded, leave):
        (q_in, k_in, v_in, cos_ref, sin_ref, low_ref, high_ref, log_ref, source_ref, wout_ref, gain_ref) = refs[:11]
        (gu_ref, d_ref) = refs[11:13]
        (full_ref, own_ref, branch_ref, wgu_ref, d_other_ref, qrot_ref, keys_ref, values_ref, o_ref, lse_ref, scale_ref) = refs[13:24]
        (terms, shard, slots, tot_send, tot_recv, pair_send, pair_recv, local) = refs[24:32]
        (ffn_send, ffn_recv, share_send, share_recv, ffn_local) = refs[32:37]
        rest = refs[37:]
        me = z, y, x, k = place()
        ctx = own_tile(me)
        head_at = pl.ds(pl.multiple_of((x * 8 + ctx) * HD, HD), HD)
        sibling = (z, y, x, 1 - k)
        barrier = pltpu.get_barrier_semaphore()
        plane_greet_all(me, [sibling])
        loaded()
        query_gain, key_gain = gain_ref[0:1, head_at], gain_ref[1:2, head_at]

        def pair(src, dst, n):
            return pltpu.make_async_remote_copy(
                src_ref=src,
                dst_ref=dst,
                send_sem=pair_send.at[n],
                recv_sem=pair_recv.at[n],
                device_id=sibling,
                device_id_type=MESH,
            )

        eye = eye_mask()
        own = z * 4 + y * 2 + x
        for i in range(8):
            piece = slice(i * HD, (i + 1) * HD)
            for side, ref in enumerate((q_in, k_in)):
                values = ref[piece, :]
                column = jnp.sum(values * values, axis=1, keepdims=True)
                slots[own, side * 8 + i : side * 8 + i + 1, :] = column_to_row(column, eye)
        values_ref[:tokens, :] = v_in[...]
        other_half = pl.ds(tokens, tokens)
        v_copy = pair(v_in, values_ref.at[other_half, :], 0)
        v_copy.start()

        def ffn_copy(t, i):
            to = ctx + t - 8 * ((ctx + t) // 8)
            at = pl.ds(pl.multiple_of(to * hidden, hidden), hidden)
            from_at = pl.ds(pl.multiple_of(ctx * part, part), part)
            return pltpu.make_async_remote_copy(
                src_ref=gu_ref.at[i, :, at],
                dst_ref=wgu_ref.at[i, from_at, :hidden],
                send_sem=ffn_send.at[i, t],
                recv_sem=ffn_recv.at[i, t],
                device_id=(to // 2, to % 2, x, k),
                device_id_type=MESH,
            )

        def ffn_ends(t):
            c = ctx + 8 - t - 8 * ((ctx + 8 - t) // 8)
            at = pl.ds(pl.multiple_of(c * part, part), part)
            return wgu_ref.at[:, at, :hidden], wgu_ref.at[:, at, hidden:]

        own_at = pl.ds(pl.multiple_of(ctx * hidden, hidden), hidden)
        ffn_own = pltpu.make_async_copy(gu_ref.at[:, :, own_at], ffn_ends(0)[0], ffn_local)
        ffn_own.start()
        down_copy = pair(d_ref, d_other_ref, 2)
        down_copy.start()

        total = sum_begin(me, slots, tot_send, tot_recv)()
        trickle = Trickle()
        trickle.add([lambda t=t, i=i: ffn_copy(t, i).start() for t in DEAL_ORDER for i in range(2)])
        trickle.tick(DEALT_FIRST)
        scales = lax.rsqrt(total / width + EPSILON)
        scale_ref[...] = scales

        def rotated(values, piece):
            return values * cos_ref[piece, :] + pltpu.roll(values, HD // 2, 1) * sin_ref[piece, :]

        for i in range(8):
            piece = slice(i * HD, (i + 1) * HD)
            factor = row_to_column(scales[8 + i : 9 + i, :], eye)
            keys_ref[piece, :] = rotated(k_in[piece, :] * factor * key_gain, piece).astype(BF)
        k_copy = pair(keys_ref.at[:tokens, :], keys_ref.at[other_half, :], 1)
        k_copy.start()
        for i in range(8):
            piece = slice(i * HD, (i + 1) * HD)
            factor = row_to_column(scales[i : i + 1, :], eye)
            qrot_ref[piece, :] = rotated(q_in[piece, :] * factor * query_gain, piece).astype(BF)
        v_copy.wait()
        k_copy.wait()

        def produce(zp):
            at = pl.ds(pl.multiple_of(zp * group, group), group)
            raw, allowed = masked_scores(
                qrot_ref[at, :], keys_ref[...], low_ref[at, :], high_ref[at, :], log_ref[...]
            )
            raw = jnp.where(allowed, raw, MASKED)
            top = jnp.max(raw, axis=1, keepdims=True)
            weights = jnp.exp(raw - top)
            total_weight = jnp.sum(weights, axis=1, keepdims=True)
            out = jnp.dot(weights.astype(BF), values_ref[...], preferred_element_type=F32)
            out = out * (1.0 / total_weight)
            o_ref[at, :] = out
            lse_ref[at, :] = top + jnp.log(total_weight)
            terms[at, :] = jnp.dot(
                out.astype(BF), wout_ref[...], preferred_element_type=F32
            ).astype(BF)

        def finish(strip, total):
            branch_ref[strip] = total
            h = source_ref[strip].astype(F32) + total * row_scale(total) * gain_ref[2:3, :]
            own_ref[strip] = h
            shard[strip] = h.astype(BF)

        settle = reduce_plane(
            me,
            terms,
            rows,
            rest[:N_REDUCE],
            TURNS_ATTENTION[0],
            produce,
            finish,
            lambda: leave(qrot_ref, keys_ref, values_ref, o_ref, lse_ref, scale_ref),
            lambda: trickle.tick(FORWARD_RATE, FORWARD_EVERY),
        )
        view = gather_view(full_ref, rows)
        keep = pltpu.make_async_copy(shard, view(own), local)
        keep.start()

        def share(t):
            src, dst = ffn_ends(t)
            return pltpu.make_async_remote_copy(
                src_ref=src,
                dst_ref=dst,
                send_sem=share_send.at[t],
                recv_sem=share_recv.at[t],
                device_id=sibling,
                device_id_type=MESH,
            )

        def ffn_landed(t):
            for i in range(2):
                src = ffn_ends(t)[0].at[i]
                pltpu.make_async_remote_copy(
                    src_ref=src,
                    dst_ref=src,
                    send_sem=ffn_send.at[i, t],
                    recv_sem=ffn_recv.at[i, t],
                    device_id=sibling,
                    device_id_type=MESH,
                ).wait_recv()

        gather_plane(
            me,
            shard,
            view,
            rest[N_REDUCE:],
            TURNS_ATTENTION[1],
            lambda step: leave(own_ref, branch_ref) if step == 0 else None,
            tick=lambda: trickle.tick(FORWARD_RATE, FORWARD_EVERY),
        )
        trickle.flush()
        ffn_own.wait()
        share(0).start()
        for t in DEAL_ORDER:
            ffn_landed(t)
            share(t).start()
        keep.wait()
        settle()
        for t in range(8):
            share(t).wait()
            for i in range(2):
                if t > 0:
                    ffn_copy(t, i).wait_send()
        down_copy.wait()

    shape = jax.ShapeDtypeStruct
    return comm_call(
        body,
        "attention_forward",
        1,
        (
            shape((tokens, width), BF),
            shape((rows, width), F32),
            shape((rows, width), F32),
            shape((2, width, 2 * hidden), BF),
            shape((hidden, width), BF),
            shape((tokens, HD), BF),
            shape((2 * tokens, HD), BF),
            shape((2 * tokens, HD), BF),
            shape((tokens, HD), F32),
            shape((tokens, 1), F32),
            shape((16, HD), F32),
        ),
        [VMEM] * 11 + [ANY, ANY],
        (ANY, VMEM, VMEM, ANY, ANY, VMEM, VMEM, VMEM, VMEM, VMEM, VMEM),
        [
            pltpu.VMEM((tokens, width), BF),
            pltpu.VMEM((rows, width), BF),
            pltpu.VMEM((16, 16, HD), F32),
            DMA((16,)),
            DMA((16,)),
            DMA((3,)),
            DMA((3,)),
            DMA,
            DMA((2, 8)),
            DMA((2, 8)),
            DMA((8,)),
            DMA((8,)),
            DMA,
            *reduce_scratch(rows, width),
            *GATHER_SEMS,
        ],
    )(query, key, value, *tables, *bounds, logical, source, out_weight, gains, gu_stage, down_own)


def ffn_forward(source, gu_w, down_w, residual, cotangent, gain):
    tokens, width = source.shape
    rows, group = tokens // 16, tokens // 4
    hidden = 2 * down_w[0].shape[0]

    def body(*refs, loaded, leave):
        (h_any, gu_any, d_any, d_any2, res_ref, cot_ref, gain_ref) = refs[:7]
        (full_ref, out_ref, gg_ref, for_gate_out, for_up_out, m_out) = refs[7:13]
        (hs, gu, dw, terms, shard, result, load_sem, local, out_send, out_recv) = refs[13:23]
        (for_gate_ref, for_up_ref, m_ref, leave_sem) = refs[23:27]
        scratch = refs[27:]
        me = z, y, x, k = place()

        def h_load(zp):
            at = pl.ds(pl.multiple_of(zp * group, group), group)
            return pltpu.make_async_copy(h_any.at[at, :], hs.at[at, :], load_sem.at[zp])

        order = [near_first(step, z) for step in (3, 2, 1, 0)]
        gu_load = pltpu.make_async_copy(gu_any, gu, load_sem.at[4])
        d_loads = [
            pltpu.make_async_copy(d_any, dw.at[: hidden // 2, :], load_sem.at[5]),
            pltpu.make_async_copy(d_any2, dw.at[hidden // 2 :, :], load_sem.at[6]),
        ]
        for load in (h_load(order[0]), gu_load, *d_loads):
            load.start()
        for zp in order[1:]:
            h_load(zp).start()
        greet_plane(me, pair_devices(me))
        loaded()
        gg_ref[...] = jnp.zeros_like(gg_ref)
        gu_load.wait()

        def leave(zp):
            at = pl.ds(pl.multiple_of(zp * group, group), group)
            pairs = ((for_gate_ref, for_gate_out), (for_up_ref, for_up_out), (m_ref, m_out))
            return [
                pltpu.make_async_copy(src.at[at, :], dst.at[at, :], leave_sem.at[i, zp])
                for i, (src, dst) in enumerate(pairs)
            ]

        def produce(zp):
            at = pl.ds(pl.multiple_of(zp * group, group), group)
            h_load(zp).wait()
            tile = hs[at, :]
            gate = jnp.dot(tile, gu[0], preferred_element_type=F32)
            up = jnp.dot(tile, gu[1], preferred_element_type=F32)
            sig = jax.nn.sigmoid(gate)
            silu = gate * sig
            mixed = (silu * up).astype(BF)
            for_gate_ref[at, :] = up * sig * (1.0 + gate * (1.0 - sig))
            for_up_ref[at, :] = silu
            m_ref[at, :] = mixed
            for copy in leave(zp):
                copy.start()
            terms[at, :] = jnp.dot(mixed, dw[...], preferred_element_type=F32).astype(BF)

        def finish(strip, total):
            gain_row = gain_ref[3:4, :]
            out = res_ref[strip] + total * row_scale(total) * gain_row
            result[strip] = out.astype(BF)
            back, term = norm_back_strip(cot_ref[strip].astype(F32), total, gain_row)
            gg_ref[...] += term
            shard[strip] = back.astype(BF)

        for load in d_loads:
            load.wait()
        settle = reduce_plane(me, terms, rows, scratch[:N_REDUCE], EVEN, produce, finish)
        view = gather_view(full_ref, rows)
        keep = pltpu.make_async_copy(shard, view(me[0] * 4 + me[1] * 2 + me[2]), local)
        keep.start()
        copies, own = hand_out_copies(me, result, out_ref, out_send, out_recv)
        for copy in copies:
            copy.start()
        own.start()
        gather_plane(me, shard, view, scratch[N_REDUCE:], EVEN)
        keep.wait()
        settle()
        for zp in range(4):
            for copy in leave(zp):
                copy.wait()
        own.wait()
        for copy in copies:
            copy.wait()

    shape = jax.ShapeDtypeStruct
    return comm_call(
        body,
        "ffn_forward",
        3,
        (
            shape((tokens, width), BF),
            shape((rows * 4, width // 4), BF),
            shape((8, width), F32),
            shape((tokens, hidden), F32),
            shape((tokens, hidden), F32),
            shape((tokens, hidden), BF),
        ),
        [ANY, ANY, ANY, ANY, VMEM, VMEM, VMEM],
        (ANY, ANY, VMEM, ANY, ANY, ANY),
        [
            pltpu.VMEM((tokens, width), BF),
            pltpu.VMEM((2, width, hidden), BF),
            pltpu.VMEM((hidden, width), BF),
            pltpu.VMEM((tokens, width), BF),
            pltpu.VMEM((rows, width), BF),
            pltpu.VMEM((rows, width), BF),
            DMA((7,)),
            DMA,
            DMA((3,)),
            DMA((4,)),
            pltpu.VMEM((tokens, hidden), F32),
            pltpu.VMEM((tokens, hidden), F32),
            pltpu.VMEM((tokens, hidden), BF),
            DMA((3, 4)),
            *reduce_scratch(rows, width),
            *GATHER_SEMS,
        ],
    )(source, gu_w, *down_w, residual, cotangent, gain)


EARLY = 5
GRADS_FIRST = 3


def grad_copies(me, src, dst, send, recv, t):
    ctx = own_tile(me)
    to = ctx + t - 8 * ((ctx + t) // 8)
    return [
        pltpu.make_async_remote_copy(
            src_ref=src.at[i],
            dst_ref=dst.at[ctx, i],
            send_sem=send.at[t, i],
            recv_sem=recv.at[t, i],
            device_id=(to // 2, to % 2, me[2], me[3]),
            device_id_type=MESH,
        )
        for i in range(3)
    ]


def grad_landed(me, dst, send, recv, t):
    ctx = own_tile(me)
    c = ctx + 8 - t - 8 * ((ctx + 8 - t) // 8)
    for i in range(3):
        pltpu.make_async_remote_copy(
            src_ref=dst.at[c, i],
            dst_ref=dst.at[c, i],
            send_sem=send.at[t, i],
            recv_sem=recv.at[t, i],
            device_id=(me[0], me[1], me[2], 1 - me[3]),
            device_id_type=MESH,
        ).wait_recv()


def ctx_greet(me, others):
    z, y, x, k = me
    barrier = pltpu.get_barrier_semaphore()

    def call(i, carry):
        to = lax.rem(z * 2 + y + i, 8)
        pl.semaphore_signal(
            barrier, inc=1, device_id=(to // 2, to % 2, x, k), device_id_type=MESH
        )
        return carry

    lax.fori_loop(1, 8, call, 0)
    for target in [(z, y, 1 - x, k), *others]:
        pl.semaphore_signal(barrier, inc=1, device_id=target, device_id_type=MESH)
    pl.semaphore_wait(barrier, 8 + len(others))


def ffn_backward(
    grad_ffn, source, gu_w, down_w, for_gate, for_up, mixed, cotangent, branch, gain, attention
):
    tokens, width = grad_ffn.shape
    rows, group = tokens // 16, tokens // 4
    hidden = 2 * down_w[0].shape[0]
    part = hidden // 2
    across = (((0,), (0,)), ((), ()))
    turned = (((1,), (1,)), ((), ()))
    scaling = 1.0 / math.sqrt(HD)

    def body(*refs, loaded, leave):
        (df_any, h_any, gu_any, d_any, d_any2, fg_any, fu_any, m_any, cot_ref, branch_ref, gain_ref) = refs[:11]
        (wout_ref, qrot_ref, keys_ref, values_ref, o_ref, lse_ref, low_ref, high_ref, log_ref) = refs[11:20]
        (full_ref, own_ref, gg_ref, in_ref, rest_ref, dq_ref, dk_ref, dv_ref) = refs[20:28]
        (df, hs, gu, dw, fg, fu, ms, dgu, terms, shard) = refs[28:38]
        (to_core, from_core, to_ctx) = refs[38:41]
        (da, dk_all, dv_all, pair_out, pair_in) = refs[41:46]
        (load_sem, local, core_send, core_recv, grad_send, grad_recv, rest_sem) = refs[46:53]
        (da_sem, pair_send, pair_recv) = refs[53:56]
        scratch = refs[56:]
        me = z, y, x, k = place()
        ctx = own_tile(me)
        order = [near_first(step, z) for step in (3, 2, 1, 0)]

        def group_load(zp):
            at = pl.ds(pl.multiple_of(zp * group, group), group)
            return [
                pltpu.make_async_copy(src.at[at, :], dst.at[at, :], load_sem.at[i, zp])
                for i, (src, dst) in enumerate(((df_any, df), (fg_any, fg), (fu_any, fu)))
            ]

        d_load = pltpu.make_async_copy(d_any, dw.at[:part, :], load_sem.at[3, 0])
        d_load2 = pltpu.make_async_copy(d_any2, dw.at[part:, :], load_sem.at[4, 0])
        gu_load = pltpu.make_async_copy(gu_any, gu, load_sem.at[3, 1])
        h_load = pltpu.make_async_copy(h_any, hs, load_sem.at[3, 2])
        m_load = pltpu.make_async_copy(m_any, ms, load_sem.at[3, 3])
        for load in (*group_load(order[0]), d_load, d_load2, gu_load):
            load.start()
        for zp in order[1:]:
            for load in group_load(zp):
                load.start()
        h_load.start()
        m_load.start()
        sibling = (z, y, x, 1 - k)
        ctx_greet(me, [sibling])
        loaded()
        gg_ref[...] = jnp.zeros_like(gg_ref)
        d_load.wait()
        d_load2.wait()

        def produce(zp):
            at = pl.ds(pl.multiple_of(zp * group, group), group)
            for load in group_load(zp):
                load.wait()
            dm = lax.dot_general(df[at, :], dw[...], turned, preferred_element_type=F32)
            dg = (dm * fg[at, :]).astype(BF)
            du = (dm * fu[at, :]).astype(BF)
            dgu[at, :hidden] = dg
            dgu[at, hidden:] = du
            terms[at, :] = (
                lax.dot_general(dg, gu[0], turned, preferred_element_type=F32)
                + lax.dot_general(du, gu[1], turned, preferred_element_type=F32)
            ).astype(BF)

        def finish(strip, total):
            grad = cot_ref[strip].astype(F32) + total
            own_ref[strip] = grad
            back, term = norm_back_strip(grad, branch_ref[strip], gain_ref[2:3, :])
            gg_ref[...] += term
            shard[strip] = back.astype(BF)

        def core_copy(t):
            return pltpu.make_async_remote_copy(
                src_ref=to_core.at[t],
                dst_ref=from_core.at[t],
                send_sem=core_send.at[t],
                recv_sem=core_recv.at[t],
                device_id=sibling,
                device_id_type=MESH,
            )

        parts = (*DEAL_ORDER, 0)

        def compute(n):
            t = parts[n]
            c = ctx + t - 8 * ((ctx + t) // 8)
            at = pl.ds(pl.multiple_of(c * part, part), part)
            up_like = lax.dot_general(hs[:, at], dgu[...], across, preferred_element_type=F32)
            down_like = lax.dot_general(ms[...], df[:, at], across, preferred_element_type=F32)
            for i in range(2):
                to_ctx[t, i] = up_like[:, 2 * i * part : (2 * i + 1) * part].astype(BF)
                to_core[t, i] = up_like[:, (2 * i + 1) * part : (2 * i + 2) * part].astype(BF)
            to_ctx[t, 2] = down_like[:part].astype(BF)
            to_core[t, 2] = down_like[part:].astype(BF)
            core_copy(t).start()

        trickle = Trickle()

        def send(n):
            t = parts[n]
            core_copy(t).wait_recv()
            to_ctx[t] = (to_ctx[t].astype(F32) + from_core[t].astype(F32)).astype(BF)
            if t == 0:
                pltpu.make_async_copy(to_ctx.at[0], in_ref.at[ctx], rest_sem.at[0]).start()
            elif n < EARLY:
                trickle.add(
                    [
                        copy.start
                        for copy in grad_copies(me, to_ctx.at[t], in_ref, grad_send, grad_recv, t)
                    ]
                )
            else:
                pltpu.make_async_copy(
                    to_ctx.at[t], rest_ref.at[n - EARLY], rest_sem.at[n - EARLY + 1]
                ).start()

        begun = []

        def next_part():
            n = len(begun)
            begun.append(n)
            if n < 8:
                compute(n)
            if BACK_LAG <= n < 8 + BACK_LAG:
                send(n - BACK_LAG)

        def tick():
            if begun:
                next_part()
            trickle.tick(BACK_RATE, BACK_EVERY)

        def da_load(step):
            at = pl.ds(pl.multiple_of(near_first(step, z) * group, group), group)
            return pltpu.make_async_copy(full_ref.at[at, :], da.at[step % 2], da_sem.at[step % 2])

        def attend_back(step):
            at = pl.ds(pl.multiple_of(near_first(step, z) * group, group), group)
            da_load(step).wait()
            grad = lax.dot_general(
                da[step % 2], wout_ref[...], turned, preferred_element_type=F32
            ).astype(BF)
            delta = jnp.sum(grad.astype(F32) * o_ref[at, :], axis=1, keepdims=True)
            q, low, high, lse = qrot_ref[at, :], low_ref[at, :], high_ref[at, :], lse_ref[at, :]
            dq_ref[at, :] = jnp.zeros((group, HD), F32)

            def work(key_at):
                key_part = keys_ref[key_at, :]
                raw, allowed = masked_scores(q, key_part, low, high, log_ref[:, key_at])
                weights = jnp.where(allowed, jnp.exp(raw - lse), 0.0)
                dp = lax.dot_general(
                    grad, values_ref[key_at, :], turned, preferred_element_type=F32
                )
                ds = (weights * (dp - delta)).astype(BF)
                dq_ref[at, :] += jnp.dot(ds, key_part, preferred_element_type=F32) * scaling
                dk_all[key_at, :] += (
                    lax.dot_general(ds, q, across, preferred_element_type=F32) * scaling
                )
                dv_all[key_at, :] += lax.dot_general(
                    weights.astype(BF), grad, across, preferred_element_type=F32
                )

            strips(2 * tokens, work, tokens)

        def arrived(step):
            if step == 0:
                keep.wait()
                dk_all[...] = jnp.zeros_like(dk_all)
                dv_all[...] = jnp.zeros_like(dv_all)
            da_load(step).start()
            if step > 0:
                attend_back(step - 1)

        def pair(n):
            return pltpu.make_async_remote_copy(
                src_ref=pair_out.at[n],
                dst_ref=pair_in.at[n],
                send_sem=pair_send.at[n],
                recv_sem=pair_recv.at[n],
                device_id=sibling,
                device_id_type=MESH,
            )

        def after_terms():
            h_load.wait()
            m_load.wait()
            for _ in range(GRADS_FIRST):
                next_part()

        gu_load.wait()
        settle = reduce_plane(
            me,
            terms,
            rows,
            scratch[:N_REDUCE],
            TURNS_FFN_BACK[0],
            produce,
            finish,
            after_terms,
            tick,
        )
        view = gather_view(full_ref, rows)
        keep = pltpu.make_async_copy(shard, view(me[0] * 4 + me[1] * 2 + me[2]), local)
        keep.start()
        gather_plane(
            me,
            shard,
            view,
            scratch[N_REDUCE:],
            TURNS_FFN_BACK[1],
            lambda step: leave(own_ref, gg_ref) if step == 0 else None,
            arrived,
            tick=tick,
            early=EARLY_LAYERS,
        )
        while len(begun) < 8 + BACK_LAG:
            next_part()
        trickle.flush()
        attend_back(3)
        pair_out[0] = dk_all[tokens:, :].astype(BF)
        pair_out[1] = dv_all[tokens:, :].astype(BF)
        pair(0).start()
        pair(1).start()
        settle()
        for n, (ref, source_ref) in enumerate(((dk_ref, dk_all), (dv_ref, dv_all))):
            pair(n).wait()
            ref[...] = source_ref[:tokens, :] + pair_in[n].astype(F32)
        for t in range(8):
            core_copy(t).wait_send()
        pltpu.make_async_copy(to_ctx.at[0], in_ref.at[ctx], rest_sem.at[0]).wait()
        for n, t in enumerate(DEAL_ORDER):
            if n < EARLY:
                grad_landed(me, in_ref, grad_send, grad_recv, t)
                for copy in grad_copies(me, to_ctx.at[t], in_ref, grad_send, grad_recv, t):
                    copy.wait_send()
            else:
                pltpu.make_async_copy(
                    to_ctx.at[t], rest_ref.at[n - EARLY], rest_sem.at[n - EARLY + 1]
                ).wait()

    shape = jax.ShapeDtypeStruct
    vmem = pltpu.VMEM
    return comm_call(
        body,
        "ffn_backward",
        4,
        (
            shape((tokens, width), BF),
            shape((rows, width), F32),
            shape((8, width), F32),
            shape((8, 3, part, part), BF),
            shape((7 - EARLY, 3, part, part), BF),
            shape((tokens, HD), F32),
            shape((tokens, HD), F32),
            shape((tokens, HD), F32),
        ),
        [*[ANY] * 8, *[VMEM] * 12],
        (ANY, VMEM, VMEM, ANY, ANY, VMEM, VMEM, VMEM),
        [
            vmem((tokens, width), BF),
            vmem((tokens, width), BF),
            vmem((2, width, hidden), BF),
            vmem((hidden, width), BF),
            vmem((tokens, hidden), F32),
            vmem((tokens, hidden), F32),
            vmem((tokens, hidden), BF),
            vmem((tokens, 2 * hidden), BF),
            vmem((tokens, width), BF),
            vmem((rows, width), BF),
            vmem((8, 3, part, part), BF),
            vmem((8, 3, part, part), BF),
            vmem((8, 3, part, part), BF),
            vmem((2, group, width), BF),
            vmem((2 * tokens, HD), F32),
            vmem((2 * tokens, HD), F32),
            vmem((2, tokens, HD), BF),
            vmem((2, tokens, HD), BF),
            DMA((5, 4)),
            DMA,
            DMA((8,)),
            DMA((8,)),
            DMA((8, 3)),
            DMA((8, 3)),
            DMA((8,)),
            DMA((2,)),
            DMA((2,)),
            DMA((2,)),
            *reduce_scratch(rows, width),
            *GATHER_SEMS,
        ],
    )(
        grad_ffn,
        source,
        gu_w,
        *down_w,
        for_gate,
        for_up,
        mixed,
        cotangent,
        branch,
        gain,
        *attention,
    )


def write_results(early, late, wall, outputs, input_grad, gains):
    part = early.shape[2]

    def body(early_ref, late_ref, wall_ref, out_ref, in_ref, gain_ref, *results):
        (out_to, in_to, gq, gk, gv, go, gg, gu, gd, *gains_to) = results
        n = pl.program_id(0)

        @pl.when(n == 0)
        def _():
            out_to[...] = out_ref[...]
            in_to[...] = in_ref[...]
            for i, ref in enumerate(gains_to):
                ref[...] = gain_ref[i : i + 1, :]

        for i, ref in enumerate((gq, gk, gv, go)):
            ref[...] = wall_ref[0, i].astype(F32)

        @pl.when(n <= EARLY)
        def _():
            for i, ref in enumerate((gg, gu, gd)):
                ref[...] = early_ref[0, i].astype(F32)

        @pl.when(n > EARLY)
        def _():
            for i, ref in enumerate((gg, gu, gd)):
                ref[...] = late_ref[0, i].astype(F32)

    shape = jax.ShapeDtypeStruct
    spec = pl.BlockSpec

    def source(n):
        ctx = lax.axis_index("z") * 2 + lax.axis_index("y")
        odd = lax.rem(n, 2)
        t = odd * (4 + n // 2) + (1 - odd) * (n // 2)
        return lax.rem(ctx + 8 - t, 8)

    rows, columns = outputs.shape
    whole = spec((rows, columns), lambda n: (0, 0))
    in_row = spec((HD, HD), lambda n: (source(n) % 2, source(n) // 2))
    in_column = spec((HD, HD), lambda n: (source(n) // 2, source(n) % 2))
    side = spec((part, part), lambda n: (0, source(n)))
    gain_spec = spec(gains.shape, lambda n: (0, 0))
    gain_row = spec((1, gains.shape[1]), lambda n: (0, 0))
    blob = (1, 3, part, part)
    return pl.pallas_call(
        body,
        name="write_results",
        grid=(8,),
        out_shape=(
            shape((rows, columns), BF),
            shape((rows, columns), BF),
            shape((2 * HD, 4 * HD), F32),
            shape((2 * HD, 4 * HD), F32),
            shape((2 * HD, 4 * HD), F32),
            shape((4 * HD, 2 * HD), F32),
            shape((part, 8 * part), F32),
            shape((part, 8 * part), F32),
            shape((8 * part, part), F32),
            *[shape((1, gains.shape[1]), F32)] * 4,
        ),
        in_specs=[
            spec(blob, lambda n: (source(jnp.minimum(n, EARLY)), 0, 0, 0)),
            spec(blob, lambda n: (source(jnp.maximum(n, EARLY + 1)), 0, 0, 0)),
            spec((1, 4, HD, HD), lambda n: (source(n), 0, 0, 0)),
            whole,
            whole,
            gain_spec,
        ],
        out_specs=(
            whole,
            whole,
            in_row,
            in_row,
            in_row,
            in_column,
            side,
            side,
            spec((part, part), lambda n: (source(n), 0)),
            *[gain_row] * 4,
        ),
        compiler_params=pltpu.CompilerParams(vmem_limit_bytes=BIG_VMEM),
    )(early, late, wall, outputs, input_grad, gains)


def close_greet(me):
    z, y, x, k = me
    barrier = pltpu.get_barrier_semaphore()

    def plane(i, carry):
        pl.semaphore_signal(barrier, inc=1, device_id=plane_peer(me, i)[1], device_id_type=MESH)
        return carry

    def others(i, carry):
        pl.semaphore_signal(
            barrier, inc=1, device_id=(i // 2, i % 2, x, 1 - k), device_id_type=MESH
        )
        return carry

    lax.fori_loop(1, 16, plane, 0)
    lax.fori_loop(0, 8, others, 0)
    pl.semaphore_signal(barrier, inc=1, device_id=(z, y, 1 - x, 1 - k), device_id_type=MESH)
    pl.semaphore_wait(barrier, 24)


def attention_backward(
    grad_attn,
    full_in,
    query,
    key,
    attended,
    grads_rotated,
    tables,
    scales,
    gains,
    qkv_w,
    grad_own,
    attn_term,
    ffn_term,
    grads_left,
):
    tokens, width = grad_attn.shape
    rows, group = tokens // 16, tokens // 4
    part = width // 4

    def body(*refs, loaded, leave):
        (da_any, x_any) = refs[:2]
        (q_ref, k_ref, o_ref, dq_in, dk_in, dv_in, cos_ref, sin_ref) = refs[2:10]
        (scale_ref, gain_ref, wqkv_ref) = refs[10:13]
        (grad_ref, attn_ref, ffn_ref, left_ref) = refs[13:17]
        (in_grad_ref, deal_in, gains_ref, ffn_in) = refs[17:21]
        (da, xs, terms, dq_ref, dk_ref) = refs[21:26]
        (dqkv, slots, result) = refs[26:29]
        (qkv_grads, out_grads, wall_out, wall_in, deal_out) = refs[29:34]
        (gain_out, gain_in, gain_own, gain_slots) = refs[34:38]
        (load_sem, pair_send, pair_recv, tot_send, tot_recv, out_send, out_recv) = refs[38:45]
        (deal_send, deal_recv, gain_send, gain_recv, grad_send, grad_recv) = refs[45:51]
        scratch = refs[51:]
        me = z, y, x, k = place()
        ctx = own_tile(me)
        own = ctx * 2 + x
        own_head = pl.ds(pl.multiple_of((x * 8 + ctx) * HD, HD), HD)
        sibling = (z, y, x, 1 - k)

        da_load = pltpu.make_async_copy(da_any, da, load_sem.at[0])
        x_load = pltpu.make_async_copy(x_any, xs, load_sem.at[1])
        x_load.start()
        da_load.start()
        close_greet(me)
        loaded()

        trickle = Trickle()

        def left_copies(n):
            return grad_copies(me, left_ref.at[n - EARLY], ffn_in, grad_send, grad_recv, DEAL_ORDER[n])

        for n in range(EARLY, 7):
            trickle.add([copy.start for copy in left_copies(n)])
        trickle.tick(CLOSE_FIRST)

        def pair(n):
            return pltpu.make_async_remote_copy(
                src_ref=wall_out.at[n] if n < 8 else gain_out,
                dst_ref=wall_in.at[n] if n < 8 else gain_in,
                send_sem=pair_send.at[n],
                recv_sem=pair_recv.at[n],
                device_id=sibling,
                device_id_type=MESH,
            )

        across = (((0,), (0,)), ((), ()))
        eye = eye_mask()

        def normed_grad(values, piece):
            return values * cos_ref[piece, :] - pltpu.roll(values, HD // 2, 1) * sin_ref[piece, :]

        def side_dots(side, source, grads, proj):
            gain_sum = jnp.zeros((8, HD), F32)
            for i in range(8):
                piece = slice(i * HD, (i + 1) * HD)
                factor = row_to_column(scale_ref[side * 8 + i : side * 8 + i + 1, :], eye)
                back = normed_grad(source[piece, :], piece)
                term = back * proj[piece, :] * factor
                for j in range(0, HD, 8):
                    gain_sum = gain_sum + term[j : j + 8, :]
                weighted = back * gain_ref[side : side + 1, own_head]
                grads[piece, :] = weighted
                dot = jnp.sum(weighted * proj[piece, :], axis=1, keepdims=True)
                slots[own, side * 8 + i : side * 8 + i + 1, :] = column_to_row(dot, eye)
            return jnp.sum(gain_sum, axis=0, keepdims=True)

        query_gain = side_dots(0, dq_in, dq_ref, q_ref)
        key_gain = side_dots(1, dk_in, dk_ref, k_ref)
        sum_end = sum_begin(me, slots, tot_send, tot_recv)
        dqkv[:, 2 * HD :] = dv_in[...].astype(BF)

        attn_sum = jnp.sum(attn_ref[...], axis=0, keepdims=True)
        ffn_sum = jnp.sum(ffn_ref[...], axis=0, keepdims=True)
        head_core = z // 2
        head_at = pl.ds(pl.multiple_of(((z % 2) * 2 + y) * HD, HD), HD)
        for mine, target in ((True, gain_own), (False, gain_out)):
            target[...] = jnp.zeros_like(target)
            for xt in range(2):
                for kt in range(2):

                    @pl.when((kt == k) if mine else (kt != k))
                    def _(xt=xt, kt=kt, target=target):
                        block = slice((2 * xt + kt) * part, (2 * xt + kt + 1) * part)
                        target[xt, 2:3, :] = attn_sum[:, block]
                        target[xt, 3:4, :] = ffn_sum[:, block]

            @pl.when((head_core == k) if mine else (head_core != k))
            def _(target=target):
                target[x, 0:1, head_at] = query_gain
                target[x, 1:2, head_at] = key_gain

        pair(8).start()

        parts = (*DEAL_ORDER, 0)

        def columns_of(n):
            c = ctx + parts[n] - 8 * ((ctx + parts[n]) // 8)
            return pl.ds(pl.multiple_of(c * 2 * HD, 2 * HD), 2 * HD)

        attended_low = o_ref[...].astype(BF)
        da_load.wait()
        for n in range(8):
            out_grads[n] = lax.dot_general(
                attended_low, da[:, columns_of(n)], across, preferred_element_type=F32
            )
        total = sum_end()
        trickle.tick(CLOSE_NEXT)
        for side, grads, proj in ((0, dq_ref, q_ref), (1, dk_ref, k_ref)):
            for i in range(8):
                piece = slice(i * HD, (i + 1) * HD)
                row = scale_ref[side * 8 + i : side * 8 + i + 1, :]
                factor = row_to_column(row, eye)
                cubed = row * row * row * total[side * 8 + i : side * 8 + i + 1, :] / width
                dqkv[piece, side * HD : (side + 1) * HD] = (
                    factor * grads[piece, :] - proj[piece, :] * row_to_column(cubed, eye)
                ).astype(BF)

        def produce(zp):
            at = pl.ds(pl.multiple_of(zp * group, group), group)
            term = jnp.zeros((group, width), F32)
            for i in range(3):
                term = term + lax.dot_general(
                    dqkv[at, i * HD : (i + 1) * HD],
                    wqkv_ref[i],
                    (((1,), (1,)), ((), ())),
                    preferred_element_type=F32,
                )
            terms[at, :] = term.astype(BF)

        gain_copies = []

        def gain_copy(i):
            other, device = plane_peer(me, i)
            return pltpu.make_async_remote_copy(
                src_ref=gain_own.at[other % 2],
                dst_ref=gain_slots.at[own],
                send_sem=gain_send.at[i],
                recv_sem=gain_recv.at[own],
                device_id=device,
                device_id_type=MESH,
            )

        number = ((z % 2) * 2 + y) * 2 + k

        def deal(n):
            c = ctx + parts[n] - 8 * ((ctx + parts[n]) // 8)
            return pltpu.make_async_remote_copy(
                src_ref=deal_out.at[n],
                dst_ref=deal_in.at[number],
                send_sem=deal_send.at[n],
                recv_sem=deal_recv.at[number],
                device_id=(c // 2, c % 2, x, head_core),
                device_id_type=MESH,
            )

        stays = k == head_core

        def deal_start(n):
            if n < 7:
                deal(n).start()
                return

            @pl.when(jnp.logical_not(stays))
            def _():
                deal(n).start()

            @pl.when(stays)
            def _():
                pltpu.make_async_copy(
                    deal_out.at[n], deal_in.at[number], deal_recv.at[number]
                ).start()

        def after_terms():
            pair(8).wait_recv()
            gain_own[...] += gain_in[...]
            gain_slots[own] = gain_own[x]

            def begin(i, carry):
                gain_copy(i).start()
                return carry

            lax.fori_loop(1, 16, begin, 0)

        x_load.wait()
        begun = []

        def halves(n, r):
            rows_at = pl.ds(pl.multiple_of(r * HD, HD), HD)
            for i in range(3):
                yield i, qkv_grads[rows_at, i * HD : (i + 1) * HD]
            yield 3, out_grads[n, :, rows_at]

        def tick():
            n = len(begun)
            begun.append(n)
            if n < 8:
                qkv_grads[...] = lax.dot_general(
                    xs[:, columns_of(n)], dqkv[...], across, preferred_element_type=F32
                )
                for i, value in halves(n, 1 - k):
                    wall_out[n, i] = value.astype(BF)
                for i, value in halves(n, k):
                    deal_out[n, i] = value.astype(BF)
                pair(n).start()
            if CLOSE_LAG <= n < 8 + CLOSE_LAG:
                last = n - CLOSE_LAG
                pair(last).wait_recv()
                deal_out[last] = (deal_out[last].astype(F32) + wall_in[last].astype(F32)).astype(BF)
                deals.add([lambda: deal_start(last)])
            deals.tick()
            trickle.tick(CLOSE_RATE)

        deals = Trickle()

        def finish(strip, total):
            result[strip] = (grad_ref[strip] + total).astype(BF)

        settle = reduce_plane(
            me,
            terms,
            rows,
            scratch,
            TURNS_CLOSE,
            produce,
            finish,
            after_terms,
            tick,
        )
        while len(begun) < 8 + CLOSE_LAG:
            tick()
        deals.flush()
        trickle.flush()
        copies, own_copy = hand_out_copies(me, result, in_grad_ref, out_send, out_recv)
        for copy in copies:
            copy.start()
        own_copy.start()
        for n in range(8):
            pltpu.make_async_copy(deal_out.at[n], deal_in.at[n], deal_recv.at[n]).wait()

        def gain_landed(i, carry):
            other, device = plane_peer(me, i)
            pltpu.make_async_remote_copy(
                src_ref=gain_slots.at[other],
                dst_ref=gain_slots.at[other],
                send_sem=gain_send.at[i],
                recv_sem=gain_recv.at[other],
                device_id=device,
                device_id_type=MESH,
            ).wait_recv()
            gain_copy(i).wait_send()
            return carry

        lax.fori_loop(1, 16, gain_landed, 0)
        gain_total = gain_slots[0]
        for i in range(1, 16):
            gain_total = gain_total + gain_slots[i]
        gains_ref[...] = gain_total
        settle()
        own_copy.wait()
        for copy in copies:
            copy.wait()
        for n in range(7):
            deal(n).wait_send()

        @pl.when(jnp.logical_not(stays))
        def _():
            deal(7).wait_send()

        for n in range(9):
            pair(n).wait_send()
        for n in range(EARLY, 7):
            grad_landed(me, ffn_in, grad_send, grad_recv, DEAL_ORDER[n])
            for copy in left_copies(n):
                copy.wait_send()

    shape = jax.ShapeDtypeStruct
    vmem = pltpu.VMEM
    return comm_call(
        body,
        "attention_backward",
        5,
        (
            shape((rows * 4, part), BF),
            shape((8, 4, HD, HD), BF),
            shape((4, part), F32),
            shape((8, *grads_left.shape[1:]), BF),
        ),
        [ANY, ANY, *[VMEM] * 14, ANY],
        (ANY, ANY, VMEM, ANY),
        [
            vmem((tokens, width), BF),
            vmem((tokens, width), BF),
            vmem((tokens, width), BF),
            vmem((tokens, HD), F32),
            vmem((tokens, HD), F32),
            vmem((tokens, 3 * HD), BF),
            vmem((16, 16, HD), F32),
            vmem((rows, width), BF),
            vmem((2 * HD, 3 * HD), F32),
            vmem((8, HD, 2 * HD), F32),
            vmem((8, 4, HD, HD), BF),
            vmem((8, 4, HD, HD), BF),
            vmem((8, 4, HD, HD), BF),
            vmem((2, 4, part), F32),
            vmem((2, 4, part), F32),
            vmem((2, 4, part), F32),
            vmem((16, 4, part), F32),
            DMA((2,)),
            DMA((9,)),
            DMA((9,)),
            DMA((16,)),
            DMA((16,)),
            DMA((3,)),
            DMA((4,)),
            DMA((8,)),
            DMA((8,)),
            DMA((16,)),
            DMA((16,)),
            DMA((8, 3)),
            DMA((8, 3)),
            *reduce_scratch(rows, width),
        ],
    )(
        grad_attn,
        full_in,
        query,
        key,
        attended,
        *grads_rotated,
        *tables,
        scales,
        gains,
        qkv_w,
        grad_own,
        attn_term,
        ffn_term,
        grads_left,
    )


def plane_layer(
    inputs,
    cotangent,
    w_query,
    w_key,
    w_value,
    w_out,
    w_gate,
    w_up,
    w_down,
    query_gain,
    key_gain,
    attn_gain,
    ffn_gain,
    lengths,
    block_order,
):
    steps = np.arange(HD // 2, dtype=np.float64) * 2.0 / HD
    frequency = np.tile(np.power(ROPE_THETA, -steps), 2)[None, :].astype(np.float32)
    full_in, source_own, own_cot, qkv_w, out_w, gains_full, gu_stage, down_own, query_proj, key_proj, value_low, cosine, sine, low, high, logical_keys = open_layer(
        inputs,
        cotangent,
        w_query,
        w_key,
        w_value,
        w_out,
        w_gate,
        w_up,
        w_down,
        query_gain[None, :],
        key_gain[None, :],
        attn_gain[None, :],
        ffn_gain[None, :],
        block_order[None, :],
        lengths[None, :],
        jnp.asarray(frequency),
    )
    tables = (cosine, sine)
    (
        residual_full,
        residual_own,
        branch_own,
        gu_w,
        down_other,
        query_rot,
        keys_all,
        values_all,
        attended,
        lse,
        scales,
    ) = attention_forward(
        query_proj,
        key_proj,
        value_low,
        tables,
        (low, high),
        logical_keys,
        source_own,
        out_w,
        gains_full,
        gu_stage,
        down_own,
    )
    grad_ffn, outputs, ffn_gain_term, for_gate, for_up, mixed = ffn_forward(
        residual_full, gu_w, (down_own, down_other), residual_own, own_cot, gains_full
    )
    grad_attn, grad_own, attn_gain_term, ffn_early, ffn_left, *grads_rotated = ffn_backward(
        grad_ffn,
        residual_full,
        gu_w,
        (down_own, down_other),
        for_gate,
        for_up,
        mixed,
        own_cot,
        branch_own,
        gains_full,
        (out_w, query_rot, keys_all, values_all, attended, lse, low, high, logical_keys),
    )
    input_grad, wall_grads, gain_grads, ffn_late = attention_backward(
        grad_attn,
        full_in,
        query_proj,
        key_proj,
        attended,
        grads_rotated,
        tables,
        scales,
        gains_full,
        qkv_w,
        grad_own,
        attn_gain_term,
        ffn_gain_term,
        ffn_left,
    )
    results = write_results(ffn_early, ffn_late, wall_grads, outputs, input_grad, gain_grads)
    return (*results[:9], *[row[0] for row in results[9:]])


def full_rows(piece):
    return lax.all_gather(piece, "head", axis=1, tiled=True)


def head_sums(term):
    return lax.psum_scatter(
        term.astype(jnp.bfloat16), "head", scatter_dimension=1, tiled=True
    ).astype(jnp.float32)


def row_single(term):
    return lax.psum(term, "head")


def row_pair(first, second):
    return lax.psum((first, second), "head")


def gather_weights(w_query, w_key, w_value, w_out, w_gate, w_up, w_down):
    row_parts = (
        lax.all_gather(w_query.astype(jnp.bfloat16), "ctx", axis=0, tiled=True),
        lax.all_gather(w_key.astype(jnp.bfloat16), "ctx", axis=0, tiled=True),
        lax.all_gather(w_value.astype(jnp.bfloat16), "ctx", axis=0, tiled=True),
        lax.all_gather(w_gate.astype(jnp.bfloat16), "ctx", axis=0, tiled=True),
        lax.all_gather(w_up.astype(jnp.bfloat16), "ctx", axis=0, tiled=True),
    )
    col_parts = (
        lax.all_gather(w_out.astype(jnp.bfloat16), "ctx", axis=1, tiled=True),
        lax.all_gather(w_down.astype(jnp.bfloat16), "ctx", axis=1, tiled=True),
    )
    return tuple(row_parts) + tuple(col_parts)


def sequence_tables(logical, lengths):
    seq_ends = jnp.cumsum(lengths)
    seq_starts = seq_ends - lengths
    number = jnp.sum((logical[:, None] >= seq_ends[None, :]).astype(jnp.int32), axis=1)
    member = number[:, None] == jnp.arange(lengths.shape[0], dtype=jnp.int32)[None, :]
    offset = logical - jnp.sum(jnp.where(member, seq_starts[None, :], 0), axis=1)
    return (number, offset)


def rotate(values, offset):
    half_dim = HD // 2
    inverse = jnp.power(ROPE_THETA, -jnp.arange(half_dim, dtype=jnp.float32) * 2.0 / HD)
    angles = offset.astype(jnp.float32)[:, None] * inverse[None, :]
    cosine = jnp.cos(angles)[:, None, :]
    sine_part = jnp.sin(angles)[:, None, :]
    first_half = values[..., :half_dim]
    second_half = values[..., half_dim:]
    return jnp.concatenate(
        [
            first_half * cosine - second_half * sine_part,
            second_half * cosine + first_half * sine_part,
        ],
        axis=-1,
    )


def norm_backward(grad_in, values, factor, gain):
    gain_term = jnp.sum(grad_in * values * factor[:, None], axis=0)
    weighted = grad_in * gain
    row_dot = row_single(jnp.sum(weighted * values, axis=1))
    grad_values = (
        factor[:, None] * weighted - values * (factor * factor * factor * row_dot / D)[:, None]
    )
    return (grad_values, gain_term)


def on_device(
    inputs,
    cotangent,
    w_query,
    w_key,
    w_value,
    w_out,
    w_gate,
    w_up,
    w_down,
    query_gain,
    key_gain,
    attn_gain,
    ffn_gain,
    lengths,
    block_order,
):
    shards = lax.axis_size("ctx")
    position = lax.axis_index("ctx")
    tok_rows, width_part = inputs.shape
    block_rows = tok_rows // shards
    total_tokens = tok_rows * shards
    local_heads = width_part // HD
    scaling = 1.0 / math.sqrt(HD)
    shard_range = jnp.arange(shards, dtype=jnp.int32)
    order_table = block_order.reshape(shards, shards)
    target = order_table % shards
    choose = target[:, :, None] == shard_range[None, None, :]
    stream = jnp.sum(jnp.where(choose, order_table[:, :, None], 0), axis=1)
    stream_blocks = jnp.transpose(stream).reshape(-1)
    logical = (
        stream_blocks[:, None] * block_rows + jnp.arange(block_rows, dtype=jnp.int32)[None, :]
    ).reshape(-1)
    own_target = lax.dynamic_index_in_dim(target, position, 0, keepdims=False)
    send_order = jnp.sum(
        jnp.where(own_target[:, None] == shard_range[None, :], shard_range[:, None], 0), axis=0
    )

    def deal_out(values):
        return values.reshape(shards, block_rows, width_part)[send_order].reshape(
            tok_rows, width_part
        )

    def undeal(values):
        return values.reshape(shards, block_rows, width_part)[own_target].reshape(
            tok_rows, width_part
        )

    local_in, local_cot = (
        lax.all_to_all(deal_out(inputs), "ctx", split_axis=0, concat_axis=0, tiled=True),
        lax.all_to_all(deal_out(cotangent), "ctx", split_axis=0, concat_axis=0, tiled=True),
    )
    number_all, offset_all = sequence_tables(logical, lengths)
    number_own = lax.dynamic_slice_in_dim(number_all, position * tok_rows, tok_rows)
    offset_own = lax.dynamic_slice_in_dim(offset_all, position * tok_rows, tok_rows)
    logical_own = lax.dynamic_slice_in_dim(logical, position * tok_rows, tok_rows)
    query_full, key_full, value_full, gate_full, up_full, out_full, down_full = gather_weights(
        w_query, w_key, w_value, w_out, w_gate, w_up, w_down
    )
    full_in = full_rows(local_in)
    query_proj = jnp.dot(full_in, query_full, preferred_element_type=jnp.float32)
    key_proj = jnp.dot(full_in, key_full, preferred_element_type=jnp.float32)
    value_proj = jnp.dot(full_in, value_full, preferred_element_type=jnp.float32)
    query_sq, key_sq = row_pair(
        jnp.sum(query_proj * query_proj, axis=1), jnp.sum(key_proj * key_proj, axis=1)
    )
    query_scale = lax.rsqrt(query_sq / D + EPSILON)
    key_scale = lax.rsqrt(key_sq / D + EPSILON)
    query_rot = rotate(
        (query_proj * query_scale[:, None] * query_gain).reshape(tok_rows, local_heads, HD),
        offset_own,
    ).astype(jnp.bfloat16)
    key_rot = rotate(
        (key_proj * key_scale[:, None] * key_gain).reshape(tok_rows, local_heads, HD), offset_own
    ).astype(jnp.bfloat16)
    value_low = value_proj.astype(jnp.bfloat16).reshape(tok_rows, local_heads, HD)
    keys_all, values_all = (
        lax.all_gather(key_rot, "ctx", axis=0, tiled=True),
        lax.all_gather(value_low, "ctx", axis=0, tiled=True),
    )
    key_span = math.gcd(total_tokens, 1024)
    key_turns = total_tokens // key_span
    pieces = (
        keys_all.reshape(key_turns, key_span, local_heads, HD),
        values_all.reshape(key_turns, key_span, local_heads, HD),
        number_all.reshape(key_turns, key_span),
        logical.reshape(key_turns, key_span),
    )

    def scores_of(key_piece, number_piece, logical_piece):
        raw_scores = (
            jnp.einsum("qhd,khd->hqk", query_rot, key_piece, preferred_element_type=jnp.float32)
            * scaling
        )
        allowed = (number_own[:, None] == number_piece[None, :]) & (
            logical_piece[None, :] <= logical_own[:, None]
        )
        return (raw_scores, allowed)

    def stat_turn(running, piece_set):
        running_max, running_sum = running
        raw_scores, allowed = scores_of(piece_set[0], piece_set[2], piece_set[3])
        masked_scores = jnp.where(allowed[None], raw_scores, MASKED)
        new_max = jnp.maximum(running_max, jnp.max(masked_scores, axis=2))
        fresh = jnp.sum(
            jnp.where(allowed[None], jnp.exp(masked_scores - new_max[..., None]), 0.0), axis=2
        )
        return ((new_max, running_sum * jnp.exp(running_max - new_max) + fresh), None)

    start_max = jnp.full((local_heads, tok_rows), MASKED, jnp.float32)
    start_sum = jnp.zeros((local_heads, tok_rows), jnp.float32)
    final_max, final_sum = lax.scan(stat_turn, (start_max, start_sum), pieces)[0]
    log_total = final_max + jnp.log(final_sum)

    def out_turn(accum, piece_set):
        raw_scores, allowed = scores_of(piece_set[0], piece_set[2], piece_set[3])
        weights_low = jnp.where(
            allowed[None], jnp.exp(raw_scores - log_total[..., None]), 0.0
        ).astype(jnp.bfloat16)
        return (
            accum
            + jnp.einsum(
                "hqk,khd->qhd", weights_low, piece_set[1], preferred_element_type=jnp.float32
            ),
            None,
        )

    attended = lax.scan(out_turn, jnp.zeros((tok_rows, local_heads, HD), jnp.float32), pieces)[0]
    attended_low = attended.reshape(tok_rows, width_part).astype(jnp.bfloat16)
    attn_part = head_sums(jnp.dot(attended_low, out_full, preferred_element_type=jnp.float32))
    attn_scale = lax.rsqrt(row_single(jnp.sum(attn_part * attn_part, axis=1)) / D + EPSILON)
    residual = local_in.astype(jnp.float32) + attn_part * attn_scale[:, None] * attn_gain
    residual_full = full_rows(residual.astype(jnp.bfloat16))
    gate_proj = jnp.dot(residual_full, gate_full, preferred_element_type=jnp.float32)
    up_proj = jnp.dot(residual_full, up_full, preferred_element_type=jnp.float32)
    gate_sigmoid = jax.nn.sigmoid(gate_proj)
    mixed_hidden = (gate_proj * gate_sigmoid * up_proj).astype(jnp.bfloat16)
    ffn_part = head_sums(jnp.dot(mixed_hidden, down_full, preferred_element_type=jnp.float32))
    ffn_scale = lax.rsqrt(row_single(jnp.sum(ffn_part * ffn_part, axis=1)) / D + EPSILON)
    result = residual + ffn_part * ffn_scale[:, None] * ffn_gain
    query_full, key_full, value_full, gate_full, up_full, out_full, down_full = gather_weights(
        w_query, w_key, w_value, w_out, w_gate, w_up, w_down
    )
    grad_result = local_cot.astype(jnp.float32)
    grad_ffn, ffn_gain_term = norm_backward(grad_result, ffn_part, ffn_scale, ffn_gain)
    grad_ffn_low = full_rows(grad_ffn.astype(jnp.bfloat16))
    down_grad = jnp.einsum(
        "tf,td->fd", mixed_hidden, grad_ffn_low, preferred_element_type=jnp.float32
    )
    grad_mixed = jnp.einsum(
        "td,fd->tf", grad_ffn_low, down_full, preferred_element_type=jnp.float32
    )
    grad_gate_low = (
        grad_mixed * up_proj * gate_sigmoid * (1.0 + gate_proj * (1.0 - gate_sigmoid))
    ).astype(jnp.bfloat16)
    grad_up_low = (grad_mixed * gate_proj * gate_sigmoid).astype(jnp.bfloat16)
    gate_grad = jnp.einsum(
        "td,tf->df", residual_full, grad_gate_low, preferred_element_type=jnp.float32
    )
    up_grad = jnp.einsum(
        "td,tf->df", residual_full, grad_up_low, preferred_element_type=jnp.float32
    )
    resid_term = jnp.einsum(
        "tf,df->td", grad_gate_low, gate_full, preferred_element_type=jnp.float32
    ) + jnp.einsum("tf,df->td", grad_up_low, up_full, preferred_element_type=jnp.float32)
    grad_residual = grad_result + head_sums(resid_term)
    grad_attn, attn_gain_term = norm_backward(grad_residual, attn_part, attn_scale, attn_gain)
    grad_attn_low = full_rows(grad_attn.astype(jnp.bfloat16))
    out_grad = jnp.einsum(
        "te,td->ed", attended_low, grad_attn_low, preferred_element_type=jnp.float32
    )
    grad_heads = (
        jnp.einsum("td,ed->te", grad_attn_low, out_full, preferred_element_type=jnp.float32)
        .astype(jnp.bfloat16)
        .reshape(tok_rows, local_heads, HD)
    )
    row_delta = jnp.transpose(jnp.sum(grad_heads.astype(jnp.float32) * attended, axis=2))

    def score_grads(key_piece, value_piece, number_piece, logical_piece):
        raw_scores, allowed = scores_of(key_piece, number_piece, logical_piece)
        probabilities = jnp.where(allowed[None], jnp.exp(raw_scores - log_total[..., None]), 0.0)
        grad_probs = jnp.einsum(
            "qhd,khd->hqk", grad_heads, value_piece, preferred_element_type=jnp.float32
        )
        grad_scores = (probabilities * (grad_probs - row_delta[..., None])).astype(jnp.bfloat16)
        return (probabilities, grad_scores)

    zero_heads = jnp.zeros((tok_rows, local_heads, HD), jnp.float32)

    def back_turn(grad_acc, piece_set):
        key_piece, value_piece, number_piece, logical_piece = piece_set
        probabilities, grad_scores = score_grads(
            key_piece, value_piece, number_piece, logical_piece
        )
        grad_acc = (
            grad_acc
            + jnp.einsum("hqk,khd->qhd", grad_scores, key_piece, preferred_element_type=jnp.float32)
            * scaling
        )
        key_term = (
            jnp.einsum("hqk,qhd->khd", grad_scores, query_rot, preferred_element_type=jnp.float32)
            * scaling
        )
        value_term = jnp.einsum(
            "hqk,qhd->khd",
            probabilities.astype(jnp.bfloat16),
            grad_heads,
            preferred_element_type=jnp.float32,
        )
        return (grad_acc, (key_term, value_term))

    grad_query_rot, key_value_terms = lax.scan(back_turn, zero_heads, pieces)
    key_terms = key_value_terms[0].reshape(total_tokens, local_heads, HD)
    value_terms = key_value_terms[1].reshape(total_tokens, local_heads, HD)
    grad_key_rot, grad_value_own = (
        lax.psum_scatter(
            key_terms.astype(jnp.bfloat16), "ctx", scatter_dimension=0, tiled=True
        ).astype(jnp.float32),
        lax.psum_scatter(
            value_terms.astype(jnp.bfloat16), "ctx", scatter_dimension=0, tiled=True
        ).astype(jnp.float32),
    )
    grad_query_normed = rotate(grad_query_rot, -offset_own).reshape(tok_rows, width_part)
    grad_key_normed = rotate(grad_key_rot, -offset_own).reshape(tok_rows, width_part)
    query_gain_term = jnp.sum(grad_query_normed * query_proj * query_scale[:, None], axis=0)
    key_gain_term = jnp.sum(grad_key_normed * key_proj * key_scale[:, None], axis=0)
    weighted_query = grad_query_normed * query_gain
    weighted_key = grad_key_normed * key_gain
    query_dot, key_dot = row_pair(
        jnp.sum(weighted_query * query_proj, axis=1), jnp.sum(weighted_key * key_proj, axis=1)
    )
    grad_query_low = (
        query_scale[:, None] * weighted_query
        - query_proj * (query_scale * query_scale * query_scale * query_dot / D)[:, None]
    ).astype(jnp.bfloat16)
    grad_key_low = (
        key_scale[:, None] * weighted_key
        - key_proj * (key_scale * key_scale * key_scale * key_dot / D)[:, None]
    ).astype(jnp.bfloat16)
    grad_value_low = grad_value_own.reshape(tok_rows, width_part).astype(jnp.bfloat16)
    query_grad = jnp.einsum(
        "td,te->de", full_in, grad_query_low, preferred_element_type=jnp.float32
    )
    key_grad = jnp.einsum("td,te->de", full_in, grad_key_low, preferred_element_type=jnp.float32)
    value_grad = jnp.einsum(
        "td,te->de", full_in, grad_value_low, preferred_element_type=jnp.float32
    )
    input_term = jnp.einsum(
        "te,de->td", grad_query_low, query_full, preferred_element_type=jnp.float32
    )
    input_term = input_term + jnp.einsum(
        "te,de->td", grad_key_low, key_full, preferred_element_type=jnp.float32
    )
    input_term = input_term + jnp.einsum(
        "te,de->td", grad_value_low, value_full, preferred_element_type=jnp.float32
    )
    grad_input = grad_residual + head_sums(input_term)
    row_grads = (
        lax.psum_scatter(
            query_grad.astype(jnp.bfloat16), "ctx", scatter_dimension=0, tiled=True
        ).astype(jnp.float32),
        lax.psum_scatter(
            key_grad.astype(jnp.bfloat16), "ctx", scatter_dimension=0, tiled=True
        ).astype(jnp.float32),
        lax.psum_scatter(
            value_grad.astype(jnp.bfloat16), "ctx", scatter_dimension=0, tiled=True
        ).astype(jnp.float32),
        lax.psum_scatter(
            gate_grad.astype(jnp.bfloat16), "ctx", scatter_dimension=0, tiled=True
        ).astype(jnp.float32),
        lax.psum_scatter(
            up_grad.astype(jnp.bfloat16), "ctx", scatter_dimension=0, tiled=True
        ).astype(jnp.float32),
    )
    col_grads = (
        lax.psum_scatter(
            out_grad.astype(jnp.bfloat16), "ctx", scatter_dimension=1, tiled=True
        ).astype(jnp.float32),
        lax.psum_scatter(
            down_grad.astype(jnp.bfloat16), "ctx", scatter_dimension=1, tiled=True
        ).astype(jnp.float32),
    )
    gain_totals = lax.psum((query_gain_term, key_gain_term, attn_gain_term, ffn_gain_term), "ctx")
    back_result, back_grad = (
        lax.all_to_all(result.astype(jnp.bfloat16), "ctx", split_axis=0, concat_axis=0, tiled=True),
        lax.all_to_all(
            grad_input.astype(jnp.bfloat16), "ctx", split_axis=0, concat_axis=0, tiled=True
        ),
    )
    return (
        undeal(back_result),
        undeal(back_grad),
        row_grads[0],
        row_grads[1],
        row_grads[2],
        col_grads[0],
        row_grads[3],
        row_grads[4],
        col_grads[1],
        gain_totals[0],
        gain_totals[1],
        gain_totals[2],
        gain_totals[3],
    )


def sharded(layer, mesh, ctx, head):
    wide, tall, line = P(ctx, head), P(head, ctx), P(head)
    return jax.shard_map(
        layer,
        mesh=mesh,
        in_specs=(
            *(wide,) * 5,
            tall,
            wide,
            wide,
            tall,
            *(line,) * 4,
            P(),
            P(),
        ),
        out_specs=(*(wide,) * 5, tall, wide, wide, tall, *(line,) * 4),
        check_vma=False,
    )


def solution(mesh):
    if dict(mesh.shape) == {"ctx": 8, "head": 4}:
        split = Mesh(mesh.devices.reshape(4, 2, 2, 2), AXES)
        return sharded(plane_layer, split, CTX, ("x", "core"))
    return sharded(on_device, mesh, "ctx", "head")
```

```python
import math

import jax
import jax.numpy as jnp
import numpy as np
from jax import lax
from jax.experimental import pallas as pl
from jax.experimental.pallas import tpu as pltpu
from jax.sharding import Mesh
from jax.sharding import PartitionSpec as P

D = 2048
HD = 128


EPSILON = 1e-06
ROPE_THETA = 500000.0
MASKED = -1e30


BF = jnp.bfloat16
F32 = jnp.float32
MESH = pl.DeviceIdType.MESH
AXES = ("z", "y", "x", "core")
CTX = ("z", "y")
STRIP = 16
ANY = pl.BlockSpec(memory_space=pl.ANY)
VMEM = pl.BlockSpec(memory_space=pltpu.VMEM)
DMA = pltpu.SemaphoreType.DMA
BIG_VMEM = 60 * 1024 * 1024


def place():
    return tuple(lax.axis_index(name) for name in AXES)


def greet(targets):
    barrier = pltpu.get_barrier_semaphore()
    for target in targets:
        pl.semaphore_signal(barrier, inc=1, device_id=target, device_id_type=MESH)
    pl.semaphore_wait(barrier, len(targets))


def near_first(step, z):
    high = z // 2
    low = z + high * (3 - 2 * z)
    value = (low, 1 - low, 2, 3)[step]
    return value + high * (3 - 2 * value)


def plane_axes(me, turn):
    z, y, x, k = me
    a = x * (1 - turn) + y * turn
    b = y * (1 - turn) + x * turn

    def slot(zp, ap, bp):
        yp = bp * (1 - turn) + ap * turn
        xp = ap * (1 - turn) + bp * turn
        return zp * 4 + yp * 2 + xp

    dev_a = (z, y * (1 - turn) + (1 - y) * turn, (1 - x) * (1 - turn) + x * turn, k)
    dev_b = (z, (1 - y) * (1 - turn) + y * turn, x * (1 - turn) + (1 - x) * turn, k)
    return a, b, slot, dev_a, dev_b


EVEN = ((0, 1),) * 4
MORE_X = ((0, 1), (1, 1)) * 2
ALL_X = ((1, 1),) * 4
TURNS_OPEN = ALL_X
TURNS_ATTENTION = (MORE_X, EVEN)
TURNS_FFN_BACK = (EVEN, EVEN)
TURNS_CLOSE = ALL_X


def layer_axes(me, turns):
    return [plane_axes(me, t0 + me[3] * (t1 - t0)) for t0, t1 in turns]


def greet_plane(me, others=()):
    z, y, x, k = me
    barrier = pltpu.get_barrier_semaphore()
    targets = [(z, 1 - y, x, k), (z, y, 1 - x, k), *others]
    for target in targets:
        pl.semaphore_signal(barrier, inc=1, device_id=target, device_id_type=MESH)

    @pl.when(z < 3)
    def _():
        pl.semaphore_signal(barrier, inc=1, device_id=(z + 1, y, x, k), device_id_type=MESH)

    @pl.when(z > 0)
    def _():
        pl.semaphore_signal(barrier, inc=1, device_id=(z - 1, y, x, k), device_id_type=MESH)

    inner = (z + 2) // 3 - z // 3
    pl.semaphore_wait(barrier, len(targets) + 1 + inner)


GATHER_SEMS = [DMA((16,)), DMA((4,)), DMA((4,)), DMA((4,)), DMA((8,))]


DEAL_ORDER = (4, 1, 5, 2, 6, 3, 7)
OPEN_DEAL = 0
OPEN_RATE = 2
DEALT_FIRST = 5
FORWARD_RATE = 1
FORWARD_EVERY = 1
BACK_EVERY = 1
BACK_RATE = 1
CLOSE_FIRST = 0
CLOSE_NEXT = 4
SUM_LAG = 1
EARLY_LAYERS = True
BACK_LAG = 1
CLOSE_LAG = 2
CLOSE_RATE = 1


class Trickle:
    def __init__(self):
        self.waiting = []
        self.calls = 0

    def add(self, copies):
        self.waiting.extend(copies)

    def tick(self, count=1, every=1):
        self.calls += 1
        if self.calls % every:
            return
        for start in self.waiting[:count]:
            start()
        self.waiting = self.waiting[count:]

    def flush(self):
        self.tick(len(self.waiting))


def gather_plane(
    me,
    own_ref,
    view,
    sems,
    turns,
    between=lambda step: None,
    arrived=None,
    tick=lambda: None,
    early=False,
):
    z, y, x, k = me
    recv, up_send, down_send, a_send, b_send = sems
    axes = layer_axes(me, turns)

    def copy(src, index, send_sem, device):
        return pltpu.make_async_remote_copy(
            src_ref=src,
            dst_ref=view(index),
            send_sem=send_sem,
            recv_sem=recv.at[index],
            device_id=device,
            device_id_type=MESH,
        )

    def landed(index):
        copy(view(index), index, a_send.at[0], axes[0][3]).wait_recv()

    def layer_landed(step):
        tick()
        a, b, slot, dev_a, dev_b = axes[step]
        zp = near_first(step, z)
        landed(slot(zp, a, 1 - b))
        landed(slot(zp, 1 - a, 1 - b))
        if arrived is not None:
            arrived(step)

    for step in range(5):
        if step < 4:
            a, b, slot, dev_a, dev_b = axes[step]
            zp = near_first(step, z)
            index = slot(zp, a, b)
            if step == 0:
                src = own_ref
            else:
                landed(index)
                src = view(index)

            @pl.when((zp <= z) & (z < 3))
            def _():
                copy(src, index, up_send.at[zp], (z + 1, y, x, k)).start()

            @pl.when((zp >= z) & (z > 0))
            def _():
                copy(src, index, down_send.at[zp], (z - 1, y, x, k)).start()

            copy(src, index, a_send.at[step], dev_a).start()
            copy(src, index, b_send.at[step], dev_b).start()
            tick()
        if step > 0:
            a, b, slot, dev_a, dev_b = axes[step - 1]
            index = slot(near_first(step - 1, z), 1 - a, b)
            landed(index)
            copy(view(index), index, b_send.at[3 + step], dev_b).start()
            tick()
        between(step)
        if step >= 2 and early:
            layer_landed(step - 2)
    for step in ((3,) if early else range(4)):
        layer_landed(step)
    for step in range(4):
        a, b, slot, dev_a, dev_b = axes[step]
        zp = near_first(step, z)
        for ap, number in ((a, step), (1 - a, 4 + step)):
            index = slot(zp, ap, b)
            copy(view(index), index, b_send.at[number], dev_b).wait_send()
        index = slot(zp, a, b)
        copy(view(index), index, a_send.at[step], dev_a).wait_send()

        @pl.when((zp <= z) & (z < 3))
        def _():
            copy(view(index), index, up_send.at[zp], (z + 1, y, x, k)).wait_send()

        @pl.when((zp >= z) & (z > 0))
        def _():
            copy(view(index), index, down_send.at[zp], (z - 1, y, x, k)).wait_send()


def reduce_scratch(rows, width):
    return [
        pltpu.VMEM((4, 2, rows, width), BF),
        pltpu.VMEM((4, rows, width), BF),
        pltpu.VMEM((4, rows, width), BF),
        pltpu.VMEM((4, rows, width), BF),
        pltpu.VMEM((4, rows, width), BF),
        pltpu.VMEM((4, rows, width), BF),
        DMA((8,)),
        DMA((8,)),
        DMA((4,)),
        DMA((4,)),
        DMA((4,)),
        DMA((4,)),
        DMA((4,)),
    ]


N_REDUCE = 13


def strips(rows, work, strip=STRIP):
    def body(i, carry):
        work(pl.ds(pl.multiple_of(i * strip, strip), strip))
        return carry

    lax.fori_loop(0, rows // strip, body, 0)


def reduce_plane(
    me,
    terms,
    rows,
    scratch,
    turns,
    produce,
    finish,
    after_terms=lambda: None,
    tick=lambda: None,
):
    z, y, x, k = me
    (from_b, to_a, from_a, to_z, from_low, from_high) = scratch[:6]
    (b_send, b_recv, a_send, a_recv, z_send, low_recv, high_recv) = scratch[6:]
    axes = layer_axes(me, turns)[::-1]
    order = [near_first(step, z) for step in (3, 2, 1, 0)]

    def start_of(step, ap, bp):
        return pl.multiple_of(axes[step][2](order[step], ap, bp) * rows, rows)

    def copy_b(step, flip):
        a, b, slot, dev_a, dev_b = axes[step]
        zp, ap = order[step], (1 - a if flip else a)
        return pltpu.make_async_remote_copy(
            src_ref=terms.at[pl.ds(start_of(step, ap, 1 - b), rows), :],
            dst_ref=from_b.at[zp, ap],
            send_sem=b_send.at[zp * 2 + ap],
            recv_sem=b_recv.at[zp * 2 + ap],
            device_id=dev_b,
            device_id_type=MESH,
        )

    def copy_a(step):
        zp, dev_a = order[step], axes[step][3]
        return pltpu.make_async_remote_copy(
            src_ref=to_a.at[zp],
            dst_ref=from_a.at[zp],
            send_sem=a_send.at[zp],
            recv_sem=a_recv.at[zp],
            device_id=dev_a,
            device_id_type=MESH,
        )

    def copy_z(zp, target, recv, to):
        return pltpu.make_async_remote_copy(
            src_ref=to_z.at[zp],
            dst_ref=target.at[zp],
            send_sem=z_send.at[zp],
            recv_sem=recv.at[zp],
            device_id=(to, y, x, k),
            device_id_type=MESH,
        )

    def copy_up(zp):
        return copy_z(zp, from_low, low_recv, z + 1)

    def copy_down(zp):
        return copy_z(zp, from_high, high_recv, z - 1)

    def mine(step, flip, strip):
        a, b = axes[step][:2]
        at = start_of(step, 1 - a if flip else a, b) + strip.start
        return terms[pl.ds(pl.multiple_of(at, STRIP), STRIP), :].astype(F32)

    for step in range(4):
        produce(order[step])
        for flip in (True, False):
            copy_b(step, flip).start()
        tick()
    after_terms()

    for step in range(4 + SUM_LAG):
        if step < 4:
            copy_b(step, True).wait_recv()

            def first(strip, step=step):
                zp, ap = order[step], 1 - axes[step][0]
                to_a[zp, strip] = (
                    mine(step, True, strip) + from_b[zp, ap, strip].astype(F32)
                ).astype(BF)

            strips(rows, first)
            copy_a(step).start()
            tick()
        if step >= SUM_LAG:
            done = step - SUM_LAG
            tick()
            copy_b(done, False).wait_recv()
            copy_a(done).wait_recv()

            def own_sum(strip, last=done):
                zp, ap = order[last], axes[last][0]
                return (
                    mine(last, False, strip)
                    + from_b[zp, ap, strip].astype(F32)
                    + from_a[zp, strip].astype(F32)
                )

            if done < 3:
                zp = order[done]
                upward = zp > z

                @pl.when(upward & (z > 0))
                def _(zp=zp, own_sum=own_sum):
                    copy_up(zp).wait_recv()

                    def work(strip):
                        to_z[zp, strip] = (own_sum(strip) + from_low[zp, strip].astype(F32)).astype(BF)

                    strips(rows, work)

                @pl.when(jnp.logical_not(upward) & (z < 3))
                def _(zp=zp, own_sum=own_sum):
                    copy_down(zp).wait_recv()

                    def work(strip):
                        to_z[zp, strip] = (own_sum(strip) + from_high[zp, strip].astype(F32)).astype(BF)

                    strips(rows, work)

                @pl.when((z == 0) | (z == 3))
                def _(zp=zp, own_sum=own_sum):
                    def work(strip):
                        to_z[zp, strip] = own_sum(strip).astype(BF)

                    strips(rows, work)

                @pl.when(upward)
                def _(zp=zp):
                    copy_up(zp).start()

                @pl.when(jnp.logical_not(upward))
                def _(zp=zp):
                    copy_down(zp).start()

            else:

                @pl.when(z == 0)
                def _():
                    copy_down(z).wait_recv()
                    strips(rows, lambda s: finish(s, own_sum(s) + from_high[z, s].astype(F32)))

                @pl.when(z == 3)
                def _():
                    copy_up(z).wait_recv()
                    strips(rows, lambda s: finish(s, own_sum(s) + from_low[z, s].astype(F32)))

                @pl.when((z > 0) & (z < 3))
                def _():
                    copy_up(z).wait_recv()
                    copy_down(z).wait_recv()
                    strips(
                        rows,
                        lambda s: finish(
                            s,
                            own_sum(s) + from_low[z, s].astype(F32) + from_high[z, s].astype(F32),
                        ),
                    )

    def settle():
        for step in range(4):
            copy_b(step, True).wait_send()
            copy_b(step, False).wait_send()
            copy_a(step).wait_send()
        for zp in order[:3]:
            copy_up(zp).wait_send()

    return settle


def own_tile(me):
    z, y, x, k = me
    return z * 2 + y


def gather_view(out_ref, rows):
    def view(slot):
        return out_ref.at[pl.ds(pl.multiple_of(slot * rows, rows), rows), :]

    return view


def hand_out_copies(me, own_ref, out_ref, send, recv):
    z, y, x, k = me
    rows, width = own_ref.shape
    part = width // 4
    target_rows = pl.ds(pl.multiple_of(k * 2 * rows + x * rows, rows), rows)

    def copy(xt, kt, number):
        return pltpu.make_async_remote_copy(
            src_ref=own_ref.at[:, pl.ds(pl.multiple_of((2 * xt + kt) * part, part), part)],
            dst_ref=out_ref.at[target_rows, :],
            send_sem=send.at[number],
            recv_sem=recv.at[number],
            device_id=(z, y, xt, kt),
            device_id_type=MESH,
        )

    local = pltpu.make_async_copy(
        own_ref.at[:, pl.ds(pl.multiple_of((2 * x + k) * part, part), part)],
        out_ref.at[target_rows, :],
        recv.at[3],
    )
    return [copy(x, 1 - k, 0), copy(1 - x, k, 1), copy(1 - x, 1 - k, 2)], local


def pair_devices(me):
    z, y, x, k = me
    return [(z, y, x, 1 - k), (z, y, 1 - x, 1 - k)]


def row_scale(values):
    return lax.rsqrt(jnp.sum(values * values, axis=1, keepdims=True) / values.shape[1] + EPSILON)


def norm_back_strip(grad, values, gain):
    scale = row_scale(values)
    term = grad * values * scale
    weighted = grad * gain
    dot = jnp.sum(weighted * values, axis=1, keepdims=True)
    back = scale * weighted - values * (scale * scale * scale * dot / values.shape[1])
    return back, term[:8] + term[8:]


def comm_call(body, name, number, out_shape, in_specs, out_specs, scratch, lift=True):
    lifted = [i for i, spec in enumerate(in_specs) if spec is VMEM] if lift else []
    leaving = [i for i, spec in enumerate(out_specs) if spec is VMEM]
    first_out = len(in_specs)

    def with_copies(*refs):
        refs = list(refs)
        sems = refs.pop()
        count = len(lifted) + len(leaving)
        held = refs[len(refs) - count :]
        refs = refs[: len(refs) - count]
        loads, stores, begun = [], [], []
        for n, i in enumerate(lifted):
            loads.append(pltpu.make_async_copy(refs[i], held[n], sems.at[n]))
            refs[i] = held[n]
        for n, i in enumerate(leaving, len(lifted)):
            stores.append((held[n], pltpu.make_async_copy(held[n], refs[first_out + i], sems.at[n])))
            refs[first_out + i] = held[n]
        for copy in loads:
            copy.start()

        def loaded():
            for copy in loads:
                copy.wait()

        def leave(*done):
            for ref, copy in stores:
                if any(ref is other for other in done):
                    copy.start()
                    begun.append(ref)

        body(*refs, loaded=loaded, leave=leave)
        leave(*[ref for ref, _ in stores if not any(ref is other for other in begun)])
        for _, copy in stores:
            copy.wait()

    def call(*args):
        extra = [pltpu.VMEM(args[i].shape, args[i].dtype) for i in lifted]
        extra += [pltpu.VMEM(out_shape[i].shape, out_shape[i].dtype) for i in leaving]
        return pl.pallas_call(
            with_copies,
            name=name,
            out_shape=out_shape,
            in_specs=[ANY if i in lifted else spec for i, spec in enumerate(in_specs)],
            out_specs=tuple(ANY for _ in out_specs),
            scratch_shapes=[*scratch, *extra, DMA((len(extra),))],
            compiler_params=pltpu.CompilerParams(
                collective_id=number, has_side_effects=True, vmem_limit_bytes=BIG_VMEM
            ),
        )(*args)

    return call


def same_x_greet(me):
    z, y, x, k = me
    barrier = pltpu.get_barrier_semaphore()
    number = z * 4 + y * 2 + k

    def body(i, carry):
        other = lax.rem(number + i, 16)
        pl.semaphore_signal(
            barrier,
            inc=1,
            device_id=(other // 4, (other // 2) % 2, x, other % 2),
            device_id_type=MESH,
        )
        return carry

    lax.fori_loop(1, 16, body, 0)
    for kt in (k, 1 - k):
        pl.semaphore_signal(barrier, inc=1, device_id=(z, y, 1 - x, kt), device_id_type=MESH)
    pl.semaphore_wait(barrier, 17)


def masked_scores(q, keys, low, high, logical):
    raw = lax.dot_general(q, keys, (((1,), (1,)), ((), ())), preferred_element_type=F32)
    allowed = (logical >= low) & (logical <= high)
    return raw * (1.0 / math.sqrt(HD)), allowed


def eye_mask():
    return lax.broadcasted_iota(jnp.int32, (HD, HD), 0) == lax.broadcasted_iota(
        jnp.int32, (HD, HD), 1
    )


def column_to_row(column, eye):
    return jnp.sum(jnp.where(eye, column, 0.0), axis=0, keepdims=True)


def row_to_column(row, eye):
    return jnp.sum(jnp.where(eye, row, 0.0), axis=1, keepdims=True)


def open_layer(
    inputs,
    cotangent,
    w_query,
    w_key,
    w_value,
    w_out,
    w_gate,
    w_up,
    w_down,
    query_gain,
    key_gain,
    attn_gain,
    ffn_gain,
    order,
    lengths,
    frequency,
):
    rows, part = inputs.shape
    half = rows // 2
    quarter = half // 2
    tokens, width = 8 * half, 4 * part
    hidden = w_gate.shape[1]
    down = hidden // 8

    def body(*refs, loaded, leave):
        (in_ref, cot_ref, wq_ref, wk_ref, wv_ref, wo_ref, wg_ref, wu_ref, wd_ref) = refs[:9]
        gain_parts = refs[9:13]
        (order_ref, lengths_ref, frequency_ref) = refs[13:16]
        (cos_ref, sin_ref, low_ref, high_ref, log_ref) = refs[27:32]
        gain_ref = refs[-1]
        refs = refs[:10] + refs[16:27] + refs[32:-1]
        (full_out, own_out, own_cot_ref, wqkv_ref, wout_ref, gains_ref, gu_out, down_ref) = refs[10:18]
        (q_ref, k_ref, v_ref) = refs[18:21]
        (full_ref, shard, cot_half, qkv_raw, out_raw, gu_raw, d_raw) = refs[21:28]
        (qkv_stage, out_stage, gu_stage, d_stage) = refs[28:32]
        (load_sem, pair_send, pair_recv, local_sem, deal_send, deal_recv) = refs[32:38]
        (share_send, share_recv, gain_send, gain_recv, cot_sems, keep_sem) = refs[38:44]
        (down_send, down_recv) = refs[44:46]
        gather_sems = refs[46:]
        me = z, y, x, k = place()
        ctx = own_tile(me)
        sibling = (z, y, x, 1 - k)

        loads = [
            pltpu.make_async_copy(src, dst, load_sem.at[i])
            for i, (src, dst) in enumerate(
                [
                    (wq_ref, qkv_raw.at[0]),
                    (wk_ref, qkv_raw.at[1]),
                    (wv_ref, qkv_raw.at[2]),
                    (wo_ref, out_raw),
                    (wg_ref, gu_raw.at[0]),
                    (wu_ref, gu_raw.at[1]),
                    (wd_ref, d_raw),
                ]
            )
        ]
        for load in loads:
            load.start()
        same_x_greet(me)
        loaded()

        def pair_copy(src, dst, number):
            columns = pl.ds(pl.multiple_of(k * part, part), part)
            remote = pltpu.make_async_remote_copy(
                src_ref=src.at[pl.ds(pl.multiple_of((1 - k) * half, half), half), :],
                dst_ref=dst.at[:, columns],
                send_sem=pair_send.at[number],
                recv_sem=pair_recv.at[number],
                device_id=sibling,
                device_id_type=MESH,
            )
            local = pltpu.make_async_copy(
                src.at[pl.ds(pl.multiple_of(k * half, half), half), :],
                dst.at[:, columns],
                local_sem.at[number],
            )
            remote.start()
            local.start()
            return remote, local

        first = pair_copy(in_ref, shard, 0)
        second = pair_copy(cot_ref, cot_half, 1)

        for i, gain_part in enumerate(gain_parts):
            gain_ref[i : i + 1, :] = gain_part[...]

        def gain_copy(xt, kt, number):
            return pltpu.make_async_remote_copy(
                src_ref=gain_ref,
                dst_ref=gains_ref.at[:, pl.ds(pl.multiple_of((2 * x + k) * part, part), part)],
                send_sem=gain_send.at[number],
                recv_sem=gain_recv.at[number],
                device_id=(z, y, xt, kt),
                device_id_type=MESH,
            )

        gain_copies = [gain_copy(x, 1 - k, 0), gain_copy(1 - x, k, 1), gain_copy(1 - x, 1 - k, 2)]
        for copy in gain_copies:
            copy.start()
        gain_local = pltpu.make_async_copy(
            gain_ref,
            gains_ref.at[:, pl.ds(pl.multiple_of((2 * x + k) * part, part), part)],
            local_sem.at[2],
        )
        gain_local.start()

        first[0].wait_recv()
        first[1].wait()

        def view(slot):
            return full_ref.at[
                pl.ds(pl.multiple_of((slot // 2) * half, half), half),
                pl.ds(pl.multiple_of((slot % 2) * 2 * part, 2 * part), 2 * part),
            ]

        own_slot = ctx * 2 + x
        own_local = pltpu.make_async_copy(shard, view(own_slot), local_sem.at[3])
        own_local.start()

        def deal(e):
            j, r = e // 2, e % 2
            return [
                pltpu.make_async_remote_copy(
                    src_ref=src,
                    dst_ref=dst,
                    send_sem=deal_send.at[i, e],
                    recv_sem=deal_recv.at[i, ctx],
                    device_id=(2 * k + e // 4, (e // 2) % 2, x, r),
                    device_id_type=MESH,
                )
                for i, (src, dst) in enumerate(deal_ends(j, r))
            ]

        def deal_ends(j, r):
            at = pl.ds(pl.multiple_of(ctx * 2 * HD + r * HD, HD), HD)
            return (
                (
                    qkv_stage.at[:, r * HD : (r + 1) * HD, j * HD : (j + 1) * HD],
                    wqkv_ref.at[:, at, :],
                ),
                (
                    out_stage.at[j * HD : (j + 1) * HD, r * HD : (r + 1) * HD],
                    wout_ref.at[:, at],
                ),
            )

        trickle = Trickle()
        stays = k == z // 2
        own_e = (z % 2) * 4 + y * 2 + k

        def deal_all():
            for load in loads[:4]:
                load.wait()

            def round_qkv(s):
                for i in range(3):
                    qkv_stage[i, s] = qkv_raw[i, s].astype(BF)

            strips(rows, round_qkv)

            def round_out(s):
                out_stage[s] = out_raw[s].astype(BF)

            strips(2 * rows, round_out, 32)
            if OPEN_DEAL == 0:
                begin_deal()

        def begin_deal():
            trickle.add([lambda e=e: deal_start(e) for e in range(8)])

        def deal_start(e):
            @pl.when(jnp.logical_not(stays & (own_e == e)))
            def _():
                for copy in deal(e):
                    copy.start()

            @pl.when(stays & (own_e == e))
            def _():
                for i, (src, dst) in enumerate(deal_ends(e // 2, e % 2)):
                    pltpu.make_async_copy(src, dst, deal_recv.at[i, ctx]).start()

        def cot_begin():
            second[0].wait_recv()
            second[1].wait()
            cot_remote.start()
            cot_local.start()

        wide = pl.ds(pl.multiple_of(x * 2 * part, 2 * part), 2 * part)
        cot_remote = pltpu.make_async_remote_copy(
            src_ref=cot_half.at[pl.ds(pl.multiple_of((1 - x) * quarter, quarter), quarter), :],
            dst_ref=own_cot_ref.at[:, wide],
            send_sem=cot_sems.at[0],
            recv_sem=cot_sems.at[1],
            device_id=(z, y, 1 - x, k),
            device_id_type=MESH,
        )
        cot_local = pltpu.make_async_copy(
            cot_half.at[pl.ds(pl.multiple_of(x * quarter, quarter), quarter), :],
            own_cot_ref.at[:, wide],
            cot_sems.at[2],
        )

        keeps = [
            pltpu.make_async_copy(gu_stage.at[0], gu_out.at[0], keep_sem.at[0]),
            pltpu.make_async_copy(gu_stage.at[1], gu_out.at[1], keep_sem.at[1]),
            pltpu.make_async_copy(
                d_stage.at[pl.ds(pl.multiple_of(ctx * down, down), down), :],
                down_ref.at[:, pl.ds(pl.multiple_of(ctx * rows, rows), rows)],
                keep_sem.at[2],
            ),
        ]

        def down_copy(t):
            to = ctx + t - 8 * ((ctx + t) // 8)
            return pltpu.make_async_remote_copy(
                src_ref=d_stage.at[pl.ds(pl.multiple_of(to * down, down), down), :],
                dst_ref=down_ref.at[:, pl.ds(pl.multiple_of(ctx * rows, rows), rows)],
                send_sem=down_send.at[t],
                recv_sem=down_recv.at[t],
                device_id=(to // 2, to % 2, x, k),
                device_id_type=MESH,
            )

        def down_landed(t):
            c = ctx + 8 - t - 8 * ((ctx + 8 - t) // 8)
            part_of = down_ref.at[:, pl.ds(pl.multiple_of(c * rows, rows), rows)]
            pltpu.make_async_remote_copy(
                src_ref=part_of,
                dst_ref=part_of,
                send_sem=down_send.at[t],
                recv_sem=down_recv.at[t],
                device_id=sibling,
                device_id_type=MESH,
            ).wait_recv()

        def deal_down():
            trickle.add([lambda t=t: down_copy(t).start() for t in DEAL_ORDER])

        def round_up(i):
            loads[4 + i].wait()

            def work(s):
                gu_stage[i, s] = gu_raw[i, s].astype(BF)

            strips(rows, work)
            keeps[i].start()

        def round_down():
            loads[6].wait()

            def work(s):
                d_stage[s] = d_raw[s].astype(BF)

            strips(hidden, work, 128)
            keeps[2].start()

        def positions():
            blocks = order_ref.shape[1]
            square = lax.broadcasted_iota(jnp.int32, (blocks, blocks), 0)
            square = square == lax.broadcasted_iota(jnp.int32, (blocks, blocks), 1)
            column = row_to_column(order_ref[...].astype(F32), square)
            lane = lax.broadcasted_iota(jnp.int32, (1, 2 * tokens), 1)
            other = (lane >= tokens).astype(jnp.int32)
            core = k + other - 2 * k * other
            lane = lane - tokens * other
            in_half = lane & (half - 1)
            block_rows = 2 * tokens // blocks
            block = (lane - in_half) // half * (2 * half // block_rows)
            block = block + core * (half // block_rows)
            block = block + (in_half - (in_half & (block_rows - 1))) // block_rows
            match = lax.broadcasted_iota(jnp.int32, (blocks, 2 * tokens), 0) == block
            first_of = jnp.sum(jnp.where(match, column, 0.0), axis=0, keepdims=True) * block_rows
            logical = first_of + (in_half & (block_rows - 1)).astype(F32)
            log_ref[...] = logical
            own = logical[:, :tokens]
            begin = jnp.zeros_like(own)
            end = jnp.zeros((1, 1), F32)
            for j in range(lengths_ref.shape[1]):
                length = lengths_ref[:, j : j + 1].astype(F32)
                end = end + length
                begin = begin + jnp.where(own >= end, length, 0.0)
            eye = eye_mask()
            for i in range(tokens // HD):
                piece = slice(i * HD, (i + 1) * HD)
                low = row_to_column(begin[:, piece], eye)
                high = row_to_column(own[:, piece], eye)
                low_ref[piece, :] = low
                high_ref[piece, :] = high
                angles = (high - low) * frequency_ref[...]
                cos_ref[piece, :] = jnp.cos(angles)
                sine = jnp.sin(angles)
                left = lax.broadcasted_iota(jnp.int32, (HD, HD), 1) < HD // 2
                sin_ref[piece, :] = jnp.where(left, -sine, sine)
            leave(cos_ref, sin_ref, low_ref, high_ref, log_ref)

        between = [
            deal_all,
            lambda: (cot_begin(), round_down()),
            lambda: (round_up(0), round_up(1)),
            positions,
            lambda: None,
        ]

        def open_between(step):
            if 0 < step == OPEN_DEAL:
                begin_deal()
            if step == max(OPEN_DEAL, 1):
                if step == 1:
                    between[1]()
                deal_down()
                if step == 1:
                    return
            between[step]()

        def deal_wait(c):
            at = slice(c * 2 * HD, c * 2 * HD + HD)
            pltpu.make_async_copy(
                qkv_stage.at[:, :HD, :HD], wqkv_ref.at[:, at, :], deal_recv.at[0, c]
            ).wait()
            pltpu.make_async_copy(
                out_stage.at[:HD, :HD], wout_ref.at[:, at], deal_recv.at[1, c]
            ).wait()

        def share(c, r):
            at = pl.ds(pl.multiple_of(c * 2 * HD + r * HD, HD), HD)
            return [
                pltpu.make_async_remote_copy(
                    src_ref=ref,
                    dst_ref=ref,
                    send_sem=share_send.at[i, c],
                    recv_sem=share_recv.at[i, c],
                    device_id=sibling,
                    device_id_type=MESH,
                )
                for i, ref in enumerate((wqkv_ref.at[:, at, :], wout_ref.at[:, at]))
            ]

        def project_layer(step):
            if step == 0:
                trickle.flush()
                own_local.wait()
                for c in range(8):
                    deal_wait(c)
                    for copy in share(c, k):
                        copy.start()
                for c in range(8):
                    for copy in share(c, 1 - k):
                        copy.wait_recv()
                leave(wqkv_ref, wout_ref)
            at = pl.ds(pl.multiple_of(near_first(step, z) * 2 * half, 2 * half), 2 * half)
            tile = full_ref[at, :]
            q_ref[at, :] = jnp.dot(tile, wqkv_ref[0], preferred_element_type=F32)
            k_ref[at, :] = jnp.dot(tile, wqkv_ref[1], preferred_element_type=F32)
            v_ref[at, :] = jnp.dot(tile, wqkv_ref[2], preferred_element_type=F32).astype(BF)

        gather_plane(
            me,
            shard,
            view,
            gather_sems,
            TURNS_OPEN,
            open_between,
            project_layer,
            lambda: trickle.tick(OPEN_RATE),
        )

        full_keep = pltpu.make_async_copy(full_ref, full_out, keep_sem.at[3])
        full_keep.start()
        own_rows = pl.ds(pl.multiple_of(own_slot * quarter, quarter), quarter)
        own_keep = pltpu.make_async_copy(full_ref.at[own_rows, :], own_out, keep_sem.at[4])
        own_keep.start()
        for e in range(8):

            @pl.when(jnp.logical_not(stays & (own_e == e)))
            def _(e=e):
                for copy in deal(e):
                    copy.wait_send()

        for c in range(8):
            for copy in share(c, k):
                copy.wait_send()
        first[0].wait_send()
        second[0].wait_send()
        for copy in gain_copies:
            copy.wait()
        gain_local.wait()
        cot_remote.wait()
        cot_local.wait()
        for keep in (*keeps, full_keep, own_keep):
            keep.wait()
        for t in range(1, 8):
            down_landed(t)
            down_copy(t).wait_send()

    shape = jax.ShapeDtypeStruct
    return comm_call(
        body,
        "open_layer",
        0,
        (
            shape((tokens, width), BF),
            shape((quarter, width), BF),
            shape((quarter, width), BF),
            shape((3, width, HD), BF),
            shape((HD, width), BF),
            shape((4, width), F32),
            shape((2, rows, hidden), BF),
            shape((down, width), BF),
            shape((tokens, HD), F32),
            shape((tokens, HD), F32),
            shape((tokens, HD), BF),
            shape((tokens, HD), F32),
            shape((tokens, HD), F32),
            shape((tokens, 1), F32),
            shape((tokens, 1), F32),
            shape((1, 2 * tokens), F32),
        ),
        [*[ANY] * 9, *[VMEM] * 7],
        (ANY, ANY, ANY, VMEM, VMEM, ANY, ANY, ANY, VMEM, VMEM, VMEM, *[VMEM] * 5),
        [
            pltpu.VMEM((tokens, width), BF),
            pltpu.VMEM((half, 2 * part), BF),
            pltpu.VMEM((half, 2 * part), BF),
            pltpu.VMEM((3, rows, part), F32),
            pltpu.VMEM((part, rows), F32),
            pltpu.VMEM((2, rows, hidden), F32),
            pltpu.VMEM((hidden, rows), F32),
            pltpu.VMEM((3, rows, part), BF),
            pltpu.VMEM((part, rows), BF),
            pltpu.VMEM((2, rows, hidden), BF),
            pltpu.VMEM((hidden, rows), BF),
            DMA((7,)),
            DMA((2,)),
            DMA((2,)),
            DMA((4,)),
            DMA((2, 8)),
            DMA((2, 8)),
            DMA((2, 8)),
            DMA((2, 8)),
            DMA((3,)),
            DMA((3,)),
            DMA((3,)),
            DMA((5,)),
            DMA((8,)),
            DMA((8,)),
            *GATHER_SEMS,
            pltpu.VMEM((4, part), F32),
        ],
        lift=False,
    )(
        inputs,
        cotangent,
        w_query,
        w_key,
        w_value,
        w_out,
        w_gate,
        w_up,
        w_down,
        query_gain,
        key_gain,
        attn_gain,
        ffn_gain,
        order,
        lengths,
        frequency,
    )


def plane_peer(me, i):
    z, y, x, k = me
    other = lax.rem(z * 4 + y * 2 + x + i, 16)
    return other, (other // 4, (other // 2) % 2, other % 2, k)


def plane_greet_all(me, others):
    barrier = pltpu.get_barrier_semaphore()

    def call(i, carry):
        pl.semaphore_signal(barrier, inc=1, device_id=plane_peer(me, i)[1], device_id_type=MESH)
        return carry

    lax.fori_loop(1, 16, call, 0)
    for other in others:
        pl.semaphore_signal(barrier, inc=1, device_id=other, device_id_type=MESH)
    pl.semaphore_wait(barrier, 15 + len(others))


def sum_begin(me, slots, send, recv):
    own = me[0] * 4 + me[1] * 2 + me[2]

    def copy(i, slot):
        return pltpu.make_async_remote_copy(
            src_ref=slots.at[slot],
            dst_ref=slots.at[slot],
            send_sem=send.at[i],
            recv_sem=recv.at[slot],
            device_id=plane_peer(me, i)[1],
            device_id_type=MESH,
        )

    def begin(i, carry):
        copy(i, own).start()
        return carry

    def landed(i, carry):
        copy(i, plane_peer(me, i)[0]).wait_recv()
        return carry

    def sent(i, carry):
        copy(i, own).wait_send()
        return carry

    lax.fori_loop(1, 16, begin, 0)

    def end():
        lax.fori_loop(1, 16, landed, 0)
        lax.fori_loop(1, 16, sent, 0)
        total = slots[0]
        for i in range(1, 16):
            total = total + slots[i]
        return total

    return end


def attention_forward(
    query, key, value, tables, bounds, logical, source, out_weight, gains, gu_stage, down_own
):
    tokens, width = query.shape[0], source.shape[1]
    rows = tokens // 16
    group = tokens // 4
    hidden = gu_stage.shape[2] // 8
    part = width // 8

    def body(*refs, loaded, leave):
        (q_in, k_in, v_in, cos_ref, sin_ref, low_ref, high_ref, log_ref, source_ref, wout_ref, gain_ref) = refs[:11]
        (gu_ref, d_ref) = refs[11:13]
        (full_ref, own_ref, branch_ref, wgu_ref, d_other_ref, qrot_ref, keys_ref, values_ref, o_ref, lse_ref, scale_ref) = refs[13:24]
        (terms, shard, slots, tot_send, tot_recv, pair_send, pair_recv, local) = refs[24:32]
        (ffn_send, ffn_recv, share_send, share_recv, ffn_local) = refs[32:37]
        rest = refs[37:]
        me = z, y, x, k = place()
        ctx = own_tile(me)
        head_at = pl.ds(pl.multiple_of((x * 8 + ctx) * HD, HD), HD)
        sibling = (z, y, x, 1 - k)
        barrier = pltpu.get_barrier_semaphore()
        plane_greet_all(me, [sibling])
        loaded()
        query_gain, key_gain = gain_ref[0:1, head_at], gain_ref[1:2, head_at]

        def pair(src, dst, n):
            return pltpu.make_async_remote_copy(
                src_ref=src,
                dst_ref=dst,
                send_sem=pair_send.at[n],
                recv_sem=pair_recv.at[n],
                device_id=sibling,
                device_id_type=MESH,
            )

        eye = eye_mask()
        own = z * 4 + y * 2 + x
        for i in range(8):
            piece = slice(i * HD, (i + 1) * HD)
            for side, ref in enumerate((q_in, k_in)):
                values = ref[piece, :]
                column = jnp.sum(values * values, axis=1, keepdims=True)
                slots[own, side * 8 + i : side * 8 + i + 1, :] = column_to_row(column, eye)
        values_ref[:tokens, :] = v_in[...]
        other_half = pl.ds(tokens, tokens)
        v_copy = pair(v_in, values_ref.at[other_half, :], 0)
        v_copy.start()

        def ffn_copy(t, i):
            to = ctx + t - 8 * ((ctx + t) // 8)
            at = pl.ds(pl.multiple_of(to * hidden, hidden), hidden)
            from_at = pl.ds(pl.multiple_of(ctx * part, part), part)
            return pltpu.make_async_remote_copy(
                src_ref=gu_ref.at[i, :, at],
                dst_ref=wgu_ref.at[i, from_at, :hidden],
                send_sem=ffn_send.at[i, t],
                recv_sem=ffn_recv.at[i, t],
                device_id=(to // 2, to % 2, x, k),
                device_id_type=MESH,
            )

        def ffn_ends(t):
            c = ctx + 8 - t - 8 * ((ctx + 8 - t) // 8)
            at = pl.ds(pl.multiple_of(c * part, part), part)
            return wgu_ref.at[:, at, :hidden], wgu_ref.at[:, at, hidden:]

        own_at = pl.ds(pl.multiple_of(ctx * hidden, hidden), hidden)
        ffn_own = pltpu.make_async_copy(gu_ref.at[:, :, own_at], ffn_ends(0)[0], ffn_local)
        ffn_own.start()
        down_copy = pair(d_ref, d_other_ref, 2)
        down_copy.start()

        total = sum_begin(me, slots, tot_send, tot_recv)()
        trickle = Trickle()
        trickle.add([lambda t=t, i=i: ffn_copy(t, i).start() for t in DEAL_ORDER for i in range(2)])
        trickle.tick(DEALT_FIRST)
        scales = lax.rsqrt(total / width + EPSILON)
        scale_ref[...] = scales

        def rotated(values, piece):
            return values * cos_ref[piece, :] + pltpu.roll(values, HD // 2, 1) * sin_ref[piece, :]

        for i in range(8):
            piece = slice(i * HD, (i + 1) * HD)
            factor = row_to_column(scales[8 + i : 9 + i, :], eye)
            keys_ref[piece, :] = rotated(k_in[piece, :] * factor * key_gain, piece).astype(BF)
        k_copy = pair(keys_ref.at[:tokens, :], keys_ref.at[other_half, :], 1)
        k_copy.start()
        for i in range(8):
            piece = slice(i * HD, (i + 1) * HD)
            factor = row_to_column(scales[i : i + 1, :], eye)
            qrot_ref[piece, :] = rotated(q_in[piece, :] * factor * query_gain, piece).astype(BF)
        v_copy.wait()
        k_copy.wait()

        def produce(zp):
            at = pl.ds(pl.multiple_of(zp * group, group), group)
            raw, allowed = masked_scores(
                qrot_ref[at, :], keys_ref[...], low_ref[at, :], high_ref[at, :], log_ref[...]
            )
            raw = jnp.where(allowed, raw, MASKED)
            top = jnp.max(raw, axis=1, keepdims=True)
            weights = jnp.exp(raw - top)
            total_weight = jnp.sum(weights, axis=1, keepdims=True)
            out = jnp.dot(weights.astype(BF), values_ref[...], preferred_element_type=F32)
            out = out * (1.0 / total_weight)
            o_ref[at, :] = out
            lse_ref[at, :] = top + jnp.log(total_weight)
            terms[at, :] = jnp.dot(
                out.astype(BF), wout_ref[...], preferred_element_type=F32
            ).astype(BF)

        def finish(strip, total):
            branch_ref[strip] = total
            h = source_ref[strip].astype(F32) + total * row_scale(total) * gain_ref[2:3, :]
            own_ref[strip] = h
            shard[strip] = h.astype(BF)

        settle = reduce_plane(
            me,
            terms,
            rows,
            rest[:N_REDUCE],
            TURNS_ATTENTION[0],
            produce,
            finish,
            lambda: leave(qrot_ref, keys_ref, values_ref, o_ref, lse_ref, scale_ref),
            lambda: trickle.tick(FORWARD_RATE, FORWARD_EVERY),
        )
        view = gather_view(full_ref, rows)
        keep = pltpu.make_async_copy(shard, view(own), local)
        keep.start()

        def share(t):
            src, dst = ffn_ends(t)
            return pltpu.make_async_remote_copy(
                src_ref=src,
                dst_ref=dst,
                send_sem=share_send.at[t],
                recv_sem=share_recv.at[t],
                device_id=sibling,
                device_id_type=MESH,
            )

        def ffn_landed(t):
            for i in range(2):
                src = ffn_ends(t)[0].at[i]
                pltpu.make_async_remote_copy(
                    src_ref=src,
                    dst_ref=src,
                    send_sem=ffn_send.at[i, t],
                    recv_sem=ffn_recv.at[i, t],
                    device_id=sibling,
                    device_id_type=MESH,
                ).wait_recv()

        gather_plane(
            me,
            shard,
            view,
            rest[N_REDUCE:],
            TURNS_ATTENTION[1],
            lambda step: leave(own_ref, branch_ref) if step == 0 else None,
            tick=lambda: trickle.tick(FORWARD_RATE, FORWARD_EVERY),
        )
        trickle.flush()
        ffn_own.wait()
        share(0).start()
        for t in DEAL_ORDER:
            ffn_landed(t)
            share(t).start()
        keep.wait()
        settle()
        for t in range(8):
            share(t).wait()
            for i in range(2):
                if t > 0:
                    ffn_copy(t, i).wait_send()
        down_copy.wait()

    shape = jax.ShapeDtypeStruct
    return comm_call(
        body,
        "attention_forward",
        1,
        (
            shape((tokens, width), BF),
            shape((rows, width), F32),
            shape((rows, width), F32),
            shape((2, width, 2 * hidden), BF),
            shape((hidden, width), BF),
            shape((tokens, HD), BF),
            shape((2 * tokens, HD), BF),
            shape((2 * tokens, HD), BF),
            shape((tokens, HD), F32),
            shape((tokens, 1), F32),
            shape((16, HD), F32),
        ),
        [VMEM] * 11 + [ANY, ANY],
        (ANY, VMEM, VMEM, ANY, ANY, VMEM, VMEM, VMEM, VMEM, VMEM, VMEM),
        [
            pltpu.VMEM((tokens, width), BF),
            pltpu.VMEM((rows, width), BF),
            pltpu.VMEM((16, 16, HD), F32),
            DMA((16,)),
            DMA((16,)),
            DMA((3,)),
            DMA((3,)),
            DMA,
            DMA((2, 8)),
            DMA((2, 8)),
            DMA((8,)),
            DMA((8,)),
            DMA,
            *reduce_scratch(rows, width),
            *GATHER_SEMS,
        ],
    )(query, key, value, *tables, *bounds, logical, source, out_weight, gains, gu_stage, down_own)


def ffn_forward(source, gu_w, down_w, residual, cotangent, gain):
    tokens, width = source.shape
    rows, group = tokens // 16, tokens // 4
    hidden = 2 * down_w[0].shape[0]

    def body(*refs, loaded, leave):
        (h_any, gu_any, d_any, d_any2, res_ref, cot_ref, gain_ref) = refs[:7]
        (full_ref, out_ref, gg_ref, for_gate_out, for_up_out, m_out) = refs[7:13]
        (hs, gu, dw, terms, shard, result, load_sem, local, out_send, out_recv) = refs[13:23]
        (for_gate_ref, for_up_ref, m_ref, leave_sem) = refs[23:27]
        scratch = refs[27:]
        me = z, y, x, k = place()

        def h_load(zp):
            at = pl.ds(pl.multiple_of(zp * group, group), group)
            return pltpu.make_async_copy(h_any.at[at, :], hs.at[at, :], load_sem.at[zp])

        order = [near_first(step, z) for step in (3, 2, 1, 0)]
        gu_load = pltpu.make_async_copy(gu_any, gu, load_sem.at[4])
        d_loads = [
            pltpu.make_async_copy(d_any, dw.at[: hidden // 2, :], load_sem.at[5]),
            pltpu.make_async_copy(d_any2, dw.at[hidden // 2 :, :], load_sem.at[6]),
        ]
        for load in (h_load(order[0]), gu_load, *d_loads):
            load.start()
        for zp in order[1:]:
            h_load(zp).start()
        greet_plane(me, pair_devices(me))
        loaded()
        gg_ref[...] = jnp.zeros_like(gg_ref)
        gu_load.wait()

        def leave(zp):
            at = pl.ds(pl.multiple_of(zp * group, group), group)
            pairs = ((for_gate_ref, for_gate_out), (for_up_ref, for_up_out), (m_ref, m_out))
            return [
                pltpu.make_async_copy(src.at[at, :], dst.at[at, :], leave_sem.at[i, zp])
                for i, (src, dst) in enumerate(pairs)
            ]

        def produce(zp):
            at = pl.ds(pl.multiple_of(zp * group, group), group)
            h_load(zp).wait()
            tile = hs[at, :]
            gate = jnp.dot(tile, gu[0], preferred_element_type=F32)
            up = jnp.dot(tile, gu[1], preferred_element_type=F32)
            sig = jax.nn.sigmoid(gate)
            silu = gate * sig
            mixed = (silu * up).astype(BF)
            for_gate_ref[at, :] = up * sig * (1.0 + gate * (1.0 - sig))
            for_up_ref[at, :] = silu
            m_ref[at, :] = mixed
            for copy in leave(zp):
                copy.start()
            terms[at, :] = jnp.dot(mixed, dw[...], preferred_element_type=F32).astype(BF)

        def finish(strip, total):
            gain_row = gain_ref[3:4, :]
            out = res_ref[strip] + total * row_scale(total) * gain_row
            result[strip] = out.astype(BF)
            back, term = norm_back_strip(cot_ref[strip].astype(F32), total, gain_row)
            gg_ref[...] += term
            shard[strip] = back.astype(BF)

        for load in d_loads:
            load.wait()
        settle = reduce_plane(me, terms, rows, scratch[:N_REDUCE], EVEN, produce, finish)
        view = gather_view(full_ref, rows)
        keep = pltpu.make_async_copy(shard, view(me[0] * 4 + me[1] * 2 + me[2]), local)
        keep.start()
        copies, own = hand_out_copies(me, result, out_ref, out_send, out_recv)
        for copy in copies:
            copy.start()
        own.start()
        gather_plane(me, shard, view, scratch[N_REDUCE:], EVEN)
        keep.wait()
        settle()
        for zp in range(4):
            for copy in leave(zp):
                copy.wait()
        own.wait()
        for copy in copies:
            copy.wait()

    shape = jax.ShapeDtypeStruct
    return comm_call(
        body,
        "ffn_forward",
        3,
        (
            shape((tokens, width), BF),
            shape((rows * 4, width // 4), BF),
            shape((8, width), F32),
            shape((tokens, hidden), F32),
            shape((tokens, hidden), F32),
            shape((tokens, hidden), BF),
        ),
        [ANY, ANY, ANY, ANY, VMEM, VMEM, VMEM],
        (ANY, ANY, VMEM, ANY, ANY, ANY),
        [
            pltpu.VMEM((tokens, width), BF),
            pltpu.VMEM((2, width, hidden), BF),
            pltpu.VMEM((hidden, width), BF),
            pltpu.VMEM((tokens, width), BF),
            pltpu.VMEM((rows, width), BF),
            pltpu.VMEM((rows, width), BF),
            DMA((7,)),
            DMA,
            DMA((3,)),
            DMA((4,)),
            pltpu.VMEM((tokens, hidden), F32),
            pltpu.VMEM((tokens, hidden), F32),
            pltpu.VMEM((tokens, hidden), BF),
            DMA((3, 4)),
            *reduce_scratch(rows, width),
            *GATHER_SEMS,
        ],
    )(source, gu_w, *down_w, residual, cotangent, gain)


EARLY = 5
GRADS_FIRST = 3


def grad_copies(me, src, dst, send, recv, t):
    ctx = own_tile(me)
    to = ctx + t - 8 * ((ctx + t) // 8)
    return [
        pltpu.make_async_remote_copy(
            src_ref=src.at[i],
            dst_ref=dst.at[ctx, i],
            send_sem=send.at[t, i],
            recv_sem=recv.at[t, i],
            device_id=(to // 2, to % 2, me[2], me[3]),
            device_id_type=MESH,
        )
        for i in range(3)
    ]


def grad_landed(me, dst, send, recv, t):
    ctx = own_tile(me)
    c = ctx + 8 - t - 8 * ((ctx + 8 - t) // 8)
    for i in range(3):
        pltpu.make_async_remote_copy(
            src_ref=dst.at[c, i],
            dst_ref=dst.at[c, i],
            send_sem=send.at[t, i],
            recv_sem=recv.at[t, i],
            device_id=(me[0], me[1], me[2], 1 - me[3]),
            device_id_type=MESH,
        ).wait_recv()


def ctx_greet(me, others):
    z, y, x, k = me
    barrier = pltpu.get_barrier_semaphore()

    def call(i, carry):
        to = lax.rem(z * 2 + y + i, 8)
        pl.semaphore_signal(
            barrier, inc=1, device_id=(to // 2, to % 2, x, k), device_id_type=MESH
        )
        return carry

    lax.fori_loop(1, 8, call, 0)
    for target in [(z, y, 1 - x, k), *others]:
        pl.semaphore_signal(barrier, inc=1, device_id=target, device_id_type=MESH)
    pl.semaphore_wait(barrier, 8 + len(others))


def ffn_backward(
    grad_ffn, source, gu_w, down_w, for_gate, for_up, mixed, cotangent, branch, gain, attention
):
    tokens, width = grad_ffn.shape
    rows, group = tokens // 16, tokens // 4
    hidden = 2 * down_w[0].shape[0]
    part = hidden // 2
    across = (((0,), (0,)), ((), ()))
    turned = (((1,), (1,)), ((), ()))
    scaling = 1.0 / math.sqrt(HD)

    def body(*refs, loaded, leave):
        (df_any, h_any, gu_any, d_any, d_any2, fg_any, fu_any, m_any, cot_ref, branch_ref, gain_ref) = refs[:11]
        (wout_ref, qrot_ref, keys_ref, values_ref, o_ref, lse_ref, low_ref, high_ref, log_ref) = refs[11:20]
        (full_ref, own_ref, gg_ref, in_ref, rest_ref, dq_ref, dk_ref, dv_ref) = refs[20:28]
        (df, hs, gu, dw, fg, fu, ms, dgu, terms, shard) = refs[28:38]
        (to_core, from_core, to_ctx) = refs[38:41]
        (da, dk_all, dv_all, pair_out, pair_in) = refs[41:46]
        (load_sem, local, core_send, core_recv, grad_send, grad_recv, rest_sem) = refs[46:53]
        (da_sem, pair_send, pair_recv) = refs[53:56]
        scratch = refs[56:]
        me = z, y, x, k = place()
        ctx = own_tile(me)
        order = [near_first(step, z) for step in (3, 2, 1, 0)]

        def group_load(zp):
            at = pl.ds(pl.multiple_of(zp * group, group), group)
            return [
                pltpu.make_async_copy(src.at[at, :], dst.at[at, :], load_sem.at[i, zp])
                for i, (src, dst) in enumerate(((df_any, df), (fg_any, fg), (fu_any, fu)))
            ]

        d_load = pltpu.make_async_copy(d_any, dw.at[:part, :], load_sem.at[3, 0])
        d_load2 = pltpu.make_async_copy(d_any2, dw.at[part:, :], load_sem.at[4, 0])
        gu_load = pltpu.make_async_copy(gu_any, gu, load_sem.at[3, 1])
        h_load = pltpu.make_async_copy(h_any, hs, load_sem.at[3, 2])
        m_load = pltpu.make_async_copy(m_any, ms, load_sem.at[3, 3])
        for load in (*group_load(order[0]), d_load, d_load2, gu_load):
            load.start()
        for zp in order[1:]:
            for load in group_load(zp):
                load.start()
        h_load.start()
        m_load.start()
        sibling = (z, y, x, 1 - k)
        ctx_greet(me, [sibling])
        loaded()
        gg_ref[...] = jnp.zeros_like(gg_ref)
        d_load.wait()
        d_load2.wait()

        def produce(zp):
            at = pl.ds(pl.multiple_of(zp * group, group), group)
            for load in group_load(zp):
                load.wait()
            dm = lax.dot_general(df[at, :], dw[...], turned, preferred_element_type=F32)
            dg = (dm * fg[at, :]).astype(BF)
            du = (dm * fu[at, :]).astype(BF)
            dgu[at, :hidden] = dg
            dgu[at, hidden:] = du
            terms[at, :] = (
                lax.dot_general(dg, gu[0], turned, preferred_element_type=F32)
                + lax.dot_general(du, gu[1], turned, preferred_element_type=F32)
            ).astype(BF)

        def finish(strip, total):
            grad = cot_ref[strip].astype(F32) + total
            own_ref[strip] = grad
            back, term = norm_back_strip(grad, branch_ref[strip], gain_ref[2:3, :])
            gg_ref[...] += term
            shard[strip] = back.astype(BF)

        def core_copy(t):
            return pltpu.make_async_remote_copy(
                src_ref=to_core.at[t],
                dst_ref=from_core.at[t],
                send_sem=core_send.at[t],
                recv_sem=core_recv.at[t],
                device_id=sibling,
                device_id_type=MESH,
            )

        parts = (*DEAL_ORDER, 0)

        def compute(n):
            t = parts[n]
            c = ctx + t - 8 * ((ctx + t) // 8)
            at = pl.ds(pl.multiple_of(c * part, part), part)
            up_like = lax.dot_general(hs[:, at], dgu[...], across, preferred_element_type=F32)
            down_like = lax.dot_general(ms[...], df[:, at], across, preferred_element_type=F32)
            for i in range(2):
                to_ctx[t, i] = up_like[:, 2 * i * part : (2 * i + 1) * part].astype(BF)
                to_core[t, i] = up_like[:, (2 * i + 1) * part : (2 * i + 2) * part].astype(BF)
            to_ctx[t, 2] = down_like[:part].astype(BF)
            to_core[t, 2] = down_like[part:].astype(BF)
            core_copy(t).start()

        trickle = Trickle()

        def send(n):
            t = parts[n]
            core_copy(t).wait_recv()
            to_ctx[t] = (to_ctx[t].astype(F32) + from_core[t].astype(F32)).astype(BF)
            if t == 0:
                pltpu.make_async_copy(to_ctx.at[0], in_ref.at[ctx], rest_sem.at[0]).start()
            elif n < EARLY:
                trickle.add(
                    [
                        copy.start
                        for copy in grad_copies(me, to_ctx.at[t], in_ref, grad_send, grad_recv, t)
                    ]
                )
            else:
                pltpu.make_async_copy(
                    to_ctx.at[t], rest_ref.at[n - EARLY], rest_sem.at[n - EARLY + 1]
                ).start()

        begun = []

        def next_part():
            n = len(begun)
            begun.append(n)
            if n < 8:
                compute(n)
            if BACK_LAG <= n < 8 + BACK_LAG:
                send(n - BACK_LAG)

        def tick():
            if begun:
                next_part()
            trickle.tick(BACK_RATE, BACK_EVERY)

        def da_load(step):
            at = pl.ds(pl.multiple_of(near_first(step, z) * group, group), group)
            return pltpu.make_async_copy(full_ref.at[at, :], da.at[step % 2], da_sem.at[step % 2])

        def attend_back(step):
            at = pl.ds(pl.multiple_of(near_first(step, z) * group, group), group)
            da_load(step).wait()
            grad = lax.dot_general(
                da[step % 2], wout_ref[...], turned, preferred_element_type=F32
            ).astype(BF)
            delta = jnp.sum(grad.astype(F32) * o_ref[at, :], axis=1, keepdims=True)
            q, low, high, lse = qrot_ref[at, :], low_ref[at, :], high_ref[at, :], lse_ref[at, :]
            dq_ref[at, :] = jnp.zeros((group, HD), F32)

            def work(key_at):
                key_part = keys_ref[key_at, :]
                raw, allowed = masked_scores(q, key_part, low, high, log_ref[:, key_at])
                weights = jnp.where(allowed, jnp.exp(raw - lse), 0.0)
                dp = lax.dot_general(
                    grad, values_ref[key_at, :], turned, preferred_element_type=F32
                )
                ds = (weights * (dp - delta)).astype(BF)
                dq_ref[at, :] += jnp.dot(ds, key_part, preferred_element_type=F32) * scaling
                dk_all[key_at, :] += (
                    lax.dot_general(ds, q, across, preferred_element_type=F32) * scaling
                )
                dv_all[key_at, :] += lax.dot_general(
                    weights.astype(BF), grad, across, preferred_element_type=F32
                )

            strips(2 * tokens, work, tokens)

        def arrived(step):
            if step == 0:
                keep.wait()
                dk_all[...] = jnp.zeros_like(dk_all)
                dv_all[...] = jnp.zeros_like(dv_all)
            da_load(step).start()
            if step > 0:
                attend_back(step - 1)

        def pair(n):
            return pltpu.make_async_remote_copy(
                src_ref=pair_out.at[n],
                dst_ref=pair_in.at[n],
                send_sem=pair_send.at[n],
                recv_sem=pair_recv.at[n],
                device_id=sibling,
                device_id_type=MESH,
            )

        def after_terms():
            h_load.wait()
            m_load.wait()
            for _ in range(GRADS_FIRST):
                next_part()

        gu_load.wait()
        settle = reduce_plane(
            me,
            terms,
            rows,
            scratch[:N_REDUCE],
            TURNS_FFN_BACK[0],
            produce,
            finish,
            after_terms,
            tick,
        )
        view = gather_view(full_ref, rows)
        keep = pltpu.make_async_copy(shard, view(me[0] * 4 + me[1] * 2 + me[2]), local)
        keep.start()
        gather_plane(
            me,
            shard,
            view,
            scratch[N_REDUCE:],
            TURNS_FFN_BACK[1],
            lambda step: leave(own_ref, gg_ref) if step == 0 else None,
            arrived,
            tick=tick,
            early=EARLY_LAYERS,
        )
        while len(begun) < 8 + BACK_LAG:
            next_part()
        trickle.flush()
        attend_back(3)
        pair_out[0] = dk_all[tokens:, :].astype(BF)
        pair_out[1] = dv_all[tokens:, :].astype(BF)
        pair(0).start()
        pair(1).start()
        settle()
        for n, (ref, source_ref) in enumerate(((dk_ref, dk_all), (dv_ref, dv_all))):
            pair(n).wait()
            ref[...] = source_ref[:tokens, :] + pair_in[n].astype(F32)
        for t in range(8):
            core_copy(t).wait_send()
        pltpu.make_async_copy(to_ctx.at[0], in_ref.at[ctx], rest_sem.at[0]).wait()
        for n, t in enumerate(DEAL_ORDER):
            if n < EARLY:
                grad_landed(me, in_ref, grad_send, grad_recv, t)
                for copy in grad_copies(me, to_ctx.at[t], in_ref, grad_send, grad_recv, t):
                    copy.wait_send()
            else:
                pltpu.make_async_copy(
                    to_ctx.at[t], rest_ref.at[n - EARLY], rest_sem.at[n - EARLY + 1]
                ).wait()

    shape = jax.ShapeDtypeStruct
    vmem = pltpu.VMEM
    return comm_call(
        body,
        "ffn_backward",
        4,
        (
            shape((tokens, width), BF),
            shape((rows, width), F32),
            shape((8, width), F32),
            shape((8, 3, part, part), BF),
            shape((7 - EARLY, 3, part, part), BF),
            shape((tokens, HD), F32),
            shape((tokens, HD), F32),
            shape((tokens, HD), F32),
        ),
        [*[ANY] * 8, *[VMEM] * 12],
        (ANY, VMEM, VMEM, ANY, ANY, VMEM, VMEM, VMEM),
        [
            vmem((tokens, width), BF),
            vmem((tokens, width), BF),
            vmem((2, width, hidden), BF),
            vmem((hidden, width), BF),
            vmem((tokens, hidden), F32),
            vmem((tokens, hidden), F32),
            vmem((tokens, hidden), BF),
            vmem((tokens, 2 * hidden), BF),
            vmem((tokens, width), BF),
            vmem((rows, width), BF),
            vmem((8, 3, part, part), BF),
            vmem((8, 3, part, part), BF),
            vmem((8, 3, part, part), BF),
            vmem((2, group, width), BF),
            vmem((2 * tokens, HD), F32),
            vmem((2 * tokens, HD), F32),
            vmem((2, tokens, HD), BF),
            vmem((2, tokens, HD), BF),
            DMA((5, 4)),
            DMA,
            DMA((8,)),
            DMA((8,)),
            DMA((8, 3)),
            DMA((8, 3)),
            DMA((8,)),
            DMA((2,)),
            DMA((2,)),
            DMA((2,)),
            *reduce_scratch(rows, width),
            *GATHER_SEMS,
        ],
    )(
        grad_ffn,
        source,
        gu_w,
        *down_w,
        for_gate,
        for_up,
        mixed,
        cotangent,
        branch,
        gain,
        *attention,
    )


def write_results(early, late, wall, outputs, input_grad, gains):
    part = early.shape[2]
    rows, columns = outputs.shape

    def body(*refs):
        (early_ref, late_ref, wall_ref, out_ref, in_ref, gain_ref) = refs[:6]
        (out_to, in_to, gq, gk, gv, go, gg, gu, gd) = refs[6:15]
        gains_to = refs[15:19]
        (blob, wall_in, wide, wall_wide, out_wide, load_sem, store_sem, wall_sem) = refs[19:]
        ctx = lax.axis_index("z") * 2 + lax.axis_index("y")
        loads, stores = [], []
        for n, t in enumerate((0, *DEAL_ORDER)):
            c = lax.rem(ctx + 8 - t, 8)
            source = early_ref if n <= EARLY else late_ref
            loads.append(pltpu.make_async_copy(source.at[c], blob.at[n], load_sem.at[n]))
            at = pl.ds(pl.multiple_of(c * part, part), part)
            ends = (gg.at[:, at], gu.at[:, at], gd.at[at, :])
            stores.append(
                [
                    pltpu.make_async_copy(wide.at[n, i], end, store_sem.at[n, i])
                    for i, end in enumerate(ends)
                ]
            )
        wall_load = pltpu.make_async_copy(wall_ref, wall_in, wall_sem.at[0])
        for copy in (*loads, wall_load):
            copy.start()
        for i, ref in enumerate(gains_to):
            ref[...] = gain_ref[i : i + 1, :]
        out_to[...] = out_ref[...]
        in_to[...] = in_ref[...]
        for n in range(8):
            loads[n].wait()
            for i in range(3):

                def work(strip, n=n, i=i):
                    wide[n, i, strip] = blob[n, i, strip].astype(F32)

                strips(part, work, 64)
                stores[n][i].start()
        wall_load.wait()
        for n in range(8):
            j, r = n // 2, n % 2
            for i in range(3):
                wall_wide[i, r * HD : (r + 1) * HD, j * HD : (j + 1) * HD] = wall_in[n, i].astype(F32)
            out_wide[j * HD : (j + 1) * HD, r * HD : (r + 1) * HD] = wall_in[n, 3].astype(F32)
        last = [
            pltpu.make_async_copy(wall_wide.at[i], ref, wall_sem.at[1 + i])
            for i, ref in enumerate((gq, gk, gv))
        ]
        last.append(pltpu.make_async_copy(out_wide, go, wall_sem.at[4]))
        for copy in last:
            copy.start()
        for copy in last:
            copy.wait()
        for group in stores:
            for copy in group:
                copy.wait()

    shape = jax.ShapeDtypeStruct
    vmem = pltpu.VMEM
    return pl.pallas_call(
        body,
        name="write_results",
        out_shape=(
            shape((rows, columns), BF),
            shape((rows, columns), BF),
            shape((2 * HD, 4 * HD), F32),
            shape((2 * HD, 4 * HD), F32),
            shape((2 * HD, 4 * HD), F32),
            shape((4 * HD, 2 * HD), F32),
            shape((part, 8 * part), F32),
            shape((part, 8 * part), F32),
            shape((8 * part, part), F32),
            *[shape((1, gains.shape[1]), F32)] * 4,
        ),
        in_specs=[ANY, ANY, ANY, VMEM, VMEM, VMEM],
        out_specs=(VMEM, VMEM, *[ANY] * 7, *[VMEM] * 4),
        scratch_shapes=[
            vmem((8, 3, part, part), BF),
            vmem((8, 4, HD, HD), BF),
            vmem((8, 3, part, part), F32),
            vmem((3, 2 * HD, 4 * HD), F32),
            vmem((4 * HD, 2 * HD), F32),
            DMA((8,)),
            DMA((8, 3)),
            DMA((5,)),
        ],
        compiler_params=pltpu.CompilerParams(vmem_limit_bytes=BIG_VMEM),
    )(early, late, wall, outputs, input_grad, gains)


def close_greet(me):
    z, y, x, k = me
    barrier = pltpu.get_barrier_semaphore()

    def plane(i, carry):
        pl.semaphore_signal(barrier, inc=1, device_id=plane_peer(me, i)[1], device_id_type=MESH)
        return carry

    def others(i, carry):
        pl.semaphore_signal(
            barrier, inc=1, device_id=(i // 2, i % 2, x, 1 - k), device_id_type=MESH
        )
        return carry

    lax.fori_loop(1, 16, plane, 0)
    lax.fori_loop(0, 8, others, 0)
    pl.semaphore_signal(barrier, inc=1, device_id=(z, y, 1 - x, 1 - k), device_id_type=MESH)
    pl.semaphore_wait(barrier, 24)


def attention_backward(
    grad_attn,
    full_in,
    query,
    key,
    attended,
    grads_rotated,
    tables,
    scales,
    gains,
    qkv_w,
    grad_own,
    attn_term,
    ffn_term,
    grads_left,
):
    tokens, width = grad_attn.shape
    rows, group = tokens // 16, tokens // 4
    part = width // 4

    def body(*refs, loaded, leave):
        (da_any, x_any) = refs[:2]
        (q_ref, k_ref, o_ref, dq_in, dk_in, dv_in, cos_ref, sin_ref) = refs[2:10]
        (scale_ref, gain_ref, wqkv_ref) = refs[10:13]
        (grad_ref, attn_ref, ffn_ref, left_ref) = refs[13:17]
        (in_grad_ref, deal_in, gains_ref, ffn_in) = refs[17:21]
        (da, xs, terms, dq_ref, dk_ref) = refs[21:26]
        (dqkv, slots, result) = refs[26:29]
        (qkv_grads, out_grads, wall_out, wall_in, deal_out) = refs[29:34]
        (gain_out, gain_in, gain_own, gain_slots) = refs[34:38]
        (load_sem, pair_send, pair_recv, tot_send, tot_recv, out_send, out_recv) = refs[38:45]
        (deal_send, deal_recv, gain_send, gain_recv, grad_send, grad_recv) = refs[45:51]
        scratch = refs[51:]
        me = z, y, x, k = place()
        ctx = own_tile(me)
        own = ctx * 2 + x
        own_head = pl.ds(pl.multiple_of((x * 8 + ctx) * HD, HD), HD)
        sibling = (z, y, x, 1 - k)

        da_load = pltpu.make_async_copy(da_any, da, load_sem.at[0])
        x_load = pltpu.make_async_copy(x_any, xs, load_sem.at[1])
        x_load.start()
        da_load.start()
        close_greet(me)
        loaded()

        trickle = Trickle()

        def left_copies(n):
            return grad_copies(me, left_ref.at[n - EARLY], ffn_in, grad_send, grad_recv, DEAL_ORDER[n])

        for n in range(EARLY, 7):
            trickle.add([copy.start for copy in left_copies(n)])
        trickle.tick(CLOSE_FIRST)

        def pair(n):
            return pltpu.make_async_remote_copy(
                src_ref=wall_out.at[n] if n < 8 else gain_out,
                dst_ref=wall_in.at[n] if n < 8 else gain_in,
                send_sem=pair_send.at[n],
                recv_sem=pair_recv.at[n],
                device_id=sibling,
                device_id_type=MESH,
            )

        across = (((0,), (0,)), ((), ()))
        eye = eye_mask()

        def normed_grad(values, piece):
            return values * cos_ref[piece, :] - pltpu.roll(values, HD // 2, 1) * sin_ref[piece, :]

        def side_dots(side, source, grads, proj):
            gain_sum = jnp.zeros((8, HD), F32)
            for i in range(8):
                piece = slice(i * HD, (i + 1) * HD)
                factor = row_to_column(scale_ref[side * 8 + i : side * 8 + i + 1, :], eye)
                back = normed_grad(source[piece, :], piece)
                term = back * proj[piece, :] * factor
                for j in range(0, HD, 8):
                    gain_sum = gain_sum + term[j : j + 8, :]
                weighted = back * gain_ref[side : side + 1, own_head]
                grads[piece, :] = weighted
                dot = jnp.sum(weighted * proj[piece, :], axis=1, keepdims=True)
                slots[own, side * 8 + i : side * 8 + i + 1, :] = column_to_row(dot, eye)
            return jnp.sum(gain_sum, axis=0, keepdims=True)

        query_gain = side_dots(0, dq_in, dq_ref, q_ref)
        key_gain = side_dots(1, dk_in, dk_ref, k_ref)
        sum_end = sum_begin(me, slots, tot_send, tot_recv)
        dqkv[:, 2 * HD :] = dv_in[...].astype(BF)

        attn_sum = jnp.sum(attn_ref[...], axis=0, keepdims=True)
        ffn_sum = jnp.sum(ffn_ref[...], axis=0, keepdims=True)
        head_core = z // 2
        head_at = pl.ds(pl.multiple_of(((z % 2) * 2 + y) * HD, HD), HD)
        for mine, target in ((True, gain_own), (False, gain_out)):
            target[...] = jnp.zeros_like(target)
            for xt in range(2):
                for kt in range(2):

                    @pl.when((kt == k) if mine else (kt != k))
                    def _(xt=xt, kt=kt, target=target):
                        block = slice((2 * xt + kt) * part, (2 * xt + kt + 1) * part)
                        target[xt, 2:3, :] = attn_sum[:, block]
                        target[xt, 3:4, :] = ffn_sum[:, block]

            @pl.when((head_core == k) if mine else (head_core != k))
            def _(target=target):
                target[x, 0:1, head_at] = query_gain
                target[x, 1:2, head_at] = key_gain

        pair(8).start()

        parts = (*DEAL_ORDER, 0)

        def columns_of(n):
            c = ctx + parts[n] - 8 * ((ctx + parts[n]) // 8)
            return pl.ds(pl.multiple_of(c * 2 * HD, 2 * HD), 2 * HD)

        attended_low = o_ref[...].astype(BF)
        da_load.wait()
        for n in range(8):
            out_grads[n] = lax.dot_general(
                attended_low, da[:, columns_of(n)], across, preferred_element_type=F32
            )
        total = sum_end()
        trickle.tick(CLOSE_NEXT)
        for side, grads, proj in ((0, dq_ref, q_ref), (1, dk_ref, k_ref)):
            for i in range(8):
                piece = slice(i * HD, (i + 1) * HD)
                row = scale_ref[side * 8 + i : side * 8 + i + 1, :]
                factor = row_to_column(row, eye)
                cubed = row * row * row * total[side * 8 + i : side * 8 + i + 1, :] / width
                dqkv[piece, side * HD : (side + 1) * HD] = (
                    factor * grads[piece, :] - proj[piece, :] * row_to_column(cubed, eye)
                ).astype(BF)

        def produce(zp):
            at = pl.ds(pl.multiple_of(zp * group, group), group)
            term = jnp.zeros((group, width), F32)
            for i in range(3):
                term = term + lax.dot_general(
                    dqkv[at, i * HD : (i + 1) * HD],
                    wqkv_ref[i],
                    (((1,), (1,)), ((), ())),
                    preferred_element_type=F32,
                )
            terms[at, :] = term.astype(BF)

        gain_copies = []

        def gain_copy(i):
            other, device = plane_peer(me, i)
            return pltpu.make_async_remote_copy(
                src_ref=gain_own.at[other % 2],
                dst_ref=gain_slots.at[own],
                send_sem=gain_send.at[i],
                recv_sem=gain_recv.at[own],
                device_id=device,
                device_id_type=MESH,
            )

        number = ((z % 2) * 2 + y) * 2 + k

        def deal(n):
            c = ctx + parts[n] - 8 * ((ctx + parts[n]) // 8)
            return pltpu.make_async_remote_copy(
                src_ref=deal_out.at[n],
                dst_ref=deal_in.at[number],
                send_sem=deal_send.at[n],
                recv_sem=deal_recv.at[number],
                device_id=(c // 2, c % 2, x, head_core),
                device_id_type=MESH,
            )

        stays = k == head_core

        def deal_start(n):
            if n < 7:
                deal(n).start()
                return

            @pl.when(jnp.logical_not(stays))
            def _():
                deal(n).start()

            @pl.when(stays)
            def _():
                pltpu.make_async_copy(
                    deal_out.at[n], deal_in.at[number], deal_recv.at[number]
                ).start()

        def after_terms():
            pair(8).wait_recv()
            gain_own[...] += gain_in[...]
            gain_slots[own] = gain_own[x]

            def begin(i, carry):
                gain_copy(i).start()
                return carry

            lax.fori_loop(1, 16, begin, 0)

        x_load.wait()
        begun = []

        def halves(n, r):
            rows_at = pl.ds(pl.multiple_of(r * HD, HD), HD)
            for i in range(3):
                yield i, qkv_grads[rows_at, i * HD : (i + 1) * HD]
            yield 3, out_grads[n, :, rows_at]

        def tick():
            n = len(begun)
            begun.append(n)
            if n < 8:
                qkv_grads[...] = lax.dot_general(
                    xs[:, columns_of(n)], dqkv[...], across, preferred_element_type=F32
                )
                for i, value in halves(n, 1 - k):
                    wall_out[n, i] = value.astype(BF)
                for i, value in halves(n, k):
                    deal_out[n, i] = value.astype(BF)
                pair(n).start()
            if CLOSE_LAG <= n < 8 + CLOSE_LAG:
                last = n - CLOSE_LAG
                pair(last).wait_recv()
                deal_out[last] = (deal_out[last].astype(F32) + wall_in[last].astype(F32)).astype(BF)
                deals.add([lambda: deal_start(last)])
            deals.tick()
            trickle.tick(CLOSE_RATE)

        deals = Trickle()

        def finish(strip, total):
            result[strip] = (grad_ref[strip] + total).astype(BF)

        settle = reduce_plane(
            me,
            terms,
            rows,
            scratch,
            TURNS_CLOSE,
            produce,
            finish,
            after_terms,
            tick,
        )
        while len(begun) < 8 + CLOSE_LAG:
            tick()
        deals.flush()
        trickle.flush()
        copies, own_copy = hand_out_copies(me, result, in_grad_ref, out_send, out_recv)
        for copy in copies:
            copy.start()
        own_copy.start()
        for n in range(8):
            pltpu.make_async_copy(deal_out.at[n], deal_in.at[n], deal_recv.at[n]).wait()

        def gain_landed(i, carry):
            other, device = plane_peer(me, i)
            pltpu.make_async_remote_copy(
                src_ref=gain_slots.at[other],
                dst_ref=gain_slots.at[other],
                send_sem=gain_send.at[i],
                recv_sem=gain_recv.at[other],
                device_id=device,
                device_id_type=MESH,
            ).wait_recv()
            gain_copy(i).wait_send()
            return carry

        lax.fori_loop(1, 16, gain_landed, 0)
        gain_total = gain_slots[0]
        for i in range(1, 16):
            gain_total = gain_total + gain_slots[i]
        gains_ref[...] = gain_total
        settle()
        own_copy.wait()
        for copy in copies:
            copy.wait()
        for n in range(7):
            deal(n).wait_send()

        @pl.when(jnp.logical_not(stays))
        def _():
            deal(7).wait_send()

        for n in range(9):
            pair(n).wait_send()
        for n in range(EARLY, 7):
            grad_landed(me, ffn_in, grad_send, grad_recv, DEAL_ORDER[n])
            for copy in left_copies(n):
                copy.wait_send()

    shape = jax.ShapeDtypeStruct
    vmem = pltpu.VMEM
    return comm_call(
        body,
        "attention_backward",
        5,
        (
            shape((rows * 4, part), BF),
            shape((8, 4, HD, HD), BF),
            shape((4, part), F32),
            shape((8, *grads_left.shape[1:]), BF),
        ),
        [ANY, ANY, *[VMEM] * 14, ANY],
        (ANY, ANY, VMEM, ANY),
        [
            vmem((tokens, width), BF),
            vmem((tokens, width), BF),
            vmem((tokens, width), BF),
            vmem((tokens, HD), F32),
            vmem((tokens, HD), F32),
            vmem((tokens, 3 * HD), BF),
            vmem((16, 16, HD), F32),
            vmem((rows, width), BF),
            vmem((2 * HD, 3 * HD), F32),
            vmem((8, HD, 2 * HD), F32),
            vmem((8, 4, HD, HD), BF),
            vmem((8, 4, HD, HD), BF),
            vmem((8, 4, HD, HD), BF),
            vmem((2, 4, part), F32),
            vmem((2, 4, part), F32),
            vmem((2, 4, part), F32),
            vmem((16, 4, part), F32),
            DMA((2,)),
            DMA((9,)),
            DMA((9,)),
            DMA((16,)),
            DMA((16,)),
            DMA((3,)),
            DMA((4,)),
            DMA((8,)),
            DMA((8,)),
            DMA((16,)),
            DMA((16,)),
            DMA((8, 3)),
            DMA((8, 3)),
            *reduce_scratch(rows, width),
        ],
    )(
        grad_attn,
        full_in,
        query,
        key,
        attended,
        *grads_rotated,
        *tables,
        scales,
        gains,
        qkv_w,
        grad_own,
        attn_term,
        ffn_term,
        grads_left,
    )


def plane_layer(
    inputs,
    cotangent,
    w_query,
    w_key,
    w_value,
    w_out,
    w_gate,
    w_up,
    w_down,
    query_gain,
    key_gain,
    attn_gain,
    ffn_gain,
    lengths,
    block_order,
):
    steps = np.arange(HD // 2, dtype=np.float64) * 2.0 / HD
    frequency = np.tile(np.power(ROPE_THETA, -steps), 2)[None, :].astype(np.float32)
    full_in, source_own, own_cot, qkv_w, out_w, gains_full, gu_stage, down_own, query_proj, key_proj, value_low, cosine, sine, low, high, logical_keys = open_layer(
        inputs,
        cotangent,
        w_query,
        w_key,
        w_value,
        w_out,
        w_gate,
        w_up,
        w_down,
        query_gain[None, :],
        key_gain[None, :],
        attn_gain[None, :],
        ffn_gain[None, :],
        block_order[None, :],
        lengths[None, :],
        jnp.asarray(frequency),
    )
    tables = (cosine, sine)
    (
        residual_full,
        residual_own,
        branch_own,
        gu_w,
        down_other,
        query_rot,
        keys_all,
        values_all,
        attended,
        lse,
        scales,
    ) = attention_forward(
        query_proj,
        key_proj,
        value_low,
        tables,
        (low, high),
        logical_keys,
        source_own,
        out_w,
        gains_full,
        gu_stage,
        down_own,
    )
    grad_ffn, outputs, ffn_gain_term, for_gate, for_up, mixed = ffn_forward(
        residual_full, gu_w, (down_own, down_other), residual_own, own_cot, gains_full
    )
    grad_attn, grad_own, attn_gain_term, ffn_early, ffn_left, *grads_rotated = ffn_backward(
        grad_ffn,
        residual_full,
        gu_w,
        (down_own, down_other),
        for_gate,
        for_up,
        mixed,
        own_cot,
        branch_own,
        gains_full,
        (out_w, query_rot, keys_all, values_all, attended, lse, low, high, logical_keys),
    )
    input_grad, wall_grads, gain_grads, ffn_late = attention_backward(
        grad_attn,
        full_in,
        query_proj,
        key_proj,
        attended,
        grads_rotated,
        tables,
        scales,
        gains_full,
        qkv_w,
        grad_own,
        attn_gain_term,
        ffn_gain_term,
        ffn_left,
    )
    results = write_results(ffn_early, ffn_late, wall_grads, outputs, input_grad, gain_grads)
    return (*results[:9], *[row[0] for row in results[9:]])


def full_rows(piece):
    return lax.all_gather(piece, "head", axis=1, tiled=True)


def head_sums(term):
    return lax.psum_scatter(
        term.astype(jnp.bfloat16), "head", scatter_dimension=1, tiled=True
    ).astype(jnp.float32)


def row_single(term):
    return lax.psum(term, "head")


def row_pair(first, second):
    return lax.psum((first, second), "head")


def gather_weights(w_query, w_key, w_value, w_out, w_gate, w_up, w_down):
    row_parts = (
        lax.all_gather(w_query.astype(jnp.bfloat16), "ctx", axis=0, tiled=True),
        lax.all_gather(w_key.astype(jnp.bfloat16), "ctx", axis=0, tiled=True),
        lax.all_gather(w_value.astype(jnp.bfloat16), "ctx", axis=0, tiled=True),
        lax.all_gather(w_gate.astype(jnp.bfloat16), "ctx", axis=0, tiled=True),
        lax.all_gather(w_up.astype(jnp.bfloat16), "ctx", axis=0, tiled=True),
    )
    col_parts = (
        lax.all_gather(w_out.astype(jnp.bfloat16), "ctx", axis=1, tiled=True),
        lax.all_gather(w_down.astype(jnp.bfloat16), "ctx", axis=1, tiled=True),
    )
    return tuple(row_parts) + tuple(col_parts)


def sequence_tables(logical, lengths):
    seq_ends = jnp.cumsum(lengths)
    seq_starts = seq_ends - lengths
    number = jnp.sum((logical[:, None] >= seq_ends[None, :]).astype(jnp.int32), axis=1)
    member = number[:, None] == jnp.arange(lengths.shape[0], dtype=jnp.int32)[None, :]
    offset = logical - jnp.sum(jnp.where(member, seq_starts[None, :], 0), axis=1)
    return (number, offset)


def rotate(values, offset):
    half_dim = HD // 2
    inverse = jnp.power(ROPE_THETA, -jnp.arange(half_dim, dtype=jnp.float32) * 2.0 / HD)
    angles = offset.astype(jnp.float32)[:, None] * inverse[None, :]
    cosine = jnp.cos(angles)[:, None, :]
    sine_part = jnp.sin(angles)[:, None, :]
    first_half = values[..., :half_dim]
    second_half = values[..., half_dim:]
    return jnp.concatenate(
        [
            first_half * cosine - second_half * sine_part,
            second_half * cosine + first_half * sine_part,
        ],
        axis=-1,
    )


def norm_backward(grad_in, values, factor, gain):
    gain_term = jnp.sum(grad_in * values * factor[:, None], axis=0)
    weighted = grad_in * gain
    row_dot = row_single(jnp.sum(weighted * values, axis=1))
    grad_values = (
        factor[:, None] * weighted - values * (factor * factor * factor * row_dot / D)[:, None]
    )
    return (grad_values, gain_term)


def on_device(
    inputs,
    cotangent,
    w_query,
    w_key,
    w_value,
    w_out,
    w_gate,
    w_up,
    w_down,
    query_gain,
    key_gain,
    attn_gain,
    ffn_gain,
    lengths,
    block_order,
):
    shards = lax.axis_size("ctx")
    position = lax.axis_index("ctx")
    tok_rows, width_part = inputs.shape
    block_rows = tok_rows // shards
    total_tokens = tok_rows * shards
    local_heads = width_part // HD
    scaling = 1.0 / math.sqrt(HD)
    shard_range = jnp.arange(shards, dtype=jnp.int32)
    order_table = block_order.reshape(shards, shards)
    target = order_table % shards
    choose = target[:, :, None] == shard_range[None, None, :]
    stream = jnp.sum(jnp.where(choose, order_table[:, :, None], 0), axis=1)
    stream_blocks = jnp.transpose(stream).reshape(-1)
    logical = (
        stream_blocks[:, None] * block_rows + jnp.arange(block_rows, dtype=jnp.int32)[None, :]
    ).reshape(-1)
    own_target = lax.dynamic_index_in_dim(target, position, 0, keepdims=False)
    send_order = jnp.sum(
        jnp.where(own_target[:, None] == shard_range[None, :], shard_range[:, None], 0), axis=0
    )

    def deal_out(values):
        return values.reshape(shards, block_rows, width_part)[send_order].reshape(
            tok_rows, width_part
        )

    def undeal(values):
        return values.reshape(shards, block_rows, width_part)[own_target].reshape(
            tok_rows, width_part
        )

    local_in, local_cot = (
        lax.all_to_all(deal_out(inputs), "ctx", split_axis=0, concat_axis=0, tiled=True),
        lax.all_to_all(deal_out(cotangent), "ctx", split_axis=0, concat_axis=0, tiled=True),
    )
    number_all, offset_all = sequence_tables(logical, lengths)
    number_own = lax.dynamic_slice_in_dim(number_all, position * tok_rows, tok_rows)
    offset_own = lax.dynamic_slice_in_dim(offset_all, position * tok_rows, tok_rows)
    logical_own = lax.dynamic_slice_in_dim(logical, position * tok_rows, tok_rows)
    query_full, key_full, value_full, gate_full, up_full, out_full, down_full = gather_weights(
        w_query, w_key, w_value, w_out, w_gate, w_up, w_down
    )
    full_in = full_rows(local_in)
    query_proj = jnp.dot(full_in, query_full, preferred_element_type=jnp.float32)
    key_proj = jnp.dot(full_in, key_full, preferred_element_type=jnp.float32)
    value_proj = jnp.dot(full_in, value_full, preferred_element_type=jnp.float32)
    query_sq, key_sq = row_pair(
        jnp.sum(query_proj * query_proj, axis=1), jnp.sum(key_proj * key_proj, axis=1)
    )
    query_scale = lax.rsqrt(query_sq / D + EPSILON)
    key_scale = lax.rsqrt(key_sq / D + EPSILON)
    query_rot = rotate(
        (query_proj * query_scale[:, None] * query_gain).reshape(tok_rows, local_heads, HD),
        offset_own,
    ).astype(jnp.bfloat16)
    key_rot = rotate(
        (key_proj * key_scale[:, None] * key_gain).reshape(tok_rows, local_heads, HD), offset_own
    ).astype(jnp.bfloat16)
    value_low = value_proj.astype(jnp.bfloat16).reshape(tok_rows, local_heads, HD)
    keys_all, values_all = (
        lax.all_gather(key_rot, "ctx", axis=0, tiled=True),
        lax.all_gather(value_low, "ctx", axis=0, tiled=True),
    )
    key_span = math.gcd(total_tokens, 1024)
    key_turns = total_tokens // key_span
    pieces = (
        keys_all.reshape(key_turns, key_span, local_heads, HD),
        values_all.reshape(key_turns, key_span, local_heads, HD),
        number_all.reshape(key_turns, key_span),
        logical.reshape(key_turns, key_span),
    )

    def scores_of(key_piece, number_piece, logical_piece):
        raw_scores = (
            jnp.einsum("qhd,khd->hqk", query_rot, key_piece, preferred_element_type=jnp.float32)
            * scaling
        )
        allowed = (number_own[:, None] == number_piece[None, :]) & (
            logical_piece[None, :] <= logical_own[:, None]
        )
        return (raw_scores, allowed)

    def stat_turn(running, piece_set):
        running_max, running_sum = running
        raw_scores, allowed = scores_of(piece_set[0], piece_set[2], piece_set[3])
        masked_scores = jnp.where(allowed[None], raw_scores, MASKED)
        new_max = jnp.maximum(running_max, jnp.max(masked_scores, axis=2))
        fresh = jnp.sum(
            jnp.where(allowed[None], jnp.exp(masked_scores - new_max[..., None]), 0.0), axis=2
        )
        return ((new_max, running_sum * jnp.exp(running_max - new_max) + fresh), None)

    start_max = jnp.full((local_heads, tok_rows), MASKED, jnp.float32)
    start_sum = jnp.zeros((local_heads, tok_rows), jnp.float32)
    final_max, final_sum = lax.scan(stat_turn, (start_max, start_sum), pieces)[0]
    log_total = final_max + jnp.log(final_sum)

    def out_turn(accum, piece_set):
        raw_scores, allowed = scores_of(piece_set[0], piece_set[2], piece_set[3])
        weights_low = jnp.where(
            allowed[None], jnp.exp(raw_scores - log_total[..., None]), 0.0
        ).astype(jnp.bfloat16)
        return (
            accum
            + jnp.einsum(
                "hqk,khd->qhd", weights_low, piece_set[1], preferred_element_type=jnp.float32
            ),
            None,
        )

    attended = lax.scan(out_turn, jnp.zeros((tok_rows, local_heads, HD), jnp.float32), pieces)[0]
    attended_low = attended.reshape(tok_rows, width_part).astype(jnp.bfloat16)
    attn_part = head_sums(jnp.dot(attended_low, out_full, preferred_element_type=jnp.float32))
    attn_scale = lax.rsqrt(row_single(jnp.sum(attn_part * attn_part, axis=1)) / D + EPSILON)
    residual = local_in.astype(jnp.float32) + attn_part * attn_scale[:, None] * attn_gain
    residual_full = full_rows(residual.astype(jnp.bfloat16))
    gate_proj = jnp.dot(residual_full, gate_full, preferred_element_type=jnp.float32)
    up_proj = jnp.dot(residual_full, up_full, preferred_element_type=jnp.float32)
    gate_sigmoid = jax.nn.sigmoid(gate_proj)
    mixed_hidden = (gate_proj * gate_sigmoid * up_proj).astype(jnp.bfloat16)
    ffn_part = head_sums(jnp.dot(mixed_hidden, down_full, preferred_element_type=jnp.float32))
    ffn_scale = lax.rsqrt(row_single(jnp.sum(ffn_part * ffn_part, axis=1)) / D + EPSILON)
    result = residual + ffn_part * ffn_scale[:, None] * ffn_gain
    query_full, key_full, value_full, gate_full, up_full, out_full, down_full = gather_weights(
        w_query, w_key, w_value, w_out, w_gate, w_up, w_down
    )
    grad_result = local_cot.astype(jnp.float32)
    grad_ffn, ffn_gain_term = norm_backward(grad_result, ffn_part, ffn_scale, ffn_gain)
    grad_ffn_low = full_rows(grad_ffn.astype(jnp.bfloat16))
    down_grad = jnp.einsum(
        "tf,td->fd", mixed_hidden, grad_ffn_low, preferred_element_type=jnp.float32
    )
    grad_mixed = jnp.einsum(
        "td,fd->tf", grad_ffn_low, down_full, preferred_element_type=jnp.float32
    )
    grad_gate_low = (
        grad_mixed * up_proj * gate_sigmoid * (1.0 + gate_proj * (1.0 - gate_sigmoid))
    ).astype(jnp.bfloat16)
    grad_up_low = (grad_mixed * gate_proj * gate_sigmoid).astype(jnp.bfloat16)
    gate_grad = jnp.einsum(
        "td,tf->df", residual_full, grad_gate_low, preferred_element_type=jnp.float32
    )
    up_grad = jnp.einsum(
        "td,tf->df", residual_full, grad_up_low, preferred_element_type=jnp.float32
    )
    resid_term = jnp.einsum(
        "tf,df->td", grad_gate_low, gate_full, preferred_element_type=jnp.float32
    ) + jnp.einsum("tf,df->td", grad_up_low, up_full, preferred_element_type=jnp.float32)
    grad_residual = grad_result + head_sums(resid_term)
    grad_attn, attn_gain_term = norm_backward(grad_residual, attn_part, attn_scale, attn_gain)
    grad_attn_low = full_rows(grad_attn.astype(jnp.bfloat16))
    out_grad = jnp.einsum(
        "te,td->ed", attended_low, grad_attn_low, preferred_element_type=jnp.float32
    )
    grad_heads = (
        jnp.einsum("td,ed->te", grad_attn_low, out_full, preferred_element_type=jnp.float32)
        .astype(jnp.bfloat16)
        .reshape(tok_rows, local_heads, HD)
    )
    row_delta = jnp.transpose(jnp.sum(grad_heads.astype(jnp.float32) * attended, axis=2))

    def score_grads(key_piece, value_piece, number_piece, logical_piece):
        raw_scores, allowed = scores_of(key_piece, number_piece, logical_piece)
        probabilities = jnp.where(allowed[None], jnp.exp(raw_scores - log_total[..., None]), 0.0)
        grad_probs = jnp.einsum(
            "qhd,khd->hqk", grad_heads, value_piece, preferred_element_type=jnp.float32
        )
        grad_scores = (probabilities * (grad_probs - row_delta[..., None])).astype(jnp.bfloat16)
        return (probabilities, grad_scores)

    zero_heads = jnp.zeros((tok_rows, local_heads, HD), jnp.float32)

    def back_turn(grad_acc, piece_set):
        key_piece, value_piece, number_piece, logical_piece = piece_set
        probabilities, grad_scores = score_grads(
            key_piece, value_piece, number_piece, logical_piece
        )
        grad_acc = (
            grad_acc
            + jnp.einsum("hqk,khd->qhd", grad_scores, key_piece, preferred_element_type=jnp.float32)
            * scaling
        )
        key_term = (
            jnp.einsum("hqk,qhd->khd", grad_scores, query_rot, preferred_element_type=jnp.float32)
            * scaling
        )
        value_term = jnp.einsum(
            "hqk,qhd->khd",
            probabilities.astype(jnp.bfloat16),
            grad_heads,
            preferred_element_type=jnp.float32,
        )
        return (grad_acc, (key_term, value_term))

    grad_query_rot, key_value_terms = lax.scan(back_turn, zero_heads, pieces)
    key_terms = key_value_terms[0].reshape(total_tokens, local_heads, HD)
    value_terms = key_value_terms[1].reshape(total_tokens, local_heads, HD)
    grad_key_rot, grad_value_own = (
        lax.psum_scatter(
            key_terms.astype(jnp.bfloat16), "ctx", scatter_dimension=0, tiled=True
        ).astype(jnp.float32),
        lax.psum_scatter(
            value_terms.astype(jnp.bfloat16), "ctx", scatter_dimension=0, tiled=True
        ).astype(jnp.float32),
    )
    grad_query_normed = rotate(grad_query_rot, -offset_own).reshape(tok_rows, width_part)
    grad_key_normed = rotate(grad_key_rot, -offset_own).reshape(tok_rows, width_part)
    query_gain_term = jnp.sum(grad_query_normed * query_proj * query_scale[:, None], axis=0)
    key_gain_term = jnp.sum(grad_key_normed * key_proj * key_scale[:, None], axis=0)
    weighted_query = grad_query_normed * query_gain
    weighted_key = grad_key_normed * key_gain
    query_dot, key_dot = row_pair(
        jnp.sum(weighted_query * query_proj, axis=1), jnp.sum(weighted_key * key_proj, axis=1)
    )
    grad_query_low = (
        query_scale[:, None] * weighted_query
        - query_proj * (query_scale * query_scale * query_scale * query_dot / D)[:, None]
    ).astype(jnp.bfloat16)
    grad_key_low = (
        key_scale[:, None] * weighted_key
        - key_proj * (key_scale * key_scale * key_scale * key_dot / D)[:, None]
    ).astype(jnp.bfloat16)
    grad_value_low = grad_value_own.reshape(tok_rows, width_part).astype(jnp.bfloat16)
    query_grad = jnp.einsum(
        "td,te->de", full_in, grad_query_low, preferred_element_type=jnp.float32
    )
    key_grad = jnp.einsum("td,te->de", full_in, grad_key_low, preferred_element_type=jnp.float32)
    value_grad = jnp.einsum(
        "td,te->de", full_in, grad_value_low, preferred_element_type=jnp.float32
    )
    input_term = jnp.einsum(
        "te,de->td", grad_query_low, query_full, preferred_element_type=jnp.float32
    )
    input_term = input_term + jnp.einsum(
        "te,de->td", grad_key_low, key_full, preferred_element_type=jnp.float32
    )
    input_term = input_term + jnp.einsum(
        "te,de->td", grad_value_low, value_full, preferred_element_type=jnp.float32
    )
    grad_input = grad_residual + head_sums(input_term)
    row_grads = (
        lax.psum_scatter(
            query_grad.astype(jnp.bfloat16), "ctx", scatter_dimension=0, tiled=True
        ).astype(jnp.float32),
        lax.psum_scatter(
            key_grad.astype(jnp.bfloat16), "ctx", scatter_dimension=0, tiled=True
        ).astype(jnp.float32),
        lax.psum_scatter(
            value_grad.astype(jnp.bfloat16), "ctx", scatter_dimension=0, tiled=True
        ).astype(jnp.float32),
        lax.psum_scatter(
            gate_grad.astype(jnp.bfloat16), "ctx", scatter_dimension=0, tiled=True
        ).astype(jnp.float32),
        lax.psum_scatter(
            up_grad.astype(jnp.bfloat16), "ctx", scatter_dimension=0, tiled=True
        ).astype(jnp.float32),
    )
    col_grads = (
        lax.psum_scatter(
            out_grad.astype(jnp.bfloat16), "ctx", scatter_dimension=1, tiled=True
        ).astype(jnp.float32),
        lax.psum_scatter(
            down_grad.astype(jnp.bfloat16), "ctx", scatter_dimension=1, tiled=True
        ).astype(jnp.float32),
    )
    gain_totals = lax.psum((query_gain_term, key_gain_term, attn_gain_term, ffn_gain_term), "ctx")
    back_result, back_grad = (
        lax.all_to_all(result.astype(jnp.bfloat16), "ctx", split_axis=0, concat_axis=0, tiled=True),
        lax.all_to_all(
            grad_input.astype(jnp.bfloat16), "ctx", split_axis=0, concat_axis=0, tiled=True
        ),
    )
    return (
        undeal(back_result),
        undeal(back_grad),
        row_grads[0],
        row_grads[1],
        row_grads[2],
        col_grads[0],
        row_grads[3],
        row_grads[4],
        col_grads[1],
        gain_totals[0],
        gain_totals[1],
        gain_totals[2],
        gain_totals[3],
    )


def sharded(layer, mesh, ctx, head):
    wide, tall, line = P(ctx, head), P(head, ctx), P(head)
    return jax.shard_map(
        layer,
        mesh=mesh,
        in_specs=(
            *(wide,) * 5,
            tall,
            wide,
            wide,
            tall,
            *(line,) * 4,
            P(),
            P(),
        ),
        out_specs=(*(wide,) * 5, tall, wide, wide, tall, *(line,) * 4),
        check_vma=False,
    )


def solution(mesh):
    if dict(mesh.shape) == {"ctx": 8, "head": 4}:
        split = Mesh(mesh.devices.reshape(4, 2, 2, 2), AXES)
        return sharded(plane_layer, split, CTX, ("x", "core"))
    return sharded(on_device, mesh, "ctx", "head")
```

```python
import math

import jax
import jax.numpy as jnp
import numpy as np
from jax import lax
from jax.experimental import pallas as pl
from jax.experimental.pallas import tpu as pltpu
from jax.sharding import Mesh
from jax.sharding import PartitionSpec as P

D = 2048
HD = 128


EPSILON = 1e-06
ROPE_THETA = 500000.0
MASKED = -1e30


BF = jnp.bfloat16
F32 = jnp.float32
MESH = pl.DeviceIdType.MESH
AXES = ("z", "y", "x", "core")
CTX = ("z", "y")
STRIP = 16
ANY = pl.BlockSpec(memory_space=pl.ANY)
VMEM = pl.BlockSpec(memory_space=pltpu.VMEM)
DMA = pltpu.SemaphoreType.DMA
BIG_VMEM = 60 * 1024 * 1024


def place():
    return tuple(lax.axis_index(name) for name in AXES)


def greet(targets):
    barrier = pltpu.get_barrier_semaphore()
    for target in targets:
        pl.semaphore_signal(barrier, inc=1, device_id=target, device_id_type=MESH)
    pl.semaphore_wait(barrier, len(targets))


def near_first(step, z):
    high = z // 2
    low = z + high * (3 - 2 * z)
    value = (low, 1 - low, 2, 3)[step]
    return value + high * (3 - 2 * value)


def plane_axes(me, turn):
    z, y, x, k = me
    a = x * (1 - turn) + y * turn
    b = y * (1 - turn) + x * turn

    def slot(zp, ap, bp):
        yp = bp * (1 - turn) + ap * turn
        xp = ap * (1 - turn) + bp * turn
        return zp * 4 + yp * 2 + xp

    dev_a = (z, y * (1 - turn) + (1 - y) * turn, (1 - x) * (1 - turn) + x * turn, k)
    dev_b = (z, (1 - y) * (1 - turn) + y * turn, x * (1 - turn) + (1 - x) * turn, k)
    return a, b, slot, dev_a, dev_b


EVEN = ((0, 1),) * 4
MORE_X = ((0, 1), (1, 1)) * 2
ALL_X = ((1, 1),) * 4
TURNS_OPEN = ALL_X
TURNS_ATTENTION = (MORE_X, EVEN)
TURNS_FFN_BACK = (EVEN, EVEN)
TURNS_CLOSE = ALL_X


def layer_axes(me, turns):
    return [plane_axes(me, t0 + me[3] * (t1 - t0)) for t0, t1 in turns]


def greet_plane(me, others=()):
    z, y, x, k = me
    barrier = pltpu.get_barrier_semaphore()
    targets = [(z, 1 - y, x, k), (z, y, 1 - x, k), *others]
    for target in targets:
        pl.semaphore_signal(barrier, inc=1, device_id=target, device_id_type=MESH)

    @pl.when(z < 3)
    def _():
        pl.semaphore_signal(barrier, inc=1, device_id=(z + 1, y, x, k), device_id_type=MESH)

    @pl.when(z > 0)
    def _():
        pl.semaphore_signal(barrier, inc=1, device_id=(z - 1, y, x, k), device_id_type=MESH)

    inner = (z + 2) // 3 - z // 3
    pl.semaphore_wait(barrier, len(targets) + 1 + inner)


GATHER_SEMS = [DMA((16,)), DMA((4,)), DMA((4,)), DMA((4,)), DMA((8,))]


DEAL_ORDER = (4, 1, 5, 2, 6, 3, 7)
OPEN_DEAL = 0
OPEN_RATE = 2
DEALT_FIRST = 5
FORWARD_RATE = 1
FORWARD_EVERY = 1
BACK_EVERY = 1
BACK_RATE = 1
CLOSE_FIRST = 0
CLOSE_NEXT = 4
SUM_LAG = 1
EARLY_LAYERS = True
BACK_LAG = 2
CLOSE_LAG = 2
CLOSE_RATE = 1


class Trickle:
    def __init__(self):
        self.waiting = []
        self.calls = 0

    def add(self, copies):
        self.waiting.extend(copies)

    def tick(self, count=1, every=1):
        self.calls += 1
        if self.calls % every:
            return
        for start in self.waiting[:count]:
            start()
        self.waiting = self.waiting[count:]

    def flush(self):
        self.tick(len(self.waiting))


def gather_plane(
    me,
    own_ref,
    view,
    sems,
    turns,
    between=lambda step: None,
    arrived=None,
    tick=lambda: None,
    early=False,
):
    z, y, x, k = me
    recv, up_send, down_send, a_send, b_send = sems
    axes = layer_axes(me, turns)

    def copy(src, index, send_sem, device):
        return pltpu.make_async_remote_copy(
            src_ref=src,
            dst_ref=view(index),
            send_sem=send_sem,
            recv_sem=recv.at[index],
            device_id=device,
            device_id_type=MESH,
        )

    def landed(index):
        copy(view(index), index, a_send.at[0], axes[0][3]).wait_recv()

    def layer_landed(step):
        tick()
        a, b, slot, dev_a, dev_b = axes[step]
        zp = near_first(step, z)
        landed(slot(zp, a, 1 - b))
        landed(slot(zp, 1 - a, 1 - b))
        if arrived is not None:
            arrived(step)

    for step in range(5):
        if step < 4:
            a, b, slot, dev_a, dev_b = axes[step]
            zp = near_first(step, z)
            index = slot(zp, a, b)
            if step == 0:
                src = own_ref
            else:
                landed(index)
                src = view(index)

            @pl.when((zp <= z) & (z < 3))
            def _():
                copy(src, index, up_send.at[zp], (z + 1, y, x, k)).start()

            @pl.when((zp >= z) & (z > 0))
            def _():
                copy(src, index, down_send.at[zp], (z - 1, y, x, k)).start()

            copy(src, index, a_send.at[step], dev_a).start()
            copy(src, index, b_send.at[step], dev_b).start()
            tick()
        if step > 0:
            a, b, slot, dev_a, dev_b = axes[step - 1]
            index = slot(near_first(step - 1, z), 1 - a, b)
            landed(index)
            copy(view(index), index, b_send.at[3 + step], dev_b).start()
            tick()
        between(step)
        if step >= 2 and early:
            layer_landed(step - 2)
    for step in ((3,) if early else range(4)):
        layer_landed(step)
    for step in range(4):
        a, b, slot, dev_a, dev_b = axes[step]
        zp = near_first(step, z)
        for ap, number in ((a, step), (1 - a, 4 + step)):
            index = slot(zp, ap, b)
            copy(view(index), index, b_send.at[number], dev_b).wait_send()
        index = slot(zp, a, b)
        copy(view(index), index, a_send.at[step], dev_a).wait_send()

        @pl.when((zp <= z) & (z < 3))
        def _():
            copy(view(index), index, up_send.at[zp], (z + 1, y, x, k)).wait_send()

        @pl.when((zp >= z) & (z > 0))
        def _():
            copy(view(index), index, down_send.at[zp], (z - 1, y, x, k)).wait_send()


def reduce_scratch(rows, width):
    return [
        pltpu.VMEM((4, 2, rows, width), BF),
        pltpu.VMEM((4, rows, width), BF),
        pltpu.VMEM((4, rows, width), BF),
        pltpu.VMEM((4, rows, width), BF),
        pltpu.VMEM((4, rows, width), BF),
        pltpu.VMEM((4, rows, width), BF),
        DMA((8,)),
        DMA((8,)),
        DMA((4,)),
        DMA((4,)),
        DMA((4,)),
        DMA((4,)),
        DMA((4,)),
    ]


N_REDUCE = 13


def strips(rows, work, strip=STRIP):
    def body(i, carry):
        work(pl.ds(pl.multiple_of(i * strip, strip), strip))
        return carry

    lax.fori_loop(0, rows // strip, body, 0)


def reduce_plane(
    me,
    terms,
    rows,
    scratch,
    turns,
    produce,
    finish,
    after_terms=lambda: None,
    tick=lambda: None,
):
    z, y, x, k = me
    (from_b, to_a, from_a, to_z, from_low, from_high) = scratch[:6]
    (b_send, b_recv, a_send, a_recv, z_send, low_recv, high_recv) = scratch[6:]
    axes = layer_axes(me, turns)[::-1]
    order = [near_first(step, z) for step in (3, 2, 1, 0)]

    def start_of(step, ap, bp):
        return pl.multiple_of(axes[step][2](order[step], ap, bp) * rows, rows)

    def copy_b(step, flip):
        a, b, slot, dev_a, dev_b = axes[step]
        zp, ap = order[step], (1 - a if flip else a)
        return pltpu.make_async_remote_copy(
            src_ref=terms.at[pl.ds(start_of(step, ap, 1 - b), rows), :],
            dst_ref=from_b.at[zp, ap],
            send_sem=b_send.at[zp * 2 + ap],
            recv_sem=b_recv.at[zp * 2 + ap],
            device_id=dev_b,
            device_id_type=MESH,
        )

    def copy_a(step):
        zp, dev_a = order[step], axes[step][3]
        return pltpu.make_async_remote_copy(
            src_ref=to_a.at[zp],
            dst_ref=from_a.at[zp],
            send_sem=a_send.at[zp],
            recv_sem=a_recv.at[zp],
            device_id=dev_a,
            device_id_type=MESH,
        )

    def copy_z(zp, target, recv, to):
        return pltpu.make_async_remote_copy(
            src_ref=to_z.at[zp],
            dst_ref=target.at[zp],
            send_sem=z_send.at[zp],
            recv_sem=recv.at[zp],
            device_id=(to, y, x, k),
            device_id_type=MESH,
        )

    def copy_up(zp):
        return copy_z(zp, from_low, low_recv, z + 1)

    def copy_down(zp):
        return copy_z(zp, from_high, high_recv, z - 1)

    def mine(step, flip, strip):
        a, b = axes[step][:2]
        at = start_of(step, 1 - a if flip else a, b) + strip.start
        return terms[pl.ds(pl.multiple_of(at, STRIP), STRIP), :].astype(F32)

    for step in range(4):
        produce(order[step])
        for flip in (True, False):
            copy_b(step, flip).start()
        tick()
    after_terms()

    for step in range(4 + SUM_LAG):
        if step < 4:
            copy_b(step, True).wait_recv()

            def first(strip, step=step):
                zp, ap = order[step], 1 - axes[step][0]
                to_a[zp, strip] = (
                    mine(step, True, strip) + from_b[zp, ap, strip].astype(F32)
                ).astype(BF)

            strips(rows, first)
            copy_a(step).start()
            tick()
        if step >= SUM_LAG:
            done = step - SUM_LAG
            tick()
            copy_b(done, False).wait_recv()
            copy_a(done).wait_recv()

            def own_sum(strip, last=done):
                zp, ap = order[last], axes[last][0]
                return (
                    mine(last, False, strip)
                    + from_b[zp, ap, strip].astype(F32)
                    + from_a[zp, strip].astype(F32)
                )

            if done < 3:
                zp = order[done]
                upward = zp > z

                @pl.when(upward & (z > 0))
                def _(zp=zp, own_sum=own_sum):
                    copy_up(zp).wait_recv()

                    def work(strip):
                        to_z[zp, strip] = (own_sum(strip) + from_low[zp, strip].astype(F32)).astype(BF)

                    strips(rows, work)

                @pl.when(jnp.logical_not(upward) & (z < 3))
                def _(zp=zp, own_sum=own_sum):
                    copy_down(zp).wait_recv()

                    def work(strip):
                        to_z[zp, strip] = (own_sum(strip) + from_high[zp, strip].astype(F32)).astype(BF)

                    strips(rows, work)

                @pl.when((z == 0) | (z == 3))
                def _(zp=zp, own_sum=own_sum):
                    def work(strip):
                        to_z[zp, strip] = own_sum(strip).astype(BF)

                    strips(rows, work)

                @pl.when(upward)
                def _(zp=zp):
                    copy_up(zp).start()

                @pl.when(jnp.logical_not(upward))
                def _(zp=zp):
                    copy_down(zp).start()

            else:

                @pl.when(z == 0)
                def _():
                    copy_down(z).wait_recv()
                    strips(rows, lambda s: finish(s, own_sum(s) + from_high[z, s].astype(F32)))

                @pl.when(z == 3)
                def _():
                    copy_up(z).wait_recv()
                    strips(rows, lambda s: finish(s, own_sum(s) + from_low[z, s].astype(F32)))

                @pl.when((z > 0) & (z < 3))
                def _():
                    copy_up(z).wait_recv()
                    copy_down(z).wait_recv()
                    strips(
                        rows,
                        lambda s: finish(
                            s,
                            own_sum(s) + from_low[z, s].astype(F32) + from_high[z, s].astype(F32),
                        ),
                    )

    def settle():
        for step in range(4):
            copy_b(step, True).wait_send()
            copy_b(step, False).wait_send()
            copy_a(step).wait_send()
        for zp in order[:3]:
            copy_up(zp).wait_send()

    return settle


def own_tile(me):
    z, y, x, k = me
    return z * 2 + y


def gather_view(out_ref, rows):
    def view(slot):
        return out_ref.at[pl.ds(pl.multiple_of(slot * rows, rows), rows), :]

    return view


def hand_out_copies(me, own_ref, out_ref, send, recv):
    z, y, x, k = me
    rows, width = own_ref.shape
    part = width // 4
    target_rows = pl.ds(pl.multiple_of(k * 2 * rows + x * rows, rows), rows)

    def copy(xt, kt, number):
        return pltpu.make_async_remote_copy(
            src_ref=own_ref.at[:, pl.ds(pl.multiple_of((2 * xt + kt) * part, part), part)],
            dst_ref=out_ref.at[target_rows, :],
            send_sem=send.at[number],
            recv_sem=recv.at[number],
            device_id=(z, y, xt, kt),
            device_id_type=MESH,
        )

    local = pltpu.make_async_copy(
        own_ref.at[:, pl.ds(pl.multiple_of((2 * x + k) * part, part), part)],
        out_ref.at[target_rows, :],
        recv.at[3],
    )
    return [copy(x, 1 - k, 0), copy(1 - x, k, 1), copy(1 - x, 1 - k, 2)], local


def pair_devices(me):
    z, y, x, k = me
    return [(z, y, x, 1 - k), (z, y, 1 - x, 1 - k)]


def row_scale(values):
    return lax.rsqrt(jnp.sum(values * values, axis=1, keepdims=True) / values.shape[1] + EPSILON)


def norm_back_strip(grad, values, gain):
    scale = row_scale(values)
    term = grad * values * scale
    weighted = grad * gain
    dot = jnp.sum(weighted * values, axis=1, keepdims=True)
    back = scale * weighted - values * (scale * scale * scale * dot / values.shape[1])
    return back, term[:8] + term[8:]


def comm_call(body, name, number, out_shape, in_specs, out_specs, scratch, lift=True):
    lifted = [i for i, spec in enumerate(in_specs) if spec is VMEM] if lift else []
    leaving = [i for i, spec in enumerate(out_specs) if spec is VMEM]
    first_out = len(in_specs)

    def with_copies(*refs):
        refs = list(refs)
        sems = refs.pop()
        count = len(lifted) + len(leaving)
        held = refs[len(refs) - count :]
        refs = refs[: len(refs) - count]
        loads, stores, begun = [], [], []
        for n, i in enumerate(lifted):
            loads.append(pltpu.make_async_copy(refs[i], held[n], sems.at[n]))
            refs[i] = held[n]
        for n, i in enumerate(leaving, len(lifted)):
            stores.append((held[n], pltpu.make_async_copy(held[n], refs[first_out + i], sems.at[n])))
            refs[first_out + i] = held[n]
        for copy in loads:
            copy.start()

        def loaded():
            for copy in loads:
                copy.wait()

        def leave(*done):
            for ref, copy in stores:
                if any(ref is other for other in done):
                    copy.start()
                    begun.append(ref)

        body(*refs, loaded=loaded, leave=leave)
        leave(*[ref for ref, _ in stores if not any(ref is other for other in begun)])
        for _, copy in stores:
            copy.wait()

    def call(*args):
        extra = [pltpu.VMEM(args[i].shape, args[i].dtype) for i in lifted]
        extra += [pltpu.VMEM(out_shape[i].shape, out_shape[i].dtype) for i in leaving]
        return pl.pallas_call(
            with_copies,
            name=name,
            out_shape=out_shape,
            in_specs=[ANY if i in lifted else spec for i, spec in enumerate(in_specs)],
            out_specs=tuple(ANY for _ in out_specs),
            scratch_shapes=[*scratch, *extra, DMA((len(extra),))],
            compiler_params=pltpu.CompilerParams(
                collective_id=number, has_side_effects=True, vmem_limit_bytes=BIG_VMEM
            ),
        )(*args)

    return call


def same_x_greet(me):
    z, y, x, k = me
    barrier = pltpu.get_barrier_semaphore()
    number = z * 4 + y * 2 + k

    def body(i, carry):
        other = lax.rem(number + i, 16)
        pl.semaphore_signal(
            barrier,
            inc=1,
            device_id=(other // 4, (other // 2) % 2, x, other % 2),
            device_id_type=MESH,
        )
        return carry

    lax.fori_loop(1, 16, body, 0)
    for kt in (k, 1 - k):
        pl.semaphore_signal(barrier, inc=1, device_id=(z, y, 1 - x, kt), device_id_type=MESH)
    pl.semaphore_wait(barrier, 17)


def masked_scores(q, keys, low, high, logical):
    raw = lax.dot_general(q, keys, (((1,), (1,)), ((), ())), preferred_element_type=F32)
    allowed = (logical >= low) & (logical <= high)
    return raw * (1.0 / math.sqrt(HD)), allowed


def eye_mask():
    return lax.broadcasted_iota(jnp.int32, (HD, HD), 0) == lax.broadcasted_iota(
        jnp.int32, (HD, HD), 1
    )


def column_to_row(column, eye):
    return jnp.sum(jnp.where(eye, column, 0.0), axis=0, keepdims=True)


def row_to_column(row, eye):
    return jnp.sum(jnp.where(eye, row, 0.0), axis=1, keepdims=True)


def open_layer(
    inputs,
    cotangent,
    w_query,
    w_key,
    w_value,
    w_out,
    w_gate,
    w_up,
    w_down,
    query_gain,
    key_gain,
    attn_gain,
    ffn_gain,
    order,
    lengths,
    frequency,
):
    rows, part = inputs.shape
    half = rows // 2
    quarter = half // 2
    tokens, width = 8 * half, 4 * part
    hidden = w_gate.shape[1]
    down = hidden // 8

    def body(*refs, loaded, leave):
        (in_ref, cot_ref, wq_ref, wk_ref, wv_ref, wo_ref, wg_ref, wu_ref, wd_ref) = refs[:9]
        gain_parts = refs[9:13]
        (order_ref, lengths_ref, frequency_ref) = refs[13:16]
        (cos_ref, sin_ref, low_ref, high_ref, log_ref) = refs[27:32]
        gain_ref = refs[-1]
        refs = refs[:10] + refs[16:27] + refs[32:-1]
        (full_out, own_out, own_cot_ref, wqkv_ref, wout_ref, gains_ref, gu_out, down_ref) = refs[10:18]
        (q_ref, k_ref, v_ref) = refs[18:21]
        (full_ref, shard, cot_half, qkv_raw, out_raw, gu_raw, d_raw) = refs[21:28]
        (qkv_stage, out_stage, gu_stage, d_stage) = refs[28:32]
        (load_sem, pair_send, pair_recv, local_sem, deal_send, deal_recv) = refs[32:38]
        (share_send, share_recv, gain_send, gain_recv, cot_sems, keep_sem) = refs[38:44]
        (down_send, down_recv) = refs[44:46]
        gather_sems = refs[46:]
        me = z, y, x, k = place()
        ctx = own_tile(me)
        sibling = (z, y, x, 1 - k)

        loads = [
            pltpu.make_async_copy(src, dst, load_sem.at[i])
            for i, (src, dst) in enumerate(
                [
                    (wq_ref, qkv_raw.at[0]),
                    (wk_ref, qkv_raw.at[1]),
                    (wv_ref, qkv_raw.at[2]),
                    (wo_ref, out_raw),
                    (wg_ref, gu_raw.at[0]),
                    (wu_ref, gu_raw.at[1]),
                    (wd_ref, d_raw),
                ]
            )
        ]
        for load in loads:
            load.start()
        same_x_greet(me)
        loaded()

        def pair_copy(src, dst, number):
            columns = pl.ds(pl.multiple_of(k * part, part), part)
            remote = pltpu.make_async_remote_copy(
                src_ref=src.at[pl.ds(pl.multiple_of((1 - k) * half, half), half), :],
                dst_ref=dst.at[:, columns],
                send_sem=pair_send.at[number],
                recv_sem=pair_recv.at[number],
                device_id=sibling,
                device_id_type=MESH,
            )
            local = pltpu.make_async_copy(
                src.at[pl.ds(pl.multiple_of(k * half, half), half), :],
                dst.at[:, columns],
                local_sem.at[number],
            )
            remote.start()
            local.start()
            return remote, local

        first = pair_copy(in_ref, shard, 0)
        second = pair_copy(cot_ref, cot_half, 1)

        for i, gain_part in enumerate(gain_parts):
            gain_ref[i : i + 1, :] = gain_part[...]

        def gain_copy(xt, kt, number):
            return pltpu.make_async_remote_copy(
                src_ref=gain_ref,
                dst_ref=gains_ref.at[:, pl.ds(pl.multiple_of((2 * x + k) * part, part), part)],
                send_sem=gain_send.at[number],
                recv_sem=gain_recv.at[number],
                device_id=(z, y, xt, kt),
                device_id_type=MESH,
            )

        gain_copies = [gain_copy(x, 1 - k, 0), gain_copy(1 - x, k, 1), gain_copy(1 - x, 1 - k, 2)]
        for copy in gain_copies:
            copy.start()
        gain_local = pltpu.make_async_copy(
            gain_ref,
            gains_ref.at[:, pl.ds(pl.multiple_of((2 * x + k) * part, part), part)],
            local_sem.at[2],
        )
        gain_local.start()

        first[0].wait_recv()
        first[1].wait()

        def view(slot):
            return full_ref.at[
                pl.ds(pl.multiple_of((slot // 2) * half, half), half),
                pl.ds(pl.multiple_of((slot % 2) * 2 * part, 2 * part), 2 * part),
            ]

        own_slot = ctx * 2 + x
        own_local = pltpu.make_async_copy(shard, view(own_slot), local_sem.at[3])
        own_local.start()

        def deal(e):
            j, r = e // 2, e % 2
            return [
                pltpu.make_async_remote_copy(
                    src_ref=src,
                    dst_ref=dst,
                    send_sem=deal_send.at[i, e],
                    recv_sem=deal_recv.at[i, ctx],
                    device_id=(2 * k + e // 4, (e // 2) % 2, x, r),
                    device_id_type=MESH,
                )
                for i, (src, dst) in enumerate(deal_ends(j, r))
            ]

        def deal_ends(j, r):
            at = pl.ds(pl.multiple_of(ctx * 2 * HD + r * HD, HD), HD)
            return (
                (
                    qkv_stage.at[:, r * HD : (r + 1) * HD, j * HD : (j + 1) * HD],
                    wqkv_ref.at[:, at, :],
                ),
                (
                    out_stage.at[j * HD : (j + 1) * HD, r * HD : (r + 1) * HD],
                    wout_ref.at[:, at],
                ),
            )

        trickle = Trickle()
        stays = k == z // 2
        own_e = (z % 2) * 4 + y * 2 + k

        def deal_all():
            for load in loads[:4]:
                load.wait()

            def round_qkv(s):
                for i in range(3):
                    qkv_stage[i, s] = qkv_raw[i, s].astype(BF)

            strips(rows, round_qkv)

            def round_out(s):
                out_stage[s] = out_raw[s].astype(BF)

            strips(2 * rows, round_out, 32)
            if OPEN_DEAL == 0:
                begin_deal()

        def begin_deal():
            trickle.add([lambda e=e: deal_start(e) for e in range(8)])

        def deal_start(e):
            @pl.when(jnp.logical_not(stays & (own_e == e)))
            def _():
                for copy in deal(e):
                    copy.start()

            @pl.when(stays & (own_e == e))
            def _():
                for i, (src, dst) in enumerate(deal_ends(e // 2, e % 2)):
                    pltpu.make_async_copy(src, dst, deal_recv.at[i, ctx]).start()

        def cot_begin():
            second[0].wait_recv()
            second[1].wait()
            cot_remote.start()
            cot_local.start()

        wide = pl.ds(pl.multiple_of(x * 2 * part, 2 * part), 2 * part)
        cot_remote = pltpu.make_async_remote_copy(
            src_ref=cot_half.at[pl.ds(pl.multiple_of((1 - x) * quarter, quarter), quarter), :],
            dst_ref=own_cot_ref.at[:, wide],
            send_sem=cot_sems.at[0],
            recv_sem=cot_sems.at[1],
            device_id=(z, y, 1 - x, k),
            device_id_type=MESH,
        )
        cot_local = pltpu.make_async_copy(
            cot_half.at[pl.ds(pl.multiple_of(x * quarter, quarter), quarter), :],
            own_cot_ref.at[:, wide],
            cot_sems.at[2],
        )

        keeps = [
            pltpu.make_async_copy(gu_stage.at[0], gu_out.at[0], keep_sem.at[0]),
            pltpu.make_async_copy(gu_stage.at[1], gu_out.at[1], keep_sem.at[1]),
            pltpu.make_async_copy(
                d_stage.at[pl.ds(pl.multiple_of(ctx * down, down), down), :],
                down_ref.at[:, pl.ds(pl.multiple_of(ctx * rows, rows), rows)],
                keep_sem.at[2],
            ),
        ]

        def down_copy(t):
            to = ctx + t - 8 * ((ctx + t) // 8)
            return pltpu.make_async_remote_copy(
                src_ref=d_stage.at[pl.ds(pl.multiple_of(to * down, down), down), :],
                dst_ref=down_ref.at[:, pl.ds(pl.multiple_of(ctx * rows, rows), rows)],
                send_sem=down_send.at[t],
                recv_sem=down_recv.at[t],
                device_id=(to // 2, to % 2, x, k),
                device_id_type=MESH,
            )

        def down_landed(t):
            c = ctx + 8 - t - 8 * ((ctx + 8 - t) // 8)
            part_of = down_ref.at[:, pl.ds(pl.multiple_of(c * rows, rows), rows)]
            pltpu.make_async_remote_copy(
                src_ref=part_of,
                dst_ref=part_of,
                send_sem=down_send.at[t],
                recv_sem=down_recv.at[t],
                device_id=sibling,
                device_id_type=MESH,
            ).wait_recv()

        def deal_down():
            trickle.add([lambda t=t: down_copy(t).start() for t in DEAL_ORDER])

        def round_up(i):
            loads[4 + i].wait()

            def work(s):
                gu_stage[i, s] = gu_raw[i, s].astype(BF)

            strips(rows, work)
            keeps[i].start()

        def round_down():
            loads[6].wait()

            def work(s):
                d_stage[s] = d_raw[s].astype(BF)

            strips(hidden, work, 128)
            keeps[2].start()

        def positions():
            blocks = order_ref.shape[1]
            square = lax.broadcasted_iota(jnp.int32, (blocks, blocks), 0)
            square = square == lax.broadcasted_iota(jnp.int32, (blocks, blocks), 1)
            column = row_to_column(order_ref[...].astype(F32), square)
            lane = lax.broadcasted_iota(jnp.int32, (1, 2 * tokens), 1)
            other = (lane >= tokens).astype(jnp.int32)
            core = k + other - 2 * k * other
            lane = lane - tokens * other
            in_half = lane & (half - 1)
            block_rows = 2 * tokens // blocks
            block = (lane - in_half) // half * (2 * half // block_rows)
            block = block + core * (half // block_rows)
            block = block + (in_half - (in_half & (block_rows - 1))) // block_rows
            match = lax.broadcasted_iota(jnp.int32, (blocks, 2 * tokens), 0) == block
            first_of = jnp.sum(jnp.where(match, column, 0.0), axis=0, keepdims=True) * block_rows
            logical = first_of + (in_half & (block_rows - 1)).astype(F32)
            log_ref[...] = logical
            own = logical[:, :tokens]
            begin = jnp.zeros_like(own)
            end = jnp.zeros((1, 1), F32)
            for j in range(lengths_ref.shape[1]):
                length = lengths_ref[:, j : j + 1].astype(F32)
                end = end + length
                begin = begin + jnp.where(own >= end, length, 0.0)
            eye = eye_mask()
            for i in range(tokens // HD):
                piece = slice(i * HD, (i + 1) * HD)
                low = row_to_column(begin[:, piece], eye)
                high = row_to_column(own[:, piece], eye)
                low_ref[piece, :] = low
                high_ref[piece, :] = high
                angles = (high - low) * frequency_ref[...]
                cos_ref[piece, :] = jnp.cos(angles)
                sine = jnp.sin(angles)
                left = lax.broadcasted_iota(jnp.int32, (HD, HD), 1) < HD // 2
                sin_ref[piece, :] = jnp.where(left, -sine, sine)
            leave(cos_ref, sin_ref, low_ref, high_ref, log_ref)

        between = [
            deal_all,
            lambda: (cot_begin(), round_down()),
            lambda: (round_up(0), round_up(1)),
            positions,
            lambda: None,
        ]

        def open_between(step):
            if 0 < step == OPEN_DEAL:
                begin_deal()
            if step == max(OPEN_DEAL, 1):
                if step == 1:
                    between[1]()
                deal_down()
                if step == 1:
                    return
            between[step]()

        def deal_wait(c):
            at = slice(c * 2 * HD, c * 2 * HD + HD)
            pltpu.make_async_copy(
                qkv_stage.at[:, :HD, :HD], wqkv_ref.at[:, at, :], deal_recv.at[0, c]
            ).wait()
            pltpu.make_async_copy(
                out_stage.at[:HD, :HD], wout_ref.at[:, at], deal_recv.at[1, c]
            ).wait()

        def share(c, r):
            at = pl.ds(pl.multiple_of(c * 2 * HD + r * HD, HD), HD)
            return [
                pltpu.make_async_remote_copy(
                    src_ref=ref,
                    dst_ref=ref,
                    send_sem=share_send.at[i, c],
                    recv_sem=share_recv.at[i, c],
                    device_id=sibling,
                    device_id_type=MESH,
                )
                for i, ref in enumerate((wqkv_ref.at[:, at, :], wout_ref.at[:, at]))
            ]

        def project_layer(step):
            if step == 0:
                trickle.flush()
                own_local.wait()
                for c in range(8):
                    deal_wait(c)
                    for copy in share(c, k):
                        copy.start()
                for c in range(8):
                    for copy in share(c, 1 - k):
                        copy.wait_recv()
                leave(wqkv_ref, wout_ref)
            at = pl.ds(pl.multiple_of(near_first(step, z) * 2 * half, 2 * half), 2 * half)
            tile = full_ref[at, :]
            q_ref[at, :] = jnp.dot(tile, wqkv_ref[0], preferred_element_type=F32)
            k_ref[at, :] = jnp.dot(tile, wqkv_ref[1], preferred_element_type=F32)
            v_ref[at, :] = jnp.dot(tile, wqkv_ref[2], preferred_element_type=F32).astype(BF)

        gather_plane(
            me,
            shard,
            view,
            gather_sems,
            TURNS_OPEN,
            open_between,
            project_layer,
            lambda: trickle.tick(OPEN_RATE),
        )

        full_keep = pltpu.make_async_copy(full_ref, full_out, keep_sem.at[3])
        full_keep.start()
        own_rows = pl.ds(pl.multiple_of(own_slot * quarter, quarter), quarter)
        own_keep = pltpu.make_async_copy(full_ref.at[own_rows, :], own_out, keep_sem.at[4])
        own_keep.start()
        for e in range(8):

            @pl.when(jnp.logical_not(stays & (own_e == e)))
            def _(e=e):
                for copy in deal(e):
                    copy.wait_send()

        for c in range(8):
            for copy in share(c, k):
                copy.wait_send()
        first[0].wait_send()
        second[0].wait_send()
        for copy in gain_copies:
            copy.wait()
        gain_local.wait()
        cot_remote.wait()
        cot_local.wait()
        for keep in (*keeps, full_keep, own_keep):
            keep.wait()
        for t in range(1, 8):
            down_landed(t)
            down_copy(t).wait_send()

    shape = jax.ShapeDtypeStruct
    return comm_call(
        body,
        "open_layer",
        0,
        (
            shape((tokens, width), BF),
            shape((quarter, width), BF),
            shape((quarter, width), BF),
            shape((3, width, HD), BF),
            shape((HD, width), BF),
            shape((4, width), F32),
            shape((2, rows, hidden), BF),
            shape((down, width), BF),
            shape((tokens, HD), F32),
            shape((tokens, HD), F32),
            shape((tokens, HD), BF),
            shape((tokens, HD), F32),
            shape((tokens, HD), F32),
            shape((tokens, 1), F32),
            shape((tokens, 1), F32),
            shape((1, 2 * tokens), F32),
        ),
        [*[ANY] * 9, *[VMEM] * 7],
        (ANY, ANY, ANY, VMEM, VMEM, ANY, ANY, ANY, VMEM, VMEM, VMEM, *[VMEM] * 5),
        [
            pltpu.VMEM((tokens, width), BF),
            pltpu.VMEM((half, 2 * part), BF),
            pltpu.VMEM((half, 2 * part), BF),
            pltpu.VMEM((3, rows, part), F32),
            pltpu.VMEM((part, rows), F32),
            pltpu.VMEM((2, rows, hidden), F32),
            pltpu.VMEM((hidden, rows), F32),
            pltpu.VMEM((3, rows, part), BF),
            pltpu.VMEM((part, rows), BF),
            pltpu.VMEM((2, rows, hidden), BF),
            pltpu.VMEM((hidden, rows), BF),
            DMA((7,)),
            DMA((2,)),
            DMA((2,)),
            DMA((4,)),
            DMA((2, 8)),
            DMA((2, 8)),
            DMA((2, 8)),
            DMA((2, 8)),
            DMA((3,)),
            DMA((3,)),
            DMA((3,)),
            DMA((5,)),
            DMA((8,)),
            DMA((8,)),
            *GATHER_SEMS,
            pltpu.VMEM((4, part), F32),
        ],
        lift=False,
    )(
        inputs,
        cotangent,
        w_query,
        w_key,
        w_value,
        w_out,
        w_gate,
        w_up,
        w_down,
        query_gain,
        key_gain,
        attn_gain,
        ffn_gain,
        order,
        lengths,
        frequency,
    )


def plane_peer(me, i):
    z, y, x, k = me
    other = lax.rem(z * 4 + y * 2 + x + i, 16)
    return other, (other // 4, (other // 2) % 2, other % 2, k)


def plane_greet_all(me, others):
    barrier = pltpu.get_barrier_semaphore()

    def call(i, carry):
        pl.semaphore_signal(barrier, inc=1, device_id=plane_peer(me, i)[1], device_id_type=MESH)
        return carry

    lax.fori_loop(1, 16, call, 0)
    for other in others:
        pl.semaphore_signal(barrier, inc=1, device_id=other, device_id_type=MESH)
    pl.semaphore_wait(barrier, 15 + len(others))


def sum_begin(me, slots, send, recv):
    own = me[0] * 4 + me[1] * 2 + me[2]

    def copy(i, slot):
        return pltpu.make_async_remote_copy(
            src_ref=slots.at[slot],
            dst_ref=slots.at[slot],
            send_sem=send.at[i],
            recv_sem=recv.at[slot],
            device_id=plane_peer(me, i)[1],
            device_id_type=MESH,
        )

    def begin(i, carry):
        copy(i, own).start()
        return carry

    def landed(i, carry):
        copy(i, plane_peer(me, i)[0]).wait_recv()
        return carry

    def sent(i, carry):
        copy(i, own).wait_send()
        return carry

    lax.fori_loop(1, 16, begin, 0)

    def end():
        lax.fori_loop(1, 16, landed, 0)
        lax.fori_loop(1, 16, sent, 0)
        total = slots[0]
        for i in range(1, 16):
            total = total + slots[i]
        return total

    return end


def attention_forward(
    query, key, value, tables, bounds, logical, source, out_weight, gains, gu_stage, down_own
):
    tokens, width = query.shape[0], source.shape[1]
    rows = tokens // 16
    group = tokens // 4
    hidden = gu_stage.shape[2] // 8
    part = width // 8

    def body(*refs, loaded, leave):
        (q_in, k_in, v_in, cos_ref, sin_ref, low_ref, high_ref, log_ref, source_ref, wout_ref, gain_ref) = refs[:11]
        (gu_ref, d_ref) = refs[11:13]
        (full_ref, own_ref, branch_ref, wgu_ref, d_other_ref, qrot_ref, keys_ref, values_ref, o_ref, lse_ref, scale_ref) = refs[13:24]
        (terms, shard, slots, tot_send, tot_recv, pair_send, pair_recv, local) = refs[24:32]
        (ffn_send, ffn_recv, share_send, share_recv, ffn_local) = refs[32:37]
        rest = refs[37:]
        me = z, y, x, k = place()
        ctx = own_tile(me)
        head_at = pl.ds(pl.multiple_of((x * 8 + ctx) * HD, HD), HD)
        sibling = (z, y, x, 1 - k)
        barrier = pltpu.get_barrier_semaphore()
        plane_greet_all(me, [sibling])
        loaded()
        query_gain, key_gain = gain_ref[0:1, head_at], gain_ref[1:2, head_at]

        def pair(src, dst, n):
            return pltpu.make_async_remote_copy(
                src_ref=src,
                dst_ref=dst,
                send_sem=pair_send.at[n],
                recv_sem=pair_recv.at[n],
                device_id=sibling,
                device_id_type=MESH,
            )

        eye = eye_mask()
        own = z * 4 + y * 2 + x
        for i in range(8):
            piece = slice(i * HD, (i + 1) * HD)
            for side, ref in enumerate((q_in, k_in)):
                values = ref[piece, :]
                column = jnp.sum(values * values, axis=1, keepdims=True)
                slots[own, side * 8 + i : side * 8 + i + 1, :] = column_to_row(column, eye)
        values_ref[:tokens, :] = v_in[...]
        other_half = pl.ds(tokens, tokens)
        v_copy = pair(v_in, values_ref.at[other_half, :], 0)
        v_copy.start()

        def ffn_copy(t, i):
            to = ctx + t - 8 * ((ctx + t) // 8)
            at = pl.ds(pl.multiple_of(to * hidden, hidden), hidden)
            from_at = pl.ds(pl.multiple_of(ctx * part, part), part)
            return pltpu.make_async_remote_copy(
                src_ref=gu_ref.at[i, :, at],
                dst_ref=wgu_ref.at[i, from_at, :hidden],
                send_sem=ffn_send.at[i, t],
                recv_sem=ffn_recv.at[i, t],
                device_id=(to // 2, to % 2, x, k),
                device_id_type=MESH,
            )

        def ffn_ends(t):
            c = ctx + 8 - t - 8 * ((ctx + 8 - t) // 8)
            at = pl.ds(pl.multiple_of(c * part, part), part)
            return wgu_ref.at[:, at, :hidden], wgu_ref.at[:, at, hidden:]

        own_at = pl.ds(pl.multiple_of(ctx * hidden, hidden), hidden)
        ffn_own = pltpu.make_async_copy(gu_ref.at[:, :, own_at], ffn_ends(0)[0], ffn_local)
        ffn_own.start()
        down_copy = pair(d_ref, d_other_ref, 2)
        down_copy.start()

        total = sum_begin(me, slots, tot_send, tot_recv)()
        trickle = Trickle()
        trickle.add([lambda t=t, i=i: ffn_copy(t, i).start() for t in DEAL_ORDER for i in range(2)])
        trickle.tick(DEALT_FIRST)
        scales = lax.rsqrt(total / width + EPSILON)
        scale_ref[...] = scales

        def rotated(values, piece):
            return values * cos_ref[piece, :] + pltpu.roll(values, HD // 2, 1) * sin_ref[piece, :]

        for i in range(8):
            piece = slice(i * HD, (i + 1) * HD)
            factor = row_to_column(scales[8 + i : 9 + i, :], eye)
            keys_ref[piece, :] = rotated(k_in[piece, :] * factor * key_gain, piece).astype(BF)
        k_copy = pair(keys_ref.at[:tokens, :], keys_ref.at[other_half, :], 1)
        k_copy.start()
        for i in range(8):
            piece = slice(i * HD, (i + 1) * HD)
            factor = row_to_column(scales[i : i + 1, :], eye)
            qrot_ref[piece, :] = rotated(q_in[piece, :] * factor * query_gain, piece).astype(BF)
        v_copy.wait()
        k_copy.wait()

        def produce(zp):
            at = pl.ds(pl.multiple_of(zp * group, group), group)
            raw, allowed = masked_scores(
                qrot_ref[at, :], keys_ref[...], low_ref[at, :], high_ref[at, :], log_ref[...]
            )
            raw = jnp.where(allowed, raw, MASKED)
            top = jnp.max(raw, axis=1, keepdims=True)
            weights = jnp.exp(raw - top)
            total_weight = jnp.sum(weights, axis=1, keepdims=True)
            out = jnp.dot(weights.astype(BF), values_ref[...], preferred_element_type=F32)
            out = out * (1.0 / total_weight)
            o_ref[at, :] = out
            lse_ref[at, :] = top + jnp.log(total_weight)
            terms[at, :] = jnp.dot(
                out.astype(BF), wout_ref[...], preferred_element_type=F32
            ).astype(BF)

        def finish(strip, total):
            branch_ref[strip] = total
            h = source_ref[strip].astype(F32) + total * row_scale(total) * gain_ref[2:3, :]
            own_ref[strip] = h
            shard[strip] = h.astype(BF)

        settle = reduce_plane(
            me,
            terms,
            rows,
            rest[:N_REDUCE],
            TURNS_ATTENTION[0],
            produce,
            finish,
            lambda: leave(qrot_ref, keys_ref, values_ref, o_ref, lse_ref, scale_ref),
            lambda: trickle.tick(FORWARD_RATE, FORWARD_EVERY),
        )
        view = gather_view(full_ref, rows)
        keep = pltpu.make_async_copy(shard, view(own), local)
        keep.start()

        def share(t):
            src, dst = ffn_ends(t)
            return pltpu.make_async_remote_copy(
                src_ref=src,
                dst_ref=dst,
                send_sem=share_send.at[t],
                recv_sem=share_recv.at[t],
                device_id=sibling,
                device_id_type=MESH,
            )

        def ffn_landed(t):
            for i in range(2):
                src = ffn_ends(t)[0].at[i]
                pltpu.make_async_remote_copy(
                    src_ref=src,
                    dst_ref=src,
                    send_sem=ffn_send.at[i, t],
                    recv_sem=ffn_recv.at[i, t],
                    device_id=sibling,
                    device_id_type=MESH,
                ).wait_recv()

        gather_plane(
            me,
            shard,
            view,
            rest[N_REDUCE:],
            TURNS_ATTENTION[1],
            lambda step: leave(own_ref, branch_ref) if step == 0 else None,
            tick=lambda: trickle.tick(FORWARD_RATE, FORWARD_EVERY),
        )
        trickle.flush()
        ffn_own.wait()
        share(0).start()
        for t in DEAL_ORDER:
            ffn_landed(t)
            share(t).start()
        keep.wait()
        settle()
        for t in range(8):
            share(t).wait()
            for i in range(2):
                if t > 0:
                    ffn_copy(t, i).wait_send()
        down_copy.wait()

    shape = jax.ShapeDtypeStruct
    return comm_call(
        body,
        "attention_forward",
        1,
        (
            shape((tokens, width), BF),
            shape((rows, width), F32),
            shape((rows, width), F32),
            shape((2, width, 2 * hidden), BF),
            shape((hidden, width), BF),
            shape((tokens, HD), BF),
            shape((2 * tokens, HD), BF),
            shape((2 * tokens, HD), BF),
            shape((tokens, HD), F32),
            shape((tokens, 1), F32),
            shape((16, HD), F32),
        ),
        [VMEM] * 11 + [ANY, ANY],
        (ANY, VMEM, VMEM, ANY, ANY, VMEM, VMEM, VMEM, VMEM, VMEM, VMEM),
        [
            pltpu.VMEM((tokens, width), BF),
            pltpu.VMEM((rows, width), BF),
            pltpu.VMEM((16, 16, HD), F32),
            DMA((16,)),
            DMA((16,)),
            DMA((3,)),
            DMA((3,)),
            DMA,
            DMA((2, 8)),
            DMA((2, 8)),
            DMA((8,)),
            DMA((8,)),
            DMA,
            *reduce_scratch(rows, width),
            *GATHER_SEMS,
        ],
    )(query, key, value, *tables, *bounds, logical, source, out_weight, gains, gu_stage, down_own)


def ffn_forward(source, gu_w, down_w, residual, cotangent, gain):
    tokens, width = source.shape
    rows, group = tokens // 16, tokens // 4
    hidden = 2 * down_w[0].shape[0]

    def body(*refs, loaded, leave):
        (h_any, gu_any, d_any, d_any2, res_ref, cot_ref, gain_ref) = refs[:7]
        (full_ref, out_ref, gg_ref, for_gate_out, for_up_out, m_out) = refs[7:13]
        (hs, gu, dw, terms, shard, result, load_sem, local, out_send, out_recv) = refs[13:23]
        (for_gate_ref, for_up_ref, m_ref, leave_sem) = refs[23:27]
        scratch = refs[27:]
        me = z, y, x, k = place()

        def h_load(zp):
            at = pl.ds(pl.multiple_of(zp * group, group), group)
            return pltpu.make_async_copy(h_any.at[at, :], hs.at[at, :], load_sem.at[zp])

        order = [near_first(step, z) for step in (3, 2, 1, 0)]
        gu_load = pltpu.make_async_copy(gu_any, gu, load_sem.at[4])
        d_loads = [
            pltpu.make_async_copy(d_any, dw.at[: hidden // 2, :], load_sem.at[5]),
            pltpu.make_async_copy(d_any2, dw.at[hidden // 2 :, :], load_sem.at[6]),
        ]
        for load in (h_load(order[0]), gu_load, *d_loads):
            load.start()
        for zp in order[1:]:
            h_load(zp).start()
        greet_plane(me, pair_devices(me))
        loaded()
        gg_ref[...] = jnp.zeros_like(gg_ref)
        gu_load.wait()

        def leave(zp):
            at = pl.ds(pl.multiple_of(zp * group, group), group)
            pairs = ((for_gate_ref, for_gate_out), (for_up_ref, for_up_out), (m_ref, m_out))
            return [
                pltpu.make_async_copy(src.at[at, :], dst.at[at, :], leave_sem.at[i, zp])
                for i, (src, dst) in enumerate(pairs)
            ]

        def produce(zp):
            at = pl.ds(pl.multiple_of(zp * group, group), group)
            h_load(zp).wait()
            tile = hs[at, :]
            gate = jnp.dot(tile, gu[0], preferred_element_type=F32)
            up = jnp.dot(tile, gu[1], preferred_element_type=F32)
            sig = jax.nn.sigmoid(gate)
            silu = gate * sig
            mixed = (silu * up).astype(BF)
            for_gate_ref[at, :] = up * sig * (1.0 + gate * (1.0 - sig))
            for_up_ref[at, :] = silu
            m_ref[at, :] = mixed
            for copy in leave(zp):
                copy.start()
            terms[at, :] = jnp.dot(mixed, dw[...], preferred_element_type=F32).astype(BF)

        def finish(strip, total):
            gain_row = gain_ref[3:4, :]
            out = res_ref[strip] + total * row_scale(total) * gain_row
            result[strip] = out.astype(BF)
            back, term = norm_back_strip(cot_ref[strip].astype(F32), total, gain_row)
            gg_ref[...] += term
            shard[strip] = back.astype(BF)

        for load in d_loads:
            load.wait()
        settle = reduce_plane(me, terms, rows, scratch[:N_REDUCE], EVEN, produce, finish)
        view = gather_view(full_ref, rows)
        keep = pltpu.make_async_copy(shard, view(me[0] * 4 + me[1] * 2 + me[2]), local)
        keep.start()
        copies, own = hand_out_copies(me, result, out_ref, out_send, out_recv)
        for copy in copies:
            copy.start()
        own.start()
        gather_plane(me, shard, view, scratch[N_REDUCE:], EVEN)
        keep.wait()
        settle()
        for zp in range(4):
            for copy in leave(zp):
                copy.wait()
        own.wait()
        for copy in copies:
            copy.wait()

    shape = jax.ShapeDtypeStruct
    return comm_call(
        body,
        "ffn_forward",
        3,
        (
            shape((tokens, width), BF),
            shape((rows * 4, width // 4), BF),
            shape((8, width), F32),
            shape((tokens, hidden), F32),
            shape((tokens, hidden), F32),
            shape((tokens, hidden), BF),
        ),
        [ANY, ANY, ANY, ANY, VMEM, VMEM, VMEM],
        (ANY, ANY, VMEM, ANY, ANY, ANY),
        [
            pltpu.VMEM((tokens, width), BF),
            pltpu.VMEM((2, width, hidden), BF),
            pltpu.VMEM((hidden, width), BF),
            pltpu.VMEM((tokens, width), BF),
            pltpu.VMEM((rows, width), BF),
            pltpu.VMEM((rows, width), BF),
            DMA((7,)),
            DMA,
            DMA((3,)),
            DMA((4,)),
            pltpu.VMEM((tokens, hidden), F32),
            pltpu.VMEM((tokens, hidden), F32),
            pltpu.VMEM((tokens, hidden), BF),
            DMA((3, 4)),
            *reduce_scratch(rows, width),
            *GATHER_SEMS,
        ],
    )(source, gu_w, *down_w, residual, cotangent, gain)


EARLY = 5
GRADS_FIRST = 4


def grad_copies(me, src, dst, send, recv, t):
    ctx = own_tile(me)
    to = ctx + t - 8 * ((ctx + t) // 8)
    return [
        pltpu.make_async_remote_copy(
            src_ref=src.at[i],
            dst_ref=dst.at[ctx, i],
            send_sem=send.at[t, i],
            recv_sem=recv.at[t, i],
            device_id=(to // 2, to % 2, me[2], me[3]),
            device_id_type=MESH,
        )
        for i in range(3)
    ]


def grad_landed(me, dst, send, recv, t):
    ctx = own_tile(me)
    c = ctx + 8 - t - 8 * ((ctx + 8 - t) // 8)
    for i in range(3):
        pltpu.make_async_remote_copy(
            src_ref=dst.at[c, i],
            dst_ref=dst.at[c, i],
            send_sem=send.at[t, i],
            recv_sem=recv.at[t, i],
            device_id=(me[0], me[1], me[2], 1 - me[3]),
            device_id_type=MESH,
        ).wait_recv()


def ctx_greet(me, others):
    z, y, x, k = me
    barrier = pltpu.get_barrier_semaphore()

    def call(i, carry):
        to = lax.rem(z * 2 + y + i, 8)
        pl.semaphore_signal(
            barrier, inc=1, device_id=(to // 2, to % 2, x, k), device_id_type=MESH
        )
        return carry

    lax.fori_loop(1, 8, call, 0)
    for target in [(z, y, 1 - x, k), *others]:
        pl.semaphore_signal(barrier, inc=1, device_id=target, device_id_type=MESH)
    pl.semaphore_wait(barrier, 8 + len(others))


def ffn_backward(
    grad_ffn, source, gu_w, down_w, for_gate, for_up, mixed, cotangent, branch, gain, attention
):
    tokens, width = grad_ffn.shape
    rows, group = tokens // 16, tokens // 4
    hidden = 2 * down_w[0].shape[0]
    part = hidden // 2
    across = (((0,), (0,)), ((), ()))
    turned = (((1,), (1,)), ((), ()))
    scaling = 1.0 / math.sqrt(HD)

    def body(*refs, loaded, leave):
        (df_any, h_any, gu_any, d_any, d_any2, fg_any, fu_any, m_any, cot_ref, branch_ref, gain_ref) = refs[:11]
        (wout_ref, qrot_ref, keys_ref, values_ref, o_ref, lse_ref, low_ref, high_ref, log_ref) = refs[11:20]
        (full_ref, own_ref, gg_ref, in_ref, rest_ref, dq_ref, dk_ref, dv_ref) = refs[20:28]
        (df, hs, gu, dw, fg, fu, ms, dgu, terms, shard) = refs[28:38]
        (to_core, from_core, to_ctx) = refs[38:41]
        (da, dk_all, dv_all, pair_out, pair_in) = refs[41:46]
        (load_sem, local, core_send, core_recv, grad_send, grad_recv, rest_sem) = refs[46:53]
        (da_sem, pair_send, pair_recv) = refs[53:56]
        scratch = refs[56:]
        me = z, y, x, k = place()
        ctx = own_tile(me)
        order = [near_first(step, z) for step in (3, 2, 1, 0)]

        def group_load(zp):
            at = pl.ds(pl.multiple_of(zp * group, group), group)
            return [
                pltpu.make_async_copy(src.at[at, :], dst.at[at, :], load_sem.at[i, zp])
                for i, (src, dst) in enumerate(((df_any, df), (fg_any, fg), (fu_any, fu)))
            ]

        d_load = pltpu.make_async_copy(d_any, dw.at[:part, :], load_sem.at[3, 0])
        d_load2 = pltpu.make_async_copy(d_any2, dw.at[part:, :], load_sem.at[4, 0])
        gu_load = pltpu.make_async_copy(gu_any, gu, load_sem.at[3, 1])
        h_load = pltpu.make_async_copy(h_any, hs, load_sem.at[3, 2])
        m_load = pltpu.make_async_copy(m_any, ms, load_sem.at[3, 3])
        for load in (*group_load(order[0]), d_load, d_load2, gu_load):
            load.start()
        for zp in order[1:]:
            for load in group_load(zp):
                load.start()
        h_load.start()
        m_load.start()
        sibling = (z, y, x, 1 - k)
        ctx_greet(me, [sibling])
        loaded()
        gg_ref[...] = jnp.zeros_like(gg_ref)
        d_load.wait()
        d_load2.wait()

        def produce(zp):
            at = pl.ds(pl.multiple_of(zp * group, group), group)
            for load in group_load(zp):
                load.wait()
            dm = lax.dot_general(df[at, :], dw[...], turned, preferred_element_type=F32)
            dg = (dm * fg[at, :]).astype(BF)
            du = (dm * fu[at, :]).astype(BF)
            dgu[at, :hidden] = dg
            dgu[at, hidden:] = du
            terms[at, :] = (
                lax.dot_general(dg, gu[0], turned, preferred_element_type=F32)
                + lax.dot_general(du, gu[1], turned, preferred_element_type=F32)
            ).astype(BF)

        def finish(strip, total):
            grad = cot_ref[strip].astype(F32) + total
            own_ref[strip] = grad
            back, term = norm_back_strip(grad, branch_ref[strip], gain_ref[2:3, :])
            gg_ref[...] += term
            shard[strip] = back.astype(BF)

        def core_copy(t):
            return pltpu.make_async_remote_copy(
                src_ref=to_core.at[t],
                dst_ref=from_core.at[t],
                send_sem=core_send.at[t],
                recv_sem=core_recv.at[t],
                device_id=sibling,
                device_id_type=MESH,
            )

        parts = (*DEAL_ORDER, 0)

        def compute(n):
            t = parts[n]
            c = ctx + t - 8 * ((ctx + t) // 8)
            at = pl.ds(pl.multiple_of(c * part, part), part)
            up_like = lax.dot_general(hs[:, at], dgu[...], across, preferred_element_type=F32)
            down_like = lax.dot_general(ms[...], df[:, at], across, preferred_element_type=F32)
            for i in range(2):
                to_ctx[t, i] = up_like[:, 2 * i * part : (2 * i + 1) * part].astype(BF)
                to_core[t, i] = up_like[:, (2 * i + 1) * part : (2 * i + 2) * part].astype(BF)
            to_ctx[t, 2] = down_like[:part].astype(BF)
            to_core[t, 2] = down_like[part:].astype(BF)
            core_copy(t).start()

        trickle = Trickle()

        def send(n):
            t = parts[n]
            core_copy(t).wait_recv()
            to_ctx[t] = (to_ctx[t].astype(F32) + from_core[t].astype(F32)).astype(BF)
            if t == 0:
                pltpu.make_async_copy(to_ctx.at[0], in_ref.at[ctx], rest_sem.at[0]).start()
            elif n < EARLY:
                trickle.add(
                    [
                        copy.start
                        for copy in grad_copies(me, to_ctx.at[t], in_ref, grad_send, grad_recv, t)
                    ]
                )
            else:
                pltpu.make_async_copy(
                    to_ctx.at[t], rest_ref.at[n - EARLY], rest_sem.at[n - EARLY + 1]
                ).start()

        begun = []

        def next_part():
            n = len(begun)
            begun.append(n)
            if n < 8:
                compute(n)
            if BACK_LAG <= n < 8 + BACK_LAG:
                send(n - BACK_LAG)

        def tick():
            if begun:
                next_part()
            trickle.tick(BACK_RATE, BACK_EVERY)

        def da_load(step):
            at = pl.ds(pl.multiple_of(near_first(step, z) * group, group), group)
            return pltpu.make_async_copy(full_ref.at[at, :], da.at[step % 2], da_sem.at[step % 2])

        def attend_back(step):
            at = pl.ds(pl.multiple_of(near_first(step, z) * group, group), group)
            da_load(step).wait()
            grad = lax.dot_general(
                da[step % 2], wout_ref[...], turned, preferred_element_type=F32
            ).astype(BF)
            delta = jnp.sum(grad.astype(F32) * o_ref[at, :], axis=1, keepdims=True)
            q, low, high, lse = qrot_ref[at, :], low_ref[at, :], high_ref[at, :], lse_ref[at, :]
            dq_ref[at, :] = jnp.zeros((group, HD), F32)

            def work(key_at):
                key_part = keys_ref[key_at, :]
                raw, allowed = masked_scores(q, key_part, low, high, log_ref[:, key_at])
                weights = jnp.where(allowed, jnp.exp(raw - lse), 0.0)
                dp = lax.dot_general(
                    grad, values_ref[key_at, :], turned, preferred_element_type=F32
                )
                ds = (weights * (dp - delta)).astype(BF)
                dq_ref[at, :] += jnp.dot(ds, key_part, preferred_element_type=F32) * scaling
                dk_all[key_at, :] += (
                    lax.dot_general(ds, q, across, preferred_element_type=F32) * scaling
                )
                dv_all[key_at, :] += lax.dot_general(
                    weights.astype(BF), grad, across, preferred_element_type=F32
                )

            strips(2 * tokens, work, tokens)

        def arrived(step):
            if step == 0:
                keep.wait()
                dk_all[...] = jnp.zeros_like(dk_all)
                dv_all[...] = jnp.zeros_like(dv_all)
            da_load(step).start()
            if step > 0:
                attend_back(step - 1)

        def pair(n):
            return pltpu.make_async_remote_copy(
                src_ref=pair_out.at[n],
                dst_ref=pair_in.at[n],
                send_sem=pair_send.at[n],
                recv_sem=pair_recv.at[n],
                device_id=sibling,
                device_id_type=MESH,
            )

        def after_terms():
            h_load.wait()
            m_load.wait()
            for _ in range(GRADS_FIRST):
                next_part()

        gu_load.wait()
        settle = reduce_plane(
            me,
            terms,
            rows,
            scratch[:N_REDUCE],
            TURNS_FFN_BACK[0],
            produce,
            finish,
            after_terms,
            tick,
        )
        view = gather_view(full_ref, rows)
        keep = pltpu.make_async_copy(shard, view(me[0] * 4 + me[1] * 2 + me[2]), local)
        keep.start()
        gather_plane(
            me,
            shard,
            view,
            scratch[N_REDUCE:],
            TURNS_FFN_BACK[1],
            lambda step: leave(own_ref, gg_ref) if step == 0 else None,
            arrived,
            tick=tick,
            early=EARLY_LAYERS,
        )
        while len(begun) < 8 + BACK_LAG:
            next_part()
        trickle.flush()
        attend_back(3)
        pair_out[0] = dk_all[tokens:, :].astype(BF)
        pair_out[1] = dv_all[tokens:, :].astype(BF)
        pair(0).start()
        pair(1).start()
        settle()
        for n, (ref, source_ref) in enumerate(((dk_ref, dk_all), (dv_ref, dv_all))):
            pair(n).wait()
            ref[...] = source_ref[:tokens, :] + pair_in[n].astype(F32)
        for t in range(8):
            core_copy(t).wait_send()
        pltpu.make_async_copy(to_ctx.at[0], in_ref.at[ctx], rest_sem.at[0]).wait()
        for n, t in enumerate(DEAL_ORDER):
            if n < EARLY:
                grad_landed(me, in_ref, grad_send, grad_recv, t)
                for copy in grad_copies(me, to_ctx.at[t], in_ref, grad_send, grad_recv, t):
                    copy.wait_send()
            else:
                pltpu.make_async_copy(
                    to_ctx.at[t], rest_ref.at[n - EARLY], rest_sem.at[n - EARLY + 1]
                ).wait()

    shape = jax.ShapeDtypeStruct
    vmem = pltpu.VMEM
    return comm_call(
        body,
        "ffn_backward",
        4,
        (
            shape((tokens, width), BF),
            shape((rows, width), F32),
            shape((8, width), F32),
            shape((8, 3, part, part), BF),
            shape((7 - EARLY, 3, part, part), BF),
            shape((tokens, HD), F32),
            shape((tokens, HD), F32),
            shape((tokens, HD), F32),
        ),
        [*[ANY] * 8, *[VMEM] * 12],
        (ANY, VMEM, VMEM, ANY, ANY, VMEM, VMEM, VMEM),
        [
            vmem((tokens, width), BF),
            vmem((tokens, width), BF),
            vmem((2, width, hidden), BF),
            vmem((hidden, width), BF),
            vmem((tokens, hidden), F32),
            vmem((tokens, hidden), F32),
            vmem((tokens, hidden), BF),
            vmem((tokens, 2 * hidden), BF),
            vmem((tokens, width), BF),
            vmem((rows, width), BF),
            vmem((8, 3, part, part), BF),
            vmem((8, 3, part, part), BF),
            vmem((8, 3, part, part), BF),
            vmem((2, group, width), BF),
            vmem((2 * tokens, HD), F32),
            vmem((2 * tokens, HD), F32),
            vmem((2, tokens, HD), BF),
            vmem((2, tokens, HD), BF),
            DMA((5, 4)),
            DMA,
            DMA((8,)),
            DMA((8,)),
            DMA((8, 3)),
            DMA((8, 3)),
            DMA((8,)),
            DMA((2,)),
            DMA((2,)),
            DMA((2,)),
            *reduce_scratch(rows, width),
            *GATHER_SEMS,
        ],
    )(
        grad_ffn,
        source,
        gu_w,
        *down_w,
        for_gate,
        for_up,
        mixed,
        cotangent,
        branch,
        gain,
        *attention,
    )


def write_results(early, late, wall, outputs, input_grad, gains):
    part = early.shape[2]
    rows, columns = outputs.shape

    def body(*refs):
        (early_ref, late_ref, wall_ref, out_ref, in_ref, gain_ref) = refs[:6]
        (out_to, in_to, gq, gk, gv, go, gg, gu, gd) = refs[6:15]
        gains_to = refs[15:19]
        (blob, wall_in, wide, wall_wide, out_wide, load_sem, store_sem, wall_sem) = refs[19:]
        ctx = lax.axis_index("z") * 2 + lax.axis_index("y")
        loads, stores = [], []
        for n, t in enumerate((0, *DEAL_ORDER)):
            c = lax.rem(ctx + 8 - t, 8)
            source = early_ref if n <= EARLY else late_ref
            loads.append(pltpu.make_async_copy(source.at[c], blob.at[n], load_sem.at[n]))
            at = pl.ds(pl.multiple_of(c * part, part), part)
            ends = (gg.at[:, at], gu.at[:, at], gd.at[at, :])
            stores.append(
                [
                    pltpu.make_async_copy(wide.at[n, i], end, store_sem.at[n, i])
                    for i, end in enumerate(ends)
                ]
            )
        wall_load = pltpu.make_async_copy(wall_ref, wall_in, wall_sem.at[0])
        for copy in (*loads, wall_load):
            copy.start()
        for i, ref in enumerate(gains_to):
            ref[...] = gain_ref[i : i + 1, :]
        out_to[...] = out_ref[...]
        in_to[...] = in_ref[...]
        for n in range(8):
            loads[n].wait()
            for i in range(3):

                def work(strip, n=n, i=i):
                    wide[n, i, strip] = blob[n, i, strip].astype(F32)

                strips(part, work, 64)
                stores[n][i].start()
        wall_load.wait()
        for n in range(8):
            j, r = n // 2, n % 2
            for i in range(3):
                wall_wide[i, r * HD : (r + 1) * HD, j * HD : (j + 1) * HD] = wall_in[n, i].astype(F32)
            out_wide[j * HD : (j + 1) * HD, r * HD : (r + 1) * HD] = wall_in[n, 3].astype(F32)
        last = [
            pltpu.make_async_copy(wall_wide.at[i], ref, wall_sem.at[1 + i])
            for i, ref in enumerate((gq, gk, gv))
        ]
        last.append(pltpu.make_async_copy(out_wide, go, wall_sem.at[4]))
        for copy in last:
            copy.start()
        for copy in last:
            copy.wait()
        for group in stores:
            for copy in group:
                copy.wait()

    shape = jax.ShapeDtypeStruct
    vmem = pltpu.VMEM
    return pl.pallas_call(
        body,
        name="write_results",
        out_shape=(
            shape((rows, columns), BF),
            shape((rows, columns), BF),
            shape((2 * HD, 4 * HD), F32),
            shape((2 * HD, 4 * HD), F32),
            shape((2 * HD, 4 * HD), F32),
            shape((4 * HD, 2 * HD), F32),
            shape((part, 8 * part), F32),
            shape((part, 8 * part), F32),
            shape((8 * part, part), F32),
            *[shape((1, gains.shape[1]), F32)] * 4,
        ),
        in_specs=[ANY, ANY, ANY, VMEM, VMEM, VMEM],
        out_specs=(VMEM, VMEM, *[ANY] * 7, *[VMEM] * 4),
        scratch_shapes=[
            vmem((8, 3, part, part), BF),
            vmem((8, 4, HD, HD), BF),
            vmem((8, 3, part, part), F32),
            vmem((3, 2 * HD, 4 * HD), F32),
            vmem((4 * HD, 2 * HD), F32),
            DMA((8,)),
            DMA((8, 3)),
            DMA((5,)),
        ],
        compiler_params=pltpu.CompilerParams(vmem_limit_bytes=BIG_VMEM),
    )(early, late, wall, outputs, input_grad, gains)


def close_greet(me):
    z, y, x, k = me
    barrier = pltpu.get_barrier_semaphore()

    def plane(i, carry):
        pl.semaphore_signal(barrier, inc=1, device_id=plane_peer(me, i)[1], device_id_type=MESH)
        return carry

    def others(i, carry):
        pl.semaphore_signal(
            barrier, inc=1, device_id=(i // 2, i % 2, x, 1 - k), device_id_type=MESH
        )
        return carry

    lax.fori_loop(1, 16, plane, 0)
    lax.fori_loop(0, 8, others, 0)
    pl.semaphore_signal(barrier, inc=1, device_id=(z, y, 1 - x, 1 - k), device_id_type=MESH)
    pl.semaphore_wait(barrier, 24)


def attention_backward(
    grad_attn,
    full_in,
    query,
    key,
    attended,
    grads_rotated,
    tables,
    scales,
    gains,
    qkv_w,
    grad_own,
    attn_term,
    ffn_term,
    grads_left,
):
    tokens, width = grad_attn.shape
    rows, group = tokens // 16, tokens // 4
    part = width // 4

    def body(*refs, loaded, leave):
        (da_any, x_any) = refs[:2]
        (q_ref, k_ref, o_ref, dq_in, dk_in, dv_in, cos_ref, sin_ref) = refs[2:10]
        (scale_ref, gain_ref, wqkv_ref) = refs[10:13]
        (grad_ref, attn_ref, ffn_ref, left_ref) = refs[13:17]
        (in_grad_ref, deal_in, gains_ref, ffn_in) = refs[17:21]
        (da, xs, terms, dq_ref, dk_ref) = refs[21:26]
        (dqkv, slots, result) = refs[26:29]
        (qkv_grads, out_grads, wall_out, wall_in, deal_out) = refs[29:34]
        (gain_out, gain_in, gain_own, gain_slots) = refs[34:38]
        (load_sem, pair_send, pair_recv, tot_send, tot_recv, out_send, out_recv) = refs[38:45]
        (deal_send, deal_recv, gain_send, gain_recv, grad_send, grad_recv) = refs[45:51]
        scratch = refs[51:]
        me = z, y, x, k = place()
        ctx = own_tile(me)
        own = ctx * 2 + x
        own_head = pl.ds(pl.multiple_of((x * 8 + ctx) * HD, HD), HD)
        sibling = (z, y, x, 1 - k)

        da_load = pltpu.make_async_copy(da_any, da, load_sem.at[0])
        x_load = pltpu.make_async_copy(x_any, xs, load_sem.at[1])
        x_load.start()
        da_load.start()
        close_greet(me)
        loaded()

        trickle = Trickle()

        def left_copies(n):
            return grad_copies(me, left_ref.at[n - EARLY], ffn_in, grad_send, grad_recv, DEAL_ORDER[n])

        for n in range(EARLY, 7):
            trickle.add([copy.start for copy in left_copies(n)])
        trickle.tick(CLOSE_FIRST)

        def pair(n):
            return pltpu.make_async_remote_copy(
                src_ref=wall_out.at[n] if n < 8 else gain_out,
                dst_ref=wall_in.at[n] if n < 8 else gain_in,
                send_sem=pair_send.at[n],
                recv_sem=pair_recv.at[n],
                device_id=sibling,
                device_id_type=MESH,
            )

        across = (((0,), (0,)), ((), ()))
        eye = eye_mask()

        def normed_grad(values, piece):
            return values * cos_ref[piece, :] - pltpu.roll(values, HD // 2, 1) * sin_ref[piece, :]

        def side_dots(side, source, grads, proj):
            gain_sum = jnp.zeros((8, HD), F32)
            for i in range(8):
                piece = slice(i * HD, (i + 1) * HD)
                factor = row_to_column(scale_ref[side * 8 + i : side * 8 + i + 1, :], eye)
                back = normed_grad(source[piece, :], piece)
                term = back * proj[piece, :] * factor
                for j in range(0, HD, 8):
                    gain_sum = gain_sum + term[j : j + 8, :]
                weighted = back * gain_ref[side : side + 1, own_head]
                grads[piece, :] = weighted
                dot = jnp.sum(weighted * proj[piece, :], axis=1, keepdims=True)
                slots[own, side * 8 + i : side * 8 + i + 1, :] = column_to_row(dot, eye)
            return jnp.sum(gain_sum, axis=0, keepdims=True)

        query_gain = side_dots(0, dq_in, dq_ref, q_ref)
        key_gain = side_dots(1, dk_in, dk_ref, k_ref)
        sum_end = sum_begin(me, slots, tot_send, tot_recv)
        dqkv[:, 2 * HD :] = dv_in[...].astype(BF)

        attn_sum = jnp.sum(attn_ref[...], axis=0, keepdims=True)
        ffn_sum = jnp.sum(ffn_ref[...], axis=0, keepdims=True)
        head_core = z // 2
        head_at = pl.ds(pl.multiple_of(((z % 2) * 2 + y) * HD, HD), HD)
        for mine, target in ((True, gain_own), (False, gain_out)):
            target[...] = jnp.zeros_like(target)
            for xt in range(2):
                for kt in range(2):

                    @pl.when((kt == k) if mine else (kt != k))
                    def _(xt=xt, kt=kt, target=target):
                        block = slice((2 * xt + kt) * part, (2 * xt + kt + 1) * part)
                        target[xt, 2:3, :] = attn_sum[:, block]
                        target[xt, 3:4, :] = ffn_sum[:, block]

            @pl.when((head_core == k) if mine else (head_core != k))
            def _(target=target):
                target[x, 0:1, head_at] = query_gain
                target[x, 1:2, head_at] = key_gain

        pair(8).start()

        parts = (*DEAL_ORDER, 0)

        def columns_of(n):
            c = ctx + parts[n] - 8 * ((ctx + parts[n]) // 8)
            return pl.ds(pl.multiple_of(c * 2 * HD, 2 * HD), 2 * HD)

        attended_low = o_ref[...].astype(BF)
        da_load.wait()
        for n in range(8):
            out_grads[n] = lax.dot_general(
                attended_low, da[:, columns_of(n)], across, preferred_element_type=F32
            )
        total = sum_end()
        trickle.tick(CLOSE_NEXT)
        for side, grads, proj in ((0, dq_ref, q_ref), (1, dk_ref, k_ref)):
            for i in range(8):
                piece = slice(i * HD, (i + 1) * HD)
                row = scale_ref[side * 8 + i : side * 8 + i + 1, :]
                factor = row_to_column(row, eye)
                cubed = row * row * row * total[side * 8 + i : side * 8 + i + 1, :] / width
                dqkv[piece, side * HD : (side + 1) * HD] = (
                    factor * grads[piece, :] - proj[piece, :] * row_to_column(cubed, eye)
                ).astype(BF)

        def produce(zp):
            at = pl.ds(pl.multiple_of(zp * group, group), group)
            term = jnp.zeros((group, width), F32)
            for i in range(3):
                term = term + lax.dot_general(
                    dqkv[at, i * HD : (i + 1) * HD],
                    wqkv_ref[i],
                    (((1,), (1,)), ((), ())),
                    preferred_element_type=F32,
                )
            terms[at, :] = term.astype(BF)

        gain_copies = []

        def gain_copy(i):
            other, device = plane_peer(me, i)
            return pltpu.make_async_remote_copy(
                src_ref=gain_own.at[other % 2],
                dst_ref=gain_slots.at[own],
                send_sem=gain_send.at[i],
                recv_sem=gain_recv.at[own],
                device_id=device,
                device_id_type=MESH,
            )

        number = ((z % 2) * 2 + y) * 2 + k

        def deal(n):
            c = ctx + parts[n] - 8 * ((ctx + parts[n]) // 8)
            return pltpu.make_async_remote_copy(
                src_ref=deal_out.at[n],
                dst_ref=deal_in.at[number],
                send_sem=deal_send.at[n],
                recv_sem=deal_recv.at[number],
                device_id=(c // 2, c % 2, x, head_core),
                device_id_type=MESH,
            )

        stays = k == head_core

        def deal_start(n):
            if n < 7:
                deal(n).start()
                return

            @pl.when(jnp.logical_not(stays))
            def _():
                deal(n).start()

            @pl.when(stays)
            def _():
                pltpu.make_async_copy(
                    deal_out.at[n], deal_in.at[number], deal_recv.at[number]
                ).start()

        def after_terms():
            pair(8).wait_recv()
            gain_own[...] += gain_in[...]
            gain_slots[own] = gain_own[x]

            def begin(i, carry):
                gain_copy(i).start()
                return carry

            lax.fori_loop(1, 16, begin, 0)

        x_load.wait()
        begun = []

        def halves(n, r):
            rows_at = pl.ds(pl.multiple_of(r * HD, HD), HD)
            for i in range(3):
                yield i, qkv_grads[rows_at, i * HD : (i + 1) * HD]
            yield 3, out_grads[n, :, rows_at]

        def tick():
            n = len(begun)
            begun.append(n)
            if n < 8:
                qkv_grads[...] = lax.dot_general(
                    xs[:, columns_of(n)], dqkv[...], across, preferred_element_type=F32
                )
                for i, value in halves(n, 1 - k):
                    wall_out[n, i] = value.astype(BF)
                for i, value in halves(n, k):
                    deal_out[n, i] = value.astype(BF)
                pair(n).start()
            if CLOSE_LAG <= n < 8 + CLOSE_LAG:
                last = n - CLOSE_LAG
                pair(last).wait_recv()
                deal_out[last] = (deal_out[last].astype(F32) + wall_in[last].astype(F32)).astype(BF)
                deals.add([lambda: deal_start(last)])
            deals.tick()
            trickle.tick(CLOSE_RATE)

        deals = Trickle()

        def finish(strip, total):
            result[strip] = (grad_ref[strip] + total).astype(BF)

        settle = reduce_plane(
            me,
            terms,
            rows,
            scratch,
            TURNS_CLOSE,
            produce,
            finish,
            after_terms,
            tick,
        )
        while len(begun) < 8 + CLOSE_LAG:
            tick()
        deals.flush()
        trickle.flush()
        copies, own_copy = hand_out_copies(me, result, in_grad_ref, out_send, out_recv)
        for copy in copies:
            copy.start()
        own_copy.start()
        for n in range(8):
            pltpu.make_async_copy(deal_out.at[n], deal_in.at[n], deal_recv.at[n]).wait()

        def gain_landed(i, carry):
            other, device = plane_peer(me, i)
            pltpu.make_async_remote_copy(
                src_ref=gain_slots.at[other],
                dst_ref=gain_slots.at[other],
                send_sem=gain_send.at[i],
                recv_sem=gain_recv.at[other],
                device_id=device,
                device_id_type=MESH,
            ).wait_recv()
            gain_copy(i).wait_send()
            return carry

        lax.fori_loop(1, 16, gain_landed, 0)
        gain_total = gain_slots[0]
        for i in range(1, 16):
            gain_total = gain_total + gain_slots[i]
        gains_ref[...] = gain_total
        settle()
        own_copy.wait()
        for copy in copies:
            copy.wait()
        for n in range(7):
            deal(n).wait_send()

        @pl.when(jnp.logical_not(stays))
        def _():
            deal(7).wait_send()

        for n in range(9):
            pair(n).wait_send()
        for n in range(EARLY, 7):
            grad_landed(me, ffn_in, grad_send, grad_recv, DEAL_ORDER[n])
            for copy in left_copies(n):
                copy.wait_send()

    shape = jax.ShapeDtypeStruct
    vmem = pltpu.VMEM
    return comm_call(
        body,
        "attention_backward",
        5,
        (
            shape((rows * 4, part), BF),
            shape((8, 4, HD, HD), BF),
            shape((4, part), F32),
            shape((8, *grads_left.shape[1:]), BF),
        ),
        [ANY, ANY, *[VMEM] * 14, ANY],
        (ANY, ANY, VMEM, ANY),
        [
            vmem((tokens, width), BF),
            vmem((tokens, width), BF),
            vmem((tokens, width), BF),
            vmem((tokens, HD), F32),
            vmem((tokens, HD), F32),
            vmem((tokens, 3 * HD), BF),
            vmem((16, 16, HD), F32),
            vmem((rows, width), BF),
            vmem((2 * HD, 3 * HD), F32),
            vmem((8, HD, 2 * HD), F32),
            vmem((8, 4, HD, HD), BF),
            vmem((8, 4, HD, HD), BF),
            vmem((8, 4, HD, HD), BF),
            vmem((2, 4, part), F32),
            vmem((2, 4, part), F32),
            vmem((2, 4, part), F32),
            vmem((16, 4, part), F32),
            DMA((2,)),
            DMA((9,)),
            DMA((9,)),
            DMA((16,)),
            DMA((16,)),
            DMA((3,)),
            DMA((4,)),
            DMA((8,)),
            DMA((8,)),
            DMA((16,)),
            DMA((16,)),
            DMA((8, 3)),
            DMA((8, 3)),
            *reduce_scratch(rows, width),
        ],
    )(
        grad_attn,
        full_in,
        query,
        key,
        attended,
        *grads_rotated,
        *tables,
        scales,
        gains,
        qkv_w,
        grad_own,
        attn_term,
        ffn_term,
        grads_left,
    )


def plane_layer(
    inputs,
    cotangent,
    w_query,
    w_key,
    w_value,
    w_out,
    w_gate,
    w_up,
    w_down,
    query_gain,
    key_gain,
    attn_gain,
    ffn_gain,
    lengths,
    block_order,
):
    steps = np.arange(HD // 2, dtype=np.float64) * 2.0 / HD
    frequency = np.tile(np.power(ROPE_THETA, -steps), 2)[None, :].astype(np.float32)
    full_in, source_own, own_cot, qkv_w, out_w, gains_full, gu_stage, down_own, query_proj, key_proj, value_low, cosine, sine, low, high, logical_keys = open_layer(
        inputs,
        cotangent,
        w_query,
        w_key,
        w_value,
        w_out,
        w_gate,
        w_up,
        w_down,
        query_gain[None, :],
        key_gain[None, :],
        attn_gain[None, :],
        ffn_gain[None, :],
        block_order[None, :],
        lengths[None, :],
        jnp.asarray(frequency),
    )
    tables = (cosine, sine)
    (
        residual_full,
        residual_own,
        branch_own,
        gu_w,
        down_other,
        query_rot,
        keys_all,
        values_all,
        attended,
        lse,
        scales,
    ) = attention_forward(
        query_proj,
        key_proj,
        value_low,
        tables,
        (low, high),
        logical_keys,
        source_own,
        out_w,
        gains_full,
        gu_stage,
        down_own,
    )
    grad_ffn, outputs, ffn_gain_term, for_gate, for_up, mixed = ffn_forward(
        residual_full, gu_w, (down_own, down_other), residual_own, own_cot, gains_full
    )
    grad_attn, grad_own, attn_gain_term, ffn_early, ffn_left, *grads_rotated = ffn_backward(
        grad_ffn,
        residual_full,
        gu_w,
        (down_own, down_other),
        for_gate,
        for_up,
        mixed,
        own_cot,
        branch_own,
        gains_full,
        (out_w, query_rot, keys_all, values_all, attended, lse, low, high, logical_keys),
    )
    input_grad, wall_grads, gain_grads, ffn_late = attention_backward(
        grad_attn,
        full_in,
        query_proj,
        key_proj,
        attended,
        grads_rotated,
        tables,
        scales,
        gains_full,
        qkv_w,
        grad_own,
        attn_gain_term,
        ffn_gain_term,
        ffn_left,
    )
    results = write_results(ffn_early, ffn_late, wall_grads, outputs, input_grad, gain_grads)
    return (*results[:9], *[row[0] for row in results[9:]])


def full_rows(piece):
    return lax.all_gather(piece, "head", axis=1, tiled=True)


def head_sums(term):
    return lax.psum_scatter(
        term.astype(jnp.bfloat16), "head", scatter_dimension=1, tiled=True
    ).astype(jnp.float32)


def row_single(term):
    return lax.psum(term, "head")


def row_pair(first, second):
    return lax.psum((first, second), "head")


def gather_weights(w_query, w_key, w_value, w_out, w_gate, w_up, w_down):
    row_parts = (
        lax.all_gather(w_query.astype(jnp.bfloat16), "ctx", axis=0, tiled=True),
        lax.all_gather(w_key.astype(jnp.bfloat16), "ctx", axis=0, tiled=True),
        lax.all_gather(w_value.astype(jnp.bfloat16), "ctx", axis=0, tiled=True),
        lax.all_gather(w_gate.astype(jnp.bfloat16), "ctx", axis=0, tiled=True),
        lax.all_gather(w_up.astype(jnp.bfloat16), "ctx", axis=0, tiled=True),
    )
    col_parts = (
        lax.all_gather(w_out.astype(jnp.bfloat16), "ctx", axis=1, tiled=True),
        lax.all_gather(w_down.astype(jnp.bfloat16), "ctx", axis=1, tiled=True),
    )
    return tuple(row_parts) + tuple(col_parts)


def sequence_tables(logical, lengths):
    seq_ends = jnp.cumsum(lengths)
    seq_starts = seq_ends - lengths
    number = jnp.sum((logical[:, None] >= seq_ends[None, :]).astype(jnp.int32), axis=1)
    member = number[:, None] == jnp.arange(lengths.shape[0], dtype=jnp.int32)[None, :]
    offset = logical - jnp.sum(jnp.where(member, seq_starts[None, :], 0), axis=1)
    return (number, offset)


def rotate(values, offset):
    half_dim = HD // 2
    inverse = jnp.power(ROPE_THETA, -jnp.arange(half_dim, dtype=jnp.float32) * 2.0 / HD)
    angles = offset.astype(jnp.float32)[:, None] * inverse[None, :]
    cosine = jnp.cos(angles)[:, None, :]
    sine_part = jnp.sin(angles)[:, None, :]
    first_half = values[..., :half_dim]
    second_half = values[..., half_dim:]
    return jnp.concatenate(
        [
            first_half * cosine - second_half * sine_part,
            second_half * cosine + first_half * sine_part,
        ],
        axis=-1,
    )


def norm_backward(grad_in, values, factor, gain):
    gain_term = jnp.sum(grad_in * values * factor[:, None], axis=0)
    weighted = grad_in * gain
    row_dot = row_single(jnp.sum(weighted * values, axis=1))
    grad_values = (
        factor[:, None] * weighted - values * (factor * factor * factor * row_dot / D)[:, None]
    )
    return (grad_values, gain_term)


def on_device(
    inputs,
    cotangent,
    w_query,
    w_key,
    w_value,
    w_out,
    w_gate,
    w_up,
    w_down,
    query_gain,
    key_gain,
    attn_gain,
    ffn_gain,
    lengths,
    block_order,
):
    shards = lax.axis_size("ctx")
    position = lax.axis_index("ctx")
    tok_rows, width_part = inputs.shape
    block_rows = tok_rows // shards
    total_tokens = tok_rows * shards
    local_heads = width_part // HD
    scaling = 1.0 / math.sqrt(HD)
    shard_range = jnp.arange(shards, dtype=jnp.int32)
    order_table = block_order.reshape(shards, shards)
    target = order_table % shards
    choose = target[:, :, None] == shard_range[None, None, :]
    stream = jnp.sum(jnp.where(choose, order_table[:, :, None], 0), axis=1)
    stream_blocks = jnp.transpose(stream).reshape(-1)
    logical = (
        stream_blocks[:, None] * block_rows + jnp.arange(block_rows, dtype=jnp.int32)[None, :]
    ).reshape(-1)
    own_target = lax.dynamic_index_in_dim(target, position, 0, keepdims=False)
    send_order = jnp.sum(
        jnp.where(own_target[:, None] == shard_range[None, :], shard_range[:, None], 0), axis=0
    )

    def deal_out(values):
        return values.reshape(shards, block_rows, width_part)[send_order].reshape(
            tok_rows, width_part
        )

    def undeal(values):
        return values.reshape(shards, block_rows, width_part)[own_target].reshape(
            tok_rows, width_part
        )

    local_in, local_cot = (
        lax.all_to_all(deal_out(inputs), "ctx", split_axis=0, concat_axis=0, tiled=True),
        lax.all_to_all(deal_out(cotangent), "ctx", split_axis=0, concat_axis=0, tiled=True),
    )
    number_all, offset_all = sequence_tables(logical, lengths)
    number_own = lax.dynamic_slice_in_dim(number_all, position * tok_rows, tok_rows)
    offset_own = lax.dynamic_slice_in_dim(offset_all, position * tok_rows, tok_rows)
    logical_own = lax.dynamic_slice_in_dim(logical, position * tok_rows, tok_rows)
    query_full, key_full, value_full, gate_full, up_full, out_full, down_full = gather_weights(
        w_query, w_key, w_value, w_out, w_gate, w_up, w_down
    )
    full_in = full_rows(local_in)
    query_proj = jnp.dot(full_in, query_full, preferred_element_type=jnp.float32)
    key_proj = jnp.dot(full_in, key_full, preferred_element_type=jnp.float32)
    value_proj = jnp.dot(full_in, value_full, preferred_element_type=jnp.float32)
    query_sq, key_sq = row_pair(
        jnp.sum(query_proj * query_proj, axis=1), jnp.sum(key_proj * key_proj, axis=1)
    )
    query_scale = lax.rsqrt(query_sq / D + EPSILON)
    key_scale = lax.rsqrt(key_sq / D + EPSILON)
    query_rot = rotate(
        (query_proj * query_scale[:, None] * query_gain).reshape(tok_rows, local_heads, HD),
        offset_own,
    ).astype(jnp.bfloat16)
    key_rot = rotate(
        (key_proj * key_scale[:, None] * key_gain).reshape(tok_rows, local_heads, HD), offset_own
    ).astype(jnp.bfloat16)
    value_low = value_proj.astype(jnp.bfloat16).reshape(tok_rows, local_heads, HD)
    keys_all, values_all = (
        lax.all_gather(key_rot, "ctx", axis=0, tiled=True),
        lax.all_gather(value_low, "ctx", axis=0, tiled=True),
    )
    key_span = math.gcd(total_tokens, 1024)
    key_turns = total_tokens // key_span
    pieces = (
        keys_all.reshape(key_turns, key_span, local_heads, HD),
        values_all.reshape(key_turns, key_span, local_heads, HD),
        number_all.reshape(key_turns, key_span),
        logical.reshape(key_turns, key_span),
    )

    def scores_of(key_piece, number_piece, logical_piece):
        raw_scores = (
            jnp.einsum("qhd,khd->hqk", query_rot, key_piece, preferred_element_type=jnp.float32)
            * scaling
        )
        allowed = (number_own[:, None] == number_piece[None, :]) & (
            logical_piece[None, :] <= logical_own[:, None]
        )
        return (raw_scores, allowed)

    def stat_turn(running, piece_set):
        running_max, running_sum = running
        raw_scores, allowed = scores_of(piece_set[0], piece_set[2], piece_set[3])
        masked_scores = jnp.where(allowed[None], raw_scores, MASKED)
        new_max = jnp.maximum(running_max, jnp.max(masked_scores, axis=2))
        fresh = jnp.sum(
            jnp.where(allowed[None], jnp.exp(masked_scores - new_max[..., None]), 0.0), axis=2
        )
        return ((new_max, running_sum * jnp.exp(running_max - new_max) + fresh), None)

    start_max = jnp.full((local_heads, tok_rows), MASKED, jnp.float32)
    start_sum = jnp.zeros((local_heads, tok_rows), jnp.float32)
    final_max, final_sum = lax.scan(stat_turn, (start_max, start_sum), pieces)[0]
    log_total = final_max + jnp.log(final_sum)

    def out_turn(accum, piece_set):
        raw_scores, allowed = scores_of(piece_set[0], piece_set[2], piece_set[3])
        weights_low = jnp.where(
            allowed[None], jnp.exp(raw_scores - log_total[..., None]), 0.0
        ).astype(jnp.bfloat16)
        return (
            accum
            + jnp.einsum(
                "hqk,khd->qhd", weights_low, piece_set[1], preferred_element_type=jnp.float32
            ),
            None,
        )

    attended = lax.scan(out_turn, jnp.zeros((tok_rows, local_heads, HD), jnp.float32), pieces)[0]
    attended_low = attended.reshape(tok_rows, width_part).astype(jnp.bfloat16)
    attn_part = head_sums(jnp.dot(attended_low, out_full, preferred_element_type=jnp.float32))
    attn_scale = lax.rsqrt(row_single(jnp.sum(attn_part * attn_part, axis=1)) / D + EPSILON)
    residual = local_in.astype(jnp.float32) + attn_part * attn_scale[:, None] * attn_gain
    residual_full = full_rows(residual.astype(jnp.bfloat16))
    gate_proj = jnp.dot(residual_full, gate_full, preferred_element_type=jnp.float32)
    up_proj = jnp.dot(residual_full, up_full, preferred_element_type=jnp.float32)
    gate_sigmoid = jax.nn.sigmoid(gate_proj)
    mixed_hidden = (gate_proj * gate_sigmoid * up_proj).astype(jnp.bfloat16)
    ffn_part = head_sums(jnp.dot(mixed_hidden, down_full, preferred_element_type=jnp.float32))
    ffn_scale = lax.rsqrt(row_single(jnp.sum(ffn_part * ffn_part, axis=1)) / D + EPSILON)
    result = residual + ffn_part * ffn_scale[:, None] * ffn_gain
    query_full, key_full, value_full, gate_full, up_full, out_full, down_full = gather_weights(
        w_query, w_key, w_value, w_out, w_gate, w_up, w_down
    )
    grad_result = local_cot.astype(jnp.float32)
    grad_ffn, ffn_gain_term = norm_backward(grad_result, ffn_part, ffn_scale, ffn_gain)
    grad_ffn_low = full_rows(grad_ffn.astype(jnp.bfloat16))
    down_grad = jnp.einsum(
        "tf,td->fd", mixed_hidden, grad_ffn_low, preferred_element_type=jnp.float32
    )
    grad_mixed = jnp.einsum(
        "td,fd->tf", grad_ffn_low, down_full, preferred_element_type=jnp.float32
    )
    grad_gate_low = (
        grad_mixed * up_proj * gate_sigmoid * (1.0 + gate_proj * (1.0 - gate_sigmoid))
    ).astype(jnp.bfloat16)
    grad_up_low = (grad_mixed * gate_proj * gate_sigmoid).astype(jnp.bfloat16)
    gate_grad = jnp.einsum(
        "td,tf->df", residual_full, grad_gate_low, preferred_element_type=jnp.float32
    )
    up_grad = jnp.einsum(
        "td,tf->df", residual_full, grad_up_low, preferred_element_type=jnp.float32
    )
    resid_term = jnp.einsum(
        "tf,df->td", grad_gate_low, gate_full, preferred_element_type=jnp.float32
    ) + jnp.einsum("tf,df->td", grad_up_low, up_full, preferred_element_type=jnp.float32)
    grad_residual = grad_result + head_sums(resid_term)
    grad_attn, attn_gain_term = norm_backward(grad_residual, attn_part, attn_scale, attn_gain)
    grad_attn_low = full_rows(grad_attn.astype(jnp.bfloat16))
    out_grad = jnp.einsum(
        "te,td->ed", attended_low, grad_attn_low, preferred_element_type=jnp.float32
    )
    grad_heads = (
        jnp.einsum("td,ed->te", grad_attn_low, out_full, preferred_element_type=jnp.float32)
        .astype(jnp.bfloat16)
        .reshape(tok_rows, local_heads, HD)
    )
    row_delta = jnp.transpose(jnp.sum(grad_heads.astype(jnp.float32) * attended, axis=2))

    def score_grads(key_piece, value_piece, number_piece, logical_piece):
        raw_scores, allowed = scores_of(key_piece, number_piece, logical_piece)
        probabilities = jnp.where(allowed[None], jnp.exp(raw_scores - log_total[..., None]), 0.0)
        grad_probs = jnp.einsum(
            "qhd,khd->hqk", grad_heads, value_piece, preferred_element_type=jnp.float32
        )
        grad_scores = (probabilities * (grad_probs - row_delta[..., None])).astype(jnp.bfloat16)
        return (probabilities, grad_scores)

    zero_heads = jnp.zeros((tok_rows, local_heads, HD), jnp.float32)

    def back_turn(grad_acc, piece_set):
        key_piece, value_piece, number_piece, logical_piece = piece_set
        probabilities, grad_scores = score_grads(
            key_piece, value_piece, number_piece, logical_piece
        )
        grad_acc = (
            grad_acc
            + jnp.einsum("hqk,khd->qhd", grad_scores, key_piece, preferred_element_type=jnp.float32)
            * scaling
        )
        key_term = (
            jnp.einsum("hqk,qhd->khd", grad_scores, query_rot, preferred_element_type=jnp.float32)
            * scaling
        )
        value_term = jnp.einsum(
            "hqk,qhd->khd",
            probabilities.astype(jnp.bfloat16),
            grad_heads,
            preferred_element_type=jnp.float32,
        )
        return (grad_acc, (key_term, value_term))

    grad_query_rot, key_value_terms = lax.scan(back_turn, zero_heads, pieces)
    key_terms = key_value_terms[0].reshape(total_tokens, local_heads, HD)
    value_terms = key_value_terms[1].reshape(total_tokens, local_heads, HD)
    grad_key_rot, grad_value_own = (
        lax.psum_scatter(
            key_terms.astype(jnp.bfloat16), "ctx", scatter_dimension=0, tiled=True
        ).astype(jnp.float32),
        lax.psum_scatter(
            value_terms.astype(jnp.bfloat16), "ctx", scatter_dimension=0, tiled=True
        ).astype(jnp.float32),
    )
    grad_query_normed = rotate(grad_query_rot, -offset_own).reshape(tok_rows, width_part)
    grad_key_normed = rotate(grad_key_rot, -offset_own).reshape(tok_rows, width_part)
    query_gain_term = jnp.sum(grad_query_normed * query_proj * query_scale[:, None], axis=0)
    key_gain_term = jnp.sum(grad_key_normed * key_proj * key_scale[:, None], axis=0)
    weighted_query = grad_query_normed * query_gain
    weighted_key = grad_key_normed * key_gain
    query_dot, key_dot = row_pair(
        jnp.sum(weighted_query * query_proj, axis=1), jnp.sum(weighted_key * key_proj, axis=1)
    )
    grad_query_low = (
        query_scale[:, None] * weighted_query
        - query_proj * (query_scale * query_scale * query_scale * query_dot / D)[:, None]
    ).astype(jnp.bfloat16)
    grad_key_low = (
        key_scale[:, None] * weighted_key
        - key_proj * (key_scale * key_scale * key_scale * key_dot / D)[:, None]
    ).astype(jnp.bfloat16)
    grad_value_low = grad_value_own.reshape(tok_rows, width_part).astype(jnp.bfloat16)
    query_grad = jnp.einsum(
        "td,te->de", full_in, grad_query_low, preferred_element_type=jnp.float32
    )
    key_grad = jnp.einsum("td,te->de", full_in, grad_key_low, preferred_element_type=jnp.float32)
    value_grad = jnp.einsum(
        "td,te->de", full_in, grad_value_low, preferred_element_type=jnp.float32
    )
    input_term = jnp.einsum(
        "te,de->td", grad_query_low, query_full, preferred_element_type=jnp.float32
    )
    input_term = input_term + jnp.einsum(
        "te,de->td", grad_key_low, key_full, preferred_element_type=jnp.float32
    )
    input_term = input_term + jnp.einsum(
        "te,de->td", grad_value_low, value_full, preferred_element_type=jnp.float32
    )
    grad_input = grad_residual + head_sums(input_term)
    row_grads = (
        lax.psum_scatter(
            query_grad.astype(jnp.bfloat16), "ctx", scatter_dimension=0, tiled=True
        ).astype(jnp.float32),
        lax.psum_scatter(
            key_grad.astype(jnp.bfloat16), "ctx", scatter_dimension=0, tiled=True
        ).astype(jnp.float32),
        lax.psum_scatter(
            value_grad.astype(jnp.bfloat16), "ctx", scatter_dimension=0, tiled=True
        ).astype(jnp.float32),
        lax.psum_scatter(
            gate_grad.astype(jnp.bfloat16), "ctx", scatter_dimension=0, tiled=True
        ).astype(jnp.float32),
        lax.psum_scatter(
            up_grad.astype(jnp.bfloat16), "ctx", scatter_dimension=0, tiled=True
        ).astype(jnp.float32),
    )
    col_grads = (
        lax.psum_scatter(
            out_grad.astype(jnp.bfloat16), "ctx", scatter_dimension=1, tiled=True
        ).astype(jnp.float32),
        lax.psum_scatter(
            down_grad.astype(jnp.bfloat16), "ctx", scatter_dimension=1, tiled=True
        ).astype(jnp.float32),
    )
    gain_totals = lax.psum((query_gain_term, key_gain_term, attn_gain_term, ffn_gain_term), "ctx")
    back_result, back_grad = (
        lax.all_to_all(result.astype(jnp.bfloat16), "ctx", split_axis=0, concat_axis=0, tiled=True),
        lax.all_to_all(
            grad_input.astype(jnp.bfloat16), "ctx", split_axis=0, concat_axis=0, tiled=True
        ),
    )
    return (
        undeal(back_result),
        undeal(back_grad),
        row_grads[0],
        row_grads[1],
        row_grads[2],
        col_grads[0],
        row_grads[3],
        row_grads[4],
        col_grads[1],
        gain_totals[0],
        gain_totals[1],
        gain_totals[2],
        gain_totals[3],
    )


def sharded(layer, mesh, ctx, head):
    wide, tall, line = P(ctx, head), P(head, ctx), P(head)
    return jax.shard_map(
        layer,
        mesh=mesh,
        in_specs=(
            *(wide,) * 5,
            tall,
            wide,
            wide,
            tall,
            *(line,) * 4,
            P(),
            P(),
        ),
        out_specs=(*(wide,) * 5, tall, wide, wide, tall, *(line,) * 4),
        check_vma=False,
    )


def solution(mesh):
    if dict(mesh.shape) == {"ctx": 8, "head": 4}:
        split = Mesh(mesh.devices.reshape(4, 2, 2, 2), AXES)
        return sharded(plane_layer, split, CTX, ("x", "core"))
    return sharded(on_device, mesh, "ctx", "head")
```
